32 devices in a mesh: pipe: 2 (over core), grp: 4 (over y, x), dp: 4 (over z).
Axes of the slice: x: 2, y: 2, z: 4, core: 2. Of those that a mesh axis runs over, the one named last changes fastest.
Arguments:
- token_ids: int32 [64, 512], P(('grp', 'dp')), may hold values from 0 to 30521
- lengths: int32 [64], P(('grp', 'dp')), may hold values from 1 to 512, as said below
- masked_at: int32 [64, 64], P(('grp', 'dp')), may hold values from 0 to 511, as said below
- labels: int32 [64, 64], P(('grp', 'dp')), may hold values from 0 to 30521
- word_table: float32 [30720, 1024], P(('pipe', 'grp', 'dp')), may hold values from -0.36 to 0.36
- word_first: float32 [30720, 1024], P(('pipe', 'grp', 'dp')), may hold values from -1.9073486e-06 to 1.9073486e-06
- word_second: float32 [30720, 1024], P(('pipe', 'grp', 'dp')), may hold values from 8.798889e-15 to 3.5195557e-14
- pos_table: float32 [512, 1024], P(None, ('pipe', 'grp', 'dp')), may hold values from -0.36 to 0.36
- pos_first: float32 [512, 1024], P(None, ('pipe', 'grp', 'dp')), may hold values from -1.9073486e-06 to 1.9073486e-06
- pos_second: float32 [512, 1024], P(None, ('pipe', 'grp', 'dp')), may hold values from 8.798889e-15 to 3.5195557e-14
- qkv_weight: float32 [1024, 3072], P(('pipe', 'grp', 'dp')), may hold values from -0.1875 to 0.1875
- qkv_first: float32 [1024, 3072], P(('pipe', 'grp', 'dp')), may hold values from -1.9073486e-06 to 1.9073486e-06
- qkv_second: float32 [1024, 3072], P(('pipe', 'grp', 'dp')), may hold values from 8.798889e-15 to 3.5195557e-14
- square_weight: float32 [2, 1024, 1024], P(None, ('pipe', 'grp', 'dp')), may hold values from -0.5 to 0.5
- square_first: float32 [2, 1024, 1024], P(None, ('pipe', 'grp', 'dp')), may hold values from -1.9073486e-06 to 1.9073486e-06
- square_second: float32 [2, 1024, 1024], P(None, ('pipe', 'grp', 'dp')), may hold values from 8.798889e-15 to 3.5195557e-14
- up_weight: float32 [1024, 4096], P(('pipe', 'grp', 'dp')), may hold values from -0.1875 to 0.1875
- up_first: float32 [1024, 4096], P(('pipe', 'grp', 'dp')), may hold values from -1.9073486e-06 to 1.9073486e-06
- up_second: float32 [1024, 4096], P(('pipe', 'grp', 'dp')), may hold values from 8.798889e-15 to 3.5195557e-14
- down_weight: float32 [4096, 1024], P(('pipe', 'grp', 'dp')), may hold values from -0.09375 to 0.09375
- down_first: float32 [4096, 1024], P(('pipe', 'grp', 'dp')), may hold values from -1.9073486e-06 to 1.9073486e-06
- down_second: float32 [4096, 1024], P(('pipe', 'grp', 'dp')), may hold values from 8.798889e-15 to 3.5195557e-14
- vec_table: float32 [19, 1024], P(None, ('pipe', 'grp', 'dp')), may hold values from -1.9 to 1.9
- vec_first: float32 [19, 1024], P(None, ('pipe', 'grp', 'dp')), may hold values from -1.9073486e-06 to 1.9073486e-06
- vec_second: float32 [19, 1024], P(None, ('pipe', 'grp', 'dp')), may hold values from 8.798889e-15 to 3.5195557e-14
- head_bias: float32 [30522], replicated, may hold values from -3 to 3
- bias_first: float32 [30522], replicated, may hold values from -1.9073486e-06 to 1.9073486e-06
- bias_second: float32 [30522], replicated, may hold values from 8.798889e-15 to 3.5195557e-14
Outputs:
- word_new: float32 [30720, 1024], P(('pipe', 'grp', 'dp'))
- word_first_new: float32 [30720, 1024], P(('pipe', 'grp', 'dp'))
- word_second_new: float32 [30720, 1024], P(('pipe', 'grp', 'dp'))
- pos_new: float32 [512, 1024], P(None, ('pipe', 'grp', 'dp'))
- pos_first_new: float32 [512, 1024], P(None, ('pipe', 'grp', 'dp'))
- pos_second_new: float32 [512, 1024], P(None, ('pipe', 'grp', 'dp'))
- qkv_new: float32 [1024, 3072], P(('pipe', 'grp', 'dp'))
- qkv_first_new: float32 [1024, 3072], P(('pipe', 'grp', 'dp'))
- qkv_second_new: float32 [1024, 3072], P(('pipe', 'grp', 'dp'))
- square_new: float32 [2, 1024, 1024], P(None, ('pipe', 'grp', 'dp'))
- square_first_new: float32 [2, 1024, 1024], P(None, ('pipe', 'grp', 'dp'))
- square_second_new: float32 [2, 1024, 1024], P(None, ('pipe', 'grp', 'dp'))
- up_new: float32 [1024, 4096], P(('pipe', 'grp', 'dp'))
- up_first_new: float32 [1024, 4096], P(('pipe', 'grp', 'dp'))
- up_second_new: float32 [1024, 4096], P(('pipe', 'grp', 'dp'))
- down_new: float32 [4096, 1024], P(('pipe', 'grp', 'dp'))
- down_first_new: float32 [4096, 1024], P(('pipe', 'grp', 'dp'))
- down_second_new: float32 [4096, 1024], P(('pipe', 'grp', 'dp'))
- vec_new: float32 [19, 1024], P(None, ('pipe', 'grp', 'dp'))
- vec_first_new: float32 [19, 1024], P(None, ('pipe', 'grp', 'dp'))
- vec_second_new: float32 [19, 1024], P(None, ('pipe', 'grp', 'dp'))
- bias_new: float32 [30522], replicated
- bias_first_new: float32 [30522], replicated
- bias_second_new: float32 [30522], replicated
- loss_sum: float32 [], replicated
- masked_count: float32 [], replicated
- grad_norm: float32 [], replicated
The draws below stay inside these ranges and needn't reach their ends.
Inputs may be any that keep to these rules, and one draw needn't show every extreme that they name: `lengths`: sequence 0 is 512 long; the others lie between 1 and 512. `masked_at`: every position lies below its sequence's length; the first masked slot of sequence 0 is position 511.
All inputs are finite; a program needn't handle non-finite values.
Results may differ from the reference program's by a relative error of at most 0.012.
The reference program's roundings to bfloat16 on the way count: a program that leaves them out, or rounds other values in their place, can miss the bound.
Values may be sent and summed in bfloat16 or wider, within the bound.
A program may use at most 512 MiB of HBM per device.

```python
import jax
import jax.numpy as jnp
from jax import lax

D = 1024
H = 16
FF = 4096
V = 30522
L = 512
MP = 64
MB = 4
STEP = 10
SEQS = 64
VP = 30720
R = 19
NPARAM = 45460282
N_DP = 4


def shared_lengths(key):
    first_key, second_key = jax.random.split(key)
    sequence = jnp.arange(SEQS, dtype=jnp.int32)
    level = sequence // MB % N_DP
    lowest = L // 5
    ceiling = lowest + (L - lowest) * level // max(N_DP - 1, 1)
    shrink = 2 ** jax.random.randint(first_key, (SEQS,), 0, 3)
    extra = jax.random.randint(second_key, (SEQS,), 1, L // 32 + 2)
    value = jnp.clip(ceiling // shrink + extra, 1, L)
    return jnp.where(sequence == 0, L, value).astype(jnp.int32)


def draw_lengths(key, part):
    return shared_lengths(key)


def draw_masked_at(key, part):
    lengths = shared_lengths(key)
    key = jax.random.fold_in(key, 5)
    positions = jax.random.randint(key, (SEQS, MP), 0, lengths[:, None]).astype(jnp.int32)
    return positions.at[0, 0].set(L - 1).astype(jnp.int32)


def draw_vec_table(key, part):
    key = jax.random.fold_in(key, 7)
    first_key, second_key = jax.random.split(key)
    rising = 0.5 + jnp.arange(D, dtype=jnp.float32) / D
    base = jax.random.normal(first_key, (R, D), jnp.float32)
    factor = jax.random.uniform(second_key, (R, D), jnp.float32, 0.8, 1.2)
    rows = jnp.arange(R)[:, None]
    is_gain = (rows == 2) | (rows == 7) | (rows == 10) | (rows == 13)
    value = jnp.where(is_gain, rising * factor, jnp.where(rows < 2, 0.06 * base, 0.2 * base))
    return jnp.clip(value, -1.9, 1.9).astype(jnp.float32)


def touch_ends(drawn, stream_key, low, largest):
    index_at = [jax.random.randint(jax.random.fold_in(stream_key, axis), (), 0, length) for axis, length in enumerate(drawn.shape)]
    longest = drawn.shape.index(max(drawn.shape))
    neighbour = index_at[:longest] + [(index_at[longest] + 1) % drawn.shape[longest]] + index_at[longest + 1:]
    return drawn.at[tuple(index_at)].set(low).at[tuple(neighbour)].set(largest)


def block_levels(rng, extent, cuts, smallest, largest):
    loudness, own = 1.0, jax.random.fold_in(rng, 6)
    for axis_at, parts in cuts:
        steps = jnp.exp(jax.random.uniform(jax.random.fold_in(own, axis_at), (parts,), jnp.float32, smallest / len(cuts), largest / len(cuts)))
        loudness = loudness * jnp.repeat(steps, extent[axis_at] // parts).reshape([-1 if axis == axis_at else 1 for axis in range(len(extent))])
    return loudness


def gaussian(stream_key, extent, deviation, most, shards=(), held_as=jnp.bfloat16):
    array = jax.random.normal(stream_key, extent, jnp.float32) * deviation
    if len(shards) > 0:
        array = block_levels(stream_key, extent, shards, -0.22, 0.18) * array
    return jnp.clip(array, min=-most, max=most).astype(held_as)


def setup_inputs(seed: int = 0) -> dict:
    key_of = jax.random.split(jax.random.key(seed), 29)
    return {
        "token_ids": touch_ends(jax.random.randint(key_of[0], (SEQS, L), 0, V), jax.random.fold_in(key_of[0], 1), 0, V - 1).astype(jnp.int32),
        "lengths": draw_lengths(jax.random.fold_in(key_of[28], 71), 0),
        "masked_at": draw_masked_at(jax.random.fold_in(key_of[28], 71), 0),
        "labels": touch_ends(jax.random.randint(key_of[3], (SEQS, MP), 0, V), jax.random.fold_in(key_of[3], 1), 0, V - 1).astype(jnp.int32),
        "word_table": gaussian(key_of[4], (VP, D), 0.06, 0.36, ((0, 32),), jnp.float32),
        "word_first": gaussian(key_of[5], (VP, D), (0.0022 / NPARAM ** 0.5), 1.9073486328125e-06, ((0, 32),), jnp.float32),
        "word_second": jnp.clip(8.79888931761821e-15 + 2.639666795285463e-14 * jax.random.uniform(key_of[6], (VP, D), jnp.float32) ** block_levels(key_of[6], (VP, D), ((0, 32),), -0.2, 0.2), 8.79888931761821e-15, 3.519555727047284e-14),
        "pos_table": gaussian(key_of[7], (L, D), 0.06, 0.36, ((1, 32),), jnp.float32),
        "pos_first": gaussian(key_of[8], (L, D), (0.0022 / NPARAM ** 0.5), 1.9073486328125e-06, ((1, 32),), jnp.float32),
        "pos_second": jnp.clip(8.79888931761821e-15 + 2.639666795285463e-14 * jax.random.uniform(key_of[9], (L, D), jnp.float32) ** block_levels(key_of[9], (L, D), ((1, 32),), -0.2, 0.2), 8.79888931761821e-15, 3.519555727047284e-14),
        "qkv_weight": gaussian(key_of[10], (D, 3 * D), D ** -0.5, 0.1875, ((0, 32),), jnp.float32),
        "qkv_first": gaussian(key_of[11], (D, 3 * D), (0.0022 / NPARAM ** 0.5), 1.9073486328125e-06, ((0, 32),), jnp.float32),
        "qkv_second": jnp.clip(8.79888931761821e-15 + 2.639666795285463e-14 * jax.random.uniform(key_of[12], (D, 3 * D), jnp.float32) ** block_levels(key_of[12], (D, 3 * D), ((0, 32),), -0.2, 0.2), 8.79888931761821e-15, 3.519555727047284e-14),
        "square_weight": gaussian(key_of[13], (2, D, D), (D // 8) ** -0.5, 0.5, ((1, 32),), jnp.float32),
        "square_first": gaussian(key_of[14], (2, D, D), (0.0022 / NPARAM ** 0.5), 1.9073486328125e-06, ((1, 32),), jnp.float32),
        "square_second": jnp.clip(8.79888931761821e-15 + 2.639666795285463e-14 * jax.random.uniform(key_of[15], (2, D, D), jnp.float32) ** block_levels(key_of[15], (2, D, D), ((1, 32),), -0.2, 0.2), 8.79888931761821e-15, 3.519555727047284e-14),
        "up_weight": gaussian(key_of[16], (D, FF), D ** -0.5, 0.1875, ((0, 32),), jnp.float32),
        "up_first": gaussian(key_of[17], (D, FF), (0.0022 / NPARAM ** 0.5), 1.9073486328125e-06, ((0, 32),), jnp.float32),
        "up_second": jnp.clip(8.79888931761821e-15 + 2.639666795285463e-14 * jax.random.uniform(key_of[18], (D, FF), jnp.float32) ** block_levels(key_of[18], (D, FF), ((0, 32),), -0.2, 0.2), 8.79888931761821e-15, 3.519555727047284e-14),
        "down_weight": gaussian(key_of[19], (FF, D), FF ** -0.5, 0.09375, ((0, 32),), jnp.float32),
        "down_first": gaussian(key_of[20], (FF, D), (0.0022 / NPARAM ** 0.5), 1.9073486328125e-06, ((0, 32),), jnp.float32),
        "down_second": jnp.clip(8.79888931761821e-15 + 2.639666795285463e-14 * jax.random.uniform(key_of[21], (FF, D), jnp.float32) ** block_levels(key_of[21], (FF, D), ((0, 32),), -0.2, 0.2), 8.79888931761821e-15, 3.519555727047284e-14),
        "vec_table": draw_vec_table(jax.random.fold_in(key_of[28], 71), 0),
        "vec_first": gaussian(key_of[23], (R, D), (0.0022 / NPARAM ** 0.5), 1.9073486328125e-06, ((1, 32),), jnp.float32),
        "vec_second": jnp.clip(8.79888931761821e-15 + 2.639666795285463e-14 * jax.random.uniform(key_of[24], (R, D), jnp.float32) ** block_levels(key_of[24], (R, D), ((1, 32),), -0.2, 0.2), 8.79888931761821e-15, 3.519555727047284e-14),
        "head_bias": gaussian(key_of[25], (V,), 0.5, 3.0, (), jnp.float32),
        "bias_first": gaussian(key_of[26], (V,), (0.0022 / NPARAM ** 0.5), 1.9073486328125e-06, (), jnp.float32),
        "bias_second": jnp.clip(jax.random.uniform(key_of[27], (V,), jnp.float32, 8.79888931761821e-15, 3.519555727047284e-14), 8.79888931761821e-15, 3.519555727047284e-14),
    }


@jax.custom_vjp
def low(v):
    return lax.optimization_barrier(v.astype(jnp.bfloat16)).astype(jnp.float32)

@jax.custom_vjp
def low_back(v):
    return v

def low_keep(v):
    return (low(v), None)

def low_pass(kept, grad):
    return (grad,)

def back_keep(v):
    return (v, None)

def back_low(kept, grad):
    return (low(grad),)
low.defvjp(low_keep, low_pass)
low_back.defvjp(back_keep, back_low)
highest = lax.Precision.HIGHEST
beta_one = 0.9
beta_two = 0.999
learn_rate = 0.02
vector_rate = 0.2
weight_decay = 0.01
epsilon = 1e-08
clip_norm = 0.02
norm_eps = 1e-05

def matmul(left, right):
    return jnp.dot(left, right, precision=highest)

def layer_norm(values, gain, shift):
    center = values - lax.optimization_barrier(jnp.mean(values, -1, keepdims=True))
    spread = lax.optimization_barrier(jnp.mean(center * center, -1, keepdims=True))
    return center * lax.rsqrt(spread + norm_eps) * gain + shift

def masked_counts(lengths, slots):
    return jnp.minimum(slots, (3 * lengths + 19) // 20).astype(jnp.int32)

def section_one(word_rows, pos_rows, qkv_matrix, out_matrix, vec_rows, length):
    seq_len, width = word_rows.shape
    places = jnp.arange(seq_len, dtype=jnp.int32)
    second = (places >= (length + 1) // 2)[:, None]
    embedded = word_rows + pos_rows + jnp.where(second, vec_rows[1], vec_rows[0])
    normed = layer_norm(embedded, vec_rows[2], vec_rows[3])
    proj_bias = jnp.concatenate([vec_rows[4], jnp.zeros_like(vec_rows[4]), vec_rows[5]])
    joined = low_back(low(matmul(low(normed), qkv_matrix) + proj_bias))
    heads = joined.reshape(seq_len, 3, H, width // H)
    queries, key_rows, value_rows = (heads[:, 0], heads[:, 1], heads[:, 2])
    scores = jnp.einsum('qhd,khd->hqk', queries, key_rows, precision=highest) * (width // H) ** (-0.5)
    scores = low_back(scores)
    key_live = (places < length)[None, None, :]
    scores = jnp.where(key_live, scores, -1e+30)
    row_peak = lax.optimization_barrier(jnp.max(scores, -1, keepdims=True))
    exp_scores = jnp.exp(scores - row_peak)
    probs = exp_scores / lax.optimization_barrier(jnp.sum(exp_scores, -1, keepdims=True))
    context = jnp.einsum('hqk,khd->qhd', low(probs), value_rows, precision=highest).reshape(seq_len, width)
    context = low_back(low(context))
    branch = low_back(matmul(context, out_matrix) + vec_rows[6])
    return layer_norm(normed + branch, vec_rows[7], vec_rows[8])

def section_two(hidden, places, up_matrix, down_matrix, turn_matrix, vec_rows):
    up_bias = vec_rows[15:].reshape(-1)
    inner = low_back(matmul(hidden, up_matrix) + up_bias)
    activ = low(jax.nn.gelu(inner, approximate=False))
    branch = low_back(matmul(activ, down_matrix) + vec_rows[9])
    mixed = layer_norm(hidden + branch, vec_rows[10], vec_rows[11])
    picked = jnp.take(mixed, places, axis=0)
    turned = low_back(matmul(low(picked), turn_matrix) + vec_rows[12])
    return layer_norm(jax.nn.gelu(turned, approximate=False), vec_rows[13], vec_rows[14])

def head_loss(normed, word_rows, bias_row, targets, count):
    logits = low_back(matmul(low(normed), word_rows.T)) + bias_row
    row_peak = lax.optimization_barrier(jnp.max(logits, -1, keepdims=True))
    log_total = row_peak[:, 0] + jnp.log(lax.optimization_barrier(jnp.sum(jnp.exp(logits - row_peak), -1)))
    hits = jnp.arange(logits.shape[1])[None, :] == targets[:, None]
    picked = lax.optimization_barrier(jnp.sum(jnp.where(hits, logits, 0.0), -1))
    valid = (jnp.arange(targets.shape[0]) < count).astype(jnp.float32)
    return jnp.sum(valid * (log_total - picked))

def adam_step(weight, first, second, grad, factor, rate):
    clipped = grad * factor
    first = beta_one * first + (1.0 - beta_one) * clipped
    second = beta_two * second + (1.0 - beta_two) * clipped * clipped
    first_hat = first / (1.0 - beta_one ** STEP)
    second_hat = second / (1.0 - beta_two ** STEP)
    weight = weight - rate * (first_hat / (jnp.sqrt(second_hat) + epsilon) + weight_decay * weight)
    return (weight, first, second)

def reference(token_ids, lengths, masked_at, labels, word_table, word_first, word_second, pos_table, pos_first, pos_second, qkv_weight, qkv_first, qkv_second, square_weight, square_first, square_second, up_weight, up_first, up_second, down_weight, down_first, down_second, vec_table, vec_first, vec_second, head_bias, bias_first, bias_second):
    counts = masked_counts(lengths, masked_at.shape[1])
    total = jnp.sum(counts).astype(jnp.float32)
    params = (word_table, pos_table, qkv_weight, square_weight, up_weight, down_weight, vec_table, head_bias)
    vocab = head_bias.shape[0]

    def objective(params):
        word_low, pos_low, qkv_low, square_low, up_low, down_low, vec_low = [low(item) for item in params[:7]]
        bias_row = params[7]
        head_rows = word_low[:vocab]

        def one_seq(carry, item):
            seq_ids, length, places, targets, count = item
            word_rows = jnp.take(word_low, seq_ids, axis=0)
            hidden = section_one(word_rows, pos_low, qkv_low, square_low[0], vec_low, length)
            hidden = low_back(low(hidden))
            normed = section_two(hidden, places, up_low, down_low, square_low[1], vec_low)
            return (carry + head_loss(normed, head_rows, bias_row, targets, count), None)
        loss, _ = lax.scan(jax.checkpoint(one_seq), jnp.zeros((), jnp.float32), (token_ids, lengths, masked_at, labels, counts))
        return (loss / total, loss)
    value, back_fn, loss_total = jax.vjp(objective, params, has_aux=True)
    grads = back_fn(jnp.ones((), jnp.float32))[0]
    squares = jnp.zeros((), jnp.float32)
    for grad in grads:
        squares = squares + jnp.sum(grad * grad)
    grad_norm = jnp.sqrt(squares)
    factor = clip_norm / jnp.maximum(grad_norm, clip_norm)
    states = ((word_first, word_second), (pos_first, pos_second), (qkv_first, qkv_second), (square_first, square_second), (up_first, up_second), (down_first, down_second), (vec_first, vec_second), (bias_first, bias_second))
    rates = (learn_rate, learn_rate, learn_rate, learn_rate, learn_rate, learn_rate, vector_rate, vector_rate)
    results = []
    for weight, state, grad, rate in zip(params, states, grads, rates):
        results.extend(adam_step(weight, state[0], state[1], grad, factor, rate))
    return (results[0], results[1], results[2], results[3], results[4], results[5], results[6], results[7], results[8], results[9], results[10], results[11], results[12], results[13], results[14], results[15], results[16], results[17], results[18], results[19], results[20], results[21], results[22], results[23], loss_total, total, grad_norm)
```

```python
import functools
import math

import jax
import jax.numpy as jnp
from jax import lax
from jax.experimental import pallas as pl
from jax.experimental.pallas import tpu as pltpu
from jax.sharding import PartitionSpec as P

H = 16
STEP = 10


beta_one = 0.9
beta_two = 0.999
learn_rate = 0.02
vector_rate = 0.2
weight_decay = 0.01
epsilon = 1e-08
clip_norm = 0.02
norm_eps = 1e-05
root_half = 0.7071067811865476
density_scale = 0.3989422804014327
AXES = ("pipe", "grp", "dp")
CHIPS = ("grp", "dp")
highest = lax.Precision.HIGHEST


def matmul(left, right):
    return jnp.dot(left, right, preferred_element_type=jnp.float32)


def left_transposed(left, right):
    return lax.dot_general(
        left, right, (((0,), (0,)), ((), ())), preferred_element_type=jnp.float32
    )


def right_transposed(left, right):
    return lax.dot_general(
        left, right, (((1,), (1,)), ((), ())), preferred_element_type=jnp.float32
    )


def norm_forward(values, gain, shift):
    center = values - jnp.mean(values, -1, keepdims=True)
    scale = lax.rsqrt(jnp.mean(center * center, -1, keepdims=True) + norm_eps)
    normal = center * scale
    return (normal * gain + shift, (normal, scale))


def norm_backward(grad, kept, gain):
    normal, scale = kept
    d_gain = jnp.sum(grad * normal, 0)
    d_shift = jnp.sum(grad, 0)
    d_norm = grad * gain
    d_input = scale * (
        d_norm
        - jnp.mean(d_norm, -1, keepdims=True)
        - normal * jnp.mean(d_norm * normal, -1, keepdims=True)
    )
    return (d_input, d_gain, d_shift)


def gelu_slope(values):
    return (
        0.5 * (1.0 + lax.erf(values * root_half))
        + values * jnp.exp(-0.5 * values * values) * density_scale
    )


def masked_counts(lengths, slots):
    return jnp.minimum(slots, (3 * lengths + 19) // 20)


def one_hot(indices, size, dtype):
    places = lax.broadcasted_iota(jnp.int32, indices.shape + (size,), indices.ndim)
    return (indices[..., None] == places).astype(dtype)


def rows_by_seq(pick, rows):
    return jnp.einsum("sjp,spw->sjw", pick, rows, precision=highest)


def rows_to_seq(pick, rows):
    return jnp.einsum("sjp,sjw->spw", pick, rows, precision=highest)


class Routes:
    def __init__(self, all_ids, all_live, rows_per):
        self.parts, tokens = all_ids.shape
        self.rows_per = rows_per
        self.me = lax.axis_index(AXES)
        mean = tokens / self.parts
        self.room = max(16, int(math.ceil((mean + 2.8 * math.sqrt(mean)) / 16)) * 16)
        owners = jnp.where(all_live, all_ids // rows_per, -1)
        counts = jnp.sum(one_hot(owners, self.parts, jnp.int32), 1)
        self.rounds = (jnp.max(counts) + self.room - 1) // self.room
        mine = owners == self.me
        self.out_rank = jnp.where(mine, jnp.cumsum(mine.astype(jnp.int32), 1) - 1, -1)
        self.out_row = all_ids - self.me * rows_per
        own_owners = lax.dynamic_index_in_dim(owners, self.me, 0, keepdims=False)
        hits = one_hot(own_owners, self.parts, jnp.int32)
        ranks = jnp.sum(hits * jnp.cumsum(hits, 0), 1) - 1
        self.in_rank = ranks
        self.in_owner = own_owners

    def owner_pick(self, turn):
        slots = turn * self.room + jnp.arange(self.room, dtype=jnp.int32)
        at = self.out_rank[:, None, :] == slots[None, :, None]
        row = jnp.sum(jnp.where(at, self.out_row[:, None, :] + 1, 0), 2) - 1
        return one_hot(row.reshape(-1), self.rows_per, jnp.bfloat16)

    def token_pick(self, turn):
        rank = self.in_rank - turn * self.room
        inside = (self.in_owner >= 0) & (rank >= 0) & (rank < self.room)
        slot = jnp.where(inside, self.in_owner * self.room + rank, -1)
        return one_hot(slot, self.parts * self.room, jnp.bfloat16)

    def exchange(self, rows):
        shaped = rows.reshape(self.parts, self.room, rows.shape[1])
        return lax.all_to_all(shaped, AXES, 0, 0).reshape(rows.shape)

    def table_rows(self, table, turn):
        return matmul(self.owner_pick(turn), table).astype(jnp.bfloat16)

    def token_rows(self, rows, turn):
        return left_transposed(self.token_pick(turn), rows).astype(jnp.bfloat16)

    def fetch(self, table, arrived):
        def more(turn, kept):
            rows = self.exchange(self.table_rows(table, turn))
            return kept + matmul(self.token_pick(turn), rows)

        return lax.fori_loop(1, self.rounds, more, matmul(self.token_pick(0), arrived))

    def give(self, rows, arrived):
        def more(turn, kept):
            back = self.exchange(self.token_rows(rows, turn))
            return kept + left_transposed(self.owner_pick(turn), back)

        return lax.fori_loop(
            1, self.rounds, more, left_transposed(self.owner_pick(0), arrived)
        )


def swapped(shard):
    return lax.ppermute(shard, "pipe", [(0, 1), (1, 0)])


def both_cores(rows):
    return jnp.concatenate([rows, swapped(rows)], 0)


def half_columns(rows, index):
    half = rows.shape[1] // 2
    return lax.dynamic_slice_in_dim(rows, index * half, half, 1)


def chip_sum(left, right):
    pipe = lax.axis_index("pipe")
    left = jnp.concatenate([half_columns(left, pipe), swapped(half_columns(left, 1 - pipe))], 0)
    return left_transposed(left, both_cores(right)).astype(jnp.bfloat16)


def chip_half(partial):
    half = partial.shape[0] // 2
    pipe = lax.axis_index("pipe")
    partial = partial.astype(jnp.bfloat16)
    keep = lax.dynamic_slice_in_dim(partial, pipe * half, half, 0)
    give = lax.dynamic_slice_in_dim(partial, (1 - pipe) * half, half, 0)
    return (keep.astype(jnp.float32) + swapped(give).astype(jnp.float32)).astype(jnp.bfloat16)


def device(pipe, grp, dp):
    return {"pipe": pipe, "grp": grp, "dp": dp}


def remote(source, target, send, arrive, to):
    return pltpu.make_async_remote_copy(
        src_ref=source,
        dst_ref=target,
        send_sem=send,
        recv_sem=arrive,
        device_id=device(*to),
        device_id_type=pl.DeviceIdType.MESH,
    )


def greet(others):
    barrier = pltpu.get_barrier_semaphore()
    for to in others:
        pl.semaphore_signal(
            barrier, inc=1, device_id=device(*to), device_id_type=pl.DeviceIdType.MESH
        )
    pl.semaphore_wait(barrier, len(others))


class Place:
    def __init__(self, sizes):
        self.pipes, self.grps, self.dps = sizes
        self.pipe, self.grp, self.dp = [lax.axis_index(axis) for axis in AXES]
        column, row = self.grp % 2, self.grp // 2
        self.beside = 2 * row + 1 - column
        self.below = 2 * (1 - row) + column
        self.across = 3 - self.grp

    def line(self, step):
        return (self.dp + step) % self.dps

    def behind(self, step):
        return (self.dp + self.dps - step) % self.dps

    def others(self):
        found = []
        for a in range(self.pipes):
            for b in range(self.grps):
                for c in range(self.dps):
                    if (a, b, c) != (0, 0, 0):
                        ahead = (
                            (self.pipe + a) % self.pipes,
                            (self.grp + b) % self.grps,
                            (self.dp + c) % self.dps,
                        )
                        back = (
                            (self.pipe + self.pipes - a) % self.pipes,
                            (self.grp + self.grps - b) % self.grps,
                            (self.dp + self.dps - c) % self.dps,
                        )
                        found.append((ahead, back))
        return found

    def index(self, pipe, grp, dp):
        return (pipe * self.grps + grp) * self.dps + dp


def swap_all(place, rows, arrived, send, arrive, own):
    me = place.index(place.pipe, place.grp, place.dp)
    copies = []
    for i, (ahead, back) in enumerate(place.others()):
        to = place.index(*ahead)
        copies.append(remote(rows.at[to], arrived.at[me], send.at[i], arrive.at[i], ahead))
        copies[-1].start()
    kept = pltpu.make_async_copy(rows.at[me], arrived.at[me], own)
    kept.start()

    def finish():
        for i, (ahead, back) in enumerate(place.others()):
            origin = place.index(*back)
            copies[i].wait_send()
            remote(rows.at[me], arrived.at[origin], send.at[i], arrive.at[i], ahead).wait_recv()
        kept.wait()

    return finish


def spread_kernel(sizes, row_ref, all_ref, send, arrive, own):
    place = Place(sizes)
    others = place.others()
    greet([ahead for ahead, _ in others])
    me = place.index(place.pipe, place.grp, place.dp)
    copies = []
    for i, (ahead, _) in enumerate(others):
        copies.append(remote(row_ref, all_ref.at[me], send.at[i], arrive.at[i], ahead))
        copies[-1].start()
    kept = pltpu.make_async_copy(row_ref, all_ref.at[me], own)
    kept.start()
    for i, (ahead, back) in enumerate(others):
        copies[i].wait_send()
        remote(
            row_ref, all_ref.at[place.index(*back)], send.at[i], arrive.at[i], ahead
        ).wait_recv()
    kept.wait()


def spread(row, sizes, collective):
    parts = math.prod(sizes)
    sems = pltpu.SemaphoreType.DMA((parts - 1,))
    return pl.pallas_call(
        functools.partial(spread_kernel, sizes),
        out_shape=jax.ShapeDtypeStruct((parts,) + row.shape, row.dtype),
        in_specs=[pl.BlockSpec(memory_space=pltpu.VMEM)],
        out_specs=pl.BlockSpec(memory_space=pltpu.VMEM),
        scratch_shapes=[sems, sems, pltpu.SemaphoreType.DMA],
        compiler_params=pltpu.CompilerParams(
            collective_id=collective, has_side_effects=True, vmem_limit_bytes=8 << 20
        ),
    )(row)


def stats_kernel(sizes, own_ref, all_ref, held, result, send, arrive, own, send_two, arrive_two):
    place = Place(sizes)
    others = place.others()
    greet([ahead for ahead, _ in others])
    swap_all(place, own_ref, held, send, arrive, own)()
    peaks = held[:, 0]
    peak = jnp.max(peaks, 0, keepdims=True)
    total = jnp.sum(held[:, 1] * jnp.exp(peaks - peak), 0, keepdims=True)
    label = jnp.sum(held[:, 2], 0, keepdims=True)
    result[0:1] = peak
    result[1:2] = total
    result[2:3] = label
    result[3:8] = jnp.zeros((5, result.shape[1]), jnp.float32)
    me = place.index(place.pipe, place.grp, place.dp)
    copies = []
    for i, (ahead, _) in enumerate(others):
        copies.append(remote(result, all_ref.at[me], send_two.at[i], arrive_two.at[i], ahead))
        copies[-1].start()
    all_ref[me] = result[...]
    for i, (ahead, back) in enumerate(others):
        copies[i].wait_send()
        remote(
            result, all_ref.at[place.index(*back)], send_two.at[i], arrive_two.at[i], ahead
        ).wait_recv()


def combine_stats(own, sizes, collective):
    parts, _, rows = own.shape
    sems = pltpu.SemaphoreType.DMA((parts - 1,))
    return pl.pallas_call(
        functools.partial(stats_kernel, sizes),
        out_shape=jax.ShapeDtypeStruct(own.shape, jnp.float32),
        in_specs=[pl.BlockSpec(memory_space=pltpu.VMEM)],
        out_specs=pl.BlockSpec(memory_space=pltpu.VMEM),
        scratch_shapes=[
            pltpu.VMEM(own.shape, jnp.float32),
            pltpu.VMEM((8, rows), jnp.float32),
            sems,
            sems,
            pltpu.SemaphoreType.DMA,
            sems,
            sems,
        ],
        compiler_params=pltpu.CompilerParams(
            collective_id=collective, has_side_effects=True, vmem_limit_bytes=8 << 20
        ),
    )(own)


def gather_kernel(sizes, pieces, routed, *refs):
    count = max(piece[0] for piece in pieces) + 1
    shards, refs = refs[:count], refs[count:]
    if routed:
        rows_ref, refs = refs[0], refs[1:]
    fulls, refs = refs[:count], refs[count:]
    if routed:
        arrived_ref, refs = refs[0], refs[1:]
    send, arrive, own, swap_send, swap_arrive, swap_own = refs
    place = Place(sizes)
    pipe, grp, dp = place.pipe, place.grp, place.dp
    near = place.beside * (1 - pipe) + place.below * pipe
    far = place.below * (1 - pipe) + place.beside * pipe
    core = (1 - pipe, grp, dp)
    lines = place.dps - 1
    if routed:
        greet([ahead for ahead, _ in place.others()])
    else:
        greet(
            [(pipe, grp, place.line(k + 1)) for k in range(lines)]
            + [(pipe, near, dp), (pipe, far, dp), core]
        )
    waits = []

    def view(piece, *at):
        array, first, rows = piece
        return fulls[array].at[at + ((slice(None),) * (3 - len(at))) + (pl.ds(first, rows),)]

    def launch(n, index, source, piece, to, *at):
        copy = remote(source, view(piece, *at), send.at[n, index], arrive.at[n, index], to)
        copy.start()
        waits.append(copy)

    def landed(n, index, piece, *at):
        target = view(piece, *at)
        remote(target, target, send.at[n, index], arrive.at[n, index], core).wait_recv()

    keeps = []
    for n, piece in enumerate(pieces):
        array, first, rows = piece
        source = shards[array].at[pl.ds(first, rows)]
        for k in range(lines):
            launch(n, k, source, piece, (pipe, grp, place.line(k + 1)), pipe, grp, dp)
        keeps.append(pltpu.make_async_copy(source, view(piece, pipe, grp, dp), own.at[n]))
        keeps[-1].start()
        if n == 0 and routed:
            finish = swap_all(place, rows_ref, arrived_ref, swap_send, swap_arrive, swap_own)

    def over_plane(n, piece):
        for k in range(lines):
            landed(n, k, piece, pipe, grp, place.behind(k + 1))
        keeps[n].wait()
        group = view(piece, pipe, grp)
        launch(n, lines, group, piece, (pipe, near, dp), pipe, grp)
        launch(n, lines + 1, group, piece, (pipe, far, dp), pipe, grp)
        launch(n, lines + 3, group, piece, core, pipe, grp)

    def pass_on(n, piece):
        landed(n, lines, piece, pipe, near)
        group = view(piece, pipe, near)
        launch(n, lines + 2, group, piece, (pipe, far, dp), pipe, near)
        launch(n, lines + 4, group, piece, core, pipe, near)
        landed(n, lines + 1, piece, pipe, far)
        launch(n, lines + 5, view(piece, pipe, far), piece, core, pipe, far)

    def last(n, piece):
        landed(n, lines + 2, piece, pipe, place.across)
        launch(n, lines + 6, view(piece, pipe, place.across), piece, core, pipe, place.across)

    total = len(pieces)
    for n in range(total + 2):
        if n < total:
            over_plane(n, pieces[n])
        if 1 <= n < total + 1:
            pass_on(n - 1, pieces[n - 1])
        if n >= 2:
            last(n - 2, pieces[n - 2])
    for n, piece in enumerate(pieces):
        landed(n, lines + 3, piece, 1 - pipe, grp)
        core_near = place.below * (1 - pipe) + place.beside * pipe
        core_far = place.beside * (1 - pipe) + place.below * pipe
        landed(n, lines + 4, piece, 1 - pipe, core_near)
        landed(n, lines + 5, piece, 1 - pipe, core_far)
        landed(n, lines + 6, piece, 1 - pipe, place.across)
    for copy in waits:
        copy.wait_send()
    if routed:
        finish()


def gather_all(shards, pieces, sizes, collective, rows=None):
    parts = math.prod(sizes)
    routed = rows is not None
    kinds = sizes[2] - 1 + 7
    out_shape = [jax.ShapeDtypeStruct(sizes + shard.shape, shard.dtype) for shard in shards]
    if routed:
        out_shape.append(jax.ShapeDtypeStruct(rows.shape, rows.dtype))
    operands = list(shards) + ([rows] if routed else [])
    sems = pltpu.SemaphoreType.DMA((len(pieces), kinds))
    swaps = pltpu.SemaphoreType.DMA((parts - 1 if routed else 1,))
    return pl.pallas_call(
        functools.partial(gather_kernel, sizes, tuple(pieces), routed),
        out_shape=out_shape,
        in_specs=[pl.BlockSpec(memory_space=pl.ANY)] * len(operands),
        out_specs=[pl.BlockSpec(memory_space=pl.ANY)] * len(out_shape),
        scratch_shapes=[
            sems,
            sems,
            pltpu.SemaphoreType.DMA((len(pieces),)),
            swaps,
            swaps,
            pltpu.SemaphoreType.DMA,
        ],
        compiler_params=pltpu.CompilerParams(collective_id=collective, has_side_effects=True),
    )(*operands)


def reduce_kernel(sizes, count, routed, *refs):
    partials, refs = refs[:count], refs[count:]
    if routed:
        rows_ref, refs = refs[0], refs[1:]
    sums, refs = refs[:count], refs[count:]
    if routed:
        arrived_ref, refs = refs[0], refs[1:]
    planes, refs = refs[:count], refs[count:]
    groups, refs = refs[:count], refs[count:]
    line_parts, refs = refs[:count], refs[count:]
    send, arrive, own, swap_send, swap_arrive, swap_own = refs
    place = Place(sizes)
    pipe, grp, dp = place.pipe, place.grp, place.dp
    partners = (place.beside, place.below, place.across)
    lines = place.dps - 1
    if routed:
        greet([ahead for ahead, _ in place.others()])
    else:
        greet(
            [(pipe, grp, place.line(k + 1)) for k in range(lines)]
            + [(pipe, other, dp) for other in partners]
        )
    copies, keeps = [], []
    for n in range(count):
        for j, other in enumerate(partners):
            copies.append(
                remote(
                    partials[n].at[other],
                    planes[n].at[j],
                    send.at[n, j],
                    arrive.at[n, j],
                    (pipe, other, dp),
                )
            )
            copies[-1].start()
        keeps.append(pltpu.make_async_copy(partials[n].at[grp], groups[n], own.at[n]))
        keeps[-1].start()
        if n == 0 and routed:
            finish = swap_all(place, rows_ref, arrived_ref, swap_send, swap_arrive, swap_own)
    for n in range(count):
        keeps[n].wait()
        for j in range(3):
            copies[3 * n + j].wait_recv()
        block = 16
        depth = groups[n].shape[0] // place.dps

        def add_plane(i, _, n=n):
            at = pl.ds(pl.multiple_of(i * block, block), block)
            total = groups[n][at].astype(jnp.float32)
            for j in range(3):
                total = total + planes[n][j, at].astype(jnp.float32)
            groups[n][at] = total.astype(jnp.bfloat16)
            return 0

        lax.fori_loop(0, groups[n].shape[0] // block, add_plane, 0)
        for k in range(lines):
            first = pl.multiple_of(place.line(k + 1) * depth, 16)
            copies.append(
                remote(
                    groups[n].at[pl.ds(first, depth)],
                    line_parts[n].at[k],
                    send.at[n, 3 + k],
                    arrive.at[n, 3 + k],
                    (pipe, grp, place.line(k + 1)),
                )
            )
            copies[-1].start()
    for n in range(count):
        depth = groups[n].shape[0] // place.dps
        for k in range(lines):
            copies[3 * count + lines * n + k].wait_recv()

        def add_line(i, _, n=n, depth=depth):
            at = pl.ds(pl.multiple_of(i * block, block), block)
            first = pl.multiple_of(dp * depth + i * block, block)
            total = groups[n][pl.ds(first, block)].astype(jnp.float32)
            for k in range(lines):
                total = total + line_parts[n][k, at].astype(jnp.float32)
            sums[n][at] = total
            return 0

        lax.fori_loop(0, depth // block, add_line, 0)
    for copy in copies:
        copy.wait_send()
    if routed:
        finish()


def reduce_all(partials, sizes, collective, rows=None):
    parts = math.prod(sizes)
    count = len(partials)
    routed = rows is not None
    low = jnp.bfloat16
    tall = [(partial.shape[1], partial.shape[2]) for partial in partials]
    flat = [(height // sizes[2], columns) for height, columns in tall]
    out_shape = [jax.ShapeDtypeStruct(shape, jnp.float32) for shape in flat]
    out_specs = [pl.BlockSpec(memory_space=pltpu.VMEM)] * count
    if routed:
        out_shape.append(jax.ShapeDtypeStruct(rows.shape, rows.dtype))
        out_specs.append(pl.BlockSpec(memory_space=pl.ANY))
    operands = list(partials) + ([rows] if routed else [])
    sems = pltpu.SemaphoreType.DMA((count, 3 + sizes[2] - 1))
    swaps = pltpu.SemaphoreType.DMA((parts - 1 if routed else 1,))
    return pl.pallas_call(
        functools.partial(reduce_kernel, sizes, count, routed),
        out_shape=out_shape,
        in_specs=[pl.BlockSpec(memory_space=pl.ANY)] * len(operands),
        out_specs=out_specs,
        scratch_shapes=[pltpu.VMEM((3,) + shape, low) for shape in tall]
        + [pltpu.VMEM(shape, low) for shape in tall]
        + [pltpu.VMEM((sizes[2] - 1,) + shape, low) for shape in flat]
        + [
            sems,
            sems,
            pltpu.SemaphoreType.DMA((count,)),
            swaps,
            swaps,
            pltpu.SemaphoreType.DMA,
        ],
        compiler_params=pltpu.CompilerParams(
            collective_id=collective, has_side_effects=True, vmem_limit_bytes=48 << 20
        ),
    )(*operands)


def gather_weights(shards, sizes, collective, pieces, rows=None):
    if collective is not None:
        *fulls, arrived = gather_all(shards, pieces, sizes, collective, rows)
    else:
        fulls = [lax.all_gather(shard, AXES, axis=0) for shard in shards]
        arrived = lax.all_to_all(rows, AXES, 0, 0)
    return [full.reshape(-1, full.shape[-1]) for full in fulls], arrived


def gather_rows(shard, sizes, collective):
    if collective is None:
        return lax.all_gather(shard, AXES, axis=0, tiled=True)
    cuts = 4
    size = shard.shape[0] // cuts
    pieces = [(0, i * size, size) for i in range(cuts)]
    (full,) = gather_all([shard], pieces, sizes, collective)
    return full.reshape(-1, full.shape[-1])


def reduce_chips(partials, sizes, collective, rows=None):
    if collective is not None:
        shaped = [p.reshape(sizes[1], -1, p.shape[1]) for p in partials]
        sums = reduce_all(shaped, sizes, collective, rows)
        return (sums[:-1], sums[-1]) if rows is not None else (sums, None)
    sums = [
        lax.psum_scatter(p, CHIPS, scatter_dimension=0, tiled=True).astype(jnp.float32)
        for p in partials
    ]
    return sums, lax.all_to_all(rows, AXES, 0, 0) if rows is not None else None


def spread_row(row, sizes, collective):
    if collective is None:
        return lax.all_gather(row, AXES, axis=0)
    return spread(row, sizes, collective)


def share_stats(peak, total, label, sizes, collective):
    if collective is None:
        top = lax.pmax(peak, AXES)
        total, label = lax.psum((total * jnp.exp(peak - top), label), AXES)
        return top, total, label
    parts = math.prod(sizes)
    stats = jnp.stack([peak, total, label])
    stats = jnp.pad(stats.reshape(3, parts, -1).swapaxes(0, 1), ((0, 0), (0, 5), (0, 0)))
    stats = combine_stats(stats, sizes, collective)
    return [stats[:, i].reshape(-1) for i in range(3)]


def adam_step(weight, first, second, grad, factor, rate):
    clipped = grad * factor
    first = beta_one * first + (1.0 - beta_one) * clipped
    second = beta_two * second + (1.0 - beta_two) * clipped * clipped
    first_hat = first / (1.0 - beta_one**STEP)
    second_hat = second / (1.0 - beta_two**STEP)
    weight = weight - rate * (first_hat / (jnp.sqrt(second_hat) + epsilon) + weight_decay * weight)
    return (weight, first, second)


def per_device(
    token_ids,
    lengths,
    masked_at,
    labels,
    word_table,
    word_first,
    word_second,
    pos_table,
    pos_first,
    pos_second,
    qkv_weight,
    qkv_first,
    qkv_second,
    square_weight,
    square_first,
    square_second,
    up_weight,
    up_first,
    up_second,
    down_weight,
    down_first,
    down_second,
    vec_table,
    vec_first,
    vec_second,
    head_bias,
    bias_first,
    bias_second,
):
    narrow = jnp.bfloat16
    seq_len, slots = token_ids.shape[1], masked_at.shape[1]
    width = word_table.shape[1]
    vocab = head_bias.shape[0]
    rows_per = word_table.shape[0]
    parts = lax.axis_size(AXES)
    halves = lax.axis_size("pipe")
    me = lax.axis_index(AXES)
    own = token_ids.shape[0] // halves
    first_own = lax.axis_index("pipe") * own
    head_dim = width // H
    sizes = tuple(lax.axis_size(axis) for axis in AXES)
    shards = (word_table, qkv_weight, square_weight[0], up_weight, down_weight)
    direct = sizes[:2] == (2, 4) and all(shard.shape[0] % 32 == 0 for shard in shards)
    ids = tuple(range(7)) if direct else (None,) * 7

    spare = -(seq_len + slots + 1) % 128
    packed = jnp.concatenate(
        [token_ids, labels, lengths[:, None], jnp.zeros((token_ids.shape[0], spare), jnp.int32)], 1
    )
    packed = lax.dynamic_slice_in_dim(packed, first_own, own, 0)
    packed = spread_row(packed, sizes, ids[0])
    all_ids = packed[:, :, :seq_len]
    all_labels = packed[:, :, seq_len : seq_len + slots].reshape(-1)
    all_lengths = packed[:, :, seq_len + slots]
    places = jnp.arange(seq_len, dtype=jnp.int32)
    all_live = places[None, None, :] < all_lengths[:, :, None]
    all_counts = masked_counts(all_lengths, slots)
    total = jnp.sum(all_counts).astype(jnp.float32)
    slot_index = jnp.arange(slots, dtype=jnp.int32)
    all_valid = (slot_index < all_counts[:, :, None]).astype(jnp.float32).reshape(-1)
    own_lengths = lax.dynamic_slice_in_dim(lengths, first_own, own, 0)
    masked = lax.dynamic_slice_in_dim(masked_at, first_own, own, 0)

    word_low = word_table.astype(narrow)
    routes = Routes(all_ids.reshape(parts, -1), all_live.reshape(parts, -1), rows_per)
    small = pos_table.shape[0] + vec_table.shape[0]
    spare = -small % 128
    small_low = jnp.concatenate(
        [pos_table.T, vec_table.T, jnp.zeros((pos_table.shape[1], spare), jnp.float32)], 1
    ).astype(narrow)
    low = [
        small_low,
        qkv_weight.astype(narrow),
        square_weight[0].astype(narrow),
        up_weight.astype(narrow),
        down_weight.astype(narrow),
        square_weight[1].astype(narrow),
    ]
    pieces = [(i, 0, shard.shape[0]) for i, shard in enumerate(low)]
    send = routes.table_rows(word_low, 0).reshape(parts, -1, width)
    (small_full, qkv_low, out_low, up_low, down_low, turn_low), arrived = gather_weights(
        low, sizes, ids[1], pieces, send
    )
    word_rows = routes.fetch(word_low, arrived.reshape(-1, width))
    small_full = small_full.T
    pos_low = small_full[:seq_len]
    vec_rows = small_full[seq_len:small].astype(jnp.float32)
    query_low, both_low = qkv_low[:, :width], qkv_low[:, width:]

    second = (places[None, :] >= ((own_lengths + 1) // 2)[:, None]).reshape(-1, 1)
    live = (places[None, :] < own_lengths[:, None])[:, None, None, :]
    embedded = (
        word_rows
        + jnp.tile(pos_low.astype(jnp.float32), (own, 1))
        + jnp.where(second, vec_rows[1], vec_rows[0])
    )
    start, norm_zero = norm_forward(embedded, vec_rows[2], vec_rows[3])
    start_low = start.astype(narrow)
    both_bias = jnp.concatenate([jnp.zeros_like(vec_rows[5]), vec_rows[5]])
    both = (matmul(start_low, both_low) + both_bias).astype(narrow)
    both = both.reshape(own, seq_len, 2, H, head_dim)
    key_rows, value_rows = both[:, :, 0], both[:, :, 1]
    pick = one_hot(masked, seq_len, jnp.float32)
    chosen = rows_by_seq(pick, start.reshape(own, seq_len, width)).reshape(-1, width)
    chosen_low = chosen.astype(narrow)
    queries = (matmul(chosen_low, query_low) + vec_rows[4]).astype(narrow)
    queries = queries.reshape(own, slots, H, head_dim)
    scale = head_dim ** (-0.5)
    scores = (
        jnp.einsum("sqhd,skhd->shqk", queries, key_rows, preferred_element_type=jnp.float32)
        * scale
    )
    scores = jnp.where(live, scores, -1e30)
    exp_scores = jnp.exp(scores - jnp.max(scores, -1, keepdims=True))
    probs = exp_scores / jnp.sum(exp_scores, -1, keepdims=True)
    probs_low = probs.astype(narrow)
    context = jnp.einsum(
        "shqk,skhd->sqhd", probs_low, value_rows, preferred_element_type=jnp.float32
    )
    context = context.reshape(-1, width).astype(narrow)
    branch = matmul(context, out_low) + vec_rows[6]
    hidden, norm_one = norm_forward(chosen + branch, vec_rows[7], vec_rows[8])
    hidden = hidden.astype(narrow)

    inner = matmul(hidden, up_low) + vec_rows[15:].reshape(-1)
    activ = jax.nn.gelu(inner, approximate=False).astype(narrow)
    branch = matmul(activ, down_low) + vec_rows[9]
    mixed, norm_two = norm_forward(hidden.astype(jnp.float32) + branch, vec_rows[10], vec_rows[11])
    picked = mixed.astype(narrow)
    turned = matmul(picked, turn_low) + vec_rows[12]
    normed, norm_head = norm_forward(
        jax.nn.gelu(turned, approximate=False), vec_rows[13], vec_rows[14]
    )

    all_normed = gather_rows(normed.astype(narrow), sizes, ids[2])
    column = me * rows_per + jnp.arange(rows_per, dtype=jnp.int32)
    bias_row = jnp.pad(head_bias, (0, parts * rows_per - vocab))
    bias_row = lax.dynamic_slice_in_dim(bias_row, me * rows_per, rows_per, 0)
    logits = right_transposed(all_normed, word_low) + bias_row
    logits = jnp.where(column < vocab, logits, -1e30)
    own_peak = jnp.max(logits, -1)
    own_total = jnp.sum(jnp.exp(logits - own_peak[:, None]), -1)
    hits = all_labels[:, None] == column
    own_label = jnp.sum(jnp.where(hits, logits, 0.0), -1)
    peak, exp_total, label_logit = share_stats(own_peak, own_total, own_label, sizes, ids[3])
    loss_total = jnp.sum(all_valid * (peak + jnp.log(exp_total) - label_logit))
    d_logits = (all_valid / total)[:, None] * (
        jnp.exp(logits - peak[:, None]) / exp_total[:, None] - hits.astype(jnp.float32)
    )
    d_bias = jnp.sum(d_logits, 0)
    d_logits_low = d_logits.astype(narrow)
    d_word = left_transposed(d_logits_low, all_normed)
    d_normed = chip_half(matmul(d_logits_low, word_low))
    columns = width // 2
    d_normed, _ = reduce_chips([d_normed[:, :columns], d_normed[:, columns:]], sizes, ids[4])
    d_normed = jnp.concatenate(d_normed, 1)

    d_gelu, d_gain_head, d_shift_head = norm_backward(d_normed, norm_head, vec_rows[13])
    d_turned = (d_gelu * gelu_slope(turned)).astype(narrow)
    d_turn_bias = jnp.sum(d_turned.astype(jnp.float32), 0)
    d_turn = chip_sum(picked, d_turned)
    d_picked = right_transposed(d_turned, turn_low)
    same = masked[:, :, None] == masked[:, None, :]
    earlier = slot_index[None, :] < slot_index[:, None]
    first_slot = jnp.logical_not(jnp.any(same & earlier, 2))
    merge = (same & first_slot[:, :, None]).astype(jnp.float32)
    d_mixed = rows_by_seq(merge, d_picked.reshape(own, slots, width)).reshape(-1, width)
    d_pre, d_gain_two, d_shift_two = norm_backward(d_mixed, norm_two, vec_rows[10])
    d_branch = d_pre.astype(narrow)
    d_down_bias = jnp.sum(d_branch.astype(jnp.float32), 0)
    d_down = chip_sum(activ, d_branch)
    d_inner = (right_transposed(d_branch, down_low) * gelu_slope(inner)).astype(narrow)
    d_up_bias = jnp.sum(d_inner.astype(jnp.float32), 0).reshape(-1, width)
    d_up = chip_sum(hidden, d_inner)
    d_hidden = (d_pre + right_transposed(d_inner, up_low)).astype(narrow)

    d_pre, d_gain_one, d_shift_one = norm_backward(
        d_hidden.astype(jnp.float32), norm_one, vec_rows[7]
    )
    d_branch = d_pre.astype(narrow)
    d_out_bias = jnp.sum(d_branch.astype(jnp.float32), 0)
    d_out = chip_sum(context, d_branch)
    d_context = right_transposed(d_branch, out_low).astype(narrow)
    d_context = d_context.reshape(own, slots, H, head_dim)
    d_value = jnp.einsum(
        "shqk,sqhd->skhd", probs_low, d_context, preferred_element_type=jnp.float32
    )
    d_probs = jnp.einsum(
        "sqhd,skhd->shqk", d_context, value_rows, preferred_element_type=jnp.float32
    )
    d_scores = (probs * (d_probs - jnp.sum(probs * d_probs, -1, keepdims=True))).astype(narrow)
    d_query = (
        jnp.einsum("shqk,skhd->sqhd", d_scores, key_rows, preferred_element_type=jnp.float32)
        * scale
    )
    d_query = d_query.reshape(-1, width).astype(narrow)
    d_key = (
        jnp.einsum("shqk,sqhd->skhd", d_scores, queries, preferred_element_type=jnp.float32)
        * scale
    )
    d_both = jnp.stack([d_key, d_value], 2).reshape(own * seq_len, 2 * width).astype(narrow)
    d_query_bias = jnp.sum(d_query.astype(jnp.float32), 0)
    d_value_bias = jnp.sum(d_both[:, width:].astype(jnp.float32), 0)
    d_qkv = jnp.concatenate(
        [chip_sum(chosen_low, d_query), chip_sum(start_low, d_both)], 1
    )
    d_chosen = d_pre + right_transposed(d_query, query_low)
    d_start = right_transposed(d_both, both_low) + rows_to_seq(
        pick, d_chosen.reshape(own, slots, width)
    ).reshape(-1, width)
    d_embedded, d_gain_zero, d_shift_zero = norm_backward(d_start, norm_zero, vec_rows[2])
    d_seg_zero = jnp.sum(jnp.where(second, 0.0, d_embedded), 0)
    d_seg_one = jnp.sum(jnp.where(second, d_embedded, 0.0), 0)
    d_embedded_low = d_embedded.astype(narrow)
    send = routes.token_rows(d_embedded_low, 0).reshape(parts, -1, width)
    d_small = jnp.concatenate(
        [
            jnp.sum(d_embedded.reshape(own, seq_len, width), 0),
            jnp.stack(
                [
                    d_seg_zero,
                    d_seg_one,
                    d_gain_zero,
                    d_shift_zero,
                    d_query_bias,
                    d_value_bias,
                    d_out_bias,
                    d_gain_one,
                    d_shift_one,
                    d_down_bias,
                    d_gain_two,
                    d_shift_two,
                    d_turn_bias,
                    d_gain_head,
                    d_shift_head,
                ]
            ),
            d_up_bias,
            jnp.zeros((spare, width), jnp.float32),
        ],
        0,
    )
    (own_up, own_down, own_qkv, own_turn, own_out, own_small), arrived = reduce_chips(
        [d_up, d_down, d_qkv, d_turn, d_out, chip_half(d_small.T)], sizes, ids[5], send
    )
    d_word = d_word + routes.give(d_embedded_low, arrived.reshape(-1, width))
    owned = (
        d_word,
        own_small[:, :seq_len].T,
        own_qkv,
        jnp.stack([own_out, own_turn]),
        own_up,
        own_down,
        own_small[:, seq_len:small].T,
    )
    local_squares = jnp.sum(d_bias * d_bias)
    for grad in owned:
        local_squares = local_squares + jnp.sum(grad * grad)
    spare = -(rows_per + 1) % 128
    last = jnp.concatenate([d_bias, local_squares[None], jnp.zeros((spare,), jnp.float32)])
    last = spread_row(last.reshape(8, -1), sizes, ids[6]).reshape(parts, -1)
    bias_grad = last[:, :rows_per].reshape(-1)[:vocab]
    grad_norm = jnp.sqrt(jnp.sum(last[:, rows_per]))
    factor = clip_norm / jnp.maximum(grad_norm, clip_norm)
    masters = (
        word_table,
        pos_table,
        qkv_weight,
        square_weight,
        up_weight,
        down_weight,
        vec_table,
        head_bias,
    )
    states = (
        (word_first, word_second),
        (pos_first, pos_second),
        (qkv_first, qkv_second),
        (square_first, square_second),
        (up_first, up_second),
        (down_first, down_second),
        (vec_first, vec_second),
        (bias_first, bias_second),
    )
    rates = (
        learn_rate,
        learn_rate,
        learn_rate,
        learn_rate,
        learn_rate,
        learn_rate,
        vector_rate,
        vector_rate,
    )
    grads = tuple(owned) + (bias_grad,)
    results = []
    for weight, state, grad, rate in zip(masters, states, grads, rates):
        results.extend(adam_step(weight, state[0], state[1], grad, factor, rate))
    return (
        results[0],
        results[1],
        results[2],
        results[3],
        results[4],
        results[5],
        results[6],
        results[7],
        results[8],
        results[9],
        results[10],
        results[11],
        results[12],
        results[13],
        results[14],
        results[15],
        results[16],
        results[17],
        results[18],
        results[19],
        results[20],
        results[21],
        results[22],
        results[23],
        loss_total,
        total,
        grad_norm,
    )


def solution(mesh):
    placed = (
        P(("grp", "dp"), None),
        P(("grp", "dp")),
        P(("grp", "dp"), None),
        P(("grp", "dp"), None),
        P(("pipe", "grp", "dp"), None),
        P(("pipe", "grp", "dp"), None),
        P(("pipe", "grp", "dp"), None),
        P(None, ("pipe", "grp", "dp")),
        P(None, ("pipe", "grp", "dp")),
        P(None, ("pipe", "grp", "dp")),
        P(("pipe", "grp", "dp"), None),
        P(("pipe", "grp", "dp"), None),
        P(("pipe", "grp", "dp"), None),
        P(None, ("pipe", "grp", "dp"), None),
        P(None, ("pipe", "grp", "dp"), None),
        P(None, ("pipe", "grp", "dp"), None),
        P(("pipe", "grp", "dp"), None),
        P(("pipe", "grp", "dp"), None),
        P(("pipe", "grp", "dp"), None),
        P(("pipe", "grp", "dp"), None),
        P(("pipe", "grp", "dp"), None),
        P(("pipe", "grp", "dp"), None),
        P(None, ("pipe", "grp", "dp")),
        P(None, ("pipe", "grp", "dp")),
        P(None, ("pipe", "grp", "dp")),
        P(),
        P(),
        P(),
    )
    return jax.shard_map(
        per_device,
        mesh=mesh,
        in_specs=placed,
        out_specs=(
            P(("pipe", "grp", "dp"), None),
            P(("pipe", "grp", "dp"), None),
            P(("pipe", "grp", "dp"), None),
            P(None, ("pipe", "grp", "dp")),
            P(None, ("pipe", "grp", "dp")),
            P(None, ("pipe", "grp", "dp")),
            P(("pipe", "grp", "dp"), None),
            P(("pipe", "grp", "dp"), None),
            P(("pipe", "grp", "dp"), None),
            P(None, ("pipe", "grp", "dp"), None),
            P(None, ("pipe", "grp", "dp"), None),
            P(None, ("pipe", "grp", "dp"), None),
            P(("pipe", "grp", "dp"), None),
            P(("pipe", "grp", "dp"), None),
            P(("pipe", "grp", "dp"), None),
            P(("pipe", "grp", "dp"), None),
            P(("pipe", "grp", "dp"), None),
            P(("pipe", "grp", "dp"), None),
            P(None, ("pipe", "grp", "dp")),
            P(None, ("pipe", "grp", "dp")),
            P(None, ("pipe", "grp", "dp")),
            P(),
            P(),
            P(),
            P(),
            P(),
            P(),
        ),
        check_vma=False,
    )
```

```python
import functools
import math

import jax
import jax.numpy as jnp
from jax import lax
from jax.experimental import pallas as pl
from jax.experimental.pallas import tpu as pltpu
from jax.sharding import PartitionSpec as P

H = 16
STEP = 10


beta_one = 0.9
beta_two = 0.999
learn_rate = 0.02
vector_rate = 0.2
weight_decay = 0.01
epsilon = 1e-08
clip_norm = 0.02
norm_eps = 1e-05
root_half = 0.7071067811865476
density_scale = 0.3989422804014327
AXES = ("pipe", "grp", "dp")
CHIPS = ("grp", "dp")
PLANE = ("pipe", "grp")
highest = lax.Precision.HIGHEST


def matmul(left, right):
    return jnp.dot(left, right, preferred_element_type=jnp.float32)


def left_transposed(left, right):
    return lax.dot_general(
        left, right, (((0,), (0,)), ((), ())), preferred_element_type=jnp.float32
    )


def right_transposed(left, right):
    return lax.dot_general(
        left, right, (((1,), (1,)), ((), ())), preferred_element_type=jnp.float32
    )


def norm_forward(values, gain, shift):
    center = values - jnp.mean(values, -1, keepdims=True)
    scale = lax.rsqrt(jnp.mean(center * center, -1, keepdims=True) + norm_eps)
    normal = center * scale
    return (normal * gain + shift, (normal, scale))


def norm_backward(grad, kept, gain):
    normal, scale = kept
    d_gain = jnp.sum(grad * normal, 0)
    d_shift = jnp.sum(grad, 0)
    d_norm = grad * gain
    d_input = scale * (
        d_norm
        - jnp.mean(d_norm, -1, keepdims=True)
        - normal * jnp.mean(d_norm * normal, -1, keepdims=True)
    )
    return (d_input, d_gain, d_shift)


def gelu_slope(values):
    return (
        0.5 * (1.0 + lax.erf(values * root_half))
        + values * jnp.exp(-0.5 * values * values) * density_scale
    )


def masked_counts(lengths, slots):
    return jnp.minimum(slots, (3 * lengths + 19) // 20)


def one_hot(indices, size, dtype):
    places = lax.broadcasted_iota(jnp.int32, indices.shape + (size,), indices.ndim)
    return (indices[..., None] == places).astype(dtype)


def rows_by_seq(pick, rows):
    return jnp.einsum("sjp,spw->sjw", pick, rows, precision=highest)


def rows_to_seq(pick, rows):
    return jnp.einsum("sjp,sjw->spw", pick, rows, precision=highest)


class Routes:
    def __init__(self, all_ids, all_live, rows_per):
        self.parts, tokens = all_ids.shape
        self.rows_per = rows_per
        self.me = lax.axis_index(AXES)
        mean = tokens / self.parts
        self.room = max(16, int(math.ceil((mean + 2.8 * math.sqrt(mean)) / 16)) * 16)
        owners = jnp.where(all_live, all_ids // rows_per, -1)
        counts = jnp.sum(one_hot(owners, self.parts, jnp.int32), 1)
        self.rounds = (jnp.max(counts) + self.room - 1) // self.room
        mine = owners == self.me
        order = jnp.arange(tokens, dtype=jnp.int32)
        upto = (order[:, None] <= order[None, :]).astype(jnp.bfloat16)
        ranks = matmul(mine.astype(jnp.bfloat16), upto).astype(jnp.int32)
        self.out_rank = jnp.where(mine, ranks - 1, -1)
        self.out_row = all_ids - self.me * rows_per
        own_owners = lax.dynamic_index_in_dim(owners, self.me, 0, keepdims=False)
        hits = one_hot(own_owners, self.parts, jnp.bfloat16)
        ranks = jnp.sum(hits.astype(jnp.float32) * left_transposed(upto, hits), 1)
        ranks = ranks.astype(jnp.int32) - 1
        self.in_rank = ranks
        self.in_owner = own_owners

    def owner_pick(self, turn):
        slots = turn * self.room + jnp.arange(self.room, dtype=jnp.int32)
        at = self.out_rank[:, None, :] == slots[None, :, None]
        row = jnp.sum(jnp.where(at, self.out_row[:, None, :] + 1, 0), 2) - 1
        return one_hot(row.reshape(-1), self.rows_per, jnp.bfloat16)

    def token_pick(self, turn):
        rank = self.in_rank - turn * self.room
        inside = (self.in_owner >= 0) & (rank >= 0) & (rank < self.room)
        slot = jnp.where(inside, self.in_owner * self.room + rank, -1)
        return one_hot(slot, self.parts * self.room, jnp.bfloat16)

    def exchange(self, rows):
        shaped = rows.reshape(self.parts, self.room, rows.shape[1])
        return lax.all_to_all(shaped, AXES, 0, 0).reshape(rows.shape)

    def table_rows(self, table, turn):
        return matmul(self.owner_pick(turn), table).astype(jnp.bfloat16)

    def token_rows(self, rows, turn):
        return left_transposed(self.token_pick(turn), rows).astype(jnp.bfloat16)

    def fetch(self, table, arrived):
        def more(turn, kept):
            rows = self.exchange(self.table_rows(table, turn))
            return kept + matmul(self.token_pick(turn), rows)

        return lax.fori_loop(1, self.rounds, more, matmul(self.token_pick(0), arrived))

    def give(self, rows, arrived):
        def more(turn, kept):
            back = self.exchange(self.token_rows(rows, turn))
            return kept + left_transposed(self.owner_pick(turn), back)

        return lax.fori_loop(
            1, self.rounds, more, left_transposed(self.owner_pick(0), arrived)
        )


def swapped(shard):
    return lax.ppermute(shard, "pipe", [(0, 1), (1, 0)])


def both_cores(rows):
    return jnp.concatenate([rows, swapped(rows)], 0)


def half_columns(rows, index):
    half = rows.shape[1] // 2
    return lax.dynamic_slice_in_dim(rows, index * half, half, 1)


def chip_sum(left, right):
    pipe = lax.axis_index("pipe")
    left = jnp.concatenate([half_columns(left, pipe), swapped(half_columns(left, 1 - pipe))], 0)
    return left_transposed(left, both_cores(right)).astype(jnp.bfloat16)


def chip_half(partial):
    half = partial.shape[0] // 2
    pipe = lax.axis_index("pipe")
    partial = partial.astype(jnp.bfloat16)
    keep = lax.dynamic_slice_in_dim(partial, pipe * half, half, 0)
    give = lax.dynamic_slice_in_dim(partial, (1 - pipe) * half, half, 0)
    return (keep.astype(jnp.float32) + swapped(give).astype(jnp.float32)).astype(jnp.bfloat16)


def device(pipe, grp, dp):
    return {"pipe": pipe, "grp": grp, "dp": dp}


def remote(source, target, send, arrive, to):
    return pltpu.make_async_remote_copy(
        src_ref=source,
        dst_ref=target,
        send_sem=send,
        recv_sem=arrive,
        device_id=device(*to),
        device_id_type=pl.DeviceIdType.MESH,
    )


def tell(barrier, to):
    pl.semaphore_signal(
        barrier, inc=1, device_id=device(*to), device_id_type=pl.DeviceIdType.MESH
    )


def greet(others):
    barrier = pltpu.get_barrier_semaphore()
    for to in others:
        tell(barrier, to)
    pl.semaphore_wait(barrier, len(others))


class Place:
    def __init__(self, sizes):
        self.pipes, self.grps, self.dps = sizes
        self.plane_only = self.dps == 1
        self.pipe, self.grp, self.dp = [lax.axis_index(axis) for axis in AXES]
        column, row = self.grp % 2, self.grp // 2
        self.beside = 2 * row + 1 - column
        self.below = 2 * (1 - row) + column
        self.across = 3 - self.grp

    @property
    def spot(self):
        return 0 if self.plane_only else self.dp

    def plane(self):
        found = []
        for a in range(self.pipes):
            for b in range(self.grps):
                if (a, b) != (0, 0):
                    ahead = ((self.pipe + a) % self.pipes, (self.grp + b) % self.grps)
                    back = (
                        (self.pipe + self.pipes - a) % self.pipes,
                        (self.grp + self.grps - b) % self.grps,
                    )
                    found.append((ahead, back))
        return found

    def line(self, step):
        return (self.dp + step) % self.dps

    def behind(self, step):
        return (self.dp + self.dps - step) % self.dps

    def others(self):
        found = []
        for a in range(self.pipes):
            for b in range(self.grps):
                for c in range(self.dps):
                    if (a, b, c) != (0, 0, 0):
                        ahead = (
                            (self.pipe + a) % self.pipes,
                            (self.grp + b) % self.grps,
                            (self.dp + c) % self.dps,
                        )
                        back = (
                            (self.pipe + self.pipes - a) % self.pipes,
                            (self.grp + self.grps - b) % self.grps,
                            (self.dp + self.dps - c) % self.dps,
                        )
                        found.append((ahead, back))
        return found

    def index(self, pipe, grp, dp):
        return (pipe * self.grps + grp) * self.dps + dp


def swap_all(place, rows, arrived, send, arrive, own):
    me = place.index(place.pipe, place.grp, place.dp)
    copies = []
    for i, (ahead, back) in enumerate(place.others()):
        to = place.index(*ahead)
        copies.append(remote(rows.at[to], arrived.at[me], send.at[i], arrive.at[i], ahead))
        copies[-1].start()
    kept = pltpu.make_async_copy(rows.at[me], arrived.at[me], own)
    kept.start()

    def finish():
        for i, (ahead, back) in enumerate(place.others()):
            origin = place.index(*back)
            copies[i].wait_send()
            remote(rows.at[me], arrived.at[origin], send.at[i], arrive.at[i], ahead).wait_recv()
        kept.wait()

    return finish


def swap_plane(place, rows, arrived, send, arrive, own):
    me = place.pipe * place.grps + place.grp
    copies = []
    for i, (ahead, back) in enumerate(place.plane()):
        to = ahead[0] * place.grps + ahead[1]
        copies.append(
            remote(rows.at[to], arrived.at[me], send.at[i], arrive.at[i], ahead + (place.dp,))
        )
        copies[-1].start()
    kept = pltpu.make_async_copy(rows.at[me], arrived.at[me], own)
    kept.start()

    def finish():
        for i, (ahead, back) in enumerate(place.plane()):
            origin = back[0] * place.grps + back[1]
            copies[i].wait_send()
            remote(
                rows.at[me], arrived.at[origin], send.at[i], arrive.at[i], ahead + (place.dp,)
            ).wait_recv()
        kept.wait()

    return finish


def begin_kernel(sizes, row_ref, up_ref, all_ref, arrived_ref, *sems):
    send, arrive, own, plane_send, plane_arrive, plane_own = sems
    place = Place(sizes)
    others = place.others()
    greet([ahead for ahead, _ in others])
    finish = swap_plane(place, up_ref, arrived_ref, plane_send, plane_arrive, plane_own)
    me = place.index(place.pipe, place.grp, place.dp)
    copies = []
    for i, (ahead, _) in enumerate(others):
        copies.append(remote(row_ref, all_ref.at[me], send.at[i], arrive.at[i], ahead))
        copies[-1].start()
    kept = pltpu.make_async_copy(row_ref, all_ref.at[me], own)
    kept.start()
    for i, (ahead, back) in enumerate(others):
        copies[i].wait_send()
        remote(
            row_ref, all_ref.at[place.index(*back)], send.at[i], arrive.at[i], ahead
        ).wait_recv()
    kept.wait()
    finish()


def begin(row, blocks, sizes, collective):
    parts = math.prod(sizes)
    sems = pltpu.SemaphoreType.DMA((parts - 1,))
    plane_sems = pltpu.SemaphoreType.DMA((sizes[0] * sizes[1] - 1,))
    return pl.pallas_call(
        functools.partial(begin_kernel, sizes),
        out_shape=(
            jax.ShapeDtypeStruct((parts,) + row.shape, row.dtype),
            jax.ShapeDtypeStruct(blocks.shape, blocks.dtype),
        ),
        in_specs=[pl.BlockSpec(memory_space=pltpu.VMEM)] * 2,
        out_specs=[pl.BlockSpec(memory_space=pltpu.VMEM)] * 2,
        scratch_shapes=[
            sems,
            sems,
            pltpu.SemaphoreType.DMA,
            plane_sems,
            plane_sems,
            pltpu.SemaphoreType.DMA,
        ],
        compiler_params=pltpu.CompilerParams(
            collective_id=collective, has_side_effects=True, vmem_limit_bytes=8 << 20
        ),
    )(row, blocks)


def spread_kernel(sizes, row_ref, all_ref, send, arrive, own):
    place = Place(sizes)
    others = place.others()
    greet([ahead for ahead, _ in others])
    me = place.index(place.pipe, place.grp, place.dp)
    copies = []
    for i, (ahead, _) in enumerate(others):
        copies.append(remote(row_ref, all_ref.at[me], send.at[i], arrive.at[i], ahead))
        copies[-1].start()
    kept = pltpu.make_async_copy(row_ref, all_ref.at[me], own)
    kept.start()
    for i, (ahead, back) in enumerate(others):
        copies[i].wait_send()
        remote(
            row_ref, all_ref.at[place.index(*back)], send.at[i], arrive.at[i], ahead
        ).wait_recv()
    kept.wait()


def spread(row, sizes, collective):
    parts = math.prod(sizes)
    sems = pltpu.SemaphoreType.DMA((parts - 1,))
    return pl.pallas_call(
        functools.partial(spread_kernel, sizes),
        out_shape=jax.ShapeDtypeStruct((parts,) + row.shape, row.dtype),
        in_specs=[pl.BlockSpec(memory_space=pltpu.VMEM)],
        out_specs=pl.BlockSpec(memory_space=pltpu.VMEM),
        scratch_shapes=[sems, sems, pltpu.SemaphoreType.DMA],
        compiler_params=pltpu.CompilerParams(
            collective_id=collective, has_side_effects=True, vmem_limit_bytes=8 << 20
        ),
    )(row)


def stats_kernel(sizes, own_ref, all_ref, held, result, send, arrive, own, send_two, arrive_two):
    place = Place(sizes)
    others = place.others()
    greet([ahead for ahead, _ in others])
    swap_all(place, own_ref, held, send, arrive, own)()
    peaks = held[:, 0]
    peak = jnp.max(peaks, 0, keepdims=True)
    total = jnp.sum(held[:, 1] * jnp.exp(peaks - peak), 0, keepdims=True)
    label = jnp.sum(held[:, 2], 0, keepdims=True)
    result[0:1] = peak
    result[1:2] = total
    result[2:3] = label
    result[3:8] = jnp.zeros((5, result.shape[1]), jnp.float32)
    me = place.index(place.pipe, place.grp, place.dp)
    copies = []
    for i, (ahead, _) in enumerate(others):
        copies.append(remote(result, all_ref.at[me], send_two.at[i], arrive_two.at[i], ahead))
        copies[-1].start()
    all_ref[me] = result[...]
    for i, (ahead, back) in enumerate(others):
        copies[i].wait_send()
        remote(
            result, all_ref.at[place.index(*back)], send_two.at[i], arrive_two.at[i], ahead
        ).wait_recv()


def combine_stats(own, sizes, collective):
    parts, _, rows = own.shape
    sems = pltpu.SemaphoreType.DMA((parts - 1,))
    return pl.pallas_call(
        functools.partial(stats_kernel, sizes),
        out_shape=jax.ShapeDtypeStruct(own.shape, jnp.float32),
        in_specs=[pl.BlockSpec(memory_space=pltpu.VMEM)],
        out_specs=pl.BlockSpec(memory_space=pltpu.VMEM),
        scratch_shapes=[
            pltpu.VMEM(own.shape, jnp.float32),
            pltpu.VMEM((8, rows), jnp.float32),
            sems,
            sems,
            pltpu.SemaphoreType.DMA,
            sems,
            sems,
        ],
        compiler_params=pltpu.CompilerParams(
            collective_id=collective, has_side_effects=True, vmem_limit_bytes=8 << 20
        ),
    )(own)


def gather_kernel(sizes, pieces, routed, *refs):
    count = max(piece[0] for piece in pieces) + 1
    shards, refs = refs[:count], refs[count:]
    if routed:
        rows_ref, refs = refs[0], refs[1:]
    fulls, refs = refs[:count], refs[count:]
    if routed:
        arrived_ref, refs = refs[0], refs[1:]
    send, arrive, own, swap_send, swap_arrive, swap_own = refs
    place = Place(sizes)
    pipe, grp, dp = place.pipe, place.grp, place.dp
    near = place.beside * (1 - pipe) + place.below * pipe
    far = place.below * (1 - pipe) + place.beside * pipe
    core = (1 - pipe, grp, dp)
    hops = place.dps - 1
    spot = place.spot
    ends = (dp < hops, dp > 0)
    sides = ((pipe, grp, dp + 1), (pipe, grp, dp - 1))
    both = range(2 if hops else 0)
    if routed:
        greet([ahead for ahead, _ in place.others()])
    else:
        greet(
            [(pipe, grp, place.line(k + 1)) for k in range(hops)]
            + [(pipe, near, dp), (pipe, far, dp), core]
        )
    waits = []

    def view(piece, *at):
        array, first, rows = piece
        return fulls[array].at[at + ((slice(None),) * (3 - len(at))) + (pl.ds(first, rows),)]

    def launch(n, index, source, piece, to, *at):
        copy = remote(source, view(piece, *at), send.at[n, index], arrive.at[n, index], to)
        copy.start()
        waits.append(copy)

    def landed(n, index, piece, *at):
        target = view(piece, *at)
        remote(target, target, send.at[n, index], arrive.at[n, index], core).wait_recv()

    def along(n, side, hop, finish=False):
        origin = dp - hop if side == 0 else dp + hop
        here = origin >= 0 if side == 0 else origin <= hops
        piece, index = pieces[n], side * hops + hop

        def copy():
            array, first, rows = piece
            target = view(piece, pipe, grp, origin)
            source = shards[array].at[pl.ds(first, rows)] if hop == 0 else target
            return remote(source, target, send.at[n, index], arrive.at[n, index], sides[side])

        if finish:

            @pl.when(here & ends[side])
            def _():
                copy().wait_send()

            return
        if hop > 0:

            @pl.when(here)
            def _():
                landed(n, index - 1, piece, pipe, grp, origin)

        if hop < hops:

            @pl.when(here & ends[side])
            def _():
                copy().start()

    keeps = {}

    def over_line(n, hop):
        if hop == 0:
            array, first, rows = pieces[n]
            source = shards[array].at[pl.ds(first, rows)]
            keeps[n] = pltpu.make_async_copy(source, view(pieces[n], pipe, grp, spot), own.at[n])
            keeps[n].start()
        for side in both:
            along(n, side, hop)

    def over_plane(n):
        piece = pieces[n]
        over_line(n, hops)
        keeps[n].wait()
        group = view(piece, pipe, grp)
        launch(n, 2 * hops, group, piece, (pipe, near, dp), pipe, grp)
        launch(n, 2 * hops + 1, group, piece, (pipe, far, dp), pipe, grp)
        launch(n, 2 * hops + 3, group, piece, core, pipe, grp)

    def pass_on(n):
        piece = pieces[n]
        landed(n, 2 * hops, piece, pipe, near)
        group = view(piece, pipe, near)
        launch(n, 2 * hops + 2, group, piece, (pipe, far, dp), pipe, near)
        launch(n, 2 * hops + 4, group, piece, core, pipe, near)
        landed(n, 2 * hops + 1, piece, pipe, far)
        launch(n, 2 * hops + 5, view(piece, pipe, far), piece, core, pipe, far)

    def last(n):
        piece = pieces[n]
        landed(n, 2 * hops + 2, piece, pipe, place.across)
        launch(n, 2 * hops + 6, view(piece, pipe, place.across), piece, core, pipe, place.across)

    stages = [functools.partial(over_line, hop=hop) for hop in range(hops)]
    stages += [over_plane, pass_on, last]
    total = len(pieces)
    for turn in range(total + len(stages) - 1):
        for at, stage in enumerate(stages):
            if 0 <= turn - at < total:
                stage(turn - at)
        if turn == 5 and routed:
            finish = swap_all(place, rows_ref, arrived_ref, swap_send, swap_arrive, swap_own)
    for n, piece in enumerate(pieces):
        landed(n, 2 * hops + 3, piece, 1 - pipe, grp)
        landed(n, 2 * hops + 4, piece, 1 - pipe, far)
        landed(n, 2 * hops + 5, piece, 1 - pipe, near)
        landed(n, 2 * hops + 6, piece, 1 - pipe, place.across)
        for side in both:
            for hop in range(hops):
                along(n, side, hop, finish=True)
    for copy in waits:
        copy.wait_send()
    if routed:
        finish()


def gather_all(shards, pieces, sizes, collective, rows=None):
    parts = math.prod(sizes)
    routed = rows is not None
    kinds = 2 * (sizes[2] - 1) + 7
    out_shape = [jax.ShapeDtypeStruct(sizes + shard.shape, shard.dtype) for shard in shards]
    if routed:
        out_shape.append(jax.ShapeDtypeStruct(rows.shape, rows.dtype))
    operands = list(shards) + ([rows] if routed else [])
    sems = pltpu.SemaphoreType.DMA((len(pieces), kinds))
    swaps = pltpu.SemaphoreType.DMA((parts - 1 if routed else 1,))
    return pl.pallas_call(
        functools.partial(gather_kernel, sizes, tuple(pieces), routed),
        out_shape=out_shape,
        in_specs=[pl.BlockSpec(memory_space=pl.ANY)] * len(operands),
        out_specs=[pl.BlockSpec(memory_space=pl.ANY)] * len(out_shape),
        scratch_shapes=[
            sems,
            sems,
            pltpu.SemaphoreType.DMA((len(pieces),)),
            swaps,
            swaps,
            pltpu.SemaphoreType.DMA,
        ],
        compiler_params=pltpu.CompilerParams(collective_id=collective, has_side_effects=True),
    )(*operands)


def reduce_kernel(sizes, pieces, cores, routed, *refs):
    arrays, total = max(piece[0] for piece in pieces) + 1, len(pieces)
    partials, refs = refs[:arrays], refs[arrays:]
    if routed:
        rows_ref, blocks_ref, refs = refs[0], refs[1], refs[2:]
    sums, refs = refs[:arrays], refs[arrays:]
    if routed:
        arrived_ref, blocks_arrived_ref, refs = refs[0], refs[1], refs[2:]
    chips, refs = refs[: total if cores else 0], refs[total if cores else 0 :]
    others, refs = refs[: total if cores else 0], refs[total if cores else 0 :]
    mine, refs = refs[:total], refs[total:]
    planes, refs = refs[:total], refs[total:]
    lines, refs = refs[:total], refs[total:]
    send, arrive, own, swap_send, swap_arrive, swap_own, plane_send, plane_arrive, plane_own = refs
    place = Place(sizes)
    pipe, grp, dp = place.pipe, place.grp, place.dp
    near = place.beside * (1 - pipe) + place.below * pipe
    far = place.below * (1 - pipe) + place.beside * pipe
    core = (1 - pipe, grp, dp)
    hops = place.dps - 1
    block = 16
    if routed:
        greet([ahead for ahead, _ in place.others()])
    else:
        greet(
            [(pipe, grp, place.line(k + 1)) for k in range(hops)]
            + [(pipe, near, dp), (pipe, far, dp)]
            + ([core] if cores else [])
        )
    copies = {}

    def launch(n, index, source, target, to):
        copies[n, index] = remote(source, target, send.at[n, index], arrive.at[n, index], to)
        copies[n, index].start()

    def blocks(n, body):
        deep = pieces[n][2] // block

        def one(i, _):
            at = pl.ds(pl.multiple_of(i % deep * block, block), block)
            body(i // deep, at)
            return 0

        lax.fori_loop(0, place.dps * deep, one, 0)

    def to_core(n):
        array, first, rows = pieces[n]
        if cores:
            part = partials[array].at[1 - pipe, :, :, pl.ds(first, rows)]
            launch(n, 0, part, others[n], core)
            part = partials[array].at[pipe, :, :, pl.ds(first, rows)]
            copies[n, "own"] = pltpu.make_async_copy(part, chips[n], own.at[n, 0])
            copies[n, "own"].start()

    def to_near(n):
        array, first, rows = pieces[n]
        if cores:
            copies[n, "own"].wait()
            copies[n, 0].wait_recv()
            for g in range(place.grps):

                def add(d, at, g=g):
                    left = chips[n][g, d, at].astype(jnp.float32)
                    chips[n][g, d, at] = (left + others[n][g, d, at].astype(jnp.float32)).astype(
                        jnp.bfloat16
                    )

                blocks(n, add)
            part = lambda g: chips[n].at[g]
        else:
            part = lambda g: partials[array].at[g, :, pl.ds(first, rows)]
            for j, g in enumerate((far, grp)):
                copies[n, "own", j] = pltpu.make_async_copy(part(g), mine[n].at[j], own.at[n, j])
                copies[n, "own", j].start()
        launch(n, 1, part(near), planes[n].at[1], (pipe, near, dp))
        launch(n, 2, part(place.across), planes[n].at[0], (pipe, near, dp))

    def to_far(n):
        if not cores:
            copies[n, "own", 0].wait()
            copies[n, "own", 1].wait()
        copies[n, 1].wait_recv()
        copies[n, 2].wait_recv()
        for j, g in enumerate((far, grp)):

            def add(d, at, j=j, g=g):
                left = chips[n][g, d, at] if cores else mine[n][j, d, at]
                right = planes[n][j, d, at].astype(jnp.float32)
                mine[n][j, d, at] = (left.astype(jnp.float32) + right).astype(jnp.bfloat16)

            blocks(n, add)
            if j == 0:
                launch(n, 3, mine[n].at[0], planes[n].at[2], (pipe, far, dp))

    def to_lines(n):
        copies[n, 3].wait_recv()

        def add(d, at):
            left = mine[n][1, d, at].astype(jnp.float32)
            mine[n][1, d, at] = (left + planes[n][2, d, at].astype(jnp.float32)).astype(
                jnp.bfloat16
            )

        def add_last(d, at):
            array, first, rows = pieces[n]
            left = mine[n][1, d, at].astype(jnp.float32)
            to = pl.ds(pl.multiple_of(first + at.start, block), block)
            sums[array][to] = left + planes[n][2, d, at].astype(jnp.float32)

        if hops == 0:
            blocks(n, add_last)
            return
        blocks(n, add)
        for k in range(hops):
            to = place.line(k + 1)
            launch(n, 4 + k, mine[n].at[1, to], lines[n].at[k], (pipe, grp, to))

    def to_sum(n):
        array, first, rows = pieces[n]
        for k in range(hops):
            copies[n, 4 + k].wait_recv()

        def add(i, _):
            at = pl.ds(pl.multiple_of(i * block, block), block)
            total = mine[n][1, place.spot, at].astype(jnp.float32)
            for k in range(hops):
                total = total + lines[n][k, at].astype(jnp.float32)
            sums[array][pl.ds(pl.multiple_of(first + i * block, block), block)] = total
            return 0

        lax.fori_loop(0, rows // block, add, 0)

    stages = ([to_core] if cores else []) + [to_near, to_far, to_lines]
    stages += [to_sum] if hops else []
    for turn in range(total + len(stages) - 1):
        for at, stage in enumerate(stages):
            if 0 <= turn - at < total:
                stage(turn - at)
        if turn == 0 and routed:
            finish = (
                swap_all(place, rows_ref, arrived_ref, swap_send, swap_arrive, swap_own),
                swap_plane(
                    place, blocks_ref, blocks_arrived_ref, plane_send, plane_arrive, plane_own
                ),
            )
    for key, copy in copies.items():
        if key[1] != "own":
            copy.wait_send()
    if routed:
        finish[0]()
        finish[1]()


def reduce_all(partials, pieces, sizes, collective, rows=None, plane_rows=None, cores=False):
    parts = math.prod(sizes)
    total = len(pieces)
    routed = rows is not None
    low = jnp.bfloat16
    _, grps, dps = sizes
    shapes = [(dps, size, partials[array].shape[-1]) for array, _, size in pieces]
    out_shape = [jax.ShapeDtypeStruct(partial.shape[-2:], jnp.float32) for partial in partials]
    out_specs = [pl.BlockSpec(memory_space=pltpu.VMEM)] * len(partials)
    if routed:
        for extra in (rows, plane_rows):
            out_shape.append(jax.ShapeDtypeStruct(extra.shape, extra.dtype))
            out_specs.append(pl.BlockSpec(memory_space=pl.ANY))
    operands = list(partials) + ([rows, plane_rows] if routed else [])
    sems = pltpu.SemaphoreType.DMA((total, 4 + dps - 1))
    swaps = pltpu.SemaphoreType.DMA((parts - 1 if routed else 1,))
    plane_swaps = pltpu.SemaphoreType.DMA((sizes[0] * grps - 1,))
    scratch = [pltpu.VMEM((grps,) + shape, low) for shape in shapes] * (2 if cores else 0)
    scratch += [pltpu.VMEM((2,) + shape, low) for shape in shapes]
    scratch += [pltpu.VMEM((3,) + shape, low) for shape in shapes]
    scratch += [pltpu.VMEM((max(dps - 1, 1),) + shape[1:], low) for shape in shapes]
    return pl.pallas_call(
        functools.partial(reduce_kernel, sizes, tuple(pieces), cores, routed),
        out_shape=out_shape,
        in_specs=[pl.BlockSpec(memory_space=pl.ANY)] * len(operands),
        out_specs=out_specs,
        scratch_shapes=scratch
        + [
            sems,
            sems,
            pltpu.SemaphoreType.DMA((total, 2)),
            swaps,
            swaps,
            pltpu.SemaphoreType.DMA,
            plane_swaps,
            plane_swaps,
            pltpu.SemaphoreType.DMA,
        ],
        compiler_params=pltpu.CompilerParams(
            collective_id=collective, has_side_effects=True, vmem_limit_bytes=48 << 20
        ),
    )(*operands)


def pair_rows(pair, first):
    pair = pair.astype(jnp.float32)
    low = jnp.bfloat16
    return jnp.concatenate(
        [jnp.where(first, pair, 0.0).astype(low), jnp.where(first, 0.0, pair).astype(low)], 0
    )


def pair_probs(rows, keys, live, scale):
    scores = jnp.where(live, right_transposed(rows, keys) * scale, -1e30)
    exp_scores = jnp.exp(scores - jnp.max(scores, -1, keepdims=True))
    return exp_scores / jnp.sum(exp_scores, -1, keepdims=True)


def attention_masks(lengths_ref, slots, seq_len, lanes):
    live = lax.broadcasted_iota(jnp.int32, (1, seq_len), 1) < lengths_ref[pl.program_id(0)]
    first = lax.broadcasted_iota(jnp.int32, (slots, lanes), 1) < lanes // 2
    return live, first


def attention_kernel(scale, lanes, lengths_ref, q_ref, k_ref, v_ref, out_ref):
    slots = q_ref.shape[0]
    live, first = attention_masks(lengths_ref, slots, k_ref.shape[0], lanes)
    for pair in range(q_ref.shape[1] // lanes):
        at = slice(pair * lanes, (pair + 1) * lanes)
        probs = pair_probs(pair_rows(q_ref[:, at], first), k_ref[:, at], live, scale)
        context = matmul(probs.astype(jnp.bfloat16), v_ref[:, at])
        out_ref[:, at] = jnp.where(first, context[:slots], context[slots:]).astype(jnp.bfloat16)


def attention_back_kernel(
    scale, lanes, lengths_ref, q_ref, k_ref, v_ref, grad_ref, dq_ref, dk_ref, dv_ref
):
    slots = q_ref.shape[0]
    low = jnp.bfloat16
    live, first = attention_masks(lengths_ref, slots, k_ref.shape[0], lanes)
    for pair in range(q_ref.shape[1] // lanes):
        at = slice(pair * lanes, (pair + 1) * lanes)
        rows, grads = pair_rows(q_ref[:, at], first), pair_rows(grad_ref[:, at], first)
        probs = pair_probs(rows, k_ref[:, at], live, scale)
        dv_ref[:, at] = left_transposed(probs.astype(low), grads).astype(low)
        d_probs = right_transposed(grads, v_ref[:, at])
        d_scores = probs * (d_probs - jnp.sum(probs * d_probs, -1, keepdims=True))
        d_scores = d_scores.astype(low)
        d_query = matmul(d_scores, k_ref[:, at]) * scale
        dq_ref[:, at] = jnp.where(first, d_query[:slots], d_query[slots:]).astype(low)
        dk_ref[:, at] = (left_transposed(d_scores, rows) * scale).astype(low)


def attention(lengths, queries, both, grads=None):
    own = lengths.shape[0]
    width = queries.shape[1]
    slots, seq_len = queries.shape[0] // own, both.shape[0] // own
    lanes = 2 * width // H
    scale = (width // H) ** (-0.5)
    cuts = 2
    part = width // cuts
    row = pl.BlockSpec((slots, part), lambda s, h: (s, h))
    keys = pl.BlockSpec((seq_len, part), lambda s, h: (s, h))
    values = pl.BlockSpec((seq_len, part), lambda s, h: (s, cuts + h))
    in_specs = [pl.BlockSpec(memory_space=pltpu.SMEM), row, keys, values]
    flat = jax.ShapeDtypeStruct(queries.shape, jnp.bfloat16)
    tall = jax.ShapeDtypeStruct((both.shape[0], width), jnp.bfloat16)
    if grads is None:
        return pl.pallas_call(
            functools.partial(attention_kernel, scale, lanes),
            grid=(own, cuts),
            out_shape=flat,
            in_specs=in_specs,
            out_specs=row,
        )(lengths, queries, both, both)
    return pl.pallas_call(
        functools.partial(attention_back_kernel, scale, lanes),
        grid=(own, cuts),
        out_shape=(flat, tall, tall),
        in_specs=in_specs + [row],
        out_specs=(row, keys, keys),
    )(lengths, queries, both, both, grads)


def even_pieces(array, rows, cuts):
    size = rows // cuts
    return [(array, i * size, size) for i in range(cuts)]


def start_all(row, blocks, sizes, collective):
    if collective is None:
        return lax.all_gather(row, AXES, axis=0), lax.all_to_all(blocks, PLANE, 0, 0)
    return begin(row, blocks, sizes, collective)


def gather_weights(shards, pieces, sizes, collective, rows):
    if collective is None:
        fulls = [lax.all_gather(shard, AXES, axis=0) for shard in shards]
        arrived = lax.all_to_all(rows, AXES, 0, 0)
    else:
        *fulls, arrived = gather_all(shards, pieces, sizes, collective, rows)
    return [full.reshape(-1, full.shape[-1]) for full in fulls], arrived


def gather_rows(shard, sizes, collective, cuts):
    if collective is None:
        axes = AXES if sizes[2] > 1 else PLANE
        return lax.all_gather(shard, axes, axis=0, tiled=True)
    (full,) = gather_all([shard], even_pieces(0, shard.shape[0], cuts), sizes, collective)
    return full.reshape(-1, full.shape[-1])


def sum_rows(partial, sizes, collective, cuts):
    if collective is None:
        axes = AXES if sizes[2] > 1 else PLANE
        total = lax.psum_scatter(partial, axes, scatter_dimension=0, tiled=True)
        return total.astype(jnp.float32)
    shaped = partial.reshape(sizes + (-1, partial.shape[1]))
    pieces = even_pieces(0, shaped.shape[3], cuts)
    (total,) = reduce_all([shaped], pieces, sizes, collective, cores=True)
    return total


def sum_chips(partials, pieces, sizes, collective, rows, blocks):
    if collective is not None:
        shaped = [p.reshape(sizes[1:] + (-1, p.shape[1])) for p in partials]
        *sums, rows, blocks = reduce_all(shaped, pieces, sizes, collective, rows, blocks)
        return sums, rows, blocks
    sums = [
        lax.psum_scatter(p, CHIPS, scatter_dimension=0, tiled=True).astype(jnp.float32)
        for p in partials
    ]
    return sums, lax.all_to_all(rows, AXES, 0, 0), lax.all_to_all(blocks, PLANE, 0, 0)


def line_shift(shard, step):
    size = lax.axis_size("dp")
    return lax.ppermute(shard, "dp", [(i, (i + step) % size) for i in range(size)])


def line_gather(shard, collective):
    if collective is None:
        return lax.all_gather(shard, "dp", axis=0)
    size = lax.axis_size("dp")
    me = lax.axis_index("dp")
    kept = jnp.stack([shard] + [line_shift(shard, step) for step in range(1, size)])
    order = [(me + size - i) % size for i in range(size)]
    return jnp.concatenate([lax.dynamic_slice_in_dim(kept, at, 1, 0) for at in order], 0)


def line_sum(partial, collective):
    partial = partial.astype(jnp.bfloat16)
    if collective is None:
        total = lax.psum_scatter(partial, "dp", scatter_dimension=0, tiled=False)
        return total.astype(jnp.float32)
    size = lax.axis_size("dp")
    me = lax.axis_index("dp")

    def entry(step):
        return lax.dynamic_index_in_dim(partial, (me + step) % size, 0, keepdims=False)

    total = entry(0).astype(jnp.float32)
    for step in range(1, size):
        total = total + line_shift(entry(step), step).astype(jnp.float32)
    return total


def spread_row(row, sizes, collective):
    if collective is None:
        return lax.all_gather(row, AXES, axis=0)
    return spread(row, sizes, collective)


def share_stats(peak, total, label, sizes, collective):
    if collective is None:
        top = lax.pmax(peak, AXES)
        total, label = lax.psum((total * jnp.exp(peak - top), label), AXES)
        return top, total, label
    parts = math.prod(sizes)
    stats = jnp.stack([peak, total, label])
    stats = jnp.pad(stats.reshape(3, parts, -1).swapaxes(0, 1), ((0, 0), (0, 5), (0, 0)))
    stats = combine_stats(stats, sizes, collective)
    return [stats[:, i].reshape(-1) for i in range(3)]


def adam_step(weight, first, second, grad, factor, rate):
    clipped = grad * factor
    first = beta_one * first + (1.0 - beta_one) * clipped
    second = beta_two * second + (1.0 - beta_two) * clipped * clipped
    first_hat = first / (1.0 - beta_one**STEP)
    second_hat = second / (1.0 - beta_two**STEP)
    weight = weight - rate * (first_hat / (jnp.sqrt(second_hat) + epsilon) + weight_decay * weight)
    return (weight, first, second)


def per_device(
    token_ids,
    lengths,
    masked_at,
    labels,
    word_table,
    word_first,
    word_second,
    pos_table,
    pos_first,
    pos_second,
    qkv_weight,
    qkv_first,
    qkv_second,
    square_weight,
    square_first,
    square_second,
    up_weight,
    up_first,
    up_second,
    down_weight,
    down_first,
    down_second,
    vec_table,
    vec_first,
    vec_second,
    head_bias,
    bias_first,
    bias_second,
):
    narrow = jnp.bfloat16
    seq_len, slots = token_ids.shape[1], masked_at.shape[1]
    width = word_table.shape[1]
    vocab = head_bias.shape[0]
    rows_per = word_table.shape[0]
    parts = lax.axis_size(AXES)
    halves = lax.axis_size("pipe")
    me = lax.axis_index(AXES)
    own = token_ids.shape[0] // halves
    first_own = lax.axis_index("pipe") * own
    head_dim = width // H
    sizes = tuple(lax.axis_size(axis) for axis in AXES)
    shards = (word_table, qkv_weight, square_weight[0], up_weight, down_weight)
    direct = sizes[:2] == (2, 4) and all(shard.shape[0] % 32 == 0 for shard in shards)
    ids = tuple(range(11)) if direct else (None,) * 11
    plane_sizes = sizes[:2] + (1,)

    spare = -(seq_len + slots + 1) % 128
    packed = jnp.concatenate(
        [token_ids, labels, lengths[:, None], jnp.zeros((token_ids.shape[0], spare), jnp.int32)], 1
    )
    packed = lax.dynamic_slice_in_dim(packed, first_own, own, 0)
    planes = sizes[0] * sizes[1]
    units = up_weight.shape[1] // planes
    cut = me // sizes[2]
    blocks = up_weight.astype(narrow).reshape(up_weight.shape[0], planes, units).swapaxes(0, 1)
    packed, blocks = start_all(packed, blocks, sizes, ids[0])
    down_low = line_gather(down_weight.astype(narrow), ids[0]).reshape(units, width)
    up_low = line_gather(blocks, ids[0]).swapaxes(0, 1).reshape(width, units)
    all_ids = packed[:, :, :seq_len]
    all_labels = packed[:, :, seq_len : seq_len + slots].reshape(-1)
    all_lengths = packed[:, :, seq_len + slots]
    places = jnp.arange(seq_len, dtype=jnp.int32)
    all_live = places[None, None, :] < all_lengths[:, :, None]
    all_counts = masked_counts(all_lengths, slots)
    total = jnp.sum(all_counts).astype(jnp.float32)
    slot_index = jnp.arange(slots, dtype=jnp.int32)
    all_valid = (slot_index < all_counts[:, :, None]).astype(jnp.float32).reshape(-1)
    own_lengths = lax.dynamic_slice_in_dim(lengths, first_own, own, 0)
    masked = lax.dynamic_slice_in_dim(masked_at, first_own, own, 0)

    word_low = word_table.astype(narrow)
    routes = Routes(all_ids.reshape(parts, -1), all_live.reshape(parts, -1), rows_per)
    small = pos_table.shape[0] + vec_table.shape[0]
    spare = -small % 128
    small_low = jnp.concatenate(
        [pos_table.T, vec_table.T, jnp.zeros((pos_table.shape[1], spare), jnp.float32)], 1
    ).astype(narrow)
    low = [
        small_low,
        qkv_weight.astype(narrow),
        square_weight[0].astype(narrow),
        square_weight[1].astype(narrow),
    ]
    deep = small_low.shape[0]
    pieces = [(0, 0, deep), (1, 0, deep // 2), (1, deep // 2, deep // 2), (2, 0, deep), (3, 0, deep)]
    send = routes.table_rows(word_low, 0).reshape(parts, -1, width)
    (small_full, qkv_low, out_low, turn_low), arrived = gather_weights(
        low, pieces, sizes, ids[1], send
    )
    word_rows = routes.fetch(word_low, arrived.reshape(-1, width))
    small_full = small_full.T
    pos_low = small_full[:seq_len]
    vec_rows = small_full[seq_len:small].astype(jnp.float32)
    query_low, both_low = qkv_low[:, :width], qkv_low[:, width:]

    second = (places[None, :] >= ((own_lengths + 1) // 2)[:, None]).reshape(-1, 1)
    embedded = (
        word_rows
        + jnp.tile(pos_low.astype(jnp.float32), (own, 1))
        + jnp.where(second, vec_rows[1], vec_rows[0])
    )
    start, norm_zero = norm_forward(embedded, vec_rows[2], vec_rows[3])
    start_low = start.astype(narrow)
    both_bias = jnp.concatenate([jnp.zeros_like(vec_rows[5]), vec_rows[5]])
    both = (matmul(start_low, both_low) + both_bias).astype(narrow)
    pick = one_hot(masked, seq_len, jnp.float32)
    chosen = rows_by_seq(pick, start.reshape(own, seq_len, width)).reshape(-1, width)
    chosen_low = chosen.astype(narrow)
    queries = (matmul(chosen_low, query_low) + vec_rows[4]).astype(narrow)
    context = attention(own_lengths, queries, both)
    branch = matmul(context, out_low) + vec_rows[6]
    hidden, norm_one = norm_forward(chosen + branch, vec_rows[7], vec_rows[8])
    hidden = hidden.astype(narrow)

    plane_hidden = gather_rows(hidden, plane_sizes, ids[2], 2)
    up_bias = lax.dynamic_slice_in_dim(vec_rows[15:].reshape(-1), cut * units, units, 0)
    inner = matmul(plane_hidden, up_low) + up_bias
    activ = jax.nn.gelu(inner, approximate=False).astype(narrow)
    branch = sum_rows(matmul(activ, down_low).astype(narrow), plane_sizes, ids[3], 2) + vec_rows[9]
    mixed, norm_two = norm_forward(hidden.astype(jnp.float32) + branch, vec_rows[10], vec_rows[11])
    picked = mixed.astype(narrow)
    turned = matmul(picked, turn_low) + vec_rows[12]
    normed, norm_head = norm_forward(
        jax.nn.gelu(turned, approximate=False), vec_rows[13], vec_rows[14]
    )

    all_normed = gather_rows(normed.astype(narrow), sizes, ids[4], 4)
    column = me * rows_per + jnp.arange(rows_per, dtype=jnp.int32)
    bias_row = jnp.pad(head_bias, (0, parts * rows_per - vocab))
    bias_row = lax.dynamic_slice_in_dim(bias_row, me * rows_per, rows_per, 0)
    logits = right_transposed(all_normed, word_low) + bias_row
    logits = jnp.where(column < vocab, logits, -1e30)
    own_peak = jnp.max(logits, -1)
    own_total = jnp.sum(jnp.exp(logits - own_peak[:, None]), -1)
    hits = all_labels[:, None] == column
    own_label = jnp.sum(jnp.where(hits, logits, 0.0), -1)
    peak, exp_total, label_logit = share_stats(own_peak, own_total, own_label, sizes, ids[5])
    loss_total = jnp.sum(all_valid * (peak + jnp.log(exp_total) - label_logit))
    d_logits = (all_valid / total)[:, None] * (
        jnp.exp(logits - peak[:, None]) / exp_total[:, None] - hits.astype(jnp.float32)
    )
    d_bias = jnp.sum(d_logits, 0)
    d_logits_low = d_logits.astype(narrow)
    d_word = left_transposed(d_logits_low, all_normed)
    d_normed = sum_rows(matmul(d_logits_low, word_low).astype(narrow), sizes, ids[6], 8)

    d_gelu, d_gain_head, d_shift_head = norm_backward(d_normed, norm_head, vec_rows[13])
    d_turned = (d_gelu * gelu_slope(turned)).astype(narrow)
    d_turn_bias = jnp.sum(d_turned.astype(jnp.float32), 0)
    d_turn = chip_sum(picked, d_turned)
    d_picked = right_transposed(d_turned, turn_low)
    same = masked[:, :, None] == masked[:, None, :]
    earlier = slot_index[None, :] < slot_index[:, None]
    first_slot = jnp.logical_not(jnp.any(same & earlier, 2))
    merge = (same & first_slot[:, :, None]).astype(jnp.float32)
    d_mixed = rows_by_seq(merge, d_picked.reshape(own, slots, width)).reshape(-1, width)
    d_pre, d_gain_two, d_shift_two = norm_backward(d_mixed, norm_two, vec_rows[10])
    d_branch = d_pre.astype(narrow)
    d_down_bias = jnp.sum(d_branch.astype(jnp.float32), 0)
    plane_branch = gather_rows(d_branch, plane_sizes, ids[7], 2)
    own_down = line_sum(
        left_transposed(activ, plane_branch).reshape(sizes[2], -1, width), ids[7]
    )
    d_inner = (right_transposed(plane_branch, down_low) * gelu_slope(inner)).astype(narrow)
    d_up_bias = jnp.sum(d_inner.astype(jnp.float32), 0)
    d_up_bias = lax.dynamic_update_slice_in_dim(
        jnp.zeros((planes * units,), jnp.float32), d_up_bias, cut * units, 0
    ).reshape(-1, width)
    d_up = left_transposed(plane_hidden, d_inner).reshape(planes, sizes[2], -1, units)
    up_blocks = line_sum(d_up.swapaxes(0, 1), ids[7]).astype(narrow)
    d_hidden = sum_rows(right_transposed(d_inner, up_low).astype(narrow), plane_sizes, ids[8], 2)
    d_hidden = (d_pre + d_hidden).astype(narrow)

    d_pre, d_gain_one, d_shift_one = norm_backward(
        d_hidden.astype(jnp.float32), norm_one, vec_rows[7]
    )
    d_branch = d_pre.astype(narrow)
    d_out_bias = jnp.sum(d_branch.astype(jnp.float32), 0)
    d_out = chip_sum(context, d_branch)
    d_context = right_transposed(d_branch, out_low).astype(narrow)
    d_query, d_key, d_value = attention(own_lengths, queries, both, d_context)
    d_query_bias = jnp.sum(d_query.astype(jnp.float32), 0)
    d_value_bias = jnp.sum(d_value.astype(jnp.float32), 0)
    d_qkv = [
        chip_sum(chosen_low, d_query),
        chip_sum(start_low, d_key),
        chip_sum(start_low, d_value),
    ]
    d_chosen = d_pre + right_transposed(d_query, query_low)
    d_both = jnp.concatenate([d_key, d_value], 1)
    d_start = right_transposed(d_both, both_low) + rows_to_seq(
        pick, d_chosen.reshape(own, slots, width)
    ).reshape(-1, width)
    d_embedded, d_gain_zero, d_shift_zero = norm_backward(d_start, norm_zero, vec_rows[2])
    d_seg_zero = jnp.sum(jnp.where(second, 0.0, d_embedded), 0)
    d_seg_one = jnp.sum(jnp.where(second, d_embedded, 0.0), 0)
    d_embedded_low = d_embedded.astype(narrow)
    send = routes.token_rows(d_embedded_low, 0).reshape(parts, -1, width)
    d_small = jnp.concatenate(
        [
            jnp.sum(d_embedded.reshape(own, seq_len, width), 0),
            jnp.stack(
                [
                    d_seg_zero,
                    d_seg_one,
                    d_gain_zero,
                    d_shift_zero,
                    d_query_bias,
                    d_value_bias,
                    d_out_bias,
                    d_gain_one,
                    d_shift_one,
                    d_down_bias,
                    d_gain_two,
                    d_shift_two,
                    d_turn_bias,
                    d_gain_head,
                    d_shift_head,
                ]
            ),
            d_up_bias,
            jnp.zeros((spare, width), jnp.float32),
        ],
        0,
    )
    partials = [d_out, d_turn] + d_qkv + [chip_half(d_small.T)]
    pieces = [(i, 0, deep) for i in range(6)]
    (own_out, own_turn, own_q, own_k, own_v, own_small), arrived, up_blocks = sum_chips(
        partials, pieces, sizes, ids[9], send, up_blocks
    )
    own_qkv = jnp.concatenate([own_q, own_k, own_v], 1)
    own_up = up_blocks.swapaxes(0, 1).reshape(up_weight.shape).astype(jnp.float32)
    d_word = d_word + routes.give(d_embedded_low, arrived.reshape(-1, width))
    owned = (
        d_word,
        own_small[:, :seq_len].T,
        own_qkv,
        jnp.stack([own_out, own_turn]),
        own_up,
        own_down,
        own_small[:, seq_len:small].T,
    )
    local_squares = jnp.sum(d_bias * d_bias)
    for grad in owned:
        local_squares = local_squares + jnp.sum(grad * grad)
    spare = -(rows_per + 1) % 128
    last = jnp.concatenate([d_bias, local_squares[None], jnp.zeros((spare,), jnp.float32)])
    last = spread_row(last.reshape(8, -1), sizes, ids[10]).reshape(parts, -1)
    bias_grad = last[:, :rows_per].reshape(-1)[:vocab]
    grad_norm = jnp.sqrt(jnp.sum(last[:, rows_per]))
    factor = clip_norm / jnp.maximum(grad_norm, clip_norm)
    masters = (
        word_table,
        pos_table,
        qkv_weight,
        square_weight,
        up_weight,
        down_weight,
        vec_table,
        head_bias,
    )
    states = (
        (word_first, word_second),
        (pos_first, pos_second),
        (qkv_first, qkv_second),
        (square_first, square_second),
        (up_first, up_second),
        (down_first, down_second),
        (vec_first, vec_second),
        (bias_first, bias_second),
    )
    rates = (
        learn_rate,
        learn_rate,
        learn_rate,
        learn_rate,
        learn_rate,
        learn_rate,
        vector_rate,
        vector_rate,
    )
    grads = tuple(owned) + (bias_grad,)
    results = []
    for weight, state, grad, rate in zip(masters, states, grads, rates):
        results.extend(adam_step(weight, state[0], state[1], grad, factor, rate))
    return (
        results[0],
        results[1],
        results[2],
        results[3],
        results[4],
        results[5],
        results[6],
        results[7],
        results[8],
        results[9],
        results[10],
        results[11],
        results[12],
        results[13],
        results[14],
        results[15],
        results[16],
        results[17],
        results[18],
        results[19],
        results[20],
        results[21],
        results[22],
        results[23],
        loss_total,
        total,
        grad_norm,
    )


def solution(mesh):
    placed = (
        P(("grp", "dp"), None),
        P(("grp", "dp")),
        P(("grp", "dp"), None),
        P(("grp", "dp"), None),
        P(("pipe", "grp", "dp"), None),
        P(("pipe", "grp", "dp"), None),
        P(("pipe", "grp", "dp"), None),
        P(None, ("pipe", "grp", "dp")),
        P(None, ("pipe", "grp", "dp")),
        P(None, ("pipe", "grp", "dp")),
        P(("pipe", "grp", "dp"), None),
        P(("pipe", "grp", "dp"), None),
        P(("pipe", "grp", "dp"), None),
        P(None, ("pipe", "grp", "dp"), None),
        P(None, ("pipe", "grp", "dp"), None),
        P(None, ("pipe", "grp", "dp"), None),
        P(("pipe", "grp", "dp"), None),
        P(("pipe", "grp", "dp"), None),
        P(("pipe", "grp", "dp"), None),
        P(("pipe", "grp", "dp"), None),
        P(("pipe", "grp", "dp"), None),
        P(("pipe", "grp", "dp"), None),
        P(None, ("pipe", "grp", "dp")),
        P(None, ("pipe", "grp", "dp")),
        P(None, ("pipe", "grp", "dp")),
        P(),
        P(),
        P(),
    )
    return jax.shard_map(
        per_device,
        mesh=mesh,
        in_specs=placed,
        out_specs=(
            P(("pipe", "grp", "dp"), None),
            P(("pipe", "grp", "dp"), None),
            P(("pipe", "grp", "dp"), None),
            P(None, ("pipe", "grp", "dp")),
            P(None, ("pipe", "grp", "dp")),
            P(None, ("pipe", "grp", "dp")),
            P(("pipe", "grp", "dp"), None),
            P(("pipe", "grp", "dp"), None),
            P(("pipe", "grp", "dp"), None),
            P(None, ("pipe", "grp", "dp"), None),
            P(None, ("pipe", "grp", "dp"), None),
            P(None, ("pipe", "grp", "dp"), None),
            P(("pipe", "grp", "dp"), None),
            P(("pipe", "grp", "dp"), None),
            P(("pipe", "grp", "dp"), None),
            P(("pipe", "grp", "dp"), None),
            P(("pipe", "grp", "dp"), None),
            P(("pipe", "grp", "dp"), None),
            P(None, ("pipe", "grp", "dp")),
            P(None, ("pipe", "grp", "dp")),
            P(None, ("pipe", "grp", "dp")),
            P(),
            P(),
            P(),
            P(),
            P(),
            P(),
        ),
        check_vma=False,
    )
```

```python
import functools
import math

import jax
import jax.numpy as jnp
from jax import lax
from jax.experimental import pallas as pl
from jax.experimental.pallas import tpu as pltpu
from jax.sharding import PartitionSpec as P

H = 16
STEP = 10


beta_one = 0.9
beta_two = 0.999
learn_rate = 0.02
vector_rate = 0.2
weight_decay = 0.01
epsilon = 1e-08
clip_norm = 0.02
norm_eps = 1e-05
root_half = 0.7071067811865476
density_scale = 0.3989422804014327
AXES = ("pipe", "grp", "dp")
CHIPS = ("grp", "dp")
PLANE = ("pipe", "grp")
highest = lax.Precision.HIGHEST


def matmul(left, right):
    return jnp.dot(left, right, preferred_element_type=jnp.float32)


def left_transposed(left, right):
    return lax.dot_general(
        left, right, (((0,), (0,)), ((), ())), preferred_element_type=jnp.float32
    )


def right_transposed(left, right):
    return lax.dot_general(
        left, right, (((1,), (1,)), ((), ())), preferred_element_type=jnp.float32
    )


def norm_forward(values, gain, shift):
    center = values - jnp.mean(values, -1, keepdims=True)
    scale = lax.rsqrt(jnp.mean(center * center, -1, keepdims=True) + norm_eps)
    normal = center * scale
    return (normal * gain + shift, (normal, scale))


def norm_backward(grad, kept, gain):
    normal, scale = kept
    d_gain = jnp.sum(grad * normal, 0)
    d_shift = jnp.sum(grad, 0)
    d_norm = grad * gain
    d_input = scale * (
        d_norm
        - jnp.mean(d_norm, -1, keepdims=True)
        - normal * jnp.mean(d_norm * normal, -1, keepdims=True)
    )
    return (d_input, d_gain, d_shift)


def gelu_slope(values):
    return (
        0.5 * (1.0 + lax.erf(values * root_half))
        + values * jnp.exp(-0.5 * values * values) * density_scale
    )


def masked_counts(lengths, slots):
    return jnp.minimum(slots, (3 * lengths + 19) // 20)


def one_hot(indices, size, dtype):
    places = lax.broadcasted_iota(jnp.int32, indices.shape + (size,), indices.ndim)
    return (indices[..., None] == places).astype(dtype)


def rows_by_seq(pick, rows):
    return jnp.einsum("sjp,spw->sjw", pick, rows, precision=highest)


def rows_to_seq(pick, rows):
    return jnp.einsum("sjp,sjw->spw", pick, rows, precision=highest)


class Routes:
    def __init__(self, all_ids, all_live, rows_per):
        self.parts, tokens = all_ids.shape
        self.rows_per = rows_per
        self.me = lax.axis_index(AXES)
        mean = tokens / self.parts
        self.room = max(16, int(math.ceil((mean + 2.8 * math.sqrt(mean)) / 16)) * 16)
        owners = jnp.where(all_live, all_ids // rows_per, -1)
        counts = jnp.sum(one_hot(owners, self.parts, jnp.int32), 1)
        self.more = 16
        self.rounds = (jnp.maximum(jnp.max(counts) - self.room, 0) + self.more - 1) // self.more
        mine = owners == self.me
        order = jnp.arange(tokens, dtype=jnp.int32)
        upto = (order[:, None] <= order[None, :]).astype(jnp.bfloat16)
        ranks = matmul(mine.astype(jnp.bfloat16), upto).astype(jnp.int32)
        self.out_rank = jnp.where(mine, ranks - 1, -1)
        self.out_row = all_ids - self.me * rows_per
        own_owners = lax.dynamic_index_in_dim(owners, self.me, 0, keepdims=False)
        hits = one_hot(own_owners, self.parts, jnp.bfloat16)
        ranks = jnp.sum(hits.astype(jnp.float32) * left_transposed(upto, hits), 1)
        ranks = ranks.astype(jnp.int32) - 1
        self.in_rank = ranks
        self.in_owner = own_owners

    def owner_pick(self, first, room):
        slots = first + jnp.arange(room, dtype=jnp.int32)
        at = self.out_rank[:, None, :] == slots[None, :, None]
        row = jnp.sum(jnp.where(at, self.out_row[:, None, :] + 1, 0), 2) - 1
        return one_hot(row.reshape(-1), self.rows_per, jnp.bfloat16)

    def token_pick(self, first, room):
        rank = self.in_rank - first
        inside = (self.in_owner >= 0) & (rank >= 0) & (rank < room)
        slot = jnp.where(inside, self.in_owner * room + rank, -1)
        return one_hot(slot, self.parts * room, jnp.bfloat16)

    def exchange(self, rows):
        shaped = rows.reshape(self.parts, -1, rows.shape[-1])
        return lax.all_to_all(shaped, AXES, 0, 0).reshape(rows.shape)

    def table_rows(self, table, first, room):
        return matmul(self.owner_pick(first, room), table).astype(jnp.bfloat16)

    def token_rows(self, rows, first, room):
        return left_transposed(self.token_pick(first, room), rows).astype(jnp.bfloat16)

    def later(self, more, start):
        def one(turn, kept):
            return kept + more(self.room + turn * self.more)

        return lax.fori_loop(0, self.rounds, one, start)

    def fetch(self, table, arrived):
        def more(first):
            rows = self.exchange(self.table_rows(table, first, self.more))
            return matmul(self.token_pick(first, self.more), rows)

        return self.later(more, matmul(self.token_pick(0, self.room), arrived))

    def give(self, rows, arrived, start):
        def more(first):
            back = self.exchange(self.token_rows(rows, first, self.more))
            return left_transposed(self.owner_pick(first, self.more), back)

        start = start + left_transposed(self.owner_pick(0, self.room), arrived)
        return self.later(more, start)


def swapped(shard):
    return lax.ppermute(shard, "pipe", [(0, 1), (1, 0)])


def both_cores(rows):
    return jnp.concatenate([rows, swapped(rows)], 0)


def half_columns(rows, index):
    half = rows.shape[1] // 2
    return lax.dynamic_slice_in_dim(rows, index * half, half, 1)


def chip_sum(left, right):
    pipe = lax.axis_index("pipe")
    left = jnp.concatenate([half_columns(left, pipe), swapped(half_columns(left, 1 - pipe))], 0)
    return left_transposed(left, both_cores(right)).astype(jnp.bfloat16)


def chip_half(partial):
    half = partial.shape[0] // 2
    pipe = lax.axis_index("pipe")
    partial = partial.astype(jnp.bfloat16)
    keep = lax.dynamic_slice_in_dim(partial, pipe * half, half, 0)
    give = lax.dynamic_slice_in_dim(partial, (1 - pipe) * half, half, 0)
    return (keep.astype(jnp.float32) + swapped(give).astype(jnp.float32)).astype(jnp.bfloat16)


def device(pipe, grp, dp):
    return {"pipe": pipe, "grp": grp, "dp": dp}


def remote(source, target, send, arrive, to):
    return pltpu.make_async_remote_copy(
        src_ref=source,
        dst_ref=target,
        send_sem=send,
        recv_sem=arrive,
        device_id=device(*to),
        device_id_type=pl.DeviceIdType.MESH,
    )


def tell(barrier, to):
    pl.semaphore_signal(
        barrier, inc=1, device_id=device(*to), device_id_type=pl.DeviceIdType.MESH
    )


def greet(others):
    barrier = pltpu.get_barrier_semaphore()
    for to in others:
        tell(barrier, to)
    pl.semaphore_wait(barrier, len(others))


class Place:
    def __init__(self, sizes):
        self.pipes, self.grps, self.dps = sizes
        self.plane_only = self.dps == 1
        self.pipe, self.grp, self.dp = [lax.axis_index(axis) for axis in AXES]
        column, row = self.grp % 2, self.grp // 2
        self.beside = 2 * row + 1 - column
        self.below = 2 * (1 - row) + column
        self.across = 3 - self.grp

    @property
    def spot(self):
        return 0 if self.plane_only else self.dp

    def plane(self):
        found = []
        for a in range(self.pipes):
            for b in range(self.grps):
                if (a, b) != (0, 0):
                    ahead = ((self.pipe + a) % self.pipes, (self.grp + b) % self.grps)
                    back = (
                        (self.pipe + self.pipes - a) % self.pipes,
                        (self.grp + self.grps - b) % self.grps,
                    )
                    found.append((ahead, back))
        return found

    def line(self, step):
        return (self.dp + step) % self.dps

    def behind(self, step):
        return (self.dp + self.dps - step) % self.dps

    def others(self):
        found = []
        for a in range(self.pipes):
            for b in range(self.grps):
                for c in range(self.dps):
                    if (a, b, c) != (0, 0, 0):
                        ahead = (
                            (self.pipe + a) % self.pipes,
                            (self.grp + b) % self.grps,
                            (self.dp + c) % self.dps,
                        )
                        back = (
                            (self.pipe + self.pipes - a) % self.pipes,
                            (self.grp + self.grps - b) % self.grps,
                            (self.dp + self.dps - c) % self.dps,
                        )
                        found.append((ahead, back))
        return found

    def index(self, pipe, grp, dp):
        return (pipe * self.grps + grp) * self.dps + dp


def swap_all(place, rows, arrived, send, arrive, own):
    me = place.index(place.pipe, place.grp, place.dp)
    copies = []
    for i, (ahead, back) in enumerate(place.others()):
        to = place.index(*ahead)
        copies.append(remote(rows.at[to], arrived.at[me], send.at[i], arrive.at[i], ahead))
        copies[-1].start()
    kept = pltpu.make_async_copy(rows.at[me], arrived.at[me], own)
    kept.start()

    def finish():
        for i, (ahead, back) in enumerate(place.others()):
            origin = place.index(*back)
            copies[i].wait_send()
            remote(rows.at[me], arrived.at[origin], send.at[i], arrive.at[i], ahead).wait_recv()
        kept.wait()

    return finish


def swap_plane(place, rows, arrived, send, arrive, own):
    me = place.pipe * place.grps + place.grp
    copies = []
    for i, (ahead, back) in enumerate(place.plane()):
        to = ahead[0] * place.grps + ahead[1]
        copies.append(
            remote(rows.at[to], arrived.at[me], send.at[i], arrive.at[i], ahead + (place.dp,))
        )
        copies[-1].start()
    kept = pltpu.make_async_copy(rows.at[me], arrived.at[me], own)
    kept.start()

    def finish():
        for i, (ahead, back) in enumerate(place.plane()):
            origin = back[0] * place.grps + back[1]
            copies[i].wait_send()
            remote(
                rows.at[me], arrived.at[origin], send.at[i], arrive.at[i], ahead + (place.dp,)
            ).wait_recv()
        kept.wait()

    return finish


def begin_kernel(sizes, row_ref, up_ref, all_ref, arrived_ref, *sems):
    send, arrive, own, plane_send, plane_arrive, plane_own = sems
    place = Place(sizes)
    others = place.others()
    greet([ahead for ahead, _ in others])
    finish = swap_plane(place, up_ref, arrived_ref, plane_send, plane_arrive, plane_own)
    me = place.index(place.pipe, place.grp, place.dp)
    copies = []
    for i, (ahead, _) in enumerate(others):
        copies.append(remote(row_ref, all_ref.at[me], send.at[i], arrive.at[i], ahead))
        copies[-1].start()
    kept = pltpu.make_async_copy(row_ref, all_ref.at[me], own)
    kept.start()
    for i, (ahead, back) in enumerate(others):
        copies[i].wait_send()
        remote(
            row_ref, all_ref.at[place.index(*back)], send.at[i], arrive.at[i], ahead
        ).wait_recv()
    kept.wait()
    finish()


def begin(row, blocks, sizes, collective):
    parts = math.prod(sizes)
    sems = pltpu.SemaphoreType.DMA((parts - 1,))
    plane_sems = pltpu.SemaphoreType.DMA((sizes[0] * sizes[1] - 1,))
    return pl.pallas_call(
        functools.partial(begin_kernel, sizes),
        out_shape=(
            jax.ShapeDtypeStruct((parts,) + row.shape, row.dtype),
            jax.ShapeDtypeStruct(blocks.shape, blocks.dtype),
        ),
        in_specs=[pl.BlockSpec(memory_space=pltpu.VMEM)] * 2,
        out_specs=[pl.BlockSpec(memory_space=pltpu.VMEM)] * 2,
        scratch_shapes=[
            sems,
            sems,
            pltpu.SemaphoreType.DMA,
            plane_sems,
            plane_sems,
            pltpu.SemaphoreType.DMA,
        ],
        compiler_params=pltpu.CompilerParams(
            collective_id=collective, has_side_effects=True, vmem_limit_bytes=8 << 20
        ),
    )(row, blocks)


def spread_kernel(sizes, row_ref, all_ref, send, arrive, own):
    place = Place(sizes)
    others = place.others()
    greet([ahead for ahead, _ in others])
    me = place.index(place.pipe, place.grp, place.dp)
    copies = []
    for i, (ahead, _) in enumerate(others):
        copies.append(remote(row_ref, all_ref.at[me], send.at[i], arrive.at[i], ahead))
        copies[-1].start()
    kept = pltpu.make_async_copy(row_ref, all_ref.at[me], own)
    kept.start()
    for i, (ahead, back) in enumerate(others):
        copies[i].wait_send()
        remote(
            row_ref, all_ref.at[place.index(*back)], send.at[i], arrive.at[i], ahead
        ).wait_recv()
    kept.wait()


def spread(row, sizes, collective):
    parts = math.prod(sizes)
    sems = pltpu.SemaphoreType.DMA((parts - 1,))
    return pl.pallas_call(
        functools.partial(spread_kernel, sizes),
        out_shape=jax.ShapeDtypeStruct((parts,) + row.shape, row.dtype),
        in_specs=[pl.BlockSpec(memory_space=pltpu.VMEM)],
        out_specs=pl.BlockSpec(memory_space=pltpu.VMEM),
        scratch_shapes=[sems, sems, pltpu.SemaphoreType.DMA],
        compiler_params=pltpu.CompilerParams(
            collective_id=collective, has_side_effects=True, vmem_limit_bytes=8 << 20
        ),
    )(row)


def stats_kernel(sizes, own_ref, all_ref, held, result, send, arrive, own, send_two, arrive_two):
    place = Place(sizes)
    others = place.others()
    greet([ahead for ahead, _ in others])
    swap_all(place, own_ref, held, send, arrive, own)()
    peaks = held[:, 0]
    peak = jnp.max(peaks, 0, keepdims=True)
    total = jnp.sum(held[:, 1] * jnp.exp(peaks - peak), 0, keepdims=True)
    label = jnp.sum(held[:, 2], 0, keepdims=True)
    result[0:1] = peak
    result[1:2] = total
    result[2:3] = label
    result[3:8] = jnp.zeros((5, result.shape[1]), jnp.float32)
    me = place.index(place.pipe, place.grp, place.dp)
    copies = []
    for i, (ahead, _) in enumerate(others):
        copies.append(remote(result, all_ref.at[me], send_two.at[i], arrive_two.at[i], ahead))
        copies[-1].start()
    all_ref[me] = result[...]
    for i, (ahead, back) in enumerate(others):
        copies[i].wait_send()
        remote(
            result, all_ref.at[place.index(*back)], send_two.at[i], arrive_two.at[i], ahead
        ).wait_recv()


def combine_stats(own, sizes, collective):
    parts, _, rows = own.shape
    sems = pltpu.SemaphoreType.DMA((parts - 1,))
    return pl.pallas_call(
        functools.partial(stats_kernel, sizes),
        out_shape=jax.ShapeDtypeStruct(own.shape, jnp.float32),
        in_specs=[pl.BlockSpec(memory_space=pltpu.VMEM)],
        out_specs=pl.BlockSpec(memory_space=pltpu.VMEM),
        scratch_shapes=[
            pltpu.VMEM(own.shape, jnp.float32),
            pltpu.VMEM((8, rows), jnp.float32),
            sems,
            sems,
            pltpu.SemaphoreType.DMA,
            sems,
            sems,
        ],
        compiler_params=pltpu.CompilerParams(
            collective_id=collective, has_side_effects=True, vmem_limit_bytes=8 << 20
        ),
    )(own)


def gather_kernel(sizes, pieces, routed, *refs):
    count = max(piece[0] for piece in pieces) + 1
    shards, refs = refs[:count], refs[count:]
    if routed:
        rows_ref, refs = refs[0], refs[1:]
    fulls, refs = refs[:count], refs[count:]
    if routed:
        arrived_ref, refs = refs[0], refs[1:]
    send, arrive, own, swap_send, swap_arrive, swap_own = refs
    place = Place(sizes)
    pipe, grp, dp = place.pipe, place.grp, place.dp
    near = place.beside * (1 - pipe) + place.below * pipe
    far = place.below * (1 - pipe) + place.beside * pipe
    core = (1 - pipe, grp, dp)
    hops = place.dps - 1
    spot = place.spot
    ends = (dp < hops, dp > 0)
    sides = ((pipe, grp, dp + 1), (pipe, grp, dp - 1))
    both = range(2 if hops else 0)
    if routed:
        greet([ahead for ahead, _ in place.others()])
    else:
        greet(
            [(pipe, grp, place.line(k + 1)) for k in range(hops)]
            + [(pipe, near, dp), (pipe, far, dp), core]
        )
    waits = []

    def view(piece, *at):
        array, first, rows = piece
        return fulls[array].at[at + ((slice(None),) * (3 - len(at))) + (pl.ds(first, rows),)]

    def launch(n, index, source, piece, to, *at):
        copy = remote(source, view(piece, *at), send.at[n, index], arrive.at[n, index], to)
        copy.start()
        waits.append(copy)

    def landed(n, index, piece, *at):
        target = view(piece, *at)
        remote(target, target, send.at[n, index], arrive.at[n, index], core).wait_recv()

    def along(n, side, hop, finish=False):
        origin = dp - hop if side == 0 else dp + hop
        here = origin >= 0 if side == 0 else origin <= hops
        piece, index = pieces[n], side * hops + hop

        def copy():
            array, first, rows = piece
            target = view(piece, pipe, grp, origin)
            source = shards[array].at[pl.ds(first, rows)] if hop == 0 else target
            return remote(source, target, send.at[n, index], arrive.at[n, index], sides[side])

        if finish:

            @pl.when(here & ends[side])
            def _():
                copy().wait_send()

            return
        if hop > 0:

            @pl.when(here)
            def _():
                landed(n, index - 1, piece, pipe, grp, origin)

        if hop < hops:

            @pl.when(here & ends[side])
            def _():
                copy().start()

    keeps = {}

    def over_line(n, hop):
        if hop == 0:
            array, first, rows = pieces[n]
            source = shards[array].at[pl.ds(first, rows)]
            keeps[n] = pltpu.make_async_copy(source, view(pieces[n], pipe, grp, spot), own.at[n])
            keeps[n].start()
        for side in both:
            along(n, side, hop)

    def over_plane(n):
        array, first, rows = piece = pieces[n]
        over_line(n, hops)
        if hops:
            keeps[n].wait()
            group, at = view(piece, pipe, grp), (pipe, grp)
        else:
            group, at = shards[array].at[pl.ds(first, rows)], (pipe, grp, 0)
        launch(n, 2 * hops, group, piece, (pipe, near, dp), *at)
        launch(n, 2 * hops + 1, group, piece, (pipe, far, dp), *at)
        launch(n, 2 * hops + 3, group, piece, core, *at)

    def pass_on(n):
        piece = pieces[n]
        landed(n, 2 * hops, piece, pipe, near)
        group = view(piece, pipe, near)
        launch(n, 2 * hops + 2, group, piece, (pipe, far, dp), pipe, near)
        launch(n, 2 * hops + 4, group, piece, core, pipe, near)
        landed(n, 2 * hops + 1, piece, pipe, far)
        launch(n, 2 * hops + 5, view(piece, pipe, far), piece, core, pipe, far)

    def last(n):
        piece = pieces[n]
        landed(n, 2 * hops + 2, piece, pipe, place.across)
        launch(n, 2 * hops + 6, view(piece, pipe, place.across), piece, core, pipe, place.across)

    stages = [functools.partial(over_line, hop=hop) for hop in range(hops)]
    stages += [over_plane, pass_on, last]
    total = len(pieces)
    for turn in range(total + len(stages) - 1):
        for at, stage in enumerate(stages):
            if 0 <= turn - at < total:
                stage(turn - at)
        if turn == 5 and routed:
            finish = swap_all(place, rows_ref, arrived_ref, swap_send, swap_arrive, swap_own)
    for n, piece in enumerate(pieces):
        landed(n, 2 * hops + 3, piece, 1 - pipe, grp)
        landed(n, 2 * hops + 4, piece, 1 - pipe, far)
        landed(n, 2 * hops + 5, piece, 1 - pipe, near)
        landed(n, 2 * hops + 6, piece, 1 - pipe, place.across)
        for side in both:
            for hop in range(hops):
                along(n, side, hop, finish=True)
    for copy in waits:
        copy.wait_send()
    if not hops:
        for keep in keeps.values():
            keep.wait()
    if routed:
        finish()


def gather_all(shards, pieces, sizes, collective, rows=None):
    parts = math.prod(sizes)
    routed = rows is not None
    kinds = 2 * (sizes[2] - 1) + 7
    space = pltpu.VMEM if sizes[2] == 1 else pl.ANY
    out_shape = [jax.ShapeDtypeStruct(sizes + shard.shape, shard.dtype) for shard in shards]
    if routed:
        out_shape.append(jax.ShapeDtypeStruct(rows.shape, rows.dtype))
    operands = list(shards) + ([rows] if routed else [])
    sems = pltpu.SemaphoreType.DMA((len(pieces), kinds))
    swaps = pltpu.SemaphoreType.DMA((parts - 1 if routed else 1,))
    return pl.pallas_call(
        functools.partial(gather_kernel, sizes, tuple(pieces), routed),
        out_shape=out_shape,
        in_specs=[pl.BlockSpec(memory_space=space)] * len(operands),
        out_specs=[pl.BlockSpec(memory_space=space)] * len(out_shape),
        scratch_shapes=[
            sems,
            sems,
            pltpu.SemaphoreType.DMA((len(pieces),)),
            swaps,
            swaps,
            pltpu.SemaphoreType.DMA,
        ],
        compiler_params=pltpu.CompilerParams(
            collective_id=collective, has_side_effects=True, vmem_limit_bytes=16 << 20
        ),
    )(*operands)


def reduce_kernel(sizes, pieces, cores, swaps, *refs):
    arrays, total = max(piece[0] for piece in pieces) + 1, len(pieces)
    partials, refs = refs[:arrays], refs[arrays:]
    if swaps:
        blocks_ref, refs = refs[0], refs[1:]
    sums, refs = refs[:arrays], refs[arrays:]
    if swaps:
        blocks_arrived_ref, refs = refs[0], refs[1:]
    chips, refs = refs[: total if cores else 0], refs[total if cores else 0 :]
    others, refs = refs[: total if cores else 0], refs[total if cores else 0 :]
    mine, refs = refs[:total], refs[total:]
    planes, refs = refs[:total], refs[total:]
    lines, refs = refs[:total], refs[total:]
    send, arrive, own, plane_send, plane_arrive, plane_own = refs
    place = Place(sizes)
    pipe, grp, dp = place.pipe, place.grp, place.dp
    near = place.beside * (1 - pipe) + place.below * pipe
    far = place.below * (1 - pipe) + place.beside * pipe
    core = (1 - pipe, grp, dp)
    hops = place.dps - 1
    block = 16
    to_greet = [(pipe, grp, place.line(k + 1)) for k in range(hops)]
    if swaps:
        to_greet += [ahead + (dp,) for ahead, _ in place.plane()]
    else:
        to_greet += [(pipe, near, dp), (pipe, far, dp)] + ([core] if cores else [])
    greet(to_greet)
    copies = {}

    def launch(n, index, source, target, to):
        copies[n, index] = remote(source, target, send.at[n, index], arrive.at[n, index], to)
        copies[n, index].start()

    def blocks(n, body):
        deep = pieces[n][2] // block

        def one(i, _):
            at = pl.ds(pl.multiple_of(i % deep * block, block), block)
            body(i // deep, at)
            return 0

        lax.fori_loop(0, place.dps * deep, one, 0)

    def to_core(n):
        array, first, rows = pieces[n]
        if cores:
            part = partials[array].at[1 - pipe, :, :, pl.ds(first, rows)]
            launch(n, 0, part, others[n], core)
            part = partials[array].at[pipe, :, :, pl.ds(first, rows)]
            copies[n, "own"] = pltpu.make_async_copy(part, chips[n], own.at[n, 0])
            copies[n, "own"].start()

    def to_near(n):
        array, first, rows = pieces[n]
        if cores:
            copies[n, "own"].wait()
            copies[n, 0].wait_recv()
            for g in range(place.grps):

                def add(d, at, g=g):
                    left = chips[n][g, d, at].astype(jnp.float32)
                    chips[n][g, d, at] = (left + others[n][g, d, at].astype(jnp.float32)).astype(
                        jnp.bfloat16
                    )

                blocks(n, add)
            part = lambda g: chips[n].at[g]
        else:
            part = lambda g: partials[array].at[g, :, pl.ds(first, rows)]
            for j, g in enumerate((far, grp)):
                copies[n, "own", j] = pltpu.make_async_copy(part(g), mine[n].at[j], own.at[n, j])
                copies[n, "own", j].start()
        launch(n, 1, part(near), planes[n].at[1], (pipe, near, dp))
        launch(n, 2, part(place.across), planes[n].at[0], (pipe, near, dp))

    def to_far(n):
        if not cores:
            copies[n, "own", 0].wait()
            copies[n, "own", 1].wait()
        copies[n, 1].wait_recv()
        copies[n, 2].wait_recv()
        for j, g in enumerate((far, grp)):

            def add(d, at, j=j, g=g):
                left = chips[n][g, d, at] if cores else mine[n][j, d, at]
                right = planes[n][j, d, at].astype(jnp.float32)
                mine[n][j, d, at] = (left.astype(jnp.float32) + right).astype(jnp.bfloat16)

            blocks(n, add)
            if j == 0:
                launch(n, 3, mine[n].at[0], planes[n].at[2], (pipe, far, dp))

    def to_lines(n):
        copies[n, 3].wait_recv()

        def add(d, at):
            left = mine[n][1, d, at].astype(jnp.float32)
            mine[n][1, d, at] = (left + planes[n][2, d, at].astype(jnp.float32)).astype(
                jnp.bfloat16
            )

        def add_last(d, at):
            array, first, rows = pieces[n]
            left = mine[n][1, d, at].astype(jnp.float32)
            to = pl.ds(pl.multiple_of(first + at.start, block), block)
            sums[array][to] = left + planes[n][2, d, at].astype(jnp.float32)

        if hops == 0:
            blocks(n, add_last)
            return
        blocks(n, add)
        for k in range(hops):
            to = place.line(k + 1)
            launch(n, 4 + k, mine[n].at[1, to], lines[n].at[k], (pipe, grp, to))

    def to_sum(n):
        array, first, rows = pieces[n]
        for k in range(hops):
            copies[n, 4 + k].wait_recv()

        def add(i, _):
            at = pl.ds(pl.multiple_of(i * block, block), block)
            total = mine[n][1, place.spot, at].astype(jnp.float32)
            for k in range(hops):
                total = total + lines[n][k, at].astype(jnp.float32)
            sums[array][pl.ds(pl.multiple_of(first + i * block, block), block)] = total
            return 0

        lax.fori_loop(0, rows // block, add, 0)

    stages = ([to_core] if cores else []) + [to_near, to_far, to_lines]
    stages += [to_sum] if hops else []
    for turn in range(total + len(stages) - 1):
        for at, stage in enumerate(stages):
            if 0 <= turn - at < total:
                stage(turn - at)
        if turn == 0 and swaps:
            finish = swap_plane(
                place, blocks_ref, blocks_arrived_ref, plane_send, plane_arrive, plane_own
            )
    for key, copy in copies.items():
        if key[1] != "own":
            copy.wait_send()
    if swaps:
        finish()


def reduce_all(partials, pieces, sizes, collective, blocks=None, cores=False):
    total = len(pieces)
    swaps = blocks is not None
    low = jnp.bfloat16
    _, grps, dps = sizes
    shapes = [(dps, size, partials[array].shape[-1]) for array, _, size in pieces]
    out_shape = [jax.ShapeDtypeStruct(partial.shape[-2:], jnp.float32) for partial in partials]
    out_specs = [pl.BlockSpec(memory_space=pltpu.VMEM)] * len(partials)
    if swaps:
        out_shape.append(jax.ShapeDtypeStruct(blocks.shape, blocks.dtype))
        out_specs.append(pl.BlockSpec(memory_space=pl.ANY))
    operands = list(partials) + ([blocks] if swaps else [])
    sems = pltpu.SemaphoreType.DMA((total, 4 + dps - 1))
    plane_swaps = pltpu.SemaphoreType.DMA((sizes[0] * grps - 1,))
    scratch = [pltpu.VMEM((grps,) + shape, low) for shape in shapes] * (2 if cores else 0)
    scratch += [pltpu.VMEM((2,) + shape, low) for shape in shapes]
    scratch += [pltpu.VMEM((3,) + shape, low) for shape in shapes]
    scratch += [pltpu.VMEM((max(dps - 1, 1),) + shape[1:], low) for shape in shapes]
    return pl.pallas_call(
        functools.partial(reduce_kernel, sizes, tuple(pieces), cores, swaps),
        out_shape=out_shape,
        in_specs=[pl.BlockSpec(memory_space=pl.ANY)] * len(operands),
        out_specs=out_specs,
        scratch_shapes=scratch
        + [
            sems,
            sems,
            pltpu.SemaphoreType.DMA((total, 2)),
            plane_swaps,
            plane_swaps,
            pltpu.SemaphoreType.DMA,
        ],
        compiler_params=pltpu.CompilerParams(
            collective_id=collective, has_side_effects=True, vmem_limit_bytes=48 << 20
        ),
    )(*operands)


def pair_rows(pair, first):
    pair = pair.astype(jnp.float32)
    low = jnp.bfloat16
    return jnp.concatenate(
        [jnp.where(first, pair, 0.0).astype(low), jnp.where(first, 0.0, pair).astype(low)], 0
    )


def pair_probs(rows, keys, live, scale):
    scores = jnp.where(live, right_transposed(rows, keys) * scale, -1e30)
    exp_scores = jnp.exp(scores - jnp.max(scores, -1, keepdims=True))
    return exp_scores / jnp.sum(exp_scores, -1, keepdims=True)


def attention_masks(lengths_ref, slots, seq_len, lanes):
    live = lax.broadcasted_iota(jnp.int32, (1, seq_len), 1) < lengths_ref[pl.program_id(0)]
    first = lax.broadcasted_iota(jnp.int32, (slots, lanes), 1) < lanes // 2
    return live, first


def attention_kernel(scale, lanes, lengths_ref, q_ref, k_ref, v_ref, out_ref):
    slots = q_ref.shape[0]
    live, first = attention_masks(lengths_ref, slots, k_ref.shape[0], lanes)
    for pair in range(q_ref.shape[1] // lanes):
        at = slice(pair * lanes, (pair + 1) * lanes)
        probs = pair_probs(pair_rows(q_ref[:, at], first), k_ref[:, at], live, scale)
        context = matmul(probs.astype(jnp.bfloat16), v_ref[:, at])
        out_ref[:, at] = jnp.where(first, context[:slots], context[slots:]).astype(jnp.bfloat16)


def attention_back_kernel(
    scale, lanes, lengths_ref, q_ref, k_ref, v_ref, grad_ref, dq_ref, dk_ref, dv_ref
):
    slots = q_ref.shape[0]
    low = jnp.bfloat16
    live, first = attention_masks(lengths_ref, slots, k_ref.shape[0], lanes)
    for pair in range(q_ref.shape[1] // lanes):
        at = slice(pair * lanes, (pair + 1) * lanes)
        rows, grads = pair_rows(q_ref[:, at], first), pair_rows(grad_ref[:, at], first)
        probs = pair_probs(rows, k_ref[:, at], live, scale)
        dv_ref[:, at] = left_transposed(probs.astype(low), grads).astype(low)
        d_probs = right_transposed(grads, v_ref[:, at])
        d_scores = probs * (d_probs - jnp.sum(probs * d_probs, -1, keepdims=True))
        d_scores = d_scores.astype(low)
        d_query = matmul(d_scores, k_ref[:, at]) * scale
        dq_ref[:, at] = jnp.where(first, d_query[:slots], d_query[slots:]).astype(low)
        dk_ref[:, at] = (left_transposed(d_scores, rows) * scale).astype(low)


def attention(lengths, queries, both, grads=None):
    own = lengths.shape[0]
    width = queries.shape[1]
    slots, seq_len = queries.shape[0] // own, both.shape[0] // own
    lanes = 2 * width // H
    scale = (width // H) ** (-0.5)
    cuts = 2
    part = width // cuts
    row = pl.BlockSpec((slots, part), lambda s, h: (s, h))
    keys = pl.BlockSpec((seq_len, part), lambda s, h: (s, h))
    values = pl.BlockSpec((seq_len, part), lambda s, h: (s, cuts + h))
    in_specs = [pl.BlockSpec(memory_space=pltpu.SMEM), row, keys, values]
    flat = jax.ShapeDtypeStruct(queries.shape, jnp.bfloat16)
    tall = jax.ShapeDtypeStruct((both.shape[0], width), jnp.bfloat16)
    if grads is None:
        return pl.pallas_call(
            functools.partial(attention_kernel, scale, lanes),
            grid=(own, cuts),
            out_shape=flat,
            in_specs=in_specs,
            out_specs=row,
        )(lengths, queries, both, both)
    return pl.pallas_call(
        functools.partial(attention_back_kernel, scale, lanes),
        grid=(own, cuts),
        out_shape=(flat, tall, tall),
        in_specs=in_specs + [row],
        out_specs=(row, keys, keys),
    )(lengths, queries, both, both, grads)


def even_pieces(array, rows, cuts):
    size = rows // cuts
    return [(array, i * size, size) for i in range(cuts)]


def start_all(row, blocks, sizes, collective):
    if collective is None:
        return lax.all_gather(row, AXES, axis=0), lax.all_to_all(blocks, PLANE, 0, 0)
    return begin(row, blocks, sizes, collective)


def gather_weights(shards, pieces, sizes, collective, rows):
    if collective is None:
        fulls = [lax.all_gather(shard, AXES, axis=0) for shard in shards]
        arrived = lax.all_to_all(rows, AXES, 0, 0)
    else:
        *fulls, arrived = gather_all(shards, pieces, sizes, collective, rows)
    return [full.reshape(-1, full.shape[-1]) for full in fulls], arrived


def gather_rows(shard, sizes, collective, cuts):
    if collective is None:
        axes = AXES if sizes[2] > 1 else PLANE
        return lax.all_gather(shard, axes, axis=0, tiled=True)
    (full,) = gather_all([shard], even_pieces(0, shard.shape[0], cuts), sizes, collective)
    return full.reshape(-1, full.shape[-1])


def sum_rows(partial, sizes, collective, cuts):
    if collective is None:
        axes = AXES if sizes[2] > 1 else PLANE
        total = lax.psum_scatter(partial, axes, scatter_dimension=0, tiled=True)
        return total.astype(jnp.float32)
    shaped = partial.reshape(sizes + (-1, partial.shape[1]))
    pieces = even_pieces(0, shaped.shape[3], cuts)
    (total,) = reduce_all([shaped], pieces, sizes, collective, cores=True)
    return total


def sum_chips(partials, pieces, sizes, collective, blocks):
    if collective is not None:
        shaped = [p.reshape(sizes[1:] + (-1, p.shape[1])) for p in partials]
        *sums, blocks = reduce_all(shaped, pieces, sizes, collective, blocks)
        return sums, blocks
    sums = [
        lax.psum_scatter(p, CHIPS, scatter_dimension=0, tiled=True).astype(jnp.float32)
        for p in partials
    ]
    return sums, lax.all_to_all(blocks, PLANE, 0, 0)


def line_shift(shard, step):
    size = lax.axis_size("dp")
    return lax.ppermute(shard, "dp", [(i, (i + step) % size) for i in range(size)])


def line_gather(shard, collective):
    if collective is None:
        return lax.all_gather(shard, "dp", axis=0)
    size = lax.axis_size("dp")
    me = lax.axis_index("dp")
    kept = jnp.stack([shard] + [line_shift(shard, step) for step in range(1, size)])
    order = [(me + size - i) % size for i in range(size)]
    return jnp.concatenate([lax.dynamic_slice_in_dim(kept, at, 1, 0) for at in order], 0)


def line_sum(partial, collective):
    partial = partial.astype(jnp.bfloat16)
    if collective is None:
        total = lax.psum_scatter(partial, "dp", scatter_dimension=0, tiled=False)
        return total.astype(jnp.float32)
    size = lax.axis_size("dp")
    me = lax.axis_index("dp")

    def entry(step):
        return lax.dynamic_index_in_dim(partial, (me + step) % size, 0, keepdims=False)

    total = entry(0).astype(jnp.float32)
    for step in range(1, size):
        total = total + line_shift(entry(step), step).astype(jnp.float32)
    return total


def spread_row(row, sizes, collective):
    if collective is None:
        return lax.all_gather(row, AXES, axis=0)
    return spread(row, sizes, collective)


def share_stats(peak, total, label, sizes, collective):
    if collective is None:
        top = lax.pmax(peak, AXES)
        total, label = lax.psum((total * jnp.exp(peak - top), label), AXES)
        return top, total, label
    parts = math.prod(sizes)
    stats = jnp.stack([peak, total, label])
    stats = jnp.pad(stats.reshape(3, parts, -1).swapaxes(0, 1), ((0, 0), (0, 5), (0, 0)))
    stats = combine_stats(stats, sizes, collective)
    return [stats[:, i].reshape(-1) for i in range(3)]


def adam_step(weight, first, second, grad, factor, rate):
    clipped = grad * factor
    first = beta_one * first + (1.0 - beta_one) * clipped
    second = beta_two * second + (1.0 - beta_two) * clipped * clipped
    first_hat = first / (1.0 - beta_one**STEP)
    second_hat = second / (1.0 - beta_two**STEP)
    weight = weight - rate * (first_hat / (jnp.sqrt(second_hat) + epsilon) + weight_decay * weight)
    return (weight, first, second)


def per_device(
    token_ids,
    lengths,
    masked_at,
    labels,
    word_table,
    word_first,
    word_second,
    pos_table,
    pos_first,
    pos_second,
    qkv_weight,
    qkv_first,
    qkv_second,
    square_weight,
    square_first,
    square_second,
    up_weight,
    up_first,
    up_second,
    down_weight,
    down_first,
    down_second,
    vec_table,
    vec_first,
    vec_second,
    head_bias,
    bias_first,
    bias_second,
):
    narrow = jnp.bfloat16
    seq_len, slots = token_ids.shape[1], masked_at.shape[1]
    width = word_table.shape[1]
    vocab = head_bias.shape[0]
    rows_per = word_table.shape[0]
    parts = lax.axis_size(AXES)
    halves = lax.axis_size("pipe")
    me = lax.axis_index(AXES)
    own = token_ids.shape[0] // halves
    first_own = lax.axis_index("pipe") * own
    head_dim = width // H
    sizes = tuple(lax.axis_size(axis) for axis in AXES)
    shards = (word_table, qkv_weight, square_weight[0], up_weight, down_weight)
    direct = sizes[:2] == (2, 4) and all(shard.shape[0] % 32 == 0 for shard in shards)
    ids = tuple(range(11)) if direct else (None,) * 11
    plane_sizes = sizes[:2] + (1,)

    spare = -(seq_len + slots + 1) % 128
    packed = jnp.concatenate(
        [token_ids, labels, lengths[:, None], jnp.zeros((token_ids.shape[0], spare), jnp.int32)], 1
    )
    packed = lax.dynamic_slice_in_dim(packed, first_own, own, 0)
    planes = sizes[0] * sizes[1]
    units = up_weight.shape[1] // planes
    cut = me // sizes[2]
    blocks = up_weight.astype(narrow).reshape(up_weight.shape[0], planes, units).swapaxes(0, 1)
    packed, blocks = start_all(packed, blocks, sizes, ids[0])
    halves_low = down_weight.astype(narrow).reshape(-1, units)
    both_low = jnp.concatenate([blocks.reshape(-1, units), halves_low], 0)
    both_low = line_gather(both_low, ids[0])
    down_low = both_low[:, -halves_low.shape[0] :].reshape(units, width)
    up_low = both_low[:, : -halves_low.shape[0]].reshape(sizes[2], planes, -1, units)
    up_low = up_low.swapaxes(0, 1).reshape(width, units)
    all_ids = packed[:, :, :seq_len]
    all_labels = packed[:, :, seq_len : seq_len + slots].reshape(-1)
    all_lengths = packed[:, :, seq_len + slots]
    places = jnp.arange(seq_len, dtype=jnp.int32)
    all_live = places[None, None, :] < all_lengths[:, :, None]
    all_counts = masked_counts(all_lengths, slots)
    total = jnp.sum(all_counts).astype(jnp.float32)
    slot_index = jnp.arange(slots, dtype=jnp.int32)
    all_valid = (slot_index < all_counts[:, :, None]).astype(jnp.float32).reshape(-1)
    own_lengths = lax.dynamic_slice_in_dim(lengths, first_own, own, 0)
    masked = lax.dynamic_slice_in_dim(masked_at, first_own, own, 0)

    word_low = word_table.astype(narrow)
    routes = Routes(all_ids.reshape(parts, -1), all_live.reshape(parts, -1), rows_per)
    small = pos_table.shape[0] + vec_table.shape[0]
    spare = -small % 128
    small_low = jnp.concatenate(
        [pos_table.T, vec_table.T, jnp.zeros((pos_table.shape[1], spare), jnp.float32)], 1
    ).astype(narrow)
    low = [
        small_low,
        qkv_weight.astype(narrow),
        square_weight[0].astype(narrow),
        square_weight[1].astype(narrow),
    ]
    deep = small_low.shape[0]
    pieces = [(0, 0, deep), (1, 0, deep // 2), (1, deep // 2, deep // 2), (2, 0, deep), (3, 0, deep)]
    send = routes.table_rows(word_low, 0, routes.room).reshape(parts, -1, width)
    (small_full, qkv_low, out_low, turn_low), arrived = gather_weights(
        low, pieces, sizes, ids[1], send
    )
    word_rows = routes.fetch(word_low, arrived.reshape(-1, width))
    small_full = small_full.T
    pos_low = small_full[:seq_len]
    vec_rows = small_full[seq_len:small].astype(jnp.float32)
    query_low, both_low = qkv_low[:, :width], qkv_low[:, width:]

    second = (places[None, :] >= ((own_lengths + 1) // 2)[:, None]).reshape(-1, 1)
    embedded = (
        word_rows
        + jnp.tile(pos_low.astype(jnp.float32), (own, 1))
        + jnp.where(second, vec_rows[1], vec_rows[0])
    )
    start, norm_zero = norm_forward(embedded, vec_rows[2], vec_rows[3])
    start_low = start.astype(narrow)
    both_bias = jnp.concatenate([jnp.zeros_like(vec_rows[5]), vec_rows[5]])
    both = (matmul(start_low, both_low) + both_bias).astype(narrow)
    pick = one_hot(masked, seq_len, jnp.float32)
    chosen = rows_by_seq(pick, start.reshape(own, seq_len, width)).reshape(-1, width)
    chosen_low = chosen.astype(narrow)
    queries = (matmul(chosen_low, query_low) + vec_rows[4]).astype(narrow)
    context = attention(own_lengths, queries, both)
    branch = matmul(context, out_low) + vec_rows[6]
    hidden, norm_one = norm_forward(chosen + branch, vec_rows[7], vec_rows[8])
    hidden = hidden.astype(narrow)

    plane_hidden = gather_rows(hidden, plane_sizes, ids[2], 2)
    up_bias = lax.dynamic_slice_in_dim(vec_rows[15:].reshape(-1), cut * units, units, 0)
    inner = matmul(plane_hidden, up_low) + up_bias
    activ = jax.nn.gelu(inner, approximate=False).astype(narrow)
    branch = sum_rows(matmul(activ, down_low).astype(narrow), plane_sizes, ids[3], 2) + vec_rows[9]
    mixed, norm_two = norm_forward(hidden.astype(jnp.float32) + branch, vec_rows[10], vec_rows[11])
    picked = mixed.astype(narrow)
    turned = matmul(picked, turn_low) + vec_rows[12]
    normed, norm_head = norm_forward(
        jax.nn.gelu(turned, approximate=False), vec_rows[13], vec_rows[14]
    )

    all_normed = gather_rows(normed.astype(narrow), sizes, ids[4], 4)
    column = me * rows_per + jnp.arange(rows_per, dtype=jnp.int32)
    bias_row = jnp.pad(head_bias, (0, parts * rows_per - vocab))
    bias_row = lax.dynamic_slice_in_dim(bias_row, me * rows_per, rows_per, 0)
    logits = right_transposed(all_normed, word_low) + bias_row
    logits = jnp.where(column < vocab, logits, -1e30)
    own_peak = jnp.max(logits, -1)
    own_total = jnp.sum(jnp.exp(logits - own_peak[:, None]), -1)
    hits = all_labels[:, None] == column
    own_label = jnp.sum(jnp.where(hits, logits, 0.0), -1)
    peak, exp_total, label_logit = share_stats(own_peak, own_total, own_label, sizes, ids[5])
    loss_total = jnp.sum(all_valid * (peak + jnp.log(exp_total) - label_logit))
    d_logits = (all_valid / total)[:, None] * (
        jnp.exp(logits - peak[:, None]) / exp_total[:, None] - hits.astype(jnp.float32)
    )
    d_bias = jnp.sum(d_logits, 0)
    d_logits_low = d_logits.astype(narrow)
    d_word = left_transposed(d_logits_low, all_normed)
    d_normed = sum_rows(matmul(d_logits_low, word_low).astype(narrow), sizes, ids[6], 8)

    d_gelu, d_gain_head, d_shift_head = norm_backward(d_normed, norm_head, vec_rows[13])
    d_turned = (d_gelu * gelu_slope(turned)).astype(narrow)
    d_turn_bias = jnp.sum(d_turned.astype(jnp.float32), 0)
    d_turn = chip_sum(picked, d_turned)
    d_picked = right_transposed(d_turned, turn_low)
    same = masked[:, :, None] == masked[:, None, :]
    earlier = slot_index[None, :] < slot_index[:, None]
    first_slot = jnp.logical_not(jnp.any(same & earlier, 2))
    merge = (same & first_slot[:, :, None]).astype(jnp.float32)
    d_mixed = rows_by_seq(merge, d_picked.reshape(own, slots, width)).reshape(-1, width)
    d_pre, d_gain_two, d_shift_two = norm_backward(d_mixed, norm_two, vec_rows[10])
    d_branch = d_pre.astype(narrow)
    d_down_bias = jnp.sum(d_branch.astype(jnp.float32), 0)
    plane_branch = gather_rows(d_branch, plane_sizes, ids[7], 2)
    own_down = line_sum(
        left_transposed(activ, plane_branch).reshape(sizes[2], -1, width), ids[7]
    )
    d_inner = (right_transposed(plane_branch, down_low) * gelu_slope(inner)).astype(narrow)
    d_up_bias = jnp.sum(d_inner.astype(jnp.float32), 0)
    d_up_bias = lax.dynamic_update_slice_in_dim(
        jnp.zeros((planes * units,), jnp.float32), d_up_bias, cut * units, 0
    ).reshape(-1, width)
    d_up = left_transposed(plane_hidden, d_inner).reshape(planes, sizes[2], -1, units)
    up_blocks = line_sum(d_up.swapaxes(0, 1), ids[7]).astype(narrow)
    d_hidden = sum_rows(right_transposed(d_inner, up_low).astype(narrow), plane_sizes, ids[8], 2)
    d_hidden = (d_pre + d_hidden).astype(narrow)

    d_pre, d_gain_one, d_shift_one = norm_backward(
        d_hidden.astype(jnp.float32), norm_one, vec_rows[7]
    )
    d_branch = d_pre.astype(narrow)
    d_out_bias = jnp.sum(d_branch.astype(jnp.float32), 0)
    d_out = chip_sum(context, d_branch)
    d_context = right_transposed(d_branch, out_low).astype(narrow)
    d_query, d_key, d_value = attention(own_lengths, queries, both, d_context)
    d_query_bias = jnp.sum(d_query.astype(jnp.float32), 0)
    d_value_bias = jnp.sum(d_value.astype(jnp.float32), 0)
    d_qkv = [
        chip_sum(chosen_low, d_query),
        chip_sum(start_low, d_key),
        chip_sum(start_low, d_value),
    ]
    d_chosen = d_pre + right_transposed(d_query, query_low)
    d_both = jnp.concatenate([d_key, d_value], 1)
    d_start = right_transposed(d_both, both_low) + rows_to_seq(
        pick, d_chosen.reshape(own, slots, width)
    ).reshape(-1, width)
    d_embedded, d_gain_zero, d_shift_zero = norm_backward(d_start, norm_zero, vec_rows[2])
    d_seg_zero = jnp.sum(jnp.where(second, 0.0, d_embedded), 0)
    d_seg_one = jnp.sum(jnp.where(second, d_embedded, 0.0), 0)
    d_embedded_low = d_embedded.astype(narrow)
    arrived = routes.exchange(routes.token_rows(d_embedded_low, 0, routes.room))
    d_small = jnp.concatenate(
        [
            jnp.sum(d_embedded.reshape(own, seq_len, width), 0),
            jnp.stack(
                [
                    d_seg_zero,
                    d_seg_one,
                    d_gain_zero,
                    d_shift_zero,
                    d_query_bias,
                    d_value_bias,
                    d_out_bias,
                    d_gain_one,
                    d_shift_one,
                    d_down_bias,
                    d_gain_two,
                    d_shift_two,
                    d_turn_bias,
                    d_gain_head,
                    d_shift_head,
                ]
            ),
            d_up_bias,
            jnp.zeros((spare, width), jnp.float32),
        ],
        0,
    )
    partials = [d_out, d_turn] + d_qkv + [chip_half(d_small.T)]
    pieces = [(i, 0, deep) for i in range(6)]
    (own_out, own_turn, own_q, own_k, own_v, own_small), up_blocks = sum_chips(
        partials, pieces, sizes, ids[9], up_blocks
    )
    own_qkv = jnp.concatenate([own_q, own_k, own_v], 1)
    own_up = up_blocks.swapaxes(0, 1).reshape(up_weight.shape).astype(jnp.float32)
    d_word = routes.give(d_embedded_low, arrived, lax.optimization_barrier(d_word))
    owned = (
        d_word,
        own_small[:, :seq_len].T,
        own_qkv,
        jnp.stack([own_out, own_turn]),
        own_up,
        own_down,
        own_small[:, seq_len:small].T,
    )
    local_squares = jnp.sum(d_bias * d_bias)
    for grad in owned:
        local_squares = local_squares + jnp.sum(grad * grad)
    spare = -(rows_per + 1) % 128
    last = jnp.concatenate([d_bias, local_squares[None], jnp.zeros((spare,), jnp.float32)])
    last = spread_row(last.reshape(8, -1), sizes, ids[10]).reshape(parts, -1)
    bias_grad = last[:, :rows_per].reshape(-1)[:vocab]
    grad_norm = jnp.sqrt(jnp.sum(last[:, rows_per]))
    factor = clip_norm / jnp.maximum(grad_norm, clip_norm)
    masters = (
        word_table,
        pos_table,
        qkv_weight,
        square_weight,
        up_weight,
        down_weight,
        vec_table,
        head_bias,
    )
    states = (
        (word_first, word_second),
        (pos_first, pos_second),
        (qkv_first, qkv_second),
        (square_first, square_second),
        (up_first, up_second),
        (down_first, down_second),
        (vec_first, vec_second),
        (bias_first, bias_second),
    )
    rates = (
        learn_rate,
        learn_rate,
        learn_rate,
        learn_rate,
        learn_rate,
        learn_rate,
        vector_rate,
        vector_rate,
    )
    grads = tuple(owned) + (bias_grad,)
    results = []
    for weight, state, grad, rate in zip(masters, states, grads, rates):
        results.extend(adam_step(weight, state[0], state[1], grad, factor, rate))
    return (
        results[0],
        results[1],
        results[2],
        results[3],
        results[4],
        results[5],
        results[6],
        results[7],
        results[8],
        results[9],
        results[10],
        results[11],
        results[12],
        results[13],
        results[14],
        results[15],
        results[16],
        results[17],
        results[18],
        results[19],
        results[20],
        results[21],
        results[22],
        results[23],
        loss_total,
        total,
        grad_norm,
    )


def solution(mesh):
    placed = (
        P(("grp", "dp"), None),
        P(("grp", "dp")),
        P(("grp", "dp"), None),
        P(("grp", "dp"), None),
        P(("pipe", "grp", "dp"), None),
        P(("pipe", "grp", "dp"), None),
        P(("pipe", "grp", "dp"), None),
        P(None, ("pipe", "grp", "dp")),
        P(None, ("pipe", "grp", "dp")),
        P(None, ("pipe", "grp", "dp")),
        P(("pipe", "grp", "dp"), None),
        P(("pipe", "grp", "dp"), None),
        P(("pipe", "grp", "dp"), None),
        P(None, ("pipe", "grp", "dp"), None),
        P(None, ("pipe", "grp", "dp"), None),
        P(None, ("pipe", "grp", "dp"), None),
        P(("pipe", "grp", "dp"), None),
        P(("pipe", "grp", "dp"), None),
        P(("pipe", "grp", "dp"), None),
        P(("pipe", "grp", "dp"), None),
        P(("pipe", "grp", "dp"), None),
        P(("pipe", "grp", "dp"), None),
        P(None, ("pipe", "grp", "dp")),
        P(None, ("pipe", "grp", "dp")),
        P(None, ("pipe", "grp", "dp")),
        P(),
        P(),
        P(),
    )
    return jax.shard_map(
        per_device,
        mesh=mesh,
        in_specs=placed,
        out_specs=(
            P(("pipe", "grp", "dp"), None),
            P(("pipe", "grp", "dp"), None),
            P(("pipe", "grp", "dp"), None),
            P(None, ("pipe", "grp", "dp")),
            P(None, ("pipe", "grp", "dp")),
            P(None, ("pipe", "grp", "dp")),
            P(("pipe", "grp", "dp"), None),
            P(("pipe", "grp", "dp"), None),
            P(("pipe", "grp", "dp"), None),
            P(None, ("pipe", "grp", "dp"), None),
            P(None, ("pipe", "grp", "dp"), None),
            P(None, ("pipe", "grp", "dp"), None),
            P(("pipe", "grp", "dp"), None),
            P(("pipe", "grp", "dp"), None),
            P(("pipe", "grp", "dp"), None),
            P(("pipe", "grp", "dp"), None),
            P(("pipe", "grp", "dp"), None),
            P(("pipe", "grp", "dp"), None),
            P(None, ("pipe", "grp", "dp")),
            P(None, ("pipe", "grp", "dp")),
            P(None, ("pipe", "grp", "dp")),
            P(),
            P(),
            P(),
            P(),
            P(),
            P(),
        ),
        check_vma=False,
    )
```

```python
import functools
import math

import jax
import jax.numpy as jnp
from jax import lax
from jax.experimental import pallas as pl
from jax.experimental.pallas import tpu as pltpu
from jax.sharding import PartitionSpec as P

H = 16
STEP = 10


beta_one = 0.9
beta_two = 0.999
learn_rate = 0.02
vector_rate = 0.2
weight_decay = 0.01
epsilon = 1e-08
clip_norm = 0.02
norm_eps = 1e-05
root_half = 0.7071067811865476
density_scale = 0.3989422804014327
AXES = ("pipe", "grp", "dp")
CHIPS = ("grp", "dp")
PLANE = ("pipe", "grp")
highest = lax.Precision.HIGHEST


def matmul(left, right):
    return jnp.dot(left, right, preferred_element_type=jnp.float32)


def left_transposed(left, right):
    return lax.dot_general(
        left, right, (((0,), (0,)), ((), ())), preferred_element_type=jnp.float32
    )


def right_transposed(left, right):
    return lax.dot_general(
        left, right, (((1,), (1,)), ((), ())), preferred_element_type=jnp.float32
    )


def norm_forward(values, gain, shift):
    center = values - jnp.mean(values, -1, keepdims=True)
    scale = lax.rsqrt(jnp.mean(center * center, -1, keepdims=True) + norm_eps)
    normal = center * scale
    return (normal * gain + shift, (normal, scale))


def norm_backward(grad, kept, gain):
    normal, scale = kept
    d_gain = jnp.sum(grad * normal, 0)
    d_shift = jnp.sum(grad, 0)
    d_norm = grad * gain
    d_input = scale * (
        d_norm
        - jnp.mean(d_norm, -1, keepdims=True)
        - normal * jnp.mean(d_norm * normal, -1, keepdims=True)
    )
    return (d_input, d_gain, d_shift)


def gelu_slope(values):
    return (
        0.5 * (1.0 + lax.erf(values * root_half))
        + values * jnp.exp(-0.5 * values * values) * density_scale
    )


def masked_counts(lengths, slots):
    return jnp.minimum(slots, (3 * lengths + 19) // 20)


def one_hot(indices, size, dtype):
    places = lax.broadcasted_iota(jnp.int32, indices.shape + (size,), indices.ndim)
    return (indices[..., None] == places).astype(dtype)


def rows_by_seq(pick, rows):
    return jnp.einsum("sjp,spw->sjw", pick, rows, precision=highest)


def rows_to_seq(pick, rows):
    return jnp.einsum("sjp,sjw->spw", pick, rows, precision=highest)


class Routes:
    def __init__(self, all_ids, all_live, rows_per):
        self.parts, tokens = all_ids.shape
        self.rows_per = rows_per
        self.me = lax.axis_index(AXES)
        mean = tokens / self.parts
        self.room = max(16, int(math.ceil((mean + 2.8 * math.sqrt(mean)) / 16)) * 16)
        owners = jnp.where(all_live, all_ids // rows_per, -1)
        counts = jnp.sum(one_hot(owners, self.parts, jnp.int32), 1)
        self.more = 16
        self.rounds = (jnp.maximum(jnp.max(counts) - self.room, 0) + self.more - 1) // self.more
        mine = owners == self.me
        order = jnp.arange(tokens, dtype=jnp.int32)
        upto = (order[:, None] <= order[None, :]).astype(jnp.bfloat16)
        ranks = matmul(mine.astype(jnp.bfloat16), upto).astype(jnp.int32)
        self.out_rank = jnp.where(mine, ranks - 1, -1)
        self.out_row = all_ids - self.me * rows_per
        own_owners = lax.dynamic_index_in_dim(owners, self.me, 0, keepdims=False)
        hits = one_hot(own_owners, self.parts, jnp.bfloat16)
        ranks = jnp.sum(hits.astype(jnp.float32) * left_transposed(upto, hits), 1)
        ranks = ranks.astype(jnp.int32) - 1
        self.in_rank = ranks
        self.in_owner = own_owners

    def owner_pick(self, first, room):
        slots = first + jnp.arange(room, dtype=jnp.int32)
        at = self.out_rank[:, None, :] == slots[None, :, None]
        row = jnp.sum(jnp.where(at, self.out_row[:, None, :] + 1, 0), 2) - 1
        return one_hot(row.reshape(-1), self.rows_per, jnp.bfloat16)

    def token_pick(self, first, room):
        rank = self.in_rank - first
        inside = (self.in_owner >= 0) & (rank >= 0) & (rank < room)
        slot = jnp.where(inside, self.in_owner * room + rank, -1)
        return one_hot(slot, self.parts * room, jnp.bfloat16)

    def exchange(self, rows):
        shaped = rows.reshape(self.parts, -1, rows.shape[-1])
        return lax.all_to_all(shaped, AXES, 0, 0).reshape(rows.shape)

    def table_rows(self, table, first, room):
        return matmul(self.owner_pick(first, room), table).astype(jnp.bfloat16)

    def token_rows(self, rows, first, room):
        return left_transposed(self.token_pick(first, room), rows).astype(jnp.bfloat16)

    def later(self, more, start):
        def one(turn, kept):
            return kept + more(self.room + turn * self.more)

        return lax.fori_loop(0, self.rounds, one, start)

    def fetch(self, table, arrived):
        def more(first):
            rows = self.exchange(self.table_rows(table, first, self.more))
            return matmul(self.token_pick(first, self.more), rows)

        return self.later(more, matmul(self.token_pick(0, self.room), arrived))

    def give(self, rows, arrived, start):
        def more(first):
            back = self.exchange(self.token_rows(rows, first, self.more))
            return left_transposed(self.owner_pick(first, self.more), back)

        start = start + left_transposed(self.owner_pick(0, self.room), arrived)
        return self.later(more, start)


def swapped(shard):
    return lax.ppermute(shard, "pipe", [(0, 1), (1, 0)])


def both_cores(rows):
    return jnp.concatenate([rows, swapped(rows)], 0)


def half_columns(rows, index):
    half = rows.shape[1] // 2
    return lax.dynamic_slice_in_dim(rows, index * half, half, 1)


def both_halves(rows):
    pipe = lax.axis_index("pipe")
    return jnp.concatenate([half_columns(rows, pipe), swapped(half_columns(rows, 1 - pipe))], 0)


def chip_sum(left, right):
    return left_transposed(both_halves(left), both_cores(right)).astype(jnp.bfloat16)


def chip_half(partial):
    half = partial.shape[0] // 2
    pipe = lax.axis_index("pipe")
    partial = partial.astype(jnp.bfloat16)
    keep = lax.dynamic_slice_in_dim(partial, pipe * half, half, 0)
    give = lax.dynamic_slice_in_dim(partial, (1 - pipe) * half, half, 0)
    return (keep.astype(jnp.float32) + swapped(give).astype(jnp.float32)).astype(jnp.bfloat16)


def device(pipe, grp, dp):
    return {"pipe": pipe, "grp": grp, "dp": dp}


def remote(source, target, send, arrive, to):
    return pltpu.make_async_remote_copy(
        src_ref=source,
        dst_ref=target,
        send_sem=send,
        recv_sem=arrive,
        device_id=device(*to),
        device_id_type=pl.DeviceIdType.MESH,
    )


def tell(barrier, to):
    pl.semaphore_signal(
        barrier, inc=1, device_id=device(*to), device_id_type=pl.DeviceIdType.MESH
    )


def greet(others):
    barrier = pltpu.get_barrier_semaphore()
    for to in others:
        tell(barrier, to)
    pl.semaphore_wait(barrier, len(others))


class Place:
    def __init__(self, sizes):
        self.pipes, self.grps, self.dps = sizes
        self.plane_only = self.dps == 1
        self.pipe, self.grp, self.dp = [lax.axis_index(axis) for axis in AXES]
        column, row = self.grp % 2, self.grp // 2
        self.beside = 2 * row + 1 - column
        self.below = 2 * (1 - row) + column
        self.across = 3 - self.grp

    @property
    def spot(self):
        return 0 if self.plane_only else self.dp

    def plane(self):
        found = []
        for a in range(self.pipes):
            for b in range(self.grps):
                if (a, b) != (0, 0):
                    ahead = ((self.pipe + a) % self.pipes, (self.grp + b) % self.grps)
                    back = (
                        (self.pipe + self.pipes - a) % self.pipes,
                        (self.grp + self.grps - b) % self.grps,
                    )
                    found.append((ahead, back))
        return found

    def line(self, step):
        return (self.dp + step) % self.dps

    def behind(self, step):
        return (self.dp + self.dps - step) % self.dps

    def others(self):
        found = []
        for a in range(self.pipes):
            for b in range(self.grps):
                for c in range(self.dps):
                    if (a, b, c) != (0, 0, 0):
                        ahead = (
                            (self.pipe + a) % self.pipes,
                            (self.grp + b) % self.grps,
                            (self.dp + c) % self.dps,
                        )
                        back = (
                            (self.pipe + self.pipes - a) % self.pipes,
                            (self.grp + self.grps - b) % self.grps,
                            (self.dp + self.dps - c) % self.dps,
                        )
                        found.append((ahead, back))
        return found

    def index(self, pipe, grp, dp):
        return (pipe * self.grps + grp) * self.dps + dp


def swap_all(place, rows, arrived, send, arrive, own):
    me = place.index(place.pipe, place.grp, place.dp)
    copies = []
    for i, (ahead, back) in enumerate(place.others()):
        to = place.index(*ahead)
        copies.append(remote(rows.at[to], arrived.at[me], send.at[i], arrive.at[i], ahead))
        copies[-1].start()
    kept = pltpu.make_async_copy(rows.at[me], arrived.at[me], own)
    kept.start()

    def finish():
        for i, (ahead, back) in enumerate(place.others()):
            origin = place.index(*back)
            copies[i].wait_send()
            remote(rows.at[me], arrived.at[origin], send.at[i], arrive.at[i], ahead).wait_recv()
        kept.wait()

    return finish


def swap_plane(place, rows, arrived, send, arrive, own):
    me = place.pipe * place.grps + place.grp
    copies = []
    for i, (ahead, back) in enumerate(place.plane()):
        to = ahead[0] * place.grps + ahead[1]
        copies.append(
            remote(rows.at[to], arrived.at[me], send.at[i], arrive.at[i], ahead + (place.dp,))
        )
        copies[-1].start()
    kept = pltpu.make_async_copy(rows.at[me], arrived.at[me], own)
    kept.start()

    def finish():
        for i, (ahead, back) in enumerate(place.plane()):
            origin = back[0] * place.grps + back[1]
            copies[i].wait_send()
            remote(
                rows.at[me], arrived.at[origin], send.at[i], arrive.at[i], ahead + (place.dp,)
            ).wait_recv()
        kept.wait()

    return finish


def begin_kernel(sizes, row_ref, up_ref, all_ref, arrived_ref, *sems):
    send, arrive, own, plane_send, plane_arrive, plane_own = sems
    place = Place(sizes)
    others = place.others()
    greet([ahead for ahead, _ in others])
    finish = swap_plane(place, up_ref, arrived_ref, plane_send, plane_arrive, plane_own)
    me = place.index(place.pipe, place.grp, place.dp)
    copies = []
    for i, (ahead, _) in enumerate(others):
        copies.append(remote(row_ref, all_ref.at[me], send.at[i], arrive.at[i], ahead))
        copies[-1].start()
    kept = pltpu.make_async_copy(row_ref, all_ref.at[me], own)
    kept.start()
    for i, (ahead, back) in enumerate(others):
        copies[i].wait_send()
        remote(
            row_ref, all_ref.at[place.index(*back)], send.at[i], arrive.at[i], ahead
        ).wait_recv()
    kept.wait()
    finish()


def begin(row, blocks, sizes, collective):
    parts = math.prod(sizes)
    sems = pltpu.SemaphoreType.DMA((parts - 1,))
    plane_sems = pltpu.SemaphoreType.DMA((sizes[0] * sizes[1] - 1,))
    return pl.pallas_call(
        functools.partial(begin_kernel, sizes),
        out_shape=(
            jax.ShapeDtypeStruct((parts,) + row.shape, row.dtype),
            jax.ShapeDtypeStruct(blocks.shape, blocks.dtype),
        ),
        in_specs=[pl.BlockSpec(memory_space=pltpu.VMEM)] * 2,
        out_specs=[pl.BlockSpec(memory_space=pltpu.VMEM)] * 2,
        scratch_shapes=[
            sems,
            sems,
            pltpu.SemaphoreType.DMA,
            plane_sems,
            plane_sems,
            pltpu.SemaphoreType.DMA,
        ],
        compiler_params=pltpu.CompilerParams(
            collective_id=collective, has_side_effects=True, vmem_limit_bytes=8 << 20
        ),
    )(row, blocks)


def spread_kernel(sizes, row_ref, all_ref, send, arrive, own):
    place = Place(sizes)
    others = place.others()
    greet([ahead for ahead, _ in others])
    me = place.index(place.pipe, place.grp, place.dp)
    copies = []
    for i, (ahead, _) in enumerate(others):
        copies.append(remote(row_ref, all_ref.at[me], send.at[i], arrive.at[i], ahead))
        copies[-1].start()
    kept = pltpu.make_async_copy(row_ref, all_ref.at[me], own)
    kept.start()
    for i, (ahead, back) in enumerate(others):
        copies[i].wait_send()
        remote(
            row_ref, all_ref.at[place.index(*back)], send.at[i], arrive.at[i], ahead
        ).wait_recv()
    kept.wait()


def spread(row, sizes, collective):
    parts = math.prod(sizes)
    sems = pltpu.SemaphoreType.DMA((parts - 1,))
    return pl.pallas_call(
        functools.partial(spread_kernel, sizes),
        out_shape=jax.ShapeDtypeStruct((parts,) + row.shape, row.dtype),
        in_specs=[pl.BlockSpec(memory_space=pltpu.VMEM)],
        out_specs=pl.BlockSpec(memory_space=pltpu.VMEM),
        scratch_shapes=[sems, sems, pltpu.SemaphoreType.DMA],
        compiler_params=pltpu.CompilerParams(
            collective_id=collective, has_side_effects=True, vmem_limit_bytes=8 << 20
        ),
    )(row)


def stats_kernel(sizes, own_ref, all_ref, held, result, send, arrive, own, send_two, arrive_two):
    place = Place(sizes)
    others = place.others()
    greet([ahead for ahead, _ in others])
    swap_all(place, own_ref, held, send, arrive, own)()
    peaks = held[:, 0]
    peak = jnp.max(peaks, 0, keepdims=True)
    total = jnp.sum(held[:, 1] * jnp.exp(peaks - peak), 0, keepdims=True)
    label = jnp.sum(held[:, 2], 0, keepdims=True)
    result[0:1] = peak
    result[1:2] = total
    result[2:3] = label
    result[3:8] = jnp.zeros((5, result.shape[1]), jnp.float32)
    me = place.index(place.pipe, place.grp, place.dp)
    copies = []
    for i, (ahead, _) in enumerate(others):
        copies.append(remote(result, all_ref.at[me], send_two.at[i], arrive_two.at[i], ahead))
        copies[-1].start()
    all_ref[me] = result[...]
    for i, (ahead, back) in enumerate(others):
        copies[i].wait_send()
        remote(
            result, all_ref.at[place.index(*back)], send_two.at[i], arrive_two.at[i], ahead
        ).wait_recv()


def combine_stats(own, sizes, collective):
    parts, _, rows = own.shape
    sems = pltpu.SemaphoreType.DMA((parts - 1,))
    return pl.pallas_call(
        functools.partial(stats_kernel, sizes),
        out_shape=jax.ShapeDtypeStruct(own.shape, jnp.float32),
        in_specs=[pl.BlockSpec(memory_space=pltpu.VMEM)],
        out_specs=pl.BlockSpec(memory_space=pltpu.VMEM),
        scratch_shapes=[
            pltpu.VMEM(own.shape, jnp.float32),
            pltpu.VMEM((8, rows), jnp.float32),
            sems,
            sems,
            pltpu.SemaphoreType.DMA,
            sems,
            sems,
        ],
        compiler_params=pltpu.CompilerParams(
            collective_id=collective, has_side_effects=True, vmem_limit_bytes=8 << 20
        ),
    )(own)


def gather_kernel(sizes, pieces, routed, *refs):
    count = max(piece[0] for piece in pieces) + 1
    shards, refs = refs[:count], refs[count:]
    if routed:
        rows_ref, refs = refs[0], refs[1:]
    fulls, refs = refs[:count], refs[count:]
    if routed:
        arrived_ref, refs = refs[0], refs[1:]
    send, arrive, own, swap_send, swap_arrive, swap_own = refs
    place = Place(sizes)
    pipe, grp, dp = place.pipe, place.grp, place.dp
    near = place.beside * (1 - pipe) + place.below * pipe
    far = place.below * (1 - pipe) + place.beside * pipe
    core = (1 - pipe, grp, dp)
    hops = place.dps - 1
    spot = place.spot
    ends = (dp < hops, dp > 0)
    sides = ((pipe, grp, dp + 1), (pipe, grp, dp - 1))
    both = range(2 if hops else 0)
    if routed:
        greet([ahead for ahead, _ in place.others()])
    else:
        greet(
            [(pipe, grp, place.line(k + 1)) for k in range(hops)]
            + [(pipe, near, dp), (pipe, far, dp), core]
        )
    waits = []

    def view(piece, *at):
        array, first, rows = piece
        return fulls[array].at[at + ((slice(None),) * (3 - len(at))) + (pl.ds(first, rows),)]

    def launch(n, index, source, piece, to, *at):
        copy = remote(source, view(piece, *at), send.at[n, index], arrive.at[n, index], to)
        copy.start()
        waits.append(copy)

    def landed(n, index, piece, *at):
        target = view(piece, *at)
        remote(target, target, send.at[n, index], arrive.at[n, index], core).wait_recv()

    def along(n, side, hop, finish=False):
        origin = dp - hop if side == 0 else dp + hop
        here = origin >= 0 if side == 0 else origin <= hops
        piece, index = pieces[n], side * hops + hop

        def copy():
            array, first, rows = piece
            target = view(piece, pipe, grp, origin)
            source = shards[array].at[pl.ds(first, rows)] if hop == 0 else target
            return remote(source, target, send.at[n, index], arrive.at[n, index], sides[side])

        if finish:

            @pl.when(here & ends[side])
            def _():
                copy().wait_send()

            return
        if hop > 0:

            @pl.when(here)
            def _():
                landed(n, index - 1, piece, pipe, grp, origin)

        if hop < hops:

            @pl.when(here & ends[side])
            def _():
                copy().start()

    keeps = {}

    def over_line(n, hop):
        if hop == 0:
            array, first, rows = pieces[n]
            source = shards[array].at[pl.ds(first, rows)]
            keeps[n] = pltpu.make_async_copy(source, view(pieces[n], pipe, grp, spot), own.at[n])
            keeps[n].start()
        for side in both:
            along(n, side, hop)

    def over_plane(n):
        array, first, rows = piece = pieces[n]
        over_line(n, hops)
        if hops:
            keeps[n].wait()
            group, at = view(piece, pipe, grp), (pipe, grp)
        else:
            group, at = shards[array].at[pl.ds(first, rows)], (pipe, grp, 0)
        launch(n, 2 * hops, group, piece, (pipe, near, dp), *at)
        launch(n, 2 * hops + 1, group, piece, (pipe, far, dp), *at)
        launch(n, 2 * hops + 3, group, piece, core, *at)

    def pass_on(n):
        piece = pieces[n]
        landed(n, 2 * hops, piece, pipe, near)
        group = view(piece, pipe, near)
        launch(n, 2 * hops + 2, group, piece, (pipe, far, dp), pipe, near)
        launch(n, 2 * hops + 4, group, piece, core, pipe, near)
        landed(n, 2 * hops + 1, piece, pipe, far)
        launch(n, 2 * hops + 5, view(piece, pipe, far), piece, core, pipe, far)

    def last(n):
        piece = pieces[n]
        landed(n, 2 * hops + 2, piece, pipe, place.across)
        launch(n, 2 * hops + 6, view(piece, pipe, place.across), piece, core, pipe, place.across)

    stages = [functools.partial(over_line, hop=hop) for hop in range(hops)]
    stages += [over_plane, pass_on, last]
    total = len(pieces)
    for turn in range(total + len(stages) - 1):
        for at, stage in enumerate(stages):
            if 0 <= turn - at < total:
                stage(turn - at)
        if turn == 5 and routed:
            finish = swap_all(place, rows_ref, arrived_ref, swap_send, swap_arrive, swap_own)
    for n, piece in enumerate(pieces):
        landed(n, 2 * hops + 3, piece, 1 - pipe, grp)
        landed(n, 2 * hops + 4, piece, 1 - pipe, far)
        landed(n, 2 * hops + 5, piece, 1 - pipe, near)
        landed(n, 2 * hops + 6, piece, 1 - pipe, place.across)
        for side in both:
            for hop in range(hops):
                along(n, side, hop, finish=True)
    for copy in waits:
        copy.wait_send()
    if not hops:
        for keep in keeps.values():
            keep.wait()
    if routed:
        finish()


def gather_all(shards, pieces, sizes, collective, rows=None):
    parts = math.prod(sizes)
    routed = rows is not None
    kinds = 2 * (sizes[2] - 1) + 7
    space = pltpu.VMEM if sizes[2] == 1 else pl.ANY
    out_shape = [jax.ShapeDtypeStruct(sizes + shard.shape, shard.dtype) for shard in shards]
    if routed:
        out_shape.append(jax.ShapeDtypeStruct(rows.shape, rows.dtype))
    operands = list(shards) + ([rows] if routed else [])
    sems = pltpu.SemaphoreType.DMA((len(pieces), kinds))
    swaps = pltpu.SemaphoreType.DMA((parts - 1 if routed else 1,))
    return pl.pallas_call(
        functools.partial(gather_kernel, sizes, tuple(pieces), routed),
        out_shape=out_shape,
        in_specs=[pl.BlockSpec(memory_space=space)] * len(operands),
        out_specs=[pl.BlockSpec(memory_space=space)] * len(out_shape),
        scratch_shapes=[
            sems,
            sems,
            pltpu.SemaphoreType.DMA((len(pieces),)),
            swaps,
            swaps,
            pltpu.SemaphoreType.DMA,
        ],
        compiler_params=pltpu.CompilerParams(
            collective_id=collective, has_side_effects=True, vmem_limit_bytes=16 << 20
        ),
    )(*operands)


class Sums:
    block = 16

    def __init__(self, place, sources, chips, others, mine, planes, lines, send, arrive, own, store):
        self.place, self.sources, self.chips, self.others = place, sources, chips, others
        self.mine, self.planes, self.lines = mine, planes, lines
        self.send, self.arrive, self.own, self.store = send, arrive, own, store
        pipe, grp, dp = place.pipe, place.grp, place.dp
        self.near = place.beside * (1 - pipe) + place.below * pipe
        self.far = place.below * (1 - pipe) + place.beside * pipe
        self.copies, self.kept = {}, {}

    def launch(self, n, index, source, target, to):
        copy = remote(source, target, self.send.at[n, index], self.arrive.at[n, index], to)
        self.copies[n, index] = copy
        copy.start()

    def keep(self, n, index, source, target):
        self.kept[n, index] = pltpu.make_async_copy(source, target, self.own.at[n, index])
        self.kept[n, index].start()

    def blocks(self, n, body):
        deep = self.mine[n].shape[2] // self.block

        def one(i, _):
            body(i // deep, pl.ds(pl.multiple_of(i % deep * self.block, self.block), self.block))
            return 0

        lax.fori_loop(0, self.place.dps * deep, one, 0)

    def to_core(self, n):
        place = self.place
        if self.chips[n] is not None:
            core = (1 - place.pipe, place.grp, place.dp)
            self.launch(n, 0, self.sources[n].at[1 - place.pipe], self.others[n], core)
            self.keep(n, 0, self.sources[n].at[place.pipe], self.chips[n])

    def to_near(self, n):
        place, chip, other = self.place, self.chips[n], self.others[n]
        part = self.sources[n]
        if chip is not None:
            self.kept[n, 0].wait()
            self.copies[n, 0].wait_recv()
            for g in range(place.grps):

                def add(d, at, g=g):
                    left = chip[g, d, at].astype(jnp.float32)
                    chip[g, d, at] = (left + other[g, d, at].astype(jnp.float32)).astype(
                        jnp.bfloat16
                    )

                self.blocks(n, add)
            part = chip
        else:
            for j, g in enumerate((self.far, place.grp)):
                self.keep(n, j, part.at[g], self.mine[n].at[j])
        to = (place.pipe, self.near, place.dp)
        self.launch(n, 1, part.at[self.near], self.planes[n].at[1], to)
        self.launch(n, 2, part.at[place.across], self.planes[n].at[0], to)

    def to_far(self, n):
        place, mine, plane, chip = self.place, self.mine[n], self.planes[n], self.chips[n]
        if chip is None:
            self.kept[n, 0].wait()
            self.kept[n, 1].wait()
        self.copies[n, 1].wait_recv()
        self.copies[n, 2].wait_recv()
        for j, g in enumerate((self.far, place.grp)):

            def add(d, at, j=j, g=g):
                left = mine[j, d, at] if chip is None else chip[g, d, at]
                total = left.astype(jnp.float32) + plane[j, d, at].astype(jnp.float32)
                mine[j, d, at] = total.astype(jnp.bfloat16)

            self.blocks(n, add)
            if j == 0:
                self.launch(n, 3, mine.at[0], plane.at[2], (place.pipe, self.far, place.dp))

    def to_lines(self, n):
        place, mine, plane = self.place, self.mine[n], self.planes[n]
        self.copies[n, 3].wait_recv()
        hops = place.dps - 1

        def add(d, at):
            total = mine[1, d, at].astype(jnp.float32) + plane[2, d, at].astype(jnp.float32)
            if hops:
                mine[1, d, at] = total.astype(jnp.bfloat16)
            else:
                self.store(n, at, total)

        self.blocks(n, add)
        for k in range(hops):
            to = place.line(k + 1)
            self.launch(
                n, 4 + k, mine.at[1, to], self.lines[n].at[k], (place.pipe, place.grp, to)
            )

    def to_sum(self, n):
        place, mine, lines = self.place, self.mine[n], self.lines[n]
        for k in range(place.dps - 1):
            self.copies[n, 4 + k].wait_recv()

        def add(i, _):
            at = pl.ds(pl.multiple_of(i * self.block, self.block), self.block)
            total = mine[1, place.spot, at].astype(jnp.float32)
            for k in range(place.dps - 1):
                total = total + lines[k, at].astype(jnp.float32)
            self.store(n, at, total)
            return 0

        lax.fori_loop(0, mine.shape[2] // self.block, add, 0)

    def settle(self):
        for copy in self.copies.values():
            copy.wait_send()


def sum_scratch(shapes, cores, sizes):
    low = jnp.bfloat16
    _, grps, dps = sizes
    wide = [(dps,) + shape for shape in shapes]
    chips = [pltpu.VMEM((grps,) + shape, low) for shape, core in zip(wide, cores) if core]
    scratch = chips + chips
    scratch += [pltpu.VMEM((2,) + shape, low) for shape in wide]
    scratch += [pltpu.VMEM((3,) + shape, low) for shape in wide]
    scratch += [pltpu.VMEM((max(dps - 1, 1),) + shape, low) for shape in shapes]
    sems = pltpu.SemaphoreType.DMA((len(shapes), 4 + dps - 1))
    return scratch + [sems, sems, pltpu.SemaphoreType.DMA((len(shapes), 2))]


def sum_refs(refs, cores):
    total = len(cores)

    def spread_out(found):
        found = iter(found)
        return [next(found) if core else None for core in cores]

    chosen = sum(cores)
    groups = []
    for count in (chosen, chosen, total, total, total):
        groups.append(refs[:count])
        refs = refs[count:]
    chips, others, mine, planes, lines = groups
    return (spread_out(chips), spread_out(others), mine, planes, lines) + tuple(refs[:3]), refs[3:]


def reduce_kernel(sizes, pieces, *refs):
    partial, out, refs = refs[0], refs[1], refs[2:]
    place = Place(sizes)
    scratch, _ = sum_refs(refs, (True,) * len(pieces))

    def store(n, at, total):
        to = pl.multiple_of(pieces[n][0] + at.start, Sums.block)
        out[pl.ds(to, Sums.block)] = total

    sources = [partial.at[:, :, :, pl.ds(first, rows)] for first, rows in pieces]
    sums = Sums(place, sources, *scratch, store)
    line = [(place.pipe, place.grp, place.line(k + 1)) for k in range(place.dps - 1)]
    near, far = [(place.pipe, grp, place.dp) for grp in (sums.near, sums.far)]
    greet(line + [near, far, (1 - place.pipe, place.grp, place.dp)])
    stages = [sums.to_core, sums.to_near, sums.to_far, sums.to_lines]
    stages += [sums.to_sum] if place.dps > 1 else []
    total = len(pieces)
    for turn in range(total + len(stages) - 1):
        for at, stage in enumerate(stages):
            if 0 <= turn - at < total:
                stage(turn - at)
    sums.settle()


def reduce_all(partial, pieces, sizes, collective):
    shapes = [(rows, partial.shape[-1]) for _, rows in pieces]
    return pl.pallas_call(
        functools.partial(reduce_kernel, sizes, tuple(pieces)),
        out_shape=jax.ShapeDtypeStruct(partial.shape[-2:], jnp.float32),
        in_specs=[pl.BlockSpec(memory_space=pl.ANY)],
        out_specs=pl.BlockSpec(memory_space=pltpu.VMEM),
        scratch_shapes=sum_scratch(shapes, (True,) * len(pieces), sizes),
        compiler_params=pltpu.CompilerParams(
            collective_id=collective, has_side_effects=True, vmem_limit_bytes=48 << 20
        ),
    )(partial)


def finish_kernel(sizes, cut, *refs):
    partials, refs = refs[:3], refs[3:]
    start_ref, chosen_ref, grads, refs = refs[0], refs[1], refs[2:5], refs[5:]
    logits_ref, normed_ref, rows_ref, blocks_ref, refs = refs[0], refs[1], refs[2], refs[3], refs[4:]
    outs, refs = refs[:6], refs[6:]
    word_ref, arrived_ref, blocks_arrived_ref, refs = refs[0], refs[1], refs[2], refs[3:]
    cores = (False, False, True, False, False, False)
    scratch, refs = sum_refs(refs, cores)
    start, chosen, held, made, refs = refs[0], refs[1], refs[2:5], refs[5:8], refs[8:]
    logits, normed, refs = refs[0], refs[1], refs[2:]
    swap_send, swap_arrive, swap_own, plane_send, plane_arrive, plane_own = refs[:6]
    load, word_load, core_send, core_arrive = refs[6:]
    place = Place(sizes)
    pipe, grp, dp = place.pipe, place.grp, place.dp
    greet([ahead for ahead, _ in place.others()])

    exchanged = []
    for i in range(3):
        pltpu.make_async_copy(grads[i], held[i].at[0], load.at[2 + i]).start()
        exchanged.append(
            remote(grads[i], held[i].at[1], core_send.at[i], core_arrive.at[i], (1 - pipe, grp, dp))
        )
        exchanged[-1].start()
    pltpu.make_async_copy(start_ref, start, load.at[0]).start()
    pltpu.make_async_copy(chosen_ref, chosen, load.at[1]).start()

    def store(n, at, total):
        outs[n][at] = total

    sums = Sums(place, tuple(partials) + tuple(made), *scratch, store)
    sums.to_core(2)
    sums.to_near(0)
    sums.to_near(1)
    swap = swap_all(place, rows_ref, arrived_ref, swap_send, swap_arrive, swap_own)
    plane_swap = swap_plane(
        place, blocks_ref, blocks_arrived_ref, plane_send, plane_arrive, plane_own
    )
    sums.to_near(2)

    steps = logits_ref.shape[0] // cut

    def word_copies(step):
        slot = step % 2
        at = pl.ds(pl.multiple_of(step * cut, cut), cut)
        return (
            pltpu.make_async_copy(logits_ref.at[at], logits.at[slot], word_load.at[0, slot]),
            pltpu.make_async_copy(normed_ref.at[at], normed.at[slot], word_load.at[1, slot]),
        )

    for copy in word_copies(0):
        copy.start()

    def word_steps(first, last):
        def one(step, _):
            @pl.when(step + 1 < steps)
            def _():
                for copy in word_copies(step + 1):
                    copy.start()

            for copy in word_copies(step):
                copy.wait()
            slot = step % 2
            word_ref[...] += left_transposed(logits[slot], normed[slot])
            return 0

        lax.fori_loop(first, last, one, 0)

    word_ref[...] = jnp.zeros_like(word_ref)

    def form(i):
        pltpu.make_async_copy(grads[i], held[i].at[0], load.at[2 + i]).wait()
        exchanged[i].wait_recv()
        if i == 0:
            pltpu.make_async_copy(chosen_ref, chosen, load.at[1]).wait()
        if i == 1:
            pltpu.make_async_copy(start_ref, start, load.at[0]).wait()
        left = chosen if i == 0 else start
        right = held[i]
        wide = left.shape[1] // place.grps
        tokens = right.shape[1]

        for g in range(place.grps):
            at = pl.ds(g * wide, wide)
            total = left_transposed(left[0:tokens, at], right[0])
            total = total + left_transposed(left[tokens:, at], right[1])
            made[i][g] = total.astype(jnp.bfloat16).reshape(made[i].shape[1:])

    form(0)
    sums.to_near(3)
    sums.to_far(0)
    form(1)
    sums.to_near(4)
    sums.to_far(1)
    form(2)
    sums.to_near(5)
    sums.to_far(2)
    sums.to_lines(0)
    sums.to_lines(1)
    word_steps(0, steps // 2)
    sums.to_far(3)
    sums.to_lines(2)
    sums.to_far(4)
    sums.to_lines(3)
    sums.to_far(5)
    sums.to_lines(4)
    word_steps(steps // 2, steps)
    sums.to_lines(5)
    for n in range(6):
        sums.to_sum(n)
    sums.settle()
    for copy in exchanged:
        copy.wait_send()
    plane_swap()
    swap()


def finish_all(partials, start, chosen, grads, logits, normed, rows, blocks, sizes, collective):
    low = jnp.bfloat16
    parts = math.prod(sizes)
    _, grps, dps = sizes
    shapes = [(partial.shape[-2], partial.shape[-1]) for partial in partials]
    made = (grps, dps) + shapes[0]
    shapes += [shapes[0]] * 3
    cut = 512
    anywhere = pl.BlockSpec(memory_space=pl.ANY)
    near = pl.BlockSpec(memory_space=pltpu.VMEM)
    swaps = pltpu.SemaphoreType.DMA((parts - 1,))
    plane_swaps = pltpu.SemaphoreType.DMA((sizes[0] * grps - 1,))
    one = pltpu.SemaphoreType.DMA
    operands = (*partials, start, chosen, *grads, logits, normed, rows, blocks)
    out_shape = [jax.ShapeDtypeStruct(shape, jnp.float32) for shape in shapes]
    out_shape += [jax.ShapeDtypeStruct((logits.shape[1], normed.shape[1]), jnp.float32)]
    out_shape += [jax.ShapeDtypeStruct(extra.shape, extra.dtype) for extra in (rows, blocks)]
    return pl.pallas_call(
        functools.partial(finish_kernel, sizes, cut),
        out_shape=out_shape,
        in_specs=[anywhere] * len(operands),
        out_specs=[near] * 7 + [anywhere] * 2,
        scratch_shapes=sum_scratch(shapes, (False, False, True, False, False, False), sizes)
        + [pltpu.VMEM(start.shape, low), pltpu.VMEM(chosen.shape, low)]
        + [pltpu.VMEM((2,) + grad.shape, low) for grad in grads]
        + [pltpu.VMEM(made, low)] * 3
        + [
            pltpu.VMEM((2, cut, logits.shape[1]), low),
            pltpu.VMEM((2, cut, normed.shape[1]), low),
            swaps,
            swaps,
            one,
            plane_swaps,
            plane_swaps,
            one,
            pltpu.SemaphoreType.DMA((5,)),
            pltpu.SemaphoreType.DMA((2, 2)),
            pltpu.SemaphoreType.DMA((3,)),
            pltpu.SemaphoreType.DMA((3,)),
        ],
        compiler_params=pltpu.CompilerParams(
            collective_id=collective, has_side_effects=True, vmem_limit_bytes=56 << 20
        ),
    )(*operands)


def pair_rows(pair, first):
    pair = pair.astype(jnp.float32)
    low = jnp.bfloat16
    return jnp.concatenate(
        [jnp.where(first, pair, 0.0).astype(low), jnp.where(first, 0.0, pair).astype(low)], 0
    )


def pair_probs(rows, keys, live, scale):
    scores = jnp.where(live, right_transposed(rows, keys) * scale, -1e30)
    exp_scores = jnp.exp(scores - jnp.max(scores, -1, keepdims=True))
    return exp_scores / jnp.sum(exp_scores, -1, keepdims=True)


def attention_masks(lengths_ref, slots, seq_len, lanes):
    live = lax.broadcasted_iota(jnp.int32, (1, seq_len), 1) < lengths_ref[pl.program_id(0)]
    first = lax.broadcasted_iota(jnp.int32, (slots, lanes), 1) < lanes // 2
    return live, first


def attention_kernel(scale, lanes, lengths_ref, q_ref, k_ref, v_ref, out_ref):
    slots = q_ref.shape[0]
    live, first = attention_masks(lengths_ref, slots, k_ref.shape[0], lanes)
    for pair in range(q_ref.shape[1] // lanes):
        at = slice(pair * lanes, (pair + 1) * lanes)
        probs = pair_probs(pair_rows(q_ref[:, at], first), k_ref[:, at], live, scale)
        context = matmul(probs.astype(jnp.bfloat16), v_ref[:, at])
        out_ref[:, at] = jnp.where(first, context[:slots], context[slots:]).astype(jnp.bfloat16)


def attention_back_kernel(
    scale, lanes, lengths_ref, q_ref, k_ref, v_ref, grad_ref, dq_ref, dk_ref, dv_ref
):
    slots = q_ref.shape[0]
    low = jnp.bfloat16
    live, first = attention_masks(lengths_ref, slots, k_ref.shape[0], lanes)
    for pair in range(q_ref.shape[1] // lanes):
        at = slice(pair * lanes, (pair + 1) * lanes)
        rows, grads = pair_rows(q_ref[:, at], first), pair_rows(grad_ref[:, at], first)
        probs = pair_probs(rows, k_ref[:, at], live, scale)
        dv_ref[:, at] = left_transposed(probs.astype(low), grads).astype(low)
        d_probs = right_transposed(grads, v_ref[:, at])
        d_scores = probs * (d_probs - jnp.sum(probs * d_probs, -1, keepdims=True))
        d_scores = d_scores.astype(low)
        d_query = matmul(d_scores, k_ref[:, at]) * scale
        dq_ref[:, at] = jnp.where(first, d_query[:slots], d_query[slots:]).astype(low)
        dk_ref[:, at] = (left_transposed(d_scores, rows) * scale).astype(low)


def attention(lengths, queries, both, grads=None):
    own = lengths.shape[0]
    width = queries.shape[1]
    slots, seq_len = queries.shape[0] // own, both.shape[0] // own
    lanes = 2 * width // H
    scale = (width // H) ** (-0.5)
    cuts = 2
    part = width // cuts
    row = pl.BlockSpec((slots, part), lambda s, h: (s, h))
    keys = pl.BlockSpec((seq_len, part), lambda s, h: (s, h))
    values = pl.BlockSpec((seq_len, part), lambda s, h: (s, cuts + h))
    in_specs = [pl.BlockSpec(memory_space=pltpu.SMEM), row, keys, values]
    flat = jax.ShapeDtypeStruct(queries.shape, jnp.bfloat16)
    tall = jax.ShapeDtypeStruct((both.shape[0], width), jnp.bfloat16)
    if grads is None:
        return pl.pallas_call(
            functools.partial(attention_kernel, scale, lanes),
            grid=(own, cuts),
            out_shape=flat,
            in_specs=in_specs,
            out_specs=row,
        )(lengths, queries, both, both)
    return pl.pallas_call(
        functools.partial(attention_back_kernel, scale, lanes),
        grid=(own, cuts),
        out_shape=(flat, tall, tall),
        in_specs=in_specs + [row],
        out_specs=(row, keys, keys),
    )(lengths, queries, both, both, grads)


def even_pieces(array, rows, cuts):
    size = rows // cuts
    return [(array, i * size, size) for i in range(cuts)]


def start_all(row, blocks, sizes, collective):
    if collective is None:
        return lax.all_gather(row, AXES, axis=0), lax.all_to_all(blocks, PLANE, 0, 0)
    return begin(row, blocks, sizes, collective)


def gather_weights(shards, pieces, sizes, collective, rows):
    if collective is None:
        fulls = [lax.all_gather(shard, AXES, axis=0) for shard in shards]
        arrived = lax.all_to_all(rows, AXES, 0, 0)
    else:
        *fulls, arrived = gather_all(shards, pieces, sizes, collective, rows)
    return [full.reshape(-1, full.shape[-1]) for full in fulls], arrived


def gather_rows(shard, sizes, collective, cuts):
    if collective is None:
        axes = AXES if sizes[2] > 1 else PLANE
        return lax.all_gather(shard, axes, axis=0, tiled=True)
    (full,) = gather_all([shard], even_pieces(0, shard.shape[0], cuts), sizes, collective)
    return full.reshape(-1, full.shape[-1])


def sum_rows(partial, sizes, collective, cuts):
    if collective is None:
        axes = AXES if sizes[2] > 1 else PLANE
        total = lax.psum_scatter(partial, axes, scatter_dimension=0, tiled=True)
        return total.astype(jnp.float32)
    shaped = partial.reshape(sizes + (-1, partial.shape[1]))
    size = shaped.shape[3] // cuts
    return reduce_all(shaped, [(i * size, size) for i in range(cuts)], sizes, collective)


def sum_chips(partials, start, chosen, grads, logits, normed, rows, blocks, sizes, collective):
    if collective is not None:
        cores = len(partials) - 1
        shaped = [
            p.reshape(sizes[1 if i < cores else 0 :] + (-1, p.shape[1]))
            for i, p in enumerate(partials)
        ]
        *sums, word, rows, blocks = finish_all(
            shaped, start, chosen, grads, logits, normed, rows, blocks, sizes, collective
        )
        return sums, word, rows, blocks
    made = [
        left_transposed(left, both_cores(right)).astype(jnp.bfloat16)
        for left, right in zip((chosen, start, start), grads)
    ]
    partials = list(partials[:-1]) + [chip_half(partials[-1])] + made
    sums = [
        lax.psum_scatter(p, CHIPS, scatter_dimension=0, tiled=True).astype(jnp.float32)
        for p in partials
    ]
    rows = lax.all_to_all(rows, AXES, 0, 0)
    blocks = lax.all_to_all(blocks, PLANE, 0, 0)
    return sums, left_transposed(logits, normed), rows, blocks


def line_shift(shard, step):
    size = lax.axis_size("dp")
    return lax.ppermute(shard, "dp", [(i, (i + step) % size) for i in range(size)])


def line_gather(shard, collective):
    if collective is None:
        return lax.all_gather(shard, "dp", axis=0)
    size = lax.axis_size("dp")
    me = lax.axis_index("dp")
    kept = jnp.stack([shard] + [line_shift(shard, step) for step in range(1, size)])
    order = [(me + size - i) % size for i in range(size)]
    return jnp.concatenate([lax.dynamic_slice_in_dim(kept, at, 1, 0) for at in order], 0)


def line_sum(partial, collective):
    partial = partial.astype(jnp.bfloat16)
    if collective is None:
        total = lax.psum_scatter(partial, "dp", scatter_dimension=0, tiled=False)
        return total.astype(jnp.float32)
    size = lax.axis_size("dp")
    me = lax.axis_index("dp")

    def entry(step):
        return lax.dynamic_index_in_dim(partial, (me + step) % size, 0, keepdims=False)

    total = entry(0).astype(jnp.float32)
    for step in range(1, size):
        total = total + line_shift(entry(step), step).astype(jnp.float32)
    return total


def spread_row(row, sizes, collective):
    if collective is None:
        return lax.all_gather(row, AXES, axis=0)
    return spread(row, sizes, collective)


def share_stats(peak, total, label, sizes, collective):
    if collective is None:
        top = lax.pmax(peak, AXES)
        total, label = lax.psum((total * jnp.exp(peak - top), label), AXES)
        return top, total, label
    parts = math.prod(sizes)
    stats = jnp.stack([peak, total, label])
    stats = jnp.pad(stats.reshape(3, parts, -1).swapaxes(0, 1), ((0, 0), (0, 5), (0, 0)))
    stats = combine_stats(stats, sizes, collective)
    return [stats[:, i].reshape(-1) for i in range(3)]


def adam_step(weight, first, second, grad, factor, rate):
    clipped = grad * factor
    first = beta_one * first + (1.0 - beta_one) * clipped
    second = beta_two * second + (1.0 - beta_two) * clipped * clipped
    first_hat = first / (1.0 - beta_one**STEP)
    second_hat = second / (1.0 - beta_two**STEP)
    weight = weight - rate * (first_hat / (jnp.sqrt(second_hat) + epsilon) + weight_decay * weight)
    return (weight, first, second)


def per_device(
    token_ids,
    lengths,
    masked_at,
    labels,
    word_table,
    word_first,
    word_second,
    pos_table,
    pos_first,
    pos_second,
    qkv_weight,
    qkv_first,
    qkv_second,
    square_weight,
    square_first,
    square_second,
    up_weight,
    up_first,
    up_second,
    down_weight,
    down_first,
    down_second,
    vec_table,
    vec_first,
    vec_second,
    head_bias,
    bias_first,
    bias_second,
):
    narrow = jnp.bfloat16
    seq_len, slots = token_ids.shape[1], masked_at.shape[1]
    width = word_table.shape[1]
    vocab = head_bias.shape[0]
    rows_per = word_table.shape[0]
    parts = lax.axis_size(AXES)
    halves = lax.axis_size("pipe")
    me = lax.axis_index(AXES)
    own = token_ids.shape[0] // halves
    first_own = lax.axis_index("pipe") * own
    head_dim = width // H
    sizes = tuple(lax.axis_size(axis) for axis in AXES)
    shards = (word_table, qkv_weight, square_weight[0], up_weight, down_weight)
    direct = sizes[:2] == (2, 4) and all(shard.shape[0] % 32 == 0 for shard in shards)
    ids = tuple(range(11)) if direct else (None,) * 11
    plane_sizes = sizes[:2] + (1,)

    spare = -(seq_len + slots + 1) % 128
    packed = jnp.concatenate(
        [token_ids, labels, lengths[:, None], jnp.zeros((token_ids.shape[0], spare), jnp.int32)], 1
    )
    packed = lax.dynamic_slice_in_dim(packed, first_own, own, 0)
    planes = sizes[0] * sizes[1]
    units = up_weight.shape[1] // planes
    cut = me // sizes[2]
    blocks = up_weight.astype(narrow).reshape(up_weight.shape[0], planes, units).swapaxes(0, 1)
    packed, blocks = start_all(packed, blocks, sizes, ids[0])
    halves_low = down_weight.astype(narrow).reshape(-1, units)
    both_low = jnp.concatenate([blocks.reshape(-1, units), halves_low], 0)
    both_low = line_gather(both_low, ids[0])
    down_low = both_low[:, -halves_low.shape[0] :].reshape(units, width)
    up_low = both_low[:, : -halves_low.shape[0]].reshape(sizes[2], planes, -1, units)
    up_low = up_low.swapaxes(0, 1).reshape(width, units)
    all_ids = packed[:, :, :seq_len]
    all_labels = packed[:, :, seq_len : seq_len + slots].reshape(-1)
    all_lengths = packed[:, :, seq_len + slots]
    places = jnp.arange(seq_len, dtype=jnp.int32)
    all_live = places[None, None, :] < all_lengths[:, :, None]
    all_counts = masked_counts(all_lengths, slots)
    total = jnp.sum(all_counts).astype(jnp.float32)
    slot_index = jnp.arange(slots, dtype=jnp.int32)
    all_valid = (slot_index < all_counts[:, :, None]).astype(jnp.float32).reshape(-1)
    own_lengths = lax.dynamic_slice_in_dim(lengths, first_own, own, 0)
    masked = lax.dynamic_slice_in_dim(masked_at, first_own, own, 0)

    word_low = word_table.astype(narrow)
    routes = Routes(all_ids.reshape(parts, -1), all_live.reshape(parts, -1), rows_per)
    small = pos_table.shape[0] + vec_table.shape[0]
    spare = -small % 128
    small_low = jnp.concatenate(
        [pos_table.T, vec_table.T, jnp.zeros((pos_table.shape[1], spare), jnp.float32)], 1
    ).astype(narrow)
    low = [
        small_low,
        qkv_weight.astype(narrow),
        square_weight[0].astype(narrow),
        square_weight[1].astype(narrow),
    ]
    deep = small_low.shape[0]
    pieces = [(0, 0, deep), (1, 0, deep // 2), (1, deep // 2, deep // 2), (2, 0, deep), (3, 0, deep)]
    send = routes.table_rows(word_low, 0, routes.room).reshape(parts, -1, width)
    (small_full, qkv_low, out_low, turn_low), arrived = gather_weights(
        low, pieces, sizes, ids[1], send
    )
    word_rows = routes.fetch(word_low, arrived.reshape(-1, width))
    small_full = small_full.T
    pos_low = small_full[:seq_len]
    vec_rows = small_full[seq_len:small].astype(jnp.float32)
    query_low, both_low = qkv_low[:, :width], qkv_low[:, width:]

    second = (places[None, :] >= ((own_lengths + 1) // 2)[:, None]).reshape(-1, 1)
    embedded = (
        word_rows
        + jnp.tile(pos_low.astype(jnp.float32), (own, 1))
        + jnp.where(second, vec_rows[1], vec_rows[0])
    )
    start, norm_zero = norm_forward(embedded, vec_rows[2], vec_rows[3])
    start_low = start.astype(narrow)
    both_bias = jnp.concatenate([jnp.zeros_like(vec_rows[5]), vec_rows[5]])
    both = (matmul(start_low, both_low) + both_bias).astype(narrow)
    pick = one_hot(masked, seq_len, jnp.float32)
    chosen = rows_by_seq(pick, start.reshape(own, seq_len, width)).reshape(-1, width)
    chosen_low = chosen.astype(narrow)
    start_half, chosen_half = both_halves(start_low), both_halves(chosen_low)
    queries = (matmul(chosen_low, query_low) + vec_rows[4]).astype(narrow)
    context = attention(own_lengths, queries, both)
    branch = matmul(context, out_low) + vec_rows[6]
    hidden, norm_one = norm_forward(chosen + branch, vec_rows[7], vec_rows[8])
    hidden = hidden.astype(narrow)

    plane_hidden = gather_rows(hidden, plane_sizes, ids[2], 2)
    up_bias = lax.dynamic_slice_in_dim(vec_rows[15:].reshape(-1), cut * units, units, 0)
    inner = matmul(plane_hidden, up_low) + up_bias
    activ = jax.nn.gelu(inner, approximate=False).astype(narrow)
    branch = sum_rows(matmul(activ, down_low).astype(narrow), plane_sizes, ids[3], 2) + vec_rows[9]
    mixed, norm_two = norm_forward(hidden.astype(jnp.float32) + branch, vec_rows[10], vec_rows[11])
    picked = mixed.astype(narrow)
    turned = matmul(picked, turn_low) + vec_rows[12]
    normed, norm_head = norm_forward(
        jax.nn.gelu(turned, approximate=False), vec_rows[13], vec_rows[14]
    )

    all_normed = gather_rows(normed.astype(narrow), sizes, ids[4], 4)
    column = me * rows_per + jnp.arange(rows_per, dtype=jnp.int32)
    bias_row = jnp.pad(head_bias, (0, parts * rows_per - vocab))
    bias_row = lax.dynamic_slice_in_dim(bias_row, me * rows_per, rows_per, 0)
    logits = right_transposed(all_normed, word_low) + bias_row
    logits = jnp.where(column < vocab, logits, -1e30)
    own_peak = jnp.max(logits, -1)
    own_total = jnp.sum(jnp.exp(logits - own_peak[:, None]), -1)
    hits = all_labels[:, None] == column
    own_label = jnp.sum(jnp.where(hits, logits, 0.0), -1)
    peak, exp_total, label_logit = share_stats(own_peak, own_total, own_label, sizes, ids[5])
    loss_total = jnp.sum(all_valid * (peak + jnp.log(exp_total) - label_logit))
    d_logits = (all_valid / total)[:, None] * (
        jnp.exp(logits - peak[:, None]) / exp_total[:, None] - hits.astype(jnp.float32)
    )
    d_bias = jnp.sum(d_logits, 0)
    d_logits_low = d_logits.astype(narrow)
    d_normed = sum_rows(matmul(d_logits_low, word_low).astype(narrow), sizes, ids[6], 8)

    d_gelu, d_gain_head, d_shift_head = norm_backward(d_normed, norm_head, vec_rows[13])
    d_turned = (d_gelu * gelu_slope(turned)).astype(narrow)
    d_turn_bias = jnp.sum(d_turned.astype(jnp.float32), 0)
    d_turn = chip_sum(picked, d_turned)
    d_picked = right_transposed(d_turned, turn_low)
    same = masked[:, :, None] == masked[:, None, :]
    earlier = slot_index[None, :] < slot_index[:, None]
    first_slot = jnp.logical_not(jnp.any(same & earlier, 2))
    merge = (same & first_slot[:, :, None]).astype(jnp.float32)
    d_mixed = rows_by_seq(merge, d_picked.reshape(own, slots, width)).reshape(-1, width)
    d_pre, d_gain_two, d_shift_two = norm_backward(d_mixed, norm_two, vec_rows[10])
    d_branch = d_pre.astype(narrow)
    d_down_bias = jnp.sum(d_branch.astype(jnp.float32), 0)
    plane_branch = gather_rows(d_branch, plane_sizes, ids[7], 2)
    own_down = line_sum(
        left_transposed(activ, plane_branch).reshape(sizes[2], -1, width), ids[7]
    )
    d_inner = (right_transposed(plane_branch, down_low) * gelu_slope(inner)).astype(narrow)
    d_up_bias = jnp.sum(d_inner.astype(jnp.float32), 0)
    d_up_bias = lax.dynamic_update_slice_in_dim(
        jnp.zeros((planes * units,), jnp.float32), d_up_bias, cut * units, 0
    ).reshape(-1, width)
    d_up = left_transposed(plane_hidden, d_inner).reshape(planes, sizes[2], -1, units)
    up_blocks = line_sum(d_up.swapaxes(0, 1), ids[7]).astype(narrow)
    d_hidden = sum_rows(right_transposed(d_inner, up_low).astype(narrow), plane_sizes, ids[8], 2)
    d_hidden = (d_pre + d_hidden).astype(narrow)

    d_pre, d_gain_one, d_shift_one = norm_backward(
        d_hidden.astype(jnp.float32), norm_one, vec_rows[7]
    )
    d_branch = d_pre.astype(narrow)
    d_out_bias = jnp.sum(d_branch.astype(jnp.float32), 0)
    d_out = chip_sum(context, d_branch)
    d_context = right_transposed(d_branch, out_low).astype(narrow)
    d_query, d_key, d_value = attention(own_lengths, queries, both, d_context)
    d_query_bias = jnp.sum(d_query.astype(jnp.float32), 0)
    d_value_bias = jnp.sum(d_value.astype(jnp.float32), 0)
    d_chosen = d_pre + right_transposed(d_query, query_low)
    d_both = jnp.concatenate([d_key, d_value], 1)
    d_start = right_transposed(d_both, both_low) + rows_to_seq(
        pick, d_chosen.reshape(own, slots, width)
    ).reshape(-1, width)
    d_embedded, d_gain_zero, d_shift_zero = norm_backward(d_start, norm_zero, vec_rows[2])
    d_seg_zero = jnp.sum(jnp.where(second, 0.0, d_embedded), 0)
    d_seg_one = jnp.sum(jnp.where(second, d_embedded, 0.0), 0)
    d_embedded_low = d_embedded.astype(narrow)
    send = routes.token_rows(d_embedded_low, 0, routes.room).reshape(parts, -1, width)
    d_small = jnp.concatenate(
        [
            jnp.sum(d_embedded.reshape(own, seq_len, width), 0),
            jnp.stack(
                [
                    d_seg_zero,
                    d_seg_one,
                    d_gain_zero,
                    d_shift_zero,
                    d_query_bias,
                    d_value_bias,
                    d_out_bias,
                    d_gain_one,
                    d_shift_one,
                    d_down_bias,
                    d_gain_two,
                    d_shift_two,
                    d_turn_bias,
                    d_gain_head,
                    d_shift_head,
                ]
            ),
            d_up_bias,
            jnp.zeros((spare, width), jnp.float32),
        ],
        0,
    )
    (own_out, own_turn, own_small, own_q, own_k, own_v), d_word, arrived, up_blocks = sum_chips(
        [d_out, d_turn, d_small.T.astype(narrow)],
        start_half,
        chosen_half,
        [d_query, d_key, d_value],
        d_logits_low,
        all_normed,
        send,
        up_blocks,
        sizes,
        ids[9],
    )
    own_qkv = jnp.concatenate([own_q, own_k, own_v], 1)
    own_up = up_blocks.swapaxes(0, 1).reshape(up_weight.shape).astype(jnp.float32)
    d_word = routes.give(d_embedded_low, arrived.reshape(-1, width), d_word)
    owned = (
        d_word,
        own_small[:, :seq_len].T,
        own_qkv,
        jnp.stack([own_out, own_turn]),
        own_up,
        own_down,
        own_small[:, seq_len:small].T,
    )
    local_squares = jnp.sum(d_bias * d_bias)
    for grad in owned:
        local_squares = local_squares + jnp.sum(grad * grad)
    spare = -(rows_per + 1) % 128
    last = jnp.concatenate([d_bias, local_squares[None], jnp.zeros((spare,), jnp.float32)])
    last = spread_row(last.reshape(8, -1), sizes, ids[10]).reshape(parts, -1)
    bias_grad = last[:, :rows_per].reshape(-1)[:vocab]
    grad_norm = jnp.sqrt(jnp.sum(last[:, rows_per]))
    factor = clip_norm / jnp.maximum(grad_norm, clip_norm)
    masters = (
        word_table,
        pos_table,
        qkv_weight,
        square_weight,
        up_weight,
        down_weight,
        vec_table,
        head_bias,
    )
    states = (
        (word_first, word_second),
        (pos_first, pos_second),
        (qkv_first, qkv_second),
        (square_first, square_second),
        (up_first, up_second),
        (down_first, down_second),
        (vec_first, vec_second),
        (bias_first, bias_second),
    )
    rates = (
        learn_rate,
        learn_rate,
        learn_rate,
        learn_rate,
        learn_rate,
        learn_rate,
        vector_rate,
        vector_rate,
    )
    grads = tuple(owned) + (bias_grad,)
    results = []
    for weight, state, grad, rate in zip(masters, states, grads, rates):
        results.extend(adam_step(weight, state[0], state[1], grad, factor, rate))
    return (
        results[0],
        results[1],
        results[2],
        results[3],
        results[4],
        results[5],
        results[6],
        results[7],
        results[8],
        results[9],
        results[10],
        results[11],
        results[12],
        results[13],
        results[14],
        results[15],
        results[16],
        results[17],
        results[18],
        results[19],
        results[20],
        results[21],
        results[22],
        results[23],
        loss_total,
        total,
        grad_norm,
    )


def solution(mesh):
    placed = (
        P(("grp", "dp"), None),
        P(("grp", "dp")),
        P(("grp", "dp"), None),
        P(("grp", "dp"), None),
        P(("pipe", "grp", "dp"), None),
        P(("pipe", "grp", "dp"), None),
        P(("pipe", "grp", "dp"), None),
        P(None, ("pipe", "grp", "dp")),
        P(None, ("pipe", "grp", "dp")),
        P(None, ("pipe", "grp", "dp")),
        P(("pipe", "grp", "dp"), None),
        P(("pipe", "grp", "dp"), None),
        P(("pipe", "grp", "dp"), None),
        P(None, ("pipe", "grp", "dp"), None),
        P(None, ("pipe", "grp", "dp"), None),
        P(None, ("pipe", "grp", "dp"), None),
        P(("pipe", "grp", "dp"), None),
        P(("pipe", "grp", "dp"), None),
        P(("pipe", "grp", "dp"), None),
        P(("pipe", "grp", "dp"), None),
        P(("pipe", "grp", "dp"), None),
        P(("pipe", "grp", "dp"), None),
        P(None, ("pipe", "grp", "dp")),
        P(None, ("pipe", "grp", "dp")),
        P(None, ("pipe", "grp", "dp")),
        P(),
        P(),
        P(),
    )
    return jax.shard_map(
        per_device,
        mesh=mesh,
        in_specs=placed,
        out_specs=(
            P(("pipe", "grp", "dp"), None),
            P(("pipe", "grp", "dp"), None),
            P(("pipe", "grp", "dp"), None),
            P(None, ("pipe", "grp", "dp")),
            P(None, ("pipe", "grp", "dp")),
            P(None, ("pipe", "grp", "dp")),
            P(("pipe", "grp", "dp"), None),
            P(("pipe", "grp", "dp"), None),
            P(("pipe", "grp", "dp"), None),
            P(None, ("pipe", "grp", "dp"), None),
            P(None, ("pipe", "grp", "dp"), None),
            P(None, ("pipe", "grp", "dp"), None),
            P(("pipe", "grp", "dp"), None),
            P(("pipe", "grp", "dp"), None),
            P(("pipe", "grp", "dp"), None),
            P(("pipe", "grp", "dp"), None),
            P(("pipe", "grp", "dp"), None),
            P(("pipe", "grp", "dp"), None),
            P(None, ("pipe", "grp", "dp")),
            P(None, ("pipe", "grp", "dp")),
            P(None, ("pipe", "grp", "dp")),
            P(),
            P(),
            P(),
            P(),
            P(),
            P(),
        ),
        check_vma=False,
    )
```

```python
import functools
import math

import jax
import jax.numpy as jnp
from jax import lax
from jax.experimental import pallas as pl
from jax.experimental.pallas import tpu as pltpu
from jax.sharding import PartitionSpec as P

H = 16
STEP = 10


beta_one = 0.9
beta_two = 0.999
learn_rate = 0.02
vector_rate = 0.2
weight_decay = 0.01
epsilon = 1e-08
clip_norm = 0.02
norm_eps = 1e-05
root_half = 0.7071067811865476
density_scale = 0.3989422804014327
AXES = ("pipe", "grp", "dp")
CHIPS = ("grp", "dp")
PLANE = ("pipe", "grp")
highest = lax.Precision.HIGHEST


def matmul(left, right):
    return jnp.dot(left, right, preferred_element_type=jnp.float32)


def left_transposed(left, right):
    return lax.dot_general(
        left, right, (((0,), (0,)), ((), ())), preferred_element_type=jnp.float32
    )


def right_transposed(left, right):
    return lax.dot_general(
        left, right, (((1,), (1,)), ((), ())), preferred_element_type=jnp.float32
    )


def norm_forward(values, gain, shift):
    center = values - jnp.mean(values, -1, keepdims=True)
    scale = lax.rsqrt(jnp.mean(center * center, -1, keepdims=True) + norm_eps)
    normal = center * scale
    return (normal * gain + shift, (normal, scale))


def norm_backward(grad, kept, gain):
    normal, scale = kept
    d_gain = jnp.sum(grad * normal, 0)
    d_shift = jnp.sum(grad, 0)
    d_norm = grad * gain
    d_input = scale * (
        d_norm
        - jnp.mean(d_norm, -1, keepdims=True)
        - normal * jnp.mean(d_norm * normal, -1, keepdims=True)
    )
    return (d_input, d_gain, d_shift)


def gelu_slope(values):
    return (
        0.5 * (1.0 + lax.erf(values * root_half))
        + values * jnp.exp(-0.5 * values * values) * density_scale
    )


def masked_counts(lengths, slots):
    return jnp.minimum(slots, (3 * lengths + 19) // 20)


def one_hot(indices, size, dtype):
    places = lax.broadcasted_iota(jnp.int32, indices.shape + (size,), indices.ndim)
    return (indices[..., None] == places).astype(dtype)


def rows_by_seq(pick, rows):
    return jnp.einsum("sjp,spw->sjw", pick, rows, precision=highest)


def rows_to_seq(pick, rows):
    return jnp.einsum("sjp,sjw->spw", pick, rows, precision=highest)


class Routes:
    def __init__(self, all_ids, all_live, rows_per):
        self.parts, tokens = all_ids.shape
        self.rows_per = rows_per
        self.me = lax.axis_index(AXES)
        mean = tokens / self.parts
        self.room = max(16, int(math.ceil((mean + 2.8 * math.sqrt(mean)) / 16)) * 16)
        owners = jnp.where(all_live, all_ids // rows_per, -1)
        counts = jnp.sum(one_hot(owners, self.parts, jnp.int32), 1)
        self.more = 16
        self.rounds = (jnp.maximum(jnp.max(counts) - self.room, 0) + self.more - 1) // self.more
        mine = owners == self.me
        order = jnp.arange(tokens, dtype=jnp.int32)
        upto = (order[:, None] <= order[None, :]).astype(jnp.bfloat16)
        ranks = matmul(mine.astype(jnp.bfloat16), upto).astype(jnp.int32)
        self.out_rank = jnp.where(mine, ranks - 1, -1)
        self.out_row = all_ids - self.me * rows_per
        own_owners = lax.dynamic_index_in_dim(owners, self.me, 0, keepdims=False)
        hits = one_hot(own_owners, self.parts, jnp.bfloat16)
        ranks = jnp.sum(hits.astype(jnp.float32) * left_transposed(upto, hits), 1)
        ranks = ranks.astype(jnp.int32) - 1
        self.in_rank = ranks
        self.in_owner = own_owners

    def owner_pick(self, first, room):
        slots = first + jnp.arange(room, dtype=jnp.int32)
        at = self.out_rank[:, None, :] == slots[None, :, None]
        row = jnp.sum(jnp.where(at, self.out_row[:, None, :] + 1, 0), 2) - 1
        return one_hot(row.reshape(-1), self.rows_per, jnp.bfloat16)

    def token_pick(self, first, room):
        rank = self.in_rank - first
        inside = (self.in_owner >= 0) & (rank >= 0) & (rank < room)
        slot = jnp.where(inside, self.in_owner * room + rank, -1)
        return one_hot(slot, self.parts * room, jnp.bfloat16)

    def exchange(self, rows):
        shaped = rows.reshape(self.parts, -1, rows.shape[-1])
        return lax.all_to_all(shaped, AXES, 0, 0).reshape(rows.shape)

    def table_rows(self, table, first, room):
        return matmul(self.owner_pick(first, room), table).astype(jnp.bfloat16)

    def token_rows(self, rows, first, room):
        return left_transposed(self.token_pick(first, room), rows).astype(jnp.bfloat16)

    def later(self, more, start):
        def one(turn, kept):
            return kept + more(self.room + turn * self.more)

        return lax.fori_loop(0, self.rounds, one, start)

    def fetch(self, table, arrived):
        def more(first):
            rows = self.exchange(self.table_rows(table, first, self.more))
            return matmul(self.token_pick(first, self.more), rows)

        return self.later(more, matmul(self.token_pick(0, self.room), arrived))

    def give(self, rows, arrived, start):
        def more(first):
            back = self.exchange(self.token_rows(rows, first, self.more))
            return left_transposed(self.owner_pick(first, self.more), back)

        start = start + left_transposed(self.owner_pick(0, self.room), arrived)
        return self.later(more, start)


def swapped(shard):
    return lax.ppermute(shard, "pipe", [(0, 1), (1, 0)])


def both_cores(rows):
    return jnp.concatenate([rows, swapped(rows)], 0)


def half_columns(rows, index):
    half = rows.shape[1] // 2
    return lax.dynamic_slice_in_dim(rows, index * half, half, 1)


def both_halves(rows):
    pipe = lax.axis_index("pipe")
    return jnp.concatenate([half_columns(rows, pipe), swapped(half_columns(rows, 1 - pipe))], 0)


def chip_sum(left, right):
    return left_transposed(both_halves(left), both_cores(right)).astype(jnp.bfloat16)


def chip_half(partial):
    half = partial.shape[0] // 2
    pipe = lax.axis_index("pipe")
    partial = partial.astype(jnp.bfloat16)
    keep = lax.dynamic_slice_in_dim(partial, pipe * half, half, 0)
    give = lax.dynamic_slice_in_dim(partial, (1 - pipe) * half, half, 0)
    return (keep.astype(jnp.float32) + swapped(give).astype(jnp.float32)).astype(jnp.bfloat16)


def device(pipe, grp, dp):
    return {"pipe": pipe, "grp": grp, "dp": dp}


def remote(source, target, send, arrive, to):
    return pltpu.make_async_remote_copy(
        src_ref=source,
        dst_ref=target,
        send_sem=send,
        recv_sem=arrive,
        device_id=device(*to),
        device_id_type=pl.DeviceIdType.MESH,
    )


def tell(barrier, to):
    pl.semaphore_signal(
        barrier, inc=1, device_id=device(*to), device_id_type=pl.DeviceIdType.MESH
    )


def greet(others):
    barrier = pltpu.get_barrier_semaphore()
    for to in others:
        tell(barrier, to)
    pl.semaphore_wait(barrier, len(others))


class Place:
    def __init__(self, sizes):
        self.pipes, self.grps, self.dps = sizes
        self.plane_only = self.dps == 1
        self.pipe, self.grp, self.dp = [lax.axis_index(axis) for axis in AXES]
        column, row = self.grp % 2, self.grp // 2
        self.beside = 2 * row + 1 - column
        self.below = 2 * (1 - row) + column
        self.across = 3 - self.grp

    @property
    def spot(self):
        return 0 if self.plane_only else self.dp

    def plane(self):
        found = []
        for a in range(self.pipes):
            for b in range(self.grps):
                if (a, b) != (0, 0):
                    ahead = ((self.pipe + a) % self.pipes, (self.grp + b) % self.grps)
                    back = (
                        (self.pipe + self.pipes - a) % self.pipes,
                        (self.grp + self.grps - b) % self.grps,
                    )
                    found.append((ahead, back))
        return found

    def line(self, step):
        return (self.dp + step) % self.dps

    def behind(self, step):
        return (self.dp + self.dps - step) % self.dps

    def others(self):
        found = []
        for a in range(self.pipes):
            for b in range(self.grps):
                for c in range(self.dps):
                    if (a, b, c) != (0, 0, 0):
                        ahead = (
                            (self.pipe + a) % self.pipes,
                            (self.grp + b) % self.grps,
                            (self.dp + c) % self.dps,
                        )
                        back = (
                            (self.pipe + self.pipes - a) % self.pipes,
                            (self.grp + self.grps - b) % self.grps,
                            (self.dp + self.dps - c) % self.dps,
                        )
                        found.append((ahead, back))
        return found

    def index(self, pipe, grp, dp):
        return (pipe * self.grps + grp) * self.dps + dp


def swap_all(place, rows, arrived, send, arrive, own):
    me = place.index(place.pipe, place.grp, place.dp)
    copies = []
    for i, (ahead, back) in enumerate(place.others()):
        to = place.index(*ahead)
        copies.append(remote(rows.at[to], arrived.at[me], send.at[i], arrive.at[i], ahead))
        copies[-1].start()
    kept = pltpu.make_async_copy(rows.at[me], arrived.at[me], own)
    kept.start()

    def finish():
        for i, (ahead, back) in enumerate(place.others()):
            origin = place.index(*back)
            copies[i].wait_send()
            remote(rows.at[me], arrived.at[origin], send.at[i], arrive.at[i], ahead).wait_recv()
        kept.wait()

    return finish


def swap_plane(place, rows, arrived, send, arrive, own):
    me = place.pipe * place.grps + place.grp
    copies = []
    for i, (ahead, back) in enumerate(place.plane()):
        to = ahead[0] * place.grps + ahead[1]
        copies.append(
            remote(rows.at[to], arrived.at[me], send.at[i], arrive.at[i], ahead + (place.dp,))
        )
        copies[-1].start()
    kept = pltpu.make_async_copy(rows.at[me], arrived.at[me], own)
    kept.start()

    def finish():
        for i, (ahead, back) in enumerate(place.plane()):
            origin = back[0] * place.grps + back[1]
            copies[i].wait_send()
            remote(
                rows.at[me], arrived.at[origin], send.at[i], arrive.at[i], ahead + (place.dp,)
            ).wait_recv()
        kept.wait()

    return finish


def begin_kernel(sizes, row_ref, up_ref, all_ref, arrived_ref, *sems):
    send, arrive, own, plane_send, plane_arrive, plane_own = sems
    place = Place(sizes)
    others = place.others()
    greet([ahead for ahead, _ in others])
    finish = swap_plane(place, up_ref, arrived_ref, plane_send, plane_arrive, plane_own)
    me = place.index(place.pipe, place.grp, place.dp)
    copies = []
    for i, (ahead, _) in enumerate(others):
        copies.append(remote(row_ref, all_ref.at[me], send.at[i], arrive.at[i], ahead))
        copies[-1].start()
    kept = pltpu.make_async_copy(row_ref, all_ref.at[me], own)
    kept.start()
    for i, (ahead, back) in enumerate(others):
        copies[i].wait_send()
        remote(
            row_ref, all_ref.at[place.index(*back)], send.at[i], arrive.at[i], ahead
        ).wait_recv()
    kept.wait()
    finish()


def begin(row, blocks, sizes, collective):
    parts = math.prod(sizes)
    sems = pltpu.SemaphoreType.DMA((parts - 1,))
    plane_sems = pltpu.SemaphoreType.DMA((sizes[0] * sizes[1] - 1,))
    return pl.pallas_call(
        functools.partial(begin_kernel, sizes),
        out_shape=(
            jax.ShapeDtypeStruct((parts,) + row.shape, row.dtype),
            jax.ShapeDtypeStruct(blocks.shape, blocks.dtype),
        ),
        in_specs=[pl.BlockSpec(memory_space=pltpu.VMEM)] * 2,
        out_specs=[pl.BlockSpec(memory_space=pltpu.VMEM)] * 2,
        scratch_shapes=[
            sems,
            sems,
            pltpu.SemaphoreType.DMA,
            plane_sems,
            plane_sems,
            pltpu.SemaphoreType.DMA,
        ],
        compiler_params=pltpu.CompilerParams(
            collective_id=collective, has_side_effects=True, vmem_limit_bytes=8 << 20
        ),
    )(row, blocks)


def spread_kernel(sizes, row_ref, all_ref, send, arrive, own):
    place = Place(sizes)
    others = place.others()
    greet([ahead for ahead, _ in others])
    me = place.index(place.pipe, place.grp, place.dp)
    copies = []
    for i, (ahead, _) in enumerate(others):
        copies.append(remote(row_ref, all_ref.at[me], send.at[i], arrive.at[i], ahead))
        copies[-1].start()
    kept = pltpu.make_async_copy(row_ref, all_ref.at[me], own)
    kept.start()
    for i, (ahead, back) in enumerate(others):
        copies[i].wait_send()
        remote(
            row_ref, all_ref.at[place.index(*back)], send.at[i], arrive.at[i], ahead
        ).wait_recv()
    kept.wait()


def spread(row, sizes, collective):
    parts = math.prod(sizes)
    sems = pltpu.SemaphoreType.DMA((parts - 1,))
    return pl.pallas_call(
        functools.partial(spread_kernel, sizes),
        out_shape=jax.ShapeDtypeStruct((parts,) + row.shape, row.dtype),
        in_specs=[pl.BlockSpec(memory_space=pltpu.VMEM)],
        out_specs=pl.BlockSpec(memory_space=pltpu.VMEM),
        scratch_shapes=[sems, sems, pltpu.SemaphoreType.DMA],
        compiler_params=pltpu.CompilerParams(
            collective_id=collective, has_side_effects=True, vmem_limit_bytes=8 << 20
        ),
    )(row)


class Gather:
    def __init__(self, place, pieces, shards, fulls, send, arrive, own):
        self.place, self.pieces, self.shards, self.fulls = place, pieces, shards, fulls
        self.send, self.arrive, self.own = send, arrive, own
        pipe, grp, dp = place.pipe, place.grp, place.dp
        self.near = place.beside * (1 - pipe) + place.below * pipe
        self.far = place.below * (1 - pipe) + place.beside * pipe
        self.core = (1 - pipe, grp, dp)
        self.hops = place.dps - 1
        self.ends = (dp < self.hops, dp > 0)
        self.sides = ((pipe, grp, dp + 1), (pipe, grp, dp - 1))
        self.both = range(2 if self.hops else 0)
        self.waits, self.keeps = [], {}
        self.stages = [functools.partial(self.over_line, hop=hop) for hop in range(self.hops)]
        self.stages += [self.over_plane, self.pass_on, self.last]

    def partners(self):
        place = self.place
        pipe, grp, dp = place.pipe, place.grp, place.dp
        line = [(pipe, grp, place.line(k + 1)) for k in range(self.hops)]
        return line + [(pipe, self.near, dp), (pipe, self.far, dp), self.core]

    def view(self, n, *at):
        array, first, rows = self.pieces[n]
        return self.fulls[array].at[at + ((slice(None),) * (3 - len(at))) + (pl.ds(first, rows),)]

    def shard(self, n):
        array, first, rows = self.pieces[n]
        return self.shards[array].at[pl.ds(first, rows)]

    def launch(self, n, index, source, to, *at):
        copy = remote(
            source, self.view(n, *at), self.send.at[n, index], self.arrive.at[n, index], to
        )
        copy.start()
        self.waits.append(copy)

    def landed(self, n, index, *at):
        target = self.view(n, *at)
        remote(
            target, target, self.send.at[n, index], self.arrive.at[n, index], self.core
        ).wait_recv()

    def along(self, n, side, hop, finish=False):
        place, hops = self.place, self.hops
        origin = place.dp - hop if side == 0 else place.dp + hop
        here = origin >= 0 if side == 0 else origin <= hops
        index = side * hops + hop

        def copy():
            target = self.view(n, place.pipe, place.grp, origin)
            source = self.shard(n) if hop == 0 else target
            return remote(
                source, target, self.send.at[n, index], self.arrive.at[n, index], self.sides[side]
            )

        if finish:

            @pl.when(here & self.ends[side])
            def _():
                copy().wait_send()

            return
        if hop > 0:

            @pl.when(here)
            def _():
                self.landed(n, index - 1, place.pipe, place.grp, origin)

        if hop < hops:

            @pl.when(here & self.ends[side])
            def _():
                copy().start()

    def over_line(self, n, hop):
        place = self.place
        if hop == 0:
            target = self.view(n, place.pipe, place.grp, place.spot)
            self.keeps[n] = pltpu.make_async_copy(self.shard(n), target, self.own.at[n])
            self.keeps[n].start()
        for side in self.both:
            self.along(n, side, hop)

    def over_plane(self, n):
        place, first = self.place, 2 * self.hops
        pipe, grp, dp = place.pipe, place.grp, place.dp
        self.over_line(n, self.hops)
        if self.hops:
            self.keeps[n].wait()
            group, at = self.view(n, pipe, grp), (pipe, grp)
        else:
            group, at = self.shard(n), (pipe, grp, 0)
        self.launch(n, first, group, (pipe, self.near, dp), *at)
        self.launch(n, first + 1, group, (pipe, self.far, dp), *at)
        self.launch(n, first + 3, group, self.core, *at)

    def pass_on(self, n):
        pipe, first = self.place.pipe, 2 * self.hops
        self.landed(n, first, pipe, self.near)
        group = self.view(n, pipe, self.near)
        self.launch(n, first + 2, group, (pipe, self.far, self.place.dp), pipe, self.near)
        self.launch(n, first + 4, group, self.core, pipe, self.near)
        self.landed(n, first + 1, pipe, self.far)
        self.launch(n, first + 5, self.view(n, pipe, self.far), self.core, pipe, self.far)

    def last(self, n):
        pipe, first, across = self.place.pipe, 2 * self.hops, self.place.across
        self.landed(n, first + 2, pipe, across)
        self.launch(n, first + 6, self.view(n, pipe, across), self.core, pipe, across)

    def core_order(self):
        return (
            (),
            ((3, self.place.grp),),
            ((4, self.far), (5, self.near)),
            ((6, self.place.across),),
        )

    def from_core(self, n):
        for step in self.core_order():
            for index, grp in step:
                self.landed(n, 2 * self.hops + index, 1 - self.place.pipe, grp)

    def settle(self):
        for n in range(len(self.pieces)):
            for side in self.both:
                for hop in range(self.hops):
                    self.along(n, side, hop, finish=True)
        for copy in self.waits:
            copy.wait_send()
        if not self.hops:
            for keep in self.keeps.values():
                keep.wait()


def run_stages(stages, total, after=None):
    for turn in range(total + len(stages) - 1):
        for at, stage in enumerate(stages):
            if 0 <= turn - at < total:
                stage(turn - at)
        if after is not None:
            after(turn)


def gather_kernel(sizes, pieces, routed, *refs):
    count = max(piece[0] for piece in pieces) + 1
    shards, refs = refs[:count], refs[count:]
    if routed:
        rows_ref, refs = refs[0], refs[1:]
    fulls, refs = refs[:count], refs[count:]
    if routed:
        arrived_ref, refs = refs[0], refs[1:]
    send, arrive, own, swap_send, swap_arrive, swap_own = refs
    place = Place(sizes)
    gather = Gather(place, pieces, shards, fulls, send, arrive, own)
    greet([ahead for ahead, _ in place.others()] if routed else gather.partners())
    swaps = []

    def after(turn):
        if turn == len(pieces) and routed:
            swaps.append(
                swap_all(place, rows_ref, arrived_ref, swap_send, swap_arrive, swap_own)
            )

    run_stages(gather.stages, len(pieces), after)
    for n in range(len(pieces)):
        gather.from_core(n)
    gather.settle()
    for finish in swaps:
        finish()


def gather_all(shards, pieces, sizes, collective, rows=None):
    parts = math.prod(sizes)
    routed = rows is not None
    kinds = 2 * (sizes[2] - 1) + 7
    space = pltpu.VMEM if sizes[2] == 1 else pl.ANY
    out_shape = [jax.ShapeDtypeStruct(sizes + shard.shape, shard.dtype) for shard in shards]
    if routed:
        out_shape.append(jax.ShapeDtypeStruct(rows.shape, rows.dtype))
    operands = list(shards) + ([rows] if routed else [])
    sems = pltpu.SemaphoreType.DMA((len(pieces), kinds))
    swaps = pltpu.SemaphoreType.DMA((parts - 1 if routed else 1,))
    return pl.pallas_call(
        functools.partial(gather_kernel, sizes, tuple(pieces), routed),
        out_shape=out_shape,
        in_specs=[pl.BlockSpec(memory_space=space)] * len(operands),
        out_specs=[pl.BlockSpec(memory_space=space)] * len(out_shape),
        scratch_shapes=[
            sems,
            sems,
            pltpu.SemaphoreType.DMA((len(pieces),)),
            swaps,
            swaps,
            pltpu.SemaphoreType.DMA,
        ],
        compiler_params=pltpu.CompilerParams(
            collective_id=collective, has_side_effects=True, vmem_limit_bytes=16 << 20
        ),
    )(*operands)


class Sums:
    block = 16
    filled = False

    def __init__(self, place, sources, chips, others, mine, planes, lines, send, arrive, own, store):
        self.place, self.sources, self.chips, self.others = place, sources, chips, others
        self.mine, self.planes, self.lines = mine, planes, lines
        self.send, self.arrive, self.own, self.store = send, arrive, own, store
        pipe, grp, dp = place.pipe, place.grp, place.dp
        self.near = place.beside * (1 - pipe) + place.below * pipe
        self.far = place.below * (1 - pipe) + place.beside * pipe
        self.copies, self.kept = {}, {}

    def launch(self, n, index, source, target, to):
        copy = remote(source, target, self.send.at[n, index], self.arrive.at[n, index], to)
        self.copies[n, index] = copy
        copy.start()

    def keep(self, n, index, source, target):
        self.kept[n, index] = pltpu.make_async_copy(source, target, self.own.at[n, index])
        self.kept[n, index].start()

    def blocks(self, n, body):
        deep = self.mine[n].shape[2] // self.block

        def one(i, _):
            body(i // deep, pl.ds(pl.multiple_of(i % deep * self.block, self.block), self.block))
            return 0

        lax.fori_loop(0, self.place.dps * deep, one, 0)

    def to_core(self, n):
        place = self.place
        core = (1 - place.pipe, place.grp, place.dp)
        if self.filled:
            self.launch(n, 0, self.sources[n], self.others[n], core)
        elif self.chips[n] is not None:
            self.launch(n, 0, self.sources[n].at[1 - place.pipe], self.others[n], core)
            self.keep(n, 0, self.sources[n].at[place.pipe], self.chips[n])

    def to_near(self, n):
        place, chip, other = self.place, self.chips[n], self.others[n]
        part = self.sources[n]
        if chip is not None:
            if not self.filled:
                self.kept[n, 0].wait()
            self.copies[n, 0].wait_recv()
            for g in range(place.grps):

                def add(d, at, g=g):
                    left = chip[g, d, at].astype(jnp.float32)
                    chip[g, d, at] = (left + other[g, d, at].astype(jnp.float32)).astype(
                        jnp.bfloat16
                    )

                self.blocks(n, add)
            part = chip
        else:
            for j, g in enumerate((self.far, place.grp)):
                self.keep(n, j, part.at[g], self.mine[n].at[j])
        to = (place.pipe, self.near, place.dp)
        self.launch(n, 1, part.at[self.near], self.planes[n].at[1], to)
        self.launch(n, 2, part.at[place.across], self.planes[n].at[0], to)

    def to_far(self, n):
        place, mine, plane, chip = self.place, self.mine[n], self.planes[n], self.chips[n]
        if chip is None:
            self.kept[n, 0].wait()
            self.kept[n, 1].wait()
        self.copies[n, 1].wait_recv()
        self.copies[n, 2].wait_recv()
        for j, g in enumerate((self.far, place.grp)):

            def add(d, at, j=j, g=g):
                left = mine[j, d, at] if chip is None else chip[g, d, at]
                total = left.astype(jnp.float32) + plane[j, d, at].astype(jnp.float32)
                mine[j, d, at] = total.astype(jnp.bfloat16)

            self.blocks(n, add)
            if j == 0:
                self.launch(n, 3, mine.at[0], plane.at[2], (place.pipe, self.far, place.dp))

    def to_lines(self, n):
        place, mine, plane = self.place, self.mine[n], self.planes[n]
        self.copies[n, 3].wait_recv()
        hops = place.dps - 1

        def add(d, at):
            total = mine[1, d, at].astype(jnp.float32) + plane[2, d, at].astype(jnp.float32)
            if hops:
                mine[1, d, at] = total.astype(jnp.bfloat16)
            else:
                self.store(n, at, total)

        self.blocks(n, add)
        for k in range(hops):
            to = place.line(k + 1)
            self.launch(
                n, 4 + k, mine.at[1, to], self.lines[n].at[k], (place.pipe, place.grp, to)
            )

    def to_sum(self, n):
        place, mine, lines = self.place, self.mine[n], self.lines[n]
        for k in range(place.dps - 1):
            self.copies[n, 4 + k].wait_recv()

        def add(i, _):
            at = pl.ds(pl.multiple_of(i * self.block, self.block), self.block)
            total = mine[1, place.spot, at].astype(jnp.float32)
            for k in range(place.dps - 1):
                total = total + lines[k, at].astype(jnp.float32)
            self.store(n, at, total)
            return 0

        lax.fori_loop(0, mine.shape[2] // self.block, add, 0)

    def settle(self):
        for copy in self.copies.values():
            copy.wait_send()


def sum_scratch(shapes, cores, sizes):
    low = jnp.bfloat16
    _, grps, dps = sizes
    wide = [(dps,) + shape for shape in shapes]
    chips = [pltpu.VMEM((grps,) + shape, low) for shape, core in zip(wide, cores) if core]
    scratch = chips + chips
    scratch += [pltpu.VMEM((2,) + shape, low) for shape in wide]
    scratch += [pltpu.VMEM((3,) + shape, low) for shape in wide]
    scratch += [pltpu.VMEM((max(dps - 1, 1),) + shape, low) for shape in shapes]
    sems = pltpu.SemaphoreType.DMA((len(shapes), 4 + dps - 1))
    return scratch + [sems, sems, pltpu.SemaphoreType.DMA((len(shapes), 2))]


def sum_refs(refs, cores):
    total = len(cores)

    def spread_out(found):
        found = iter(found)
        return [next(found) if core else None for core in cores]

    chosen = sum(cores)
    groups = []
    for count in (chosen, chosen, total, total, total):
        groups.append(refs[:count])
        refs = refs[count:]
    chips, others, mine, planes, lines = groups
    return (spread_out(chips), spread_out(others), mine, planes, lines) + tuple(refs[:3]), refs[3:]


def reduce_kernel(sizes, pieces, *refs):
    partial, out, refs = refs[0], refs[1], refs[2:]
    place = Place(sizes)
    scratch, _ = sum_refs(refs, (True,) * len(pieces))

    def store(n, at, total):
        to = pl.multiple_of(pieces[n][0] + at.start, Sums.block)
        out[pl.ds(to, Sums.block)] = total

    sources = [partial.at[:, :, :, pl.ds(first, rows)] for first, rows in pieces]
    sums = Sums(place, sources, *scratch, store)
    line = [(place.pipe, place.grp, place.line(k + 1)) for k in range(place.dps - 1)]
    near, far = [(place.pipe, grp, place.dp) for grp in (sums.near, sums.far)]
    greet(line + [near, far, (1 - place.pipe, place.grp, place.dp)])
    stages = [sums.to_core, sums.to_near, sums.to_far, sums.to_lines]
    stages += [sums.to_sum] if place.dps > 1 else []
    run_stages(stages, len(pieces))
    sums.settle()


def reduce_all(partial, pieces, sizes, collective):
    shapes = [(rows, partial.shape[-1]) for _, rows in pieces]
    return pl.pallas_call(
        functools.partial(reduce_kernel, sizes, tuple(pieces)),
        out_shape=jax.ShapeDtypeStruct(partial.shape[-2:], jnp.float32),
        in_specs=[pl.BlockSpec(memory_space=pl.ANY)],
        out_specs=pl.BlockSpec(memory_space=pltpu.VMEM),
        scratch_shapes=sum_scratch(shapes, (True,) * len(pieces), sizes),
        compiler_params=pltpu.CompilerParams(
            collective_id=collective, has_side_effects=True, vmem_limit_bytes=48 << 20
        ),
    )(partial)


def finish_kernel(sizes, *refs):
    partials, refs = refs[:3], refs[3:]
    start_ref, chosen_ref, grads, refs = refs[0], refs[1], refs[2:5], refs[5:]
    rows_ref, blocks_ref, refs = refs[0], refs[1], refs[2:]
    outs, refs = refs[:6], refs[6:]
    arrived_ref, blocks_arrived_ref, refs = refs[0], refs[1], refs[2:]
    cores = (False, False, True, False, False, False)
    scratch, refs = sum_refs(refs, cores)
    start, chosen, held, made, refs = refs[0], refs[1], refs[2:5], refs[5:8], refs[8:]
    swap_send, swap_arrive, swap_own, plane_send, plane_arrive, plane_own = refs[:6]
    load, core_send, core_arrive = refs[6:]
    place = Place(sizes)
    pipe, grp, dp = place.pipe, place.grp, place.dp
    greet([ahead for ahead, _ in place.others()])

    exchanged = []
    for i in range(3):
        pltpu.make_async_copy(grads[i], held[i].at[0], load.at[2 + i]).start()
        exchanged.append(
            remote(grads[i], held[i].at[1], core_send.at[i], core_arrive.at[i], (1 - pipe, grp, dp))
        )
        exchanged[-1].start()
    pltpu.make_async_copy(start_ref, start, load.at[0]).start()
    pltpu.make_async_copy(chosen_ref, chosen, load.at[1]).start()

    def store(n, at, total):
        outs[n][at] = total

    sums = Sums(place, tuple(partials) + tuple(made), *scratch, store)
    sums.to_core(2)
    sums.to_near(0)
    sums.to_near(1)
    swap = swap_all(place, rows_ref, arrived_ref, swap_send, swap_arrive, swap_own)
    plane_swap = swap_plane(
        place, blocks_ref, blocks_arrived_ref, plane_send, plane_arrive, plane_own
    )
    sums.to_near(2)

    def form(i):
        pltpu.make_async_copy(grads[i], held[i].at[0], load.at[2 + i]).wait()
        exchanged[i].wait_recv()
        if i == 0:
            pltpu.make_async_copy(chosen_ref, chosen, load.at[1]).wait()
        if i == 1:
            pltpu.make_async_copy(start_ref, start, load.at[0]).wait()
        left = chosen if i == 0 else start
        right = held[i]
        wide = left.shape[1] // place.grps
        tokens = right.shape[1]

        for g in range(place.grps):
            at = pl.ds(g * wide, wide)
            total = left_transposed(left[0:tokens, at], right[0])
            total = total + left_transposed(left[tokens:, at], right[1])
            made[i][g] = total.astype(jnp.bfloat16).reshape(made[i].shape[1:])

    form(0)
    sums.to_near(3)
    sums.to_far(0)
    form(1)
    sums.to_near(4)
    sums.to_far(1)
    form(2)
    sums.to_near(5)
    sums.to_far(2)
    sums.to_lines(0)
    sums.to_lines(1)
    sums.to_far(3)
    sums.to_lines(2)
    sums.to_far(4)
    sums.to_lines(3)
    sums.to_far(5)
    sums.to_lines(4)
    sums.to_lines(5)
    for n in range(6):
        sums.to_sum(n)
    sums.settle()
    for copy in exchanged:
        copy.wait_send()
    plane_swap()
    swap()


def finish_all(partials, start, chosen, grads, rows, blocks, sizes, collective):
    low = jnp.bfloat16
    parts = math.prod(sizes)
    _, grps, dps = sizes
    shapes = [(partial.shape[-2], partial.shape[-1]) for partial in partials]
    made = (grps, dps) + shapes[0]
    shapes += [shapes[0]] * 3
    anywhere = pl.BlockSpec(memory_space=pl.ANY)
    near = pl.BlockSpec(memory_space=pltpu.VMEM)
    swaps = pltpu.SemaphoreType.DMA((parts - 1,))
    plane_swaps = pltpu.SemaphoreType.DMA((sizes[0] * grps - 1,))
    one = pltpu.SemaphoreType.DMA
    operands = (*partials, start, chosen, *grads, rows, blocks)
    out_shape = [jax.ShapeDtypeStruct(shape, jnp.float32) for shape in shapes]
    out_shape += [jax.ShapeDtypeStruct(extra.shape, extra.dtype) for extra in (rows, blocks)]
    return pl.pallas_call(
        functools.partial(finish_kernel, sizes),
        out_shape=out_shape,
        in_specs=[anywhere] * len(operands),
        out_specs=[near] * 6 + [anywhere] * 2,
        scratch_shapes=sum_scratch(shapes, (False, False, True, False, False, False), sizes)
        + [pltpu.VMEM(start.shape, low), pltpu.VMEM(chosen.shape, low)]
        + [pltpu.VMEM((2,) + grad.shape, low) for grad in grads]
        + [pltpu.VMEM(made, low)] * 3
        + [
            swaps,
            swaps,
            one,
            plane_swaps,
            plane_swaps,
            one,
            pltpu.SemaphoreType.DMA((5,)),
            pltpu.SemaphoreType.DMA((3,)),
            pltpu.SemaphoreType.DMA((3,)),
        ],
        compiler_params=pltpu.CompilerParams(
            collective_id=collective, has_side_effects=True, vmem_limit_bytes=56 << 20
        ),
    )(*operands)


def head_kernel(sizes, rows_per, vocab, gather_cuts, sum_cuts, *refs):
    row_ref, table, bias, info, out, word, bias_out, stats, refs = *refs[:8], refs[8:]
    full, logits, columns, laid, held, result, slopes, outgoing, refs = *refs[:8], refs[8:]
    cores = (True,) * sum_cuts
    scratch, refs = sum_refs(refs, cores)
    gather_send, gather_arrive, gather_own, swap_send, swap_arrive, swap_own = refs[:6]
    all_send, all_arrive = refs[6:]
    place = Place(sizes)
    pipes, grps, dps = sizes
    others = place.others()
    slots, width = row_ref.shape
    tall = slots // gather_cuts
    pieces = [(0, i * tall, tall) for i in range(gather_cuts)]
    gather = Gather(place, pieces, [row_ref], [full], gather_send, gather_arrive, gather_own)
    greet([ahead for ahead, _ in others])
    pipe, grp, hops = place.pipe, place.grp, dps - 1
    me = place.index(pipe, grp, place.dp)
    cells = table.shape[0]
    local = lax.broadcasted_iota(jnp.int32, (1, cells), 1)
    column = me * rows_per + local
    used = (local < rows_per) & (column < vocab)
    column = jnp.where(used, column, -1).astype(jnp.float32)
    groups = pipes * grps

    def parts(body):
        lax.fori_loop(0, pipes * grps * dps, lambda i, _: (body(i), 0)[1], 0, unroll=8)

    def spot(i):
        return i // (grps * dps), i // dps % grps, i % dps

    def fill(i):
        columns[spot(i) + (slice(None), slice(0, 8))] = info[i].T

    def form_logits(n, p, g):
        _, first, rows = pieces[n]
        at = pl.ds(first, rows)
        found = right_transposed(full[p, g, :, at].reshape(dps * rows, width), table[...])
        found = jnp.where(used, found + bias[...], -1e30)
        peak = jnp.max(found, -1, keepdims=True)
        total = jnp.sum(jnp.exp(found - peak), -1, keepdims=True)
        labels = columns[p, g, :, at, 0:1].reshape(dps * rows, 1)
        label = jnp.sum(jnp.where(column == labels, found, 0.0), -1, keepdims=True)
        logits[p, g, :, at] = found.reshape(dps, rows, cells)
        columns[p, g, :, at, 2:3] = peak.reshape(dps, rows, 1)
        columns[p, g, :, at, 3:4] = total.reshape(dps, rows, 1)
        columns[p, g, :, at, 4:5] = label.reshape(dps, rows, 1)

    def after(turn):
        if turn == 0:
            parts(fill)
        arrived = (
            ((pipe, grp),),
            ((pipe, gather.near), (pipe, gather.far)),
            ((pipe, place.across),),
            (),
        )
        for step in range(4):
            n = turn - hops - step
            if 0 <= n < gather_cuts:
                for p, g in arrived[step]:
                    form_logits(n, p, g)
                for index, g in gather.core_order()[step]:
                    gather.landed(n, 2 * hops + index, 1 - pipe, g)
                    form_logits(n, 1 - pipe, g)

    run_stages(gather.stages, gather_cuts, after)
    after(gather_cuts + hops + 2)

    def lay(i):
        laid[i] = columns[spot(i) + (slice(None), slice(0, 8))].T

    parts(lay)
    swap_all(place, laid, held, swap_send, swap_arrive, swap_own)()
    peaks = held[:, 2]
    peak = jnp.max(peaks, 0, keepdims=True)
    result[...] = jnp.zeros_like(result)
    result[0:1] = peak
    result[1:2] = jnp.sum(held[:, 3] * jnp.exp(peaks - peak), 0, keepdims=True)
    result[2:3] = jnp.sum(held[:, 4], 0, keepdims=True)
    copies = []
    for i, (ahead, _) in enumerate(others):
        copies.append(remote(result, stats.at[me], all_send.at[i], all_arrive.at[i], ahead))
        copies[-1].start()
    stats[me] = result[...]
    for i, (ahead, back) in enumerate(others):
        copies[i].wait_send()
        origin = place.index(*back)
        remote(
            result, stats.at[origin], all_send.at[i], all_arrive.at[i], ahead
        ).wait_recv()

    def back(i):
        columns[spot(i) + (slice(None), slice(8, 16))] = stats[i].T

    parts(back)

    size = slots // sum_cuts
    half = grps * dps * size

    def store(n, at, total):
        to = pl.multiple_of(n * size + at.start, Sums.block)
        out[pl.ds(to, Sums.block)] = total

    sums = Sums(place, [outgoing.at[n] for n in range(sum_cuts)], *scratch, store)
    sums.filled = True
    bias_out[...] = jnp.zeros_like(bias_out)
    word[...] = jnp.zeros_like(word)

    def form_slopes(n):
        at = pl.ds(n * size, size)

        def one(i, _):
            p, g = i // grps, i % grps
            kept = columns[p, g, :, at].reshape(dps * size, columns.shape[-1])
            found = logits[p, g, :, at].reshape(dps * size, cells)
            hits = (column == kept[:, 0:1]).astype(jnp.float32)
            slope = kept[:, 1:2] * (jnp.exp(found - kept[:, 8:9]) / kept[:, 9:10] - hits)
            bias_out[0:1] += jnp.sum(slope, 0, keepdims=True)
            slopes[n % 2, i] = slope.astype(jnp.bfloat16)
            return 0

        lax.fori_loop(0, groups, one, 0)
        for q, target in ((1 - place.pipe, outgoing.at[n]), (place.pipe, sums.chips[n])):
            left = slopes[n % 2, pl.ds(q * grps, grps)].reshape(half, cells)
            target[...] = matmul(left, table[...]).astype(jnp.bfloat16).reshape(target.shape)
        sums.to_core(n)

    def form_word(n):
        right = full[:, :, :, pl.ds(n * size, size)].reshape(pipes * half, width)
        word[...] += left_transposed(slopes[n % 2].reshape(pipes * half, cells), right)

    stages = [form_slopes, sums.to_near, sums.to_far, sums.to_lines, sums.to_sum]

    def then(turn):
        if turn < sum_cuts:
            form_word(turn)

    run_stages(stages, sum_cuts, then)
    sums.settle()
    gather.settle()


def head_all(row, table, bias, info, rows_per, vocab, sizes, collective):
    low = jnp.bfloat16
    parts = math.prod(sizes)
    pipes, grps, dps = sizes
    slots, width = row.shape
    cells = table.shape[0]
    gather_cuts, sum_cuts = 4, 8
    size = slots // sum_cuts
    near = pl.BlockSpec(memory_space=pltpu.VMEM)
    gathers = pltpu.SemaphoreType.DMA((gather_cuts, 2 * (dps - 1) + 7))
    swaps = pltpu.SemaphoreType.DMA((parts - 1,))
    return pl.pallas_call(
        functools.partial(head_kernel, sizes, rows_per, vocab, gather_cuts, sum_cuts),
        out_shape=(
            jax.ShapeDtypeStruct(row.shape, jnp.float32),
            jax.ShapeDtypeStruct(table.shape, jnp.float32),
            jax.ShapeDtypeStruct((8, cells), jnp.float32),
            jax.ShapeDtypeStruct(info.shape, jnp.float32),
        ),
        in_specs=[near] * 4,
        out_specs=[near] * 4,
        scratch_shapes=[
            pltpu.VMEM(sizes + row.shape, low),
            pltpu.VMEM(sizes + (slots, cells), jnp.float32),
            pltpu.VMEM(sizes + (slots, 16), jnp.float32),
            pltpu.VMEM(info.shape, jnp.float32),
            pltpu.VMEM(info.shape, jnp.float32),
            pltpu.VMEM(info.shape[1:], jnp.float32),
            pltpu.VMEM((2, pipes * grps, dps * size, cells), low),
            pltpu.VMEM((sum_cuts, grps, dps, size, width), low),
        ]
        + sum_scratch([(size, width)] * sum_cuts, (True,) * sum_cuts, sizes)
        + [
            gathers,
            gathers,
            pltpu.SemaphoreType.DMA((gather_cuts,)),
            swaps,
            swaps,
            pltpu.SemaphoreType.DMA,
            swaps,
            swaps,
        ],
        compiler_params=pltpu.CompilerParams(
            collective_id=collective, has_side_effects=True, vmem_limit_bytes=62 << 20
        ),
    )(row, table, bias, info)


def pair_rows(pair, first):
    pair = pair.astype(jnp.float32)
    low = jnp.bfloat16
    return jnp.concatenate(
        [jnp.where(first, pair, 0.0).astype(low), jnp.where(first, 0.0, pair).astype(low)], 0
    )


def pair_probs(rows, keys, live, scale):
    scores = jnp.where(live, right_transposed(rows, keys) * scale, -1e30)
    exp_scores = jnp.exp(scores - jnp.max(scores, -1, keepdims=True))
    return exp_scores / jnp.sum(exp_scores, -1, keepdims=True)


def attention_masks(lengths_ref, slots, seq_len, lanes):
    live = lax.broadcasted_iota(jnp.int32, (1, seq_len), 1) < lengths_ref[pl.program_id(0)]
    first = lax.broadcasted_iota(jnp.int32, (slots, lanes), 1) < lanes // 2
    return live, first


def attention_kernel(scale, lanes, lengths_ref, q_ref, k_ref, v_ref, out_ref):
    slots = q_ref.shape[0]
    live, first = attention_masks(lengths_ref, slots, k_ref.shape[0], lanes)
    for pair in range(q_ref.shape[1] // lanes):
        at = slice(pair * lanes, (pair + 1) * lanes)
        probs = pair_probs(pair_rows(q_ref[:, at], first), k_ref[:, at], live, scale)
        context = matmul(probs.astype(jnp.bfloat16), v_ref[:, at])
        out_ref[:, at] = jnp.where(first, context[:slots], context[slots:]).astype(jnp.bfloat16)


def attention_back_kernel(
    scale, lanes, lengths_ref, q_ref, k_ref, v_ref, grad_ref, dq_ref, dk_ref, dv_ref
):
    slots = q_ref.shape[0]
    low = jnp.bfloat16
    live, first = attention_masks(lengths_ref, slots, k_ref.shape[0], lanes)
    for pair in range(q_ref.shape[1] // lanes):
        at = slice(pair * lanes, (pair + 1) * lanes)
        rows, grads = pair_rows(q_ref[:, at], first), pair_rows(grad_ref[:, at], first)
        probs = pair_probs(rows, k_ref[:, at], live, scale)
        dv_ref[:, at] = left_transposed(probs.astype(low), grads).astype(low)
        d_probs = right_transposed(grads, v_ref[:, at])
        d_scores = probs * (d_probs - jnp.sum(probs * d_probs, -1, keepdims=True))
        d_scores = d_scores.astype(low)
        d_query = matmul(d_scores, k_ref[:, at]) * scale
        dq_ref[:, at] = jnp.where(first, d_query[:slots], d_query[slots:]).astype(low)
        dk_ref[:, at] = (left_transposed(d_scores, rows) * scale).astype(low)


def attention(lengths, queries, both, grads=None):
    own = lengths.shape[0]
    width = queries.shape[1]
    slots, seq_len = queries.shape[0] // own, both.shape[0] // own
    lanes = 2 * width // H
    scale = (width // H) ** (-0.5)
    cuts = 2
    part = width // cuts
    row = pl.BlockSpec((slots, part), lambda s, h: (s, h))
    keys = pl.BlockSpec((seq_len, part), lambda s, h: (s, h))
    values = pl.BlockSpec((seq_len, part), lambda s, h: (s, cuts + h))
    in_specs = [pl.BlockSpec(memory_space=pltpu.SMEM), row, keys, values]
    flat = jax.ShapeDtypeStruct(queries.shape, jnp.bfloat16)
    tall = jax.ShapeDtypeStruct((both.shape[0], width), jnp.bfloat16)
    if grads is None:
        return pl.pallas_call(
            functools.partial(attention_kernel, scale, lanes),
            grid=(own, cuts),
            out_shape=flat,
            in_specs=in_specs,
            out_specs=row,
        )(lengths, queries, both, both)
    return pl.pallas_call(
        functools.partial(attention_back_kernel, scale, lanes),
        grid=(own, cuts),
        out_shape=(flat, tall, tall),
        in_specs=in_specs + [row],
        out_specs=(row, keys, keys),
    )(lengths, queries, both, both, grads)


def even_pieces(array, rows, cuts):
    size = rows // cuts
    return [(array, i * size, size) for i in range(cuts)]


def start_all(row, blocks, sizes, collective):
    if collective is None:
        return lax.all_gather(row, AXES, axis=0), lax.all_to_all(blocks, PLANE, 0, 0)
    return begin(row, blocks, sizes, collective)


def gather_weights(shards, pieces, sizes, collective, rows):
    if collective is None:
        fulls = [lax.all_gather(shard, AXES, axis=0) for shard in shards]
        arrived = lax.all_to_all(rows, AXES, 0, 0)
    else:
        *fulls, arrived = gather_all(shards, pieces, sizes, collective, rows)
    return [full.reshape(-1, full.shape[-1]) for full in fulls], arrived


def gather_rows(shard, sizes, collective, cuts):
    if collective is None:
        axes = AXES if sizes[2] > 1 else PLANE
        return lax.all_gather(shard, axes, axis=0, tiled=True)
    (full,) = gather_all([shard], even_pieces(0, shard.shape[0], cuts), sizes, collective)
    return full.reshape(-1, full.shape[-1])


def sum_rows(partial, sizes, collective, cuts):
    if collective is None:
        axes = AXES if sizes[2] > 1 else PLANE
        total = lax.psum_scatter(partial, axes, scatter_dimension=0, tiled=True)
        return total.astype(jnp.float32)
    shaped = partial.reshape(sizes + (-1, partial.shape[1]))
    size = shaped.shape[3] // cuts
    return reduce_all(shaped, [(i * size, size) for i in range(cuts)], sizes, collective)


def sum_chips(partials, start, chosen, grads, rows, blocks, sizes, collective):
    if collective is not None:
        cores = len(partials) - 1
        shaped = [
            p.reshape(sizes[1 if i < cores else 0 :] + (-1, p.shape[1]))
            for i, p in enumerate(partials)
        ]
        *sums, rows, blocks = finish_all(
            shaped, start, chosen, grads, rows, blocks, sizes, collective
        )
        return sums, rows, blocks
    made = [
        left_transposed(left, both_cores(right)).astype(jnp.bfloat16)
        for left, right in zip((chosen, start, start), grads)
    ]
    partials = list(partials[:-1]) + [chip_half(partials[-1])] + made
    sums = [
        lax.psum_scatter(p, CHIPS, scatter_dimension=0, tiled=True).astype(jnp.float32)
        for p in partials
    ]
    rows = lax.all_to_all(rows, AXES, 0, 0)
    blocks = lax.all_to_all(blocks, PLANE, 0, 0)
    return sums, rows, blocks


def line_shift(shard, step):
    size = lax.axis_size("dp")
    return lax.ppermute(shard, "dp", [(i, (i + step) % size) for i in range(size)])


def line_gather(shard, collective):
    if collective is None:
        return lax.all_gather(shard, "dp", axis=0)
    size = lax.axis_size("dp")
    me = lax.axis_index("dp")
    kept = jnp.stack([shard] + [line_shift(shard, step) for step in range(1, size)])
    order = [(me + size - i) % size for i in range(size)]
    return jnp.concatenate([lax.dynamic_slice_in_dim(kept, at, 1, 0) for at in order], 0)


def line_sum(partial, collective):
    partial = partial.astype(jnp.bfloat16)
    if collective is None:
        total = lax.psum_scatter(partial, "dp", scatter_dimension=0, tiled=False)
        return total.astype(jnp.float32)
    size = lax.axis_size("dp")
    me = lax.axis_index("dp")

    def entry(step):
        return lax.dynamic_index_in_dim(partial, (me + step) % size, 0, keepdims=False)

    total = entry(0).astype(jnp.float32)
    for step in range(1, size):
        total = total + line_shift(entry(step), step).astype(jnp.float32)
    return total


def spread_row(row, sizes, collective):
    if collective is None:
        return lax.all_gather(row, AXES, axis=0)
    return spread(row, sizes, collective)


def output_layer(row, table, bias, labels, weights, rows_per, vocab, sizes, collective):
    parts = math.prod(sizes)
    cells = rows_per + -rows_per % 128
    if collective is not None:
        table = jnp.pad(table, ((0, cells - rows_per), (0, 0)))
        bias = jnp.pad(bias, (0, cells - rows_per))[None]
        info = jnp.stack([labels.astype(jnp.float32), weights]).reshape(2, parts, -1)
        info = jnp.pad(info.swapaxes(0, 1), ((0, 0), (0, 6), (0, 0)))
        grad, word, d_bias, stats = head_all(
            row, table, bias, info, rows_per, vocab, sizes, collective
        )
        stats = [stats[:, i].reshape(-1) for i in range(3)]
        return grad, word[:rows_per], d_bias[0, :rows_per], stats
    rows = gather_rows(row, sizes, None, 1)
    column = lax.axis_index(AXES) * rows_per + jnp.arange(rows_per, dtype=jnp.int32)
    logits = jnp.where(column < vocab, right_transposed(rows, table) + bias, -1e30)
    own_peak = jnp.max(logits, -1)
    own_total = jnp.sum(jnp.exp(logits - own_peak[:, None]), -1)
    hits = labels[:, None] == column
    own_label = jnp.sum(jnp.where(hits, logits, 0.0), -1)
    peak = lax.pmax(own_peak, AXES)
    total, label = lax.psum((own_total * jnp.exp(own_peak - peak), own_label), AXES)
    slopes = weights[:, None] * (
        jnp.exp(logits - peak[:, None]) / total[:, None] - hits.astype(jnp.float32)
    )
    low = slopes.astype(jnp.bfloat16)
    grad = sum_rows(matmul(low, table).astype(jnp.bfloat16), sizes, None, 1)
    return grad, left_transposed(low, rows), jnp.sum(slopes, 0), (peak, total, label)


def adam_step(weight, first, second, grad, factor, rate):
    clipped = grad * factor
    first = beta_one * first + (1.0 - beta_one) * clipped
    second = beta_two * second + (1.0 - beta_two) * clipped * clipped
    first_hat = first / (1.0 - beta_one**STEP)
    second_hat = second / (1.0 - beta_two**STEP)
    weight = weight - rate * (first_hat / (jnp.sqrt(second_hat) + epsilon) + weight_decay * weight)
    return (weight, first, second)


def per_device(
    token_ids,
    lengths,
    masked_at,
    labels,
    word_table,
    word_first,
    word_second,
    pos_table,
    pos_first,
    pos_second,
    qkv_weight,
    qkv_first,
    qkv_second,
    square_weight,
    square_first,
    square_second,
    up_weight,
    up_first,
    up_second,
    down_weight,
    down_first,
    down_second,
    vec_table,
    vec_first,
    vec_second,
    head_bias,
    bias_first,
    bias_second,
):
    narrow = jnp.bfloat16
    seq_len, slots = token_ids.shape[1], masked_at.shape[1]
    width = word_table.shape[1]
    vocab = head_bias.shape[0]
    rows_per = word_table.shape[0]
    parts = lax.axis_size(AXES)
    halves = lax.axis_size("pipe")
    me = lax.axis_index(AXES)
    own = token_ids.shape[0] // halves
    first_own = lax.axis_index("pipe") * own
    head_dim = width // H
    sizes = tuple(lax.axis_size(axis) for axis in AXES)
    shards = (word_table, qkv_weight, square_weight[0], up_weight, down_weight)
    direct = sizes[:2] == (2, 4) and all(shard.shape[0] % 32 == 0 for shard in shards)
    ids = tuple(range(11)) if direct else (None,) * 11
    plane_sizes = sizes[:2] + (1,)

    spare = -(seq_len + slots + 1) % 128
    packed = jnp.concatenate(
        [token_ids, labels, lengths[:, None], jnp.zeros((token_ids.shape[0], spare), jnp.int32)], 1
    )
    packed = lax.dynamic_slice_in_dim(packed, first_own, own, 0)
    planes = sizes[0] * sizes[1]
    units = up_weight.shape[1] // planes
    cut = me // sizes[2]
    blocks = up_weight.astype(narrow).reshape(up_weight.shape[0], planes, units).swapaxes(0, 1)
    packed, blocks = start_all(packed, blocks, sizes, ids[0])
    halves_low = down_weight.astype(narrow).reshape(-1, units)
    both_low = jnp.concatenate([blocks.reshape(-1, units), halves_low], 0)
    both_low = line_gather(both_low, ids[0])
    down_low = both_low[:, -halves_low.shape[0] :].reshape(units, width)
    up_low = both_low[:, : -halves_low.shape[0]].reshape(sizes[2], planes, -1, units)
    up_low = up_low.swapaxes(0, 1).reshape(width, units)
    all_ids = packed[:, :, :seq_len]
    all_labels = packed[:, :, seq_len : seq_len + slots].reshape(-1)
    all_lengths = packed[:, :, seq_len + slots]
    places = jnp.arange(seq_len, dtype=jnp.int32)
    all_live = places[None, None, :] < all_lengths[:, :, None]
    all_counts = masked_counts(all_lengths, slots)
    total = jnp.sum(all_counts).astype(jnp.float32)
    slot_index = jnp.arange(slots, dtype=jnp.int32)
    all_valid = (slot_index < all_counts[:, :, None]).astype(jnp.float32).reshape(-1)
    own_lengths = lax.dynamic_slice_in_dim(lengths, first_own, own, 0)
    masked = lax.dynamic_slice_in_dim(masked_at, first_own, own, 0)

    word_low = word_table.astype(narrow)
    routes = Routes(all_ids.reshape(parts, -1), all_live.reshape(parts, -1), rows_per)
    small = pos_table.shape[0] + vec_table.shape[0]
    spare = -small % 128
    small_low = jnp.concatenate(
        [pos_table.T, vec_table.T, jnp.zeros((pos_table.shape[1], spare), jnp.float32)], 1
    ).astype(narrow)
    low = [
        small_low,
        qkv_weight.astype(narrow),
        square_weight[0].astype(narrow),
        square_weight[1].astype(narrow),
    ]
    deep = small_low.shape[0]
    pieces = [(0, 0, deep), (1, 0, deep // 2), (1, deep // 2, deep // 2), (2, 0, deep), (3, 0, deep)]
    send = routes.table_rows(word_low, 0, routes.room).reshape(parts, -1, width)
    (small_full, qkv_low, out_low, turn_low), arrived = gather_weights(
        low, pieces, sizes, ids[1], send
    )
    word_rows = routes.fetch(word_low, arrived.reshape(-1, width))
    small_full = small_full.T
    pos_low = small_full[:seq_len]
    vec_rows = small_full[seq_len:small].astype(jnp.float32)
    query_low, both_low = qkv_low[:, :width], qkv_low[:, width:]

    second = (places[None, :] >= ((own_lengths + 1) // 2)[:, None]).reshape(-1, 1)
    embedded = (
        word_rows
        + jnp.tile(pos_low.astype(jnp.float32), (own, 1))
        + jnp.where(second, vec_rows[1], vec_rows[0])
    )
    start, norm_zero = norm_forward(embedded, vec_rows[2], vec_rows[3])
    start_low = start.astype(narrow)
    both_bias = jnp.concatenate([jnp.zeros_like(vec_rows[5]), vec_rows[5]])
    both = (matmul(start_low, both_low) + both_bias).astype(narrow)
    pick = one_hot(masked, seq_len, jnp.float32)
    chosen = rows_by_seq(pick, start.reshape(own, seq_len, width)).reshape(-1, width)
    chosen_low = chosen.astype(narrow)
    start_half, chosen_half = both_halves(start_low), both_halves(chosen_low)
    queries = (matmul(chosen_low, query_low) + vec_rows[4]).astype(narrow)
    context = attention(own_lengths, queries, both)
    branch = matmul(context, out_low) + vec_rows[6]
    hidden, norm_one = norm_forward(chosen + branch, vec_rows[7], vec_rows[8])
    hidden = hidden.astype(narrow)

    plane_hidden = gather_rows(hidden, plane_sizes, ids[2], 2)
    up_bias = lax.dynamic_slice_in_dim(vec_rows[15:].reshape(-1), cut * units, units, 0)
    inner = matmul(plane_hidden, up_low) + up_bias
    activ = jax.nn.gelu(inner, approximate=False).astype(narrow)
    branch = sum_rows(matmul(activ, down_low).astype(narrow), plane_sizes, ids[3], 2) + vec_rows[9]
    mixed, norm_two = norm_forward(hidden.astype(jnp.float32) + branch, vec_rows[10], vec_rows[11])
    picked = mixed.astype(narrow)
    turned = matmul(picked, turn_low) + vec_rows[12]
    normed, norm_head = norm_forward(
        jax.nn.gelu(turned, approximate=False), vec_rows[13], vec_rows[14]
    )

    bias_row = jnp.pad(head_bias, (0, parts * rows_per - vocab))
    bias_row = lax.dynamic_slice_in_dim(bias_row, me * rows_per, rows_per, 0)
    d_normed, d_word, d_bias, (peak, exp_total, label_logit) = output_layer(
        normed.astype(narrow),
        word_low,
        bias_row,
        all_labels,
        all_valid / total,
        rows_per,
        vocab,
        sizes,
        ids[4],
    )
    loss_total = jnp.sum(all_valid * (peak + jnp.log(exp_total) - label_logit))

    d_gelu, d_gain_head, d_shift_head = norm_backward(d_normed, norm_head, vec_rows[13])
    d_turned = (d_gelu * gelu_slope(turned)).astype(narrow)
    d_turn_bias = jnp.sum(d_turned.astype(jnp.float32), 0)
    d_turn = chip_sum(picked, d_turned)
    d_picked = right_transposed(d_turned, turn_low)
    same = masked[:, :, None] == masked[:, None, :]
    earlier = slot_index[None, :] < slot_index[:, None]
    first_slot = jnp.logical_not(jnp.any(same & earlier, 2))
    merge = (same & first_slot[:, :, None]).astype(jnp.float32)
    d_mixed = rows_by_seq(merge, d_picked.reshape(own, slots, width)).reshape(-1, width)
    d_pre, d_gain_two, d_shift_two = norm_backward(d_mixed, norm_two, vec_rows[10])
    d_branch = d_pre.astype(narrow)
    d_down_bias = jnp.sum(d_branch.astype(jnp.float32), 0)
    plane_branch = gather_rows(d_branch, plane_sizes, ids[7], 2)
    d_down = left_transposed(activ, plane_branch).astype(narrow)
    d_inner = (right_transposed(plane_branch, down_low) * gelu_slope(inner)).astype(narrow)
    d_up_bias = jnp.sum(d_inner.astype(jnp.float32), 0)
    d_up_bias = lax.dynamic_update_slice_in_dim(
        jnp.zeros((planes * units,), jnp.float32), d_up_bias, cut * units, 0
    ).reshape(-1, width)
    d_up = left_transposed(plane_hidden, d_inner).astype(narrow)
    d_hidden = sum_rows(right_transposed(d_inner, up_low).astype(narrow), plane_sizes, ids[8], 2)
    d_hidden = (d_pre + d_hidden).astype(narrow)

    d_hidden, d_down, d_up = lax.optimization_barrier((d_hidden, d_down, d_up))
    own_down = line_sum(d_down.reshape(sizes[2], -1, width), ids[7])
    d_up = d_up.reshape(planes, sizes[2], -1, units).swapaxes(0, 1)
    up_blocks = line_sum(d_up, ids[7]).astype(narrow)
    d_pre, d_gain_one, d_shift_one = norm_backward(
        d_hidden.astype(jnp.float32), norm_one, vec_rows[7]
    )
    d_branch = d_pre.astype(narrow)
    d_out_bias = jnp.sum(d_branch.astype(jnp.float32), 0)
    d_out = chip_sum(context, d_branch)
    d_context = right_transposed(d_branch, out_low).astype(narrow)
    d_query, d_key, d_value = attention(own_lengths, queries, both, d_context)
    d_query_bias = jnp.sum(d_query.astype(jnp.float32), 0)
    d_value_bias = jnp.sum(d_value.astype(jnp.float32), 0)
    d_chosen = d_pre + right_transposed(d_query, query_low)
    d_both = jnp.concatenate([d_key, d_value], 1)
    d_start = right_transposed(d_both, both_low) + rows_to_seq(
        pick, d_chosen.reshape(own, slots, width)
    ).reshape(-1, width)
    d_embedded, d_gain_zero, d_shift_zero = norm_backward(d_start, norm_zero, vec_rows[2])
    d_seg_zero = jnp.sum(jnp.where(second, 0.0, d_embedded), 0)
    d_seg_one = jnp.sum(jnp.where(second, d_embedded, 0.0), 0)
    d_embedded_low = d_embedded.astype(narrow)
    send = routes.token_rows(d_embedded_low, 0, routes.room).reshape(parts, -1, width)
    d_small = jnp.concatenate(
        [
            jnp.sum(d_embedded.reshape(own, seq_len, width), 0),
            jnp.stack(
                [
                    d_seg_zero,
                    d_seg_one,
                    d_gain_zero,
                    d_shift_zero,
                    d_query_bias,
                    d_value_bias,
                    d_out_bias,
                    d_gain_one,
                    d_shift_one,
                    d_down_bias,
                    d_gain_two,
                    d_shift_two,
                    d_turn_bias,
                    d_gain_head,
                    d_shift_head,
                ]
            ),
            d_up_bias,
            jnp.zeros((spare, width), jnp.float32),
        ],
        0,
    )
    (own_out, own_turn, own_small, own_q, own_k, own_v), arrived, up_blocks = sum_chips(
        [d_out, d_turn, d_small.T.astype(narrow)],
        start_half,
        chosen_half,
        [d_query, d_key, d_value],
        send,
        up_blocks,
        sizes,
        ids[9],
    )
    own_qkv = jnp.concatenate([own_q, own_k, own_v], 1)
    own_up = up_blocks.swapaxes(0, 1).reshape(up_weight.shape).astype(jnp.float32)
    d_word = routes.give(d_embedded_low, arrived.reshape(-1, width), d_word)
    owned = (
        d_word,
        own_small[:, :seq_len].T,
        own_qkv,
        jnp.stack([own_out, own_turn]),
        own_up,
        own_down,
        own_small[:, seq_len:small].T,
    )
    local_squares = jnp.sum(d_bias * d_bias)
    for grad in owned:
        local_squares = local_squares + jnp.sum(grad * grad)
    spare = -(rows_per + 1) % 128
    last = jnp.concatenate([d_bias, local_squares[None], jnp.zeros((spare,), jnp.float32)])
    last = spread_row(last.reshape(8, -1), sizes, ids[10]).reshape(parts, -1)
    bias_grad = last[:, :rows_per].reshape(-1)[:vocab]
    grad_norm = jnp.sqrt(jnp.sum(last[:, rows_per]))
    factor = clip_norm / jnp.maximum(grad_norm, clip_norm)
    masters = (
        word_table,
        pos_table,
        qkv_weight,
        square_weight,
        up_weight,
        down_weight,
        vec_table,
        head_bias,
    )
    states = (
        (word_first, word_second),
        (pos_first, pos_second),
        (qkv_first, qkv_second),
        (square_first, square_second),
        (up_first, up_second),
        (down_first, down_second),
        (vec_first, vec_second),
        (bias_first, bias_second),
    )
    rates = (
        learn_rate,
        learn_rate,
        learn_rate,
        learn_rate,
        learn_rate,
        learn_rate,
        vector_rate,
        vector_rate,
    )
    grads = tuple(owned) + (bias_grad,)
    results = []
    for weight, state, grad, rate in zip(masters, states, grads, rates):
        results.extend(adam_step(weight, state[0], state[1], grad, factor, rate))
    return (
        results[0],
        results[1],
        results[2],
        results[3],
        results[4],
        results[5],
        results[6],
        results[7],
        results[8],
        results[9],
        results[10],
        results[11],
        results[12],
        results[13],
        results[14],
        results[15],
        results[16],
        results[17],
        results[18],
        results[19],
        results[20],
        results[21],
        results[22],
        results[23],
        loss_total,
        total,
        grad_norm,
    )


def solution(mesh):
    placed = (
        P(("grp", "dp"), None),
        P(("grp", "dp")),
        P(("grp", "dp"), None),
        P(("grp", "dp"), None),
        P(("pipe", "grp", "dp"), None),
        P(("pipe", "grp", "dp"), None),
        P(("pipe", "grp", "dp"), None),
        P(None, ("pipe", "grp", "dp")),
        P(None, ("pipe", "grp", "dp")),
        P(None, ("pipe", "grp", "dp")),
        P(("pipe", "grp", "dp"), None),
        P(("pipe", "grp", "dp"), None),
        P(("pipe", "grp", "dp"), None),
        P(None, ("pipe", "grp", "dp"), None),
        P(None, ("pipe", "grp", "dp"), None),
        P(None, ("pipe", "grp", "dp"), None),
        P(("pipe", "grp", "dp"), None),
        P(("pipe", "grp", "dp"), None),
        P(("pipe", "grp", "dp"), None),
        P(("pipe", "grp", "dp"), None),
        P(("pipe", "grp", "dp"), None),
        P(("pipe", "grp", "dp"), None),
        P(None, ("pipe", "grp", "dp")),
        P(None, ("pipe", "grp", "dp")),
        P(None, ("pipe", "grp", "dp")),
        P(),
        P(),
        P(),
    )
    return jax.shard_map(
        per_device,
        mesh=mesh,
        in_specs=placed,
        out_specs=(
            P(("pipe", "grp", "dp"), None),
            P(("pipe", "grp", "dp"), None),
            P(("pipe", "grp", "dp"), None),
            P(None, ("pipe", "grp", "dp")),
            P(None, ("pipe", "grp", "dp")),
            P(None, ("pipe", "grp", "dp")),
            P(("pipe", "grp", "dp"), None),
            P(("pipe", "grp", "dp"), None),
            P(("pipe", "grp", "dp"), None),
            P(None, ("pipe", "grp", "dp"), None),
            P(None, ("pipe", "grp", "dp"), None),
            P(None, ("pipe", "grp", "dp"), None),
            P(("pipe", "grp", "dp"), None),
            P(("pipe", "grp", "dp"), None),
            P(("pipe", "grp", "dp"), None),
            P(("pipe", "grp", "dp"), None),
            P(("pipe", "grp", "dp"), None),
            P(("pipe", "grp", "dp"), None),
            P(None, ("pipe", "grp", "dp")),
            P(None, ("pipe", "grp", "dp")),
            P(None, ("pipe", "grp", "dp")),
            P(),
            P(),
            P(),
            P(),
            P(),
            P(),
        ),
        check_vma=False,
    )
```

```python
import functools
import math

import jax
import jax.numpy as jnp
from jax import lax
from jax.experimental import pallas as pl
from jax.experimental.pallas import tpu as pltpu
from jax.sharding import PartitionSpec as P

H = 16
STEP = 10


beta_one = 0.9
beta_two = 0.999
learn_rate = 0.02
vector_rate = 0.2
weight_decay = 0.01
epsilon = 1e-08
clip_norm = 0.02
norm_eps = 1e-05
root_half = 0.7071067811865476
density_scale = 0.3989422804014327
AXES = ("pipe", "grp", "dp")
CHIPS = ("grp", "dp")
PLANE = ("pipe", "grp")
highest = lax.Precision.HIGHEST


def matmul(left, right):
    return jnp.dot(left, right, preferred_element_type=jnp.float32)


def left_transposed(left, right):
    return lax.dot_general(
        left, right, (((0,), (0,)), ((), ())), preferred_element_type=jnp.float32
    )


def right_transposed(left, right):
    return lax.dot_general(
        left, right, (((1,), (1,)), ((), ())), preferred_element_type=jnp.float32
    )


def norm_forward(values, gain, shift):
    center = values - jnp.mean(values, -1, keepdims=True)
    scale = lax.rsqrt(jnp.mean(center * center, -1, keepdims=True) + norm_eps)
    normal = center * scale
    return (normal * gain + shift, (normal, scale))


def norm_backward(grad, kept, gain):
    normal, scale = kept
    d_gain = jnp.sum(grad * normal, 0)
    d_shift = jnp.sum(grad, 0)
    d_norm = grad * gain
    d_input = scale * (
        d_norm
        - jnp.mean(d_norm, -1, keepdims=True)
        - normal * jnp.mean(d_norm * normal, -1, keepdims=True)
    )
    return (d_input, d_gain, d_shift)


def gelu_slope(values):
    return (
        0.5 * (1.0 + lax.erf(values * root_half))
        + values * jnp.exp(-0.5 * values * values) * density_scale
    )


def masked_counts(lengths, slots):
    return jnp.minimum(slots, (3 * lengths + 19) // 20)


def one_hot(indices, size, dtype):
    places = lax.broadcasted_iota(jnp.int32, indices.shape + (size,), indices.ndim)
    return (indices[..., None] == places).astype(dtype)


def rows_by_seq(pick, rows):
    return jnp.einsum("sjp,spw->sjw", pick, rows, precision=highest)


def rows_to_seq(pick, rows):
    return jnp.einsum("sjp,sjw->spw", pick, rows, precision=highest)


class Routes:
    def __init__(self, all_ids, all_live, rows_per):
        self.parts, tokens = all_ids.shape
        self.cells = rows_per + -rows_per % 128
        self.me = lax.axis_index(AXES)
        mean = tokens / self.parts
        self.room = max(16, int(math.ceil((mean + 2.8 * math.sqrt(mean)) / 16)) * 16)
        owners = jnp.where(all_live, all_ids // rows_per, -1)
        counts = jnp.sum(one_hot(owners, self.parts, jnp.int32), 1)
        self.more = 16
        self.rounds = (jnp.maximum(jnp.max(counts) - self.room, 0) + self.more - 1) // self.more
        mine = owners == self.me
        order = jnp.arange(tokens, dtype=jnp.int32)
        upto = (order[:, None] <= order[None, :]).astype(jnp.bfloat16)
        ranks = matmul(mine.astype(jnp.bfloat16), upto).astype(jnp.int32)
        self.out_rank = jnp.where(mine, ranks - 1, -1)
        self.out_row = all_ids - self.me * rows_per
        own_owners = lax.dynamic_index_in_dim(owners, self.me, 0, keepdims=False)
        hits = one_hot(own_owners, self.parts, jnp.bfloat16)
        ranks = jnp.sum(hits.astype(jnp.float32) * left_transposed(upto, hits), 1)
        ranks = ranks.astype(jnp.int32) - 1
        self.in_rank = ranks
        self.in_owner = own_owners

    def owner_pick(self, first, room):
        slots = first + jnp.arange(room, dtype=jnp.int32)
        at = self.out_rank[:, None, :] == slots[None, :, None]
        row = jnp.sum(jnp.where(at, self.out_row[:, None, :] + 1, 0), 2) - 1
        return one_hot(row.reshape(-1), self.cells, jnp.bfloat16)

    def token_pick(self, first, room):
        rank = self.in_rank - first
        inside = (self.in_owner >= 0) & (rank >= 0) & (rank < room)
        slot = jnp.where(inside, self.in_owner * room + rank, -1)
        return one_hot(slot, self.parts * room, jnp.bfloat16)

    def exchange(self, rows):
        shaped = rows.reshape(self.parts, -1, rows.shape[-1])
        return lax.all_to_all(shaped, AXES, 0, 0).reshape(rows.shape)

    def table_rows(self, table, first, room):
        return matmul(self.owner_pick(first, room), table).astype(jnp.bfloat16)

    def token_rows(self, rows, first, room):
        return left_transposed(self.token_pick(first, room), rows).astype(jnp.bfloat16)

    def later(self, more, start):
        def one(turn, kept):
            return kept + more(self.room + turn * self.more)

        return lax.fori_loop(0, self.rounds, one, start)

    def fetch(self, table, arrived):
        def more(first):
            rows = self.exchange(self.table_rows(table, first, self.more))
            return matmul(self.token_pick(first, self.more), rows)

        return self.later(more, matmul(self.token_pick(0, self.room), arrived))

    def give(self, rows, arrived, start):
        def more(first):
            back = self.exchange(self.token_rows(rows, first, self.more))
            return left_transposed(self.owner_pick(first, self.more), back)

        start = start + left_transposed(self.owner_pick(0, self.room), arrived)
        return self.later(more, start)


def swapped(shard):
    return lax.ppermute(shard, "pipe", [(0, 1), (1, 0)])


def both_cores(rows):
    return jnp.concatenate([rows, swapped(rows)], 0)


def half_columns(rows, index):
    half = rows.shape[1] // 2
    return lax.dynamic_slice_in_dim(rows, index * half, half, 1)


def both_halves(rows):
    pipe = lax.axis_index("pipe")
    return jnp.concatenate([half_columns(rows, pipe), swapped(half_columns(rows, 1 - pipe))], 0)


def chip_sum(left, right):
    return left_transposed(both_halves(left), both_cores(right)).astype(jnp.bfloat16)


def chip_half(partial):
    half = partial.shape[0] // 2
    pipe = lax.axis_index("pipe")
    partial = partial.astype(jnp.bfloat16)
    keep = lax.dynamic_slice_in_dim(partial, pipe * half, half, 0)
    give = lax.dynamic_slice_in_dim(partial, (1 - pipe) * half, half, 0)
    return (keep.astype(jnp.float32) + swapped(give).astype(jnp.float32)).astype(jnp.bfloat16)


def lasting(microseconds):
    return pl.CostEstimate(
        flops=int(microseconds * 9e8), bytes_accessed=int(microseconds * 3e6), transcendentals=0
    )


def device(pipe, grp, dp):
    return {"pipe": pipe, "grp": grp, "dp": dp}


def remote(source, target, send, arrive, to):
    return pltpu.make_async_remote_copy(
        src_ref=source,
        dst_ref=target,
        send_sem=send,
        recv_sem=arrive,
        device_id=device(*to),
        device_id_type=pl.DeviceIdType.MESH,
    )


def tell(barrier, to):
    pl.semaphore_signal(
        barrier, inc=1, device_id=device(*to), device_id_type=pl.DeviceIdType.MESH
    )


def greet(others):
    barrier = pltpu.get_barrier_semaphore()
    for to in others:
        tell(barrier, to)
    pl.semaphore_wait(barrier, len(others))


class Place:
    def __init__(self, sizes):
        self.pipes, self.grps, self.dps = sizes
        self.plane_only = self.dps == 1
        self.pipe, self.grp, self.dp = [lax.axis_index(axis) for axis in AXES]
        column, row = self.grp % 2, self.grp // 2
        self.beside = 2 * row + 1 - column
        self.below = 2 * (1 - row) + column
        self.across = 3 - self.grp

    @property
    def spot(self):
        return 0 if self.plane_only else self.dp

    def plane(self):
        found = []
        for a in range(self.pipes):
            for b in range(self.grps):
                if (a, b) != (0, 0):
                    ahead = ((self.pipe + a) % self.pipes, (self.grp + b) % self.grps)
                    back = (
                        (self.pipe + self.pipes - a) % self.pipes,
                        (self.grp + self.grps - b) % self.grps,
                    )
                    found.append((ahead, back))
        return found

    def line(self, step):
        return (self.dp + step) % self.dps

    def behind(self, step):
        return (self.dp + self.dps - step) % self.dps

    def others(self):
        found = []
        for a in range(self.pipes):
            for b in range(self.grps):
                for c in range(self.dps):
                    if (a, b, c) != (0, 0, 0):
                        ahead = (
                            (self.pipe + a) % self.pipes,
                            (self.grp + b) % self.grps,
                            (self.dp + c) % self.dps,
                        )
                        back = (
                            (self.pipe + self.pipes - a) % self.pipes,
                            (self.grp + self.grps - b) % self.grps,
                            (self.dp + self.dps - c) % self.dps,
                        )
                        found.append((ahead, back))
        return found

    def index(self, pipe, grp, dp):
        return (pipe * self.grps + grp) * self.dps + dp


def swap_all(place, rows, arrived, send, arrive, own):
    me = place.index(place.pipe, place.grp, place.dp)
    copies = []
    for i, (ahead, back) in enumerate(place.others()):
        to = place.index(*ahead)
        copies.append(remote(rows.at[to], arrived.at[me], send.at[i], arrive.at[i], ahead))
        copies[-1].start()
    kept = pltpu.make_async_copy(rows.at[me], arrived.at[me], own)
    kept.start()

    def finish():
        for i, (ahead, back) in enumerate(place.others()):
            origin = place.index(*back)
            copies[i].wait_send()
            remote(rows.at[me], arrived.at[origin], send.at[i], arrive.at[i], ahead).wait_recv()
        kept.wait()

    return finish


def swap_plane(place, rows, arrived, send, arrive, own):
    me = place.pipe * place.grps + place.grp
    copies = []
    for i, (ahead, back) in enumerate(place.plane()):
        to = ahead[0] * place.grps + ahead[1]
        copies.append(
            remote(rows.at[to], arrived.at[me], send.at[i], arrive.at[i], ahead + (place.dp,))
        )
        copies[-1].start()
    kept = pltpu.make_async_copy(rows.at[me], arrived.at[me], own)
    kept.start()

    def finish():
        for i, (ahead, back) in enumerate(place.plane()):
            origin = back[0] * place.grps + back[1]
            copies[i].wait_send()
            remote(
                rows.at[me], arrived.at[origin], send.at[i], arrive.at[i], ahead + (place.dp,)
            ).wait_recv()
        kept.wait()

    return finish


def begin_kernel(sizes, row_ref, up_ref, all_ref, arrived_ref, *sems):
    send, arrive, own, plane_send, plane_arrive, plane_own = sems
    place = Place(sizes)
    others = place.others()
    greet([ahead for ahead, _ in others])
    finish = swap_plane(place, up_ref, arrived_ref, plane_send, plane_arrive, plane_own)
    me = place.index(place.pipe, place.grp, place.dp)
    copies = []
    for i, (ahead, _) in enumerate(others):
        copies.append(remote(row_ref, all_ref.at[me], send.at[i], arrive.at[i], ahead))
        copies[-1].start()
    kept = pltpu.make_async_copy(row_ref, all_ref.at[me], own)
    kept.start()
    for i, (ahead, back) in enumerate(others):
        copies[i].wait_send()
        remote(
            row_ref, all_ref.at[place.index(*back)], send.at[i], arrive.at[i], ahead
        ).wait_recv()
    kept.wait()
    finish()


def begin(row, blocks, sizes, collective):
    parts = math.prod(sizes)
    sems = pltpu.SemaphoreType.DMA((parts - 1,))
    plane_sems = pltpu.SemaphoreType.DMA((sizes[0] * sizes[1] - 1,))
    return pl.pallas_call(
        functools.partial(begin_kernel, sizes),
        out_shape=(
            jax.ShapeDtypeStruct((parts,) + row.shape, row.dtype),
            jax.ShapeDtypeStruct(blocks.shape, blocks.dtype),
        ),
        in_specs=[pl.BlockSpec(memory_space=pltpu.VMEM)] * 2,
        out_specs=[pl.BlockSpec(memory_space=pltpu.VMEM)] * 2,
        scratch_shapes=[
            sems,
            sems,
            pltpu.SemaphoreType.DMA,
            plane_sems,
            plane_sems,
            pltpu.SemaphoreType.DMA,
        ],
        compiler_params=pltpu.CompilerParams(
            collective_id=collective, has_side_effects=True, vmem_limit_bytes=8 << 20
        ),
    )(row, blocks)


def spread_kernel(sizes, row_ref, all_ref, send, arrive, own):
    place = Place(sizes)
    others = place.others()
    greet([ahead for ahead, _ in others])
    me = place.index(place.pipe, place.grp, place.dp)
    copies = []
    for i, (ahead, _) in enumerate(others):
        copies.append(remote(row_ref, all_ref.at[me], send.at[i], arrive.at[i], ahead))
        copies[-1].start()
    kept = pltpu.make_async_copy(row_ref, all_ref.at[me], own)
    kept.start()
    for i, (ahead, back) in enumerate(others):
        copies[i].wait_send()
        remote(
            row_ref, all_ref.at[place.index(*back)], send.at[i], arrive.at[i], ahead
        ).wait_recv()
    kept.wait()


def spread(row, sizes, collective):
    parts = math.prod(sizes)
    sems = pltpu.SemaphoreType.DMA((parts - 1,))
    return pl.pallas_call(
        functools.partial(spread_kernel, sizes),
        out_shape=jax.ShapeDtypeStruct((parts,) + row.shape, row.dtype),
        in_specs=[pl.BlockSpec(memory_space=pltpu.VMEM)],
        out_specs=pl.BlockSpec(memory_space=pltpu.VMEM),
        scratch_shapes=[sems, sems, pltpu.SemaphoreType.DMA],
        compiler_params=pltpu.CompilerParams(
            collective_id=collective, has_side_effects=True, vmem_limit_bytes=8 << 20
        ),
    )(row)


class Gather:
    def __init__(self, place, pieces, shards, fulls, send, arrive, own):
        self.place, self.pieces, self.shards, self.fulls = place, pieces, shards, fulls
        self.send, self.arrive, self.own = send, arrive, own
        pipe, grp, dp = place.pipe, place.grp, place.dp
        self.near = place.beside * (1 - pipe) + place.below * pipe
        self.far = place.below * (1 - pipe) + place.beside * pipe
        self.core = (1 - pipe, grp, dp)
        self.hops = place.dps - 1
        self.ends = (dp < self.hops, dp > 0)
        self.sides = ((pipe, grp, dp + 1), (pipe, grp, dp - 1))
        self.both = range(2 if self.hops else 0)
        self.waits, self.keeps = [], {}
        self.stages = [functools.partial(self.over_line, hop=hop) for hop in range(self.hops)]
        self.stages += [self.over_plane, self.pass_on, self.last]

    def partners(self):
        place = self.place
        pipe, grp, dp = place.pipe, place.grp, place.dp
        line = [(pipe, grp, place.line(k + 1)) for k in range(self.hops)]
        return line + [(pipe, self.near, dp), (pipe, self.far, dp), self.core]

    def view(self, n, *at):
        array, first, rows = self.pieces[n]
        return self.fulls[array].at[at + ((slice(None),) * (3 - len(at))) + (pl.ds(first, rows),)]

    def shard(self, n):
        array, first, rows = self.pieces[n]
        return self.shards[array].at[pl.ds(first, rows)]

    def launch(self, n, index, source, to, *at):
        copy = remote(
            source, self.view(n, *at), self.send.at[n, index], self.arrive.at[n, index], to
        )
        copy.start()
        self.waits.append(copy)

    def landed(self, n, index, *at):
        target = self.view(n, *at)
        remote(
            target, target, self.send.at[n, index], self.arrive.at[n, index], self.core
        ).wait_recv()

    def along(self, n, side, hop, finish=False):
        place, hops = self.place, self.hops
        origin = place.dp - hop if side == 0 else place.dp + hop
        here = origin >= 0 if side == 0 else origin <= hops
        index = side * hops + hop

        def copy():
            target = self.view(n, place.pipe, place.grp, origin)
            source = self.shard(n) if hop == 0 else target
            return remote(
                source, target, self.send.at[n, index], self.arrive.at[n, index], self.sides[side]
            )

        if finish:

            @pl.when(here & self.ends[side])
            def _():
                copy().wait_send()

            return
        if hop > 0:

            @pl.when(here)
            def _():
                self.landed(n, index - 1, place.pipe, place.grp, origin)

        if hop < hops:

            @pl.when(here & self.ends[side])
            def _():
                copy().start()

    def over_line(self, n, hop):
        place = self.place
        if hop == 0:
            target = self.view(n, place.pipe, place.grp, place.spot)
            self.keeps[n] = pltpu.make_async_copy(self.shard(n), target, self.own.at[n])
            self.keeps[n].start()
        for side in self.both:
            self.along(n, side, hop)

    def over_plane(self, n):
        place, first = self.place, 2 * self.hops
        pipe, grp, dp = place.pipe, place.grp, place.dp
        self.over_line(n, self.hops)
        if self.hops:
            self.keeps[n].wait()
            group, at = self.view(n, pipe, grp), (pipe, grp)
        else:
            group, at = self.shard(n), (pipe, grp, 0)
        self.launch(n, first, group, (pipe, self.near, dp), *at)
        self.launch(n, first + 1, group, (pipe, self.far, dp), *at)
        self.launch(n, first + 3, group, self.core, *at)

    def pass_on(self, n):
        pipe, first = self.place.pipe, 2 * self.hops
        self.landed(n, first, pipe, self.near)
        group = self.view(n, pipe, self.near)
        self.launch(n, first + 2, group, (pipe, self.far, self.place.dp), pipe, self.near)
        self.launch(n, first + 4, group, self.core, pipe, self.near)
        self.landed(n, first + 1, pipe, self.far)
        self.launch(n, first + 5, self.view(n, pipe, self.far), self.core, pipe, self.far)

    def last(self, n):
        pipe, first, across = self.place.pipe, 2 * self.hops, self.place.across
        self.landed(n, first + 2, pipe, across)
        self.launch(n, first + 6, self.view(n, pipe, across), self.core, pipe, across)

    def core_order(self):
        return (
            (),
            ((3, self.place.grp),),
            ((4, self.far), (5, self.near)),
            ((6, self.place.across),),
        )

    def from_core(self, n):
        for step in self.core_order():
            for index, grp in step:
                self.landed(n, 2 * self.hops + index, 1 - self.place.pipe, grp)

    def settle(self):
        for n in range(len(self.pieces)):
            for side in self.both:
                for hop in range(self.hops):
                    self.along(n, side, hop, finish=True)
        for copy in self.waits:
            copy.wait_send()
        if not self.hops:
            for keep in self.keeps.values():
                keep.wait()


class LineGather(Gather):
    def __init__(self, place, shards, fulls, axes, send, arrive, own):
        super().__init__(place, [(n, 0, 0) for n in range(len(shards))], shards, fulls, send, arrive, own)
        self.axes = axes
        self.stages = [functools.partial(self.over_line, hop=hop) for hop in range(self.hops + 1)]

    def view(self, n, pipe, grp, origin):
        return self.fulls[n].at[(slice(None),) * self.axes[n] + (origin,)]

    def shard(self, n):
        return self.shards[n]

    def over_line(self, n, hop):
        super().over_line(n, hop)
        if hop == self.hops:
            self.keeps[n].wait()


def run_stages(stages, total, after=None):
    for turn in range(total + len(stages) - 1):
        for at, stage in enumerate(stages):
            if 0 <= turn - at < total:
                stage(turn - at)
        if after is not None:
            after(turn)


def gather_kernel(sizes, pieces, axes, routed, *refs):
    count, lines = max(piece[0] for piece in pieces) + 1, len(axes)
    shards, line_shards, refs = refs[:count], refs[count : count + lines], refs[count + lines :]
    if routed:
        rows_ref, refs = refs[0], refs[1:]
    fulls, line_fulls, refs = refs[:count], refs[count : count + lines], refs[count + lines :]
    if routed:
        arrived_ref, refs = refs[0], refs[1:]
    send, arrive, own, line_send, line_arrive, line_own, swap_send, swap_arrive, swap_own = refs
    place = Place(sizes)
    gather = Gather(place, pieces, shards, fulls, send, arrive, own)
    line = LineGather(place, line_shards, line_fulls, axes, line_send, line_arrive, line_own)
    greet([ahead for ahead, _ in place.others()] if routed else gather.partners())
    swaps = []

    def after(turn):
        for n in range(lines):
            if 0 <= turn - n <= gather.hops:
                line.over_line(n, turn - n)
        if turn == len(pieces) and routed:
            swaps.append(
                swap_all(place, rows_ref, arrived_ref, swap_send, swap_arrive, swap_own)
            )

    run_stages(gather.stages, len(pieces), after)
    for n in range(len(pieces)):
        gather.from_core(n)
    gather.settle()
    if lines:
        line.settle()
    for finish in swaps:
        finish()


def gather_all(shards, pieces, sizes, collective, rows=None, lines=(), axes=()):
    parts = math.prod(sizes)
    routed = rows is not None
    kinds = 2 * (sizes[2] - 1) + 7
    near = pl.BlockSpec(memory_space=pltpu.VMEM)
    out_shape = [jax.ShapeDtypeStruct(sizes + shard.shape, shard.dtype) for shard in shards]
    for line, axis in zip(lines, axes):
        shape = line.shape[:axis] + sizes[2:] + line.shape[axis:]
        out_shape.append(jax.ShapeDtypeStruct(shape, line.dtype))
    if routed:
        out_shape.append(jax.ShapeDtypeStruct(rows.shape, rows.dtype))
    operands = list(shards) + list(lines) + ([rows] if routed else [])
    sems = pltpu.SemaphoreType.DMA((len(pieces), kinds))
    line_sems = pltpu.SemaphoreType.DMA((max(len(lines), 1), kinds))
    swaps = pltpu.SemaphoreType.DMA((parts - 1 if routed else 1,))
    return pl.pallas_call(
        functools.partial(gather_kernel, sizes, tuple(pieces), tuple(axes), routed),
        out_shape=out_shape,
        in_specs=[near] * len(operands),
        out_specs=[near] * len(out_shape),
        scratch_shapes=[
            sems,
            sems,
            pltpu.SemaphoreType.DMA((len(pieces),)),
            line_sems,
            line_sems,
            pltpu.SemaphoreType.DMA((max(len(lines), 1),)),
            swaps,
            swaps,
            pltpu.SemaphoreType.DMA,
        ],
        compiler_params=pltpu.CompilerParams(
            collective_id=collective, has_side_effects=True, vmem_limit_bytes=40 << 20
        ),
        cost_estimate=lasting(110 if routed else 15),
    )(*operands)


class Sums:
    block = 16
    filled = False

    def __init__(self, place, sources, chips, others, mine, planes, lines, send, arrive, own, store):
        self.place, self.sources, self.chips, self.others = place, sources, chips, others
        self.mine, self.planes, self.lines = mine, planes, lines
        self.send, self.arrive, self.own, self.store = send, arrive, own, store
        pipe, grp, dp = place.pipe, place.grp, place.dp
        self.near = place.beside * (1 - pipe) + place.below * pipe
        self.far = place.below * (1 - pipe) + place.beside * pipe
        self.copies, self.kept = {}, {}

    def launch(self, n, index, source, target, to):
        copy = remote(source, target, self.send.at[n, index], self.arrive.at[n, index], to)
        self.copies[n, index] = copy
        copy.start()

    def keep(self, n, index, source, target):
        self.kept[n, index] = pltpu.make_async_copy(source, target, self.own.at[n, index])
        self.kept[n, index].start()

    def blocks(self, n, body):
        deep = self.mine[n].shape[2] // self.block

        def one(i, _):
            body(i // deep, pl.ds(pl.multiple_of(i % deep * self.block, self.block), self.block))
            return 0

        lax.fori_loop(0, self.place.dps * deep, one, 0)

    def to_core(self, n):
        place = self.place
        core = (1 - place.pipe, place.grp, place.dp)
        if self.filled:
            self.launch(n, 0, self.sources[n], self.others[n], core)
        elif self.chips[n] is not None:
            self.launch(n, 0, self.sources[n].at[1 - place.pipe], self.others[n], core)
            self.keep(n, 0, self.sources[n].at[place.pipe], self.chips[n])

    def to_near(self, n):
        place, chip, other = self.place, self.chips[n], self.others[n]
        part = self.sources[n]
        if chip is not None:
            if not self.filled:
                self.kept[n, 0].wait()
            self.copies[n, 0].wait_recv()
            for g in range(place.grps):

                def add(d, at, g=g):
                    left = chip[g, d, at].astype(jnp.float32)
                    chip[g, d, at] = (left + other[g, d, at].astype(jnp.float32)).astype(
                        jnp.bfloat16
                    )

                self.blocks(n, add)
            part = chip
        else:
            for j, g in enumerate((self.far, place.grp)):
                self.keep(n, j, part.at[g], self.mine[n].at[j])
        to = (place.pipe, self.near, place.dp)
        self.launch(n, 1, part.at[self.near], self.planes[n].at[1], to)
        self.launch(n, 2, part.at[place.across], self.planes[n].at[0], to)

    def to_far(self, n):
        place, mine, plane, chip = self.place, self.mine[n], self.planes[n], self.chips[n]
        if chip is None:
            self.kept[n, 0].wait()
            self.kept[n, 1].wait()
        self.copies[n, 1].wait_recv()
        self.copies[n, 2].wait_recv()
        for j, g in enumerate((self.far, place.grp)):

            def add(d, at, j=j, g=g):
                left = mine[j, d, at] if chip is None else chip[g, d, at]
                total = left.astype(jnp.float32) + plane[j, d, at].astype(jnp.float32)
                mine[j, d, at] = total.astype(jnp.bfloat16)

            self.blocks(n, add)
            if j == 0:
                self.launch(n, 3, mine.at[0], plane.at[2], (place.pipe, self.far, place.dp))

    def to_lines(self, n):
        place, mine, plane = self.place, self.mine[n], self.planes[n]
        self.copies[n, 3].wait_recv()
        hops = place.dps - 1

        def add(d, at):
            total = mine[1, d, at].astype(jnp.float32) + plane[2, d, at].astype(jnp.float32)
            if hops:
                mine[1, d, at] = total.astype(jnp.bfloat16)
            else:
                self.store(n, at, total)

        self.blocks(n, add)
        for k in range(hops):
            to = place.line(k + 1)
            self.launch(
                n, 4 + k, mine.at[1, to], self.lines[n].at[k], (place.pipe, place.grp, to)
            )

    def to_sum(self, n):
        place, mine, lines = self.place, self.mine[n], self.lines[n]
        for k in range(place.dps - 1):
            self.copies[n, 4 + k].wait_recv()

        def add(i, _):
            at = pl.ds(pl.multiple_of(i * self.block, self.block), self.block)
            total = mine[1, place.spot, at].astype(jnp.float32)
            for k in range(place.dps - 1):
                total = total + lines[k, at].astype(jnp.float32)
            self.store(n, at, total)
            return 0

        lax.fori_loop(0, mine.shape[2] // self.block, add, 0)

    def settle(self):
        for copy in self.copies.values():
            copy.wait_send()


def sum_scratch(shapes, cores, sizes):
    low = jnp.bfloat16
    _, grps, dps = sizes
    wide = [(dps,) + shape for shape in shapes]
    chips = [pltpu.VMEM((grps,) + shape, low) for shape, core in zip(wide, cores) if core]
    scratch = chips + chips
    scratch += [pltpu.VMEM((2,) + shape, low) for shape in wide]
    scratch += [pltpu.VMEM((3,) + shape, low) for shape in wide]
    scratch += [pltpu.VMEM((max(dps - 1, 1),) + shape, low) for shape in shapes]
    sems = pltpu.SemaphoreType.DMA((len(shapes), 4 + dps - 1))
    return scratch + [sems, sems, pltpu.SemaphoreType.DMA((len(shapes), 2))]


def sum_refs(refs, cores):
    total = len(cores)

    def spread_out(found):
        found = iter(found)
        return [next(found) if core else None for core in cores]

    chosen = sum(cores)
    groups = []
    for count in (chosen, chosen, total, total, total):
        groups.append(refs[:count])
        refs = refs[count:]
    chips, others, mine, planes, lines = groups
    return (spread_out(chips), spread_out(others), mine, planes, lines) + tuple(refs[:3]), refs[3:]


def reduce_kernel(sizes, pieces, *refs):
    partial, out, refs = refs[0], refs[1], refs[2:]
    place = Place(sizes)
    scratch, _ = sum_refs(refs, (True,) * len(pieces))

    def store(n, at, total):
        to = pl.multiple_of(pieces[n][0] + at.start, Sums.block)
        out[pl.ds(to, Sums.block)] = total

    sources = [partial.at[:, :, :, pl.ds(first, rows)] for first, rows in pieces]
    sums = Sums(place, sources, *scratch, store)
    line = [(place.pipe, place.grp, place.line(k + 1)) for k in range(place.dps - 1)]
    near, far = [(place.pipe, grp, place.dp) for grp in (sums.near, sums.far)]
    greet(line + [near, far, (1 - place.pipe, place.grp, place.dp)])
    stages = [sums.to_core, sums.to_near, sums.to_far, sums.to_lines]
    stages += [sums.to_sum] if place.dps > 1 else []
    run_stages(stages, len(pieces))
    sums.settle()


def reduce_all(partial, pieces, sizes, collective):
    shapes = [(rows, partial.shape[-1]) for _, rows in pieces]
    return pl.pallas_call(
        functools.partial(reduce_kernel, sizes, tuple(pieces)),
        out_shape=jax.ShapeDtypeStruct(partial.shape[-2:], jnp.float32),
        in_specs=[pl.BlockSpec(memory_space=pl.ANY)],
        out_specs=pl.BlockSpec(memory_space=pltpu.VMEM),
        scratch_shapes=sum_scratch(shapes, (True,) * len(pieces), sizes),
        cost_estimate=lasting(15),
        compiler_params=pltpu.CompilerParams(
            collective_id=collective, has_side_effects=True, vmem_limit_bytes=48 << 20
        ),
    )(partial)


def finish_kernel(sizes, *refs):
    lefts, rights, start, talls, refs = refs[:3], refs[3:6], refs[6], refs[7:9], refs[9:]
    small, rows_ref, blocks_ref, refs = refs[0], refs[1], refs[2], refs[3:]
    outs, arrived_ref, blocks_arrived_ref, refs = refs[:4], refs[4], refs[5], refs[6:]
    cores = (False, False, True, False, False, False)
    scratch, refs = sum_refs(refs, cores)
    other_lefts, other_rights, other_talls, made, refs = (
        refs[:3],
        refs[3:6],
        refs[6:8],
        refs[8:13],
        refs[13:],
    )
    swap_send, swap_arrive, swap_own, plane_send, plane_arrive, plane_own = refs[:6]
    core_send, core_arrive = refs[6:]
    place = Place(sizes)
    pipe, grp, dp = place.pipe, place.grp, place.dp
    greet([ahead for ahead, _ in place.others()])

    mine = tuple(lefts) + tuple(rights) + tuple(talls)
    theirs = tuple(other_lefts) + tuple(other_rights) + tuple(other_talls)
    exchanged = {}
    for i in (0, 3, 1, 4, 2, 5, 6, 7):
        exchanged[i] = remote(
            mine[i], theirs[i], core_send.at[i], core_arrive.at[i], (1 - pipe, grp, dp)
        )
        exchanged[i].start()

    def store(n, at, total):
        if n < 3:
            outs[n][at] = total
        else:
            outs[3][at, pl.ds((n - 3) * total.shape[1], total.shape[1])] = total

    sources = (made[0], made[1], small, made[2], made[3], made[4])
    sums = Sums(place, sources, *scratch, store)
    sums.to_core(2)
    swap = swap_all(place, rows_ref, arrived_ref, swap_send, swap_arrive, swap_own)
    plane_swap = swap_plane(
        place, blocks_ref, blocks_arrived_ref, plane_send, plane_arrive, plane_own
    )
    wide = made[0].shape[1] * made[0].shape[2]

    def form(i):
        exchanged[i].wait_recv()
        exchanged[3 + i].wait_recv()
        for g in range(place.grps):
            first = pl.multiple_of((pipe * place.grps + g) * wide, 128)
            at = pl.ds(first, wide)
            total = left_transposed(lefts[i][:, at], rights[i][...])
            total = total + left_transposed(other_lefts[i][:, at], other_rights[i][...])
            made[i][g] = total.astype(jnp.bfloat16).reshape(made[i].shape[1:])

    def form_tall(i):
        exchanged[6 + i].wait_recv()
        tokens = talls[i].shape[0]
        for g in range(place.grps):
            at = pl.ds(g * wide, wide)
            total = left_transposed(start[0:tokens, at], talls[i][...])
            total = total + left_transposed(start[tokens:, at], other_talls[i][...])
            made[3 + i][g] = total.astype(jnp.bfloat16).reshape(made[3 + i].shape[1:])

    form(0)
    sums.to_near(0)
    form(1)
    sums.to_near(1)
    form(2)
    sums.to_near(3)
    sums.to_near(2)
    sums.to_far(0)
    form_tall(0)
    sums.to_near(4)
    sums.to_far(1)
    form_tall(1)
    sums.to_near(5)
    sums.to_far(3)
    sums.to_far(2)
    sums.to_lines(0)
    sums.to_lines(1)
    sums.to_lines(3)
    sums.to_far(4)
    sums.to_lines(2)
    sums.to_far(5)
    sums.to_lines(4)
    sums.to_lines(5)
    for n in (0, 1, 3, 2, 4, 5):
        sums.to_sum(n)
    sums.settle()
    for copy in exchanged.values():
        copy.wait_send()
    plane_swap()
    swap()


def finish_all(lefts, rights, start, talls, small, rows, blocks, sizes, collective):
    low = jnp.bfloat16
    parts = math.prod(sizes)
    _, grps, dps = sizes
    width = lefts[0].shape[1]
    shape = (width // parts, rights[0].shape[1])
    shapes = [shape, shape, (small.shape[-2], small.shape[-1]), shape, shape, shape]
    made = pltpu.VMEM((grps, dps) + shape, low)
    anywhere = pl.BlockSpec(memory_space=pl.ANY)
    near = pl.BlockSpec(memory_space=pltpu.VMEM)
    swaps = pltpu.SemaphoreType.DMA((parts - 1,))
    plane_swaps = pltpu.SemaphoreType.DMA((sizes[0] * grps - 1,))
    one = pltpu.SemaphoreType.DMA
    operands = (*lefts, *rights, start, *talls, small, rows, blocks)
    joined = (shape[0], 3 * shape[1])
    out_shape = [jax.ShapeDtypeStruct(shape, jnp.float32) for shape in shapes[:3] + [joined]]
    out_shape += [jax.ShapeDtypeStruct(extra.shape, extra.dtype) for extra in (rows, blocks)]
    return pl.pallas_call(
        functools.partial(finish_kernel, sizes),
        out_shape=out_shape,
        in_specs=[near] * 9 + [anywhere, near, near],
        out_specs=[near] * 6,
        scratch_shapes=sum_scratch(shapes, (False, False, True, False, False, False), sizes)
        + [pltpu.VMEM(item.shape, low) for item in (*lefts, *rights, *talls)]
        + [made] * 5
        + [
            swaps,
            swaps,
            one,
            plane_swaps,
            plane_swaps,
            one,
            pltpu.SemaphoreType.DMA((8,)),
            pltpu.SemaphoreType.DMA((8,)),
        ],
        compiler_params=pltpu.CompilerParams(
            collective_id=collective, has_side_effects=True, vmem_limit_bytes=56 << 20
        ),
    )(*operands)


def head_kernel(sizes, rows_per, vocab, gather_cuts, sum_cuts, *refs):
    row_ref, table, bias, info, out, word, bias_out, stats, refs = *refs[:8], refs[8:]
    full, logits, columns, laid, held, result, slopes, outgoing, refs = *refs[:8], refs[8:]
    cores = (True,) * sum_cuts
    scratch, refs = sum_refs(refs, cores)
    gather_send, gather_arrive, gather_own, swap_send, swap_arrive, swap_own = refs[:6]
    all_send, all_arrive = refs[6:]
    place = Place(sizes)
    pipes, grps, dps = sizes
    others = place.others()
    slots, width = row_ref.shape
    tall = slots // gather_cuts
    pieces = [(0, i * tall, tall) for i in range(gather_cuts)]
    gather = Gather(place, pieces, [row_ref], [full], gather_send, gather_arrive, gather_own)
    greet([ahead for ahead, _ in others])
    pipe, grp, hops = place.pipe, place.grp, dps - 1
    me = place.index(pipe, grp, place.dp)
    cells = table.shape[0]
    local = lax.broadcasted_iota(jnp.int32, (1, cells), 1)
    column = me * rows_per + local
    used = (local < rows_per) & (column < vocab)
    column = jnp.where(used, column, -1).astype(jnp.float32)
    groups = pipes * grps

    def parts(body):
        lax.fori_loop(0, pipes * grps * dps, lambda i, _: (body(i), 0)[1], 0, unroll=8)

    def spot(i):
        return i // (grps * dps), i // dps % grps, i % dps

    def fill(i):
        columns[spot(i) + (slice(None), slice(0, 8))] = info[i].T

    def form_logits(n, p, g):
        _, first, rows = pieces[n]
        at = pl.ds(first, rows)
        found = right_transposed(full[p, g, :, at].reshape(dps * rows, width), table[...])
        found = jnp.where(used, found + bias[...], -1e30)
        peak = jnp.max(found, -1, keepdims=True)
        total = jnp.sum(jnp.exp(found - peak), -1, keepdims=True)
        labels = columns[p, g, :, at, 0:1].reshape(dps * rows, 1)
        label = jnp.sum(jnp.where(column == labels, found, 0.0), -1, keepdims=True)
        logits[p, g, :, at] = found.reshape(dps, rows, cells)
        columns[p, g, :, at, 2:3] = peak.reshape(dps, rows, 1)
        columns[p, g, :, at, 3:4] = total.reshape(dps, rows, 1)
        columns[p, g, :, at, 4:5] = label.reshape(dps, rows, 1)

    def after(turn):
        if turn == 0:
            parts(fill)
        arrived = (
            ((pipe, grp),),
            ((pipe, gather.near), (pipe, gather.far)),
            ((pipe, place.across),),
            (),
        )
        for step in range(4):
            n = turn - hops - step
            if 0 <= n < gather_cuts:
                for p, g in arrived[step]:
                    form_logits(n, p, g)
                for index, g in gather.core_order()[step]:
                    gather.landed(n, 2 * hops + index, 1 - pipe, g)
                    form_logits(n, 1 - pipe, g)

    run_stages(gather.stages, gather_cuts, after)
    after(gather_cuts + hops + 2)

    def lay(i):
        laid[i] = columns[spot(i) + (slice(None), slice(0, 8))].T

    parts(lay)
    swap_all(place, laid, held, swap_send, swap_arrive, swap_own)()
    peaks = held[:, 2]
    peak = jnp.max(peaks, 0, keepdims=True)
    result[...] = jnp.zeros_like(result)
    result[0:1] = peak
    result[1:2] = jnp.sum(held[:, 3] * jnp.exp(peaks - peak), 0, keepdims=True)
    result[2:3] = jnp.sum(held[:, 4], 0, keepdims=True)
    copies = []
    for i, (ahead, _) in enumerate(others):
        copies.append(remote(result, stats.at[me], all_send.at[i], all_arrive.at[i], ahead))
        copies[-1].start()
    stats[me] = result[...]
    for i, (ahead, back) in enumerate(others):
        copies[i].wait_send()
        origin = place.index(*back)
        remote(
            result, stats.at[origin], all_send.at[i], all_arrive.at[i], ahead
        ).wait_recv()

    def back(i):
        columns[spot(i) + (slice(None), slice(8, 16))] = stats[i].T

    parts(back)

    size = slots // sum_cuts
    half = grps * dps * size

    def store(n, at, total):
        to = pl.multiple_of(n * size + at.start, Sums.block)
        out[pl.ds(to, Sums.block)] = total

    sums = Sums(place, [outgoing.at[n] for n in range(sum_cuts)], *scratch, store)
    sums.filled = True
    bias_out[...] = jnp.zeros_like(bias_out)
    word[...] = jnp.zeros_like(word)

    def form_slopes(n):
        at = pl.ds(n * size, size)

        def one(i, _):
            p, g = i // grps, i % grps
            kept = columns[p, g, :, at].reshape(dps * size, columns.shape[-1])
            found = logits[p, g, :, at].reshape(dps * size, cells)
            hits = (column == kept[:, 0:1]).astype(jnp.float32)
            slope = kept[:, 1:2] * (jnp.exp(found - kept[:, 8:9]) / kept[:, 9:10] - hits)
            bias_out[0:1] += jnp.sum(slope, 0, keepdims=True)
            slopes[n % 2, i] = slope.astype(jnp.bfloat16)
            return 0

        lax.fori_loop(0, groups, one, 0)
        for q, target in ((1 - place.pipe, outgoing.at[n]), (place.pipe, sums.chips[n])):
            left = slopes[n % 2, pl.ds(q * grps, grps)].reshape(half, cells)
            target[...] = matmul(left, table[...]).astype(jnp.bfloat16).reshape(target.shape)
        sums.to_core(n)

    def form_word(n):
        right = full[:, :, :, pl.ds(n * size, size)].reshape(pipes * half, width)
        word[...] += left_transposed(slopes[n % 2].reshape(pipes * half, cells), right)

    stages = [form_slopes, sums.to_near, sums.to_far, sums.to_lines, sums.to_sum]

    def then(turn):
        if turn < sum_cuts:
            form_word(turn)

    run_stages(stages, sum_cuts, then)
    sums.settle()
    gather.settle()


def head_all(row, table, bias, info, rows_per, vocab, sizes, collective):
    low = jnp.bfloat16
    parts = math.prod(sizes)
    pipes, grps, dps = sizes
    slots, width = row.shape
    cells = table.shape[0]
    gather_cuts, sum_cuts = 4, 8
    size = slots // sum_cuts
    near = pl.BlockSpec(memory_space=pltpu.VMEM)
    gathers = pltpu.SemaphoreType.DMA((gather_cuts, 2 * (dps - 1) + 7))
    swaps = pltpu.SemaphoreType.DMA((parts - 1,))
    return pl.pallas_call(
        functools.partial(head_kernel, sizes, rows_per, vocab, gather_cuts, sum_cuts),
        out_shape=(
            jax.ShapeDtypeStruct(row.shape, jnp.float32),
            jax.ShapeDtypeStruct(table.shape, jnp.float32),
            jax.ShapeDtypeStruct((8, cells), jnp.float32),
            jax.ShapeDtypeStruct(info.shape, jnp.float32),
        ),
        in_specs=[near] * 4,
        out_specs=[near] * 4,
        scratch_shapes=[
            pltpu.VMEM(sizes + row.shape, low),
            pltpu.VMEM(sizes + (slots, cells), jnp.float32),
            pltpu.VMEM(sizes + (slots, 16), jnp.float32),
            pltpu.VMEM(info.shape, jnp.float32),
            pltpu.VMEM(info.shape, jnp.float32),
            pltpu.VMEM(info.shape[1:], jnp.float32),
            pltpu.VMEM((2, pipes * grps, dps * size, cells), low),
            pltpu.VMEM((sum_cuts, grps, dps, size, width), low),
        ]
        + sum_scratch([(size, width)] * sum_cuts, (True,) * sum_cuts, sizes)
        + [
            gathers,
            gathers,
            pltpu.SemaphoreType.DMA((gather_cuts,)),
            swaps,
            swaps,
            pltpu.SemaphoreType.DMA,
            swaps,
            swaps,
        ],
        compiler_params=pltpu.CompilerParams(
            collective_id=collective, has_side_effects=True, vmem_limit_bytes=62 << 20
        ),
    )(row, table, bias, info)


def pair_rows(pair, first):
    pair = pair.astype(jnp.float32)
    low = jnp.bfloat16
    return jnp.concatenate(
        [jnp.where(first, pair, 0.0).astype(low), jnp.where(first, 0.0, pair).astype(low)], 0
    )


def pair_probs(rows, keys, live, scale):
    scores = jnp.where(live, right_transposed(rows, keys) * scale, -1e30)
    exp_scores = jnp.exp(scores - jnp.max(scores, -1, keepdims=True))
    return exp_scores / jnp.sum(exp_scores, -1, keepdims=True)


def attention_masks(lengths_ref, slots, seq_len, lanes):
    live = lax.broadcasted_iota(jnp.int32, (1, seq_len), 1) < lengths_ref[pl.program_id(0)]
    first = lax.broadcasted_iota(jnp.int32, (slots, lanes), 1) < lanes // 2
    return live, first


def attention_kernel(scale, lanes, lengths_ref, q_ref, k_ref, v_ref, out_ref):
    slots = q_ref.shape[0]
    live, first = attention_masks(lengths_ref, slots, k_ref.shape[0], lanes)
    for pair in range(q_ref.shape[1] // lanes):
        at = slice(pair * lanes, (pair + 1) * lanes)
        probs = pair_probs(pair_rows(q_ref[:, at], first), k_ref[:, at], live, scale)
        context = matmul(probs.astype(jnp.bfloat16), v_ref[:, at])
        out_ref[:, at] = jnp.where(first, context[:slots], context[slots:]).astype(jnp.bfloat16)


def attention_back_kernel(
    scale, lanes, lengths_ref, q_ref, k_ref, v_ref, grad_ref, dq_ref, dk_ref, dv_ref
):
    slots = q_ref.shape[0]
    low = jnp.bfloat16
    live, first = attention_masks(lengths_ref, slots, k_ref.shape[0], lanes)
    for pair in range(q_ref.shape[1] // lanes):
        at = slice(pair * lanes, (pair + 1) * lanes)
        rows, grads = pair_rows(q_ref[:, at], first), pair_rows(grad_ref[:, at], first)
        probs = pair_probs(rows, k_ref[:, at], live, scale)
        dv_ref[:, at] = left_transposed(probs.astype(low), grads).astype(low)
        d_probs = right_transposed(grads, v_ref[:, at])
        d_scores = probs * (d_probs - jnp.sum(probs * d_probs, -1, keepdims=True))
        d_scores = d_scores.astype(low)
        d_query = matmul(d_scores, k_ref[:, at]) * scale
        dq_ref[:, at] = jnp.where(first, d_query[:slots], d_query[slots:]).astype(low)
        dk_ref[:, at] = (left_transposed(d_scores, rows) * scale).astype(low)


def attention(lengths, queries, both, grads=None):
    own = lengths.shape[0]
    width = queries.shape[1]
    slots, seq_len = queries.shape[0] // own, both.shape[0] // own
    lanes = 2 * width // H
    scale = (width // H) ** (-0.5)
    cuts = 2
    part = width // cuts
    row = pl.BlockSpec((slots, part), lambda s, h: (s, h))
    keys = pl.BlockSpec((seq_len, part), lambda s, h: (s, h))
    values = pl.BlockSpec((seq_len, part), lambda s, h: (s, cuts + h))
    in_specs = [pl.BlockSpec(memory_space=pltpu.SMEM), row, keys, values]
    flat = jax.ShapeDtypeStruct(queries.shape, jnp.bfloat16)
    tall = jax.ShapeDtypeStruct((both.shape[0], width), jnp.bfloat16)
    if grads is None:
        return pl.pallas_call(
            functools.partial(attention_kernel, scale, lanes),
            grid=(own, cuts),
            out_shape=flat,
            in_specs=in_specs,
            out_specs=row,
            cost_estimate=lasting(8),
        )(lengths, queries, both, both)
    return pl.pallas_call(
        functools.partial(attention_back_kernel, scale, lanes),
        grid=(own, cuts),
        out_shape=(flat, tall, tall),
        in_specs=in_specs + [row],
        out_specs=(row, keys, keys),
        cost_estimate=lasting(11),
    )(lengths, queries, both, both, grads)


def even_pieces(array, rows, cuts):
    size = rows // cuts
    return [(array, i * size, size) for i in range(cuts)]


def start_all(row, blocks, sizes, collective):
    if collective is None:
        return lax.all_gather(row, AXES, axis=0), lax.all_to_all(blocks, PLANE, 0, 0)
    return begin(row, blocks, sizes, collective)


def gather_weights(shards, pieces, lines, axes, sizes, collective, rows):
    if collective is None:
        fulls = [lax.all_gather(shard, AXES, axis=0) for shard in shards]
        line_fulls = [
            lax.all_gather(line, "dp", axis=axis) for line, axis in zip(lines, axes)
        ]
        arrived = lax.all_to_all(rows, AXES, 0, 0)
    else:
        *fulls, arrived = gather_all(shards, pieces, sizes, collective, rows, lines, axes)
        fulls, line_fulls = fulls[: len(shards)], fulls[len(shards) :]
    return [full.reshape(-1, full.shape[-1]) for full in fulls], line_fulls, arrived


def gather_rows(shard, sizes, collective, cuts):
    if collective is None:
        axes = AXES if sizes[2] > 1 else PLANE
        return lax.all_gather(shard, axes, axis=0, tiled=True)
    (full,) = gather_all([shard], even_pieces(0, shard.shape[0], cuts), sizes, collective)
    return full.reshape(-1, full.shape[-1])


def sum_rows(partial, sizes, collective, cuts):
    if collective is None:
        axes = AXES if sizes[2] > 1 else PLANE
        total = lax.psum_scatter(partial, axes, scatter_dimension=0, tiled=True)
        return total.astype(jnp.float32)
    shaped = partial.reshape(sizes + (-1, partial.shape[1]))
    size = shaped.shape[3] // cuts
    return reduce_all(shaped, [(i * size, size) for i in range(cuts)], sizes, collective)


def sum_chips(lefts, rights, start, talls, small, rows, blocks, sizes, collective):
    if collective is not None:
        small = small.reshape(sizes + (-1, small.shape[1]))
        *sums, rows, blocks = finish_all(
            lefts, rights, start, talls, small, rows, blocks, sizes, collective
        )
        return sums, rows, blocks
    made = [chip_sum(left, right) for left, right in zip(lefts, rights)]
    made += [left_transposed(start, both_cores(tall)).astype(jnp.bfloat16) for tall in talls]
    partials = made[:2] + [chip_half(small)] + made[2:]
    sums = [
        lax.psum_scatter(p, CHIPS, scatter_dimension=0, tiled=True).astype(jnp.float32)
        for p in partials
    ]
    sums = sums[:3] + [jnp.concatenate(sums[3:], 1)]
    rows = lax.all_to_all(rows, AXES, 0, 0)
    blocks = lax.all_to_all(blocks, PLANE, 0, 0)
    return sums, rows, blocks


def line_shift(shard, step):
    size = lax.axis_size("dp")
    return lax.ppermute(shard, "dp", [(i, (i + step) % size) for i in range(size)])


def line_sum(partial, collective):
    partial = partial.astype(jnp.bfloat16)
    if collective is None:
        total = lax.psum_scatter(partial, "dp", scatter_dimension=0, tiled=False)
        return total.astype(jnp.float32)
    size = lax.axis_size("dp")
    me = lax.axis_index("dp")

    def entry(step):
        return lax.dynamic_index_in_dim(partial, (me + step) % size, 0, keepdims=False)

    total = entry(0).astype(jnp.float32)
    for step in range(1, size):
        total = total + line_shift(entry(step), step).astype(jnp.float32)
    return total


def spread_row(row, sizes, collective):
    if collective is None:
        return lax.all_gather(row, AXES, axis=0)
    return spread(row, sizes, collective)


def output_layer(row, table, bias, labels, weights, rows_per, vocab, sizes, collective):
    parts = math.prod(sizes)
    if collective is not None:
        bias = jnp.pad(bias, (0, table.shape[0] - rows_per))[None]
        info = jnp.stack([labels.astype(jnp.float32), weights]).reshape(2, parts, -1)
        info = jnp.pad(info.swapaxes(0, 1), ((0, 0), (0, 6), (0, 0)))
        grad, word, d_bias, stats = head_all(
            row, table, bias, info, rows_per, vocab, sizes, collective
        )
        stats = [stats[:, i].reshape(-1) for i in range(3)]
        return grad, word, d_bias[0, :rows_per], stats
    rows = gather_rows(row, sizes, None, 1)
    cells = jnp.arange(table.shape[0], dtype=jnp.int32)
    column = lax.axis_index(AXES) * rows_per + cells
    column = jnp.where((cells < rows_per) & (column < vocab), column, -1)
    bias = jnp.pad(bias, (0, table.shape[0] - rows_per))
    logits = jnp.where(column >= 0, right_transposed(rows, table) + bias, -1e30)
    own_peak = jnp.max(logits, -1)
    own_total = jnp.sum(jnp.exp(logits - own_peak[:, None]), -1)
    hits = labels[:, None] == column
    own_label = jnp.sum(jnp.where(hits, logits, 0.0), -1)
    peak = lax.pmax(own_peak, AXES)
    total, label = lax.psum((own_total * jnp.exp(own_peak - peak), own_label), AXES)
    slopes = weights[:, None] * (
        jnp.exp(logits - peak[:, None]) / total[:, None] - hits.astype(jnp.float32)
    )
    low = slopes.astype(jnp.bfloat16)
    grad = sum_rows(matmul(low, table).astype(jnp.bfloat16), sizes, None, 1)
    return grad, left_transposed(low, rows), jnp.sum(slopes, 0)[:rows_per], (peak, total, label)


def adam_step(weight, first, second, grad, factor, rate):
    clipped = grad * factor
    first = beta_one * first + (1.0 - beta_one) * clipped
    second = beta_two * second + (1.0 - beta_two) * clipped * clipped
    first_hat = first / (1.0 - beta_one**STEP)
    second_hat = second / (1.0 - beta_two**STEP)
    weight = weight - rate * (first_hat / (jnp.sqrt(second_hat) + epsilon) + weight_decay * weight)
    return (weight, first, second)


def per_device(
    token_ids,
    lengths,
    masked_at,
    labels,
    word_table,
    word_first,
    word_second,
    pos_table,
    pos_first,
    pos_second,
    qkv_weight,
    qkv_first,
    qkv_second,
    square_weight,
    square_first,
    square_second,
    up_weight,
    up_first,
    up_second,
    down_weight,
    down_first,
    down_second,
    vec_table,
    vec_first,
    vec_second,
    head_bias,
    bias_first,
    bias_second,
):
    narrow = jnp.bfloat16
    seq_len, slots = token_ids.shape[1], masked_at.shape[1]
    width = word_table.shape[1]
    vocab = head_bias.shape[0]
    rows_per = word_table.shape[0]
    parts = lax.axis_size(AXES)
    halves = lax.axis_size("pipe")
    me = lax.axis_index(AXES)
    own = token_ids.shape[0] // halves
    first_own = lax.axis_index("pipe") * own
    head_dim = width // H
    sizes = tuple(lax.axis_size(axis) for axis in AXES)
    shards = (word_table, qkv_weight, square_weight[0], up_weight, down_weight)
    direct = sizes[:2] == (2, 4) and all(shard.shape[0] % 32 == 0 for shard in shards)
    ids = tuple(range(11)) if direct else (None,) * 11
    plane_sizes = sizes[:2] + (1,)

    spare = -(seq_len + slots + 1) % 128
    packed = jnp.concatenate(
        [token_ids, labels, lengths[:, None], jnp.zeros((token_ids.shape[0], spare), jnp.int32)], 1
    )
    packed = lax.dynamic_slice_in_dim(packed, first_own, own, 0)
    planes = sizes[0] * sizes[1]
    units = up_weight.shape[1] // planes
    cut = me // sizes[2]
    blocks = up_weight.astype(narrow).reshape(up_weight.shape[0], planes, units).swapaxes(0, 1)
    packed, blocks = start_all(packed, blocks, sizes, ids[0])
    all_ids = packed[:, :, :seq_len]
    all_labels = packed[:, :, seq_len : seq_len + slots].reshape(-1)
    all_lengths = packed[:, :, seq_len + slots]
    places = jnp.arange(seq_len, dtype=jnp.int32)
    all_live = places[None, None, :] < all_lengths[:, :, None]
    all_counts = masked_counts(all_lengths, slots)
    total = jnp.sum(all_counts).astype(jnp.float32)
    slot_index = jnp.arange(slots, dtype=jnp.int32)
    all_valid = (slot_index < all_counts[:, :, None]).astype(jnp.float32).reshape(-1)
    own_lengths = lax.dynamic_slice_in_dim(lengths, first_own, own, 0)
    masked = lax.dynamic_slice_in_dim(masked_at, first_own, own, 0)

    cells = rows_per + -rows_per % 128
    word_low = jnp.pad(word_table.astype(narrow), ((0, cells - rows_per), (0, 0)))
    routes = Routes(all_ids.reshape(parts, -1), all_live.reshape(parts, -1), rows_per)
    small = pos_table.shape[0] + vec_table.shape[0]
    spare = -small % 128
    small_low = jnp.concatenate(
        [pos_table.T, vec_table.T, jnp.zeros((pos_table.shape[1], spare), jnp.float32)], 1
    ).astype(narrow)
    low = [
        small_low,
        qkv_weight.astype(narrow),
        square_weight[0].astype(narrow),
        square_weight[1].astype(narrow),
    ]
    deep = small_low.shape[0]
    pieces = [(0, 0, deep), (1, 0, deep // 2), (1, deep // 2, deep // 2), (2, 0, deep), (3, 0, deep)]
    send = routes.table_rows(word_low, 0, routes.room).reshape(parts, -1, width)
    (small_full, qkv_low, out_low, turn_low), (up_low, down_low), arrived = gather_weights(
        low, pieces, [blocks, down_weight.astype(narrow)], [1, 0], sizes, ids[1], send
    )
    up_low = up_low.reshape(width, units)
    down_low = down_low.reshape(units, width)
    word_rows = routes.fetch(word_low, arrived.reshape(-1, width))
    small_full = small_full.T
    pos_low = small_full[:seq_len]
    vec_rows = small_full[seq_len:small].astype(jnp.float32)
    query_low, both_low = qkv_low[:, :width], qkv_low[:, width:]

    second = (places[None, :] >= ((own_lengths + 1) // 2)[:, None]).reshape(-1, 1)
    embedded = (
        word_rows
        + jnp.tile(pos_low.astype(jnp.float32), (own, 1))
        + jnp.where(second, vec_rows[1], vec_rows[0])
    )
    start, norm_zero = norm_forward(embedded, vec_rows[2], vec_rows[3])
    start_low = start.astype(narrow)
    both_bias = jnp.concatenate([jnp.zeros_like(vec_rows[5]), vec_rows[5]])
    both = (matmul(start_low, both_low) + both_bias).astype(narrow)
    pick = one_hot(masked, seq_len, jnp.float32)
    chosen = rows_by_seq(pick, start.reshape(own, seq_len, width)).reshape(-1, width)
    chosen_low = chosen.astype(narrow)
    start_half = both_halves(start_low)
    queries = (matmul(chosen_low, query_low) + vec_rows[4]).astype(narrow)
    context = attention(own_lengths, queries, both)
    context, start_half = lax.optimization_barrier((context, start_half))
    branch = matmul(context, out_low) + vec_rows[6]
    hidden, norm_one = norm_forward(chosen + branch, vec_rows[7], vec_rows[8])
    hidden = hidden.astype(narrow)

    plane_hidden = gather_rows(hidden, plane_sizes, ids[2], 2)
    up_bias = lax.dynamic_slice_in_dim(vec_rows[15:].reshape(-1), cut * units, units, 0)
    inner = matmul(plane_hidden, up_low) + up_bias
    activ = jax.nn.gelu(inner, approximate=False).astype(narrow)
    branch = sum_rows(matmul(activ, down_low).astype(narrow), plane_sizes, ids[3], 2) + vec_rows[9]
    mixed, norm_two = norm_forward(hidden.astype(jnp.float32) + branch, vec_rows[10], vec_rows[11])
    picked = mixed.astype(narrow)
    turned = matmul(picked, turn_low) + vec_rows[12]
    normed, norm_head = norm_forward(
        jax.nn.gelu(turned, approximate=False), vec_rows[13], vec_rows[14]
    )

    bias_row = jnp.pad(head_bias, (0, parts * rows_per - vocab))
    bias_row = lax.dynamic_slice_in_dim(bias_row, me * rows_per, rows_per, 0)
    d_normed, d_word, d_bias, (peak, exp_total, label_logit) = output_layer(
        normed.astype(narrow),
        word_low,
        bias_row,
        all_labels,
        all_valid / total,
        rows_per,
        vocab,
        sizes,
        ids[4],
    )
    loss_total = jnp.sum(all_valid * (peak + jnp.log(exp_total) - label_logit))

    d_gelu, d_gain_head, d_shift_head = norm_backward(d_normed, norm_head, vec_rows[13])
    d_turned = (d_gelu * gelu_slope(turned)).astype(narrow)
    d_turn_bias = jnp.sum(d_turned.astype(jnp.float32), 0)
    d_picked = right_transposed(d_turned, turn_low)
    same = masked[:, :, None] == masked[:, None, :]
    earlier = slot_index[None, :] < slot_index[:, None]
    first_slot = jnp.logical_not(jnp.any(same & earlier, 2))
    merge = (same & first_slot[:, :, None]).astype(jnp.float32)
    d_mixed = rows_by_seq(merge, d_picked.reshape(own, slots, width)).reshape(-1, width)
    d_pre, d_gain_two, d_shift_two = norm_backward(d_mixed, norm_two, vec_rows[10])
    d_branch = d_pre.astype(narrow)
    d_down_bias = jnp.sum(d_branch.astype(jnp.float32), 0)
    plane_branch = gather_rows(d_branch, plane_sizes, ids[7], 2)
    d_down = left_transposed(activ, plane_branch).astype(narrow)
    d_inner = (right_transposed(plane_branch, down_low) * gelu_slope(inner)).astype(narrow)
    d_up_bias = jnp.sum(d_inner.astype(jnp.float32), 0)
    d_up_bias = lax.dynamic_update_slice_in_dim(
        jnp.zeros((planes * units,), jnp.float32), d_up_bias, cut * units, 0
    ).reshape(-1, width)
    d_up = left_transposed(plane_hidden, d_inner).astype(narrow)
    d_hidden = sum_rows(right_transposed(d_inner, up_low).astype(narrow), plane_sizes, ids[8], 2)
    d_hidden = (d_pre + d_hidden).astype(narrow)

    d_hidden, d_down, d_up = lax.optimization_barrier((d_hidden, d_down, d_up))
    own_down = line_sum(d_down.reshape(sizes[2], -1, width), ids[7])
    d_up = d_up.reshape(planes, sizes[2], -1, units).swapaxes(0, 1)
    up_blocks = line_sum(d_up, ids[7]).astype(narrow)
    d_pre, d_gain_one, d_shift_one = norm_backward(
        d_hidden.astype(jnp.float32), norm_one, vec_rows[7]
    )
    d_branch = d_pre.astype(narrow)
    d_out_bias = jnp.sum(d_branch.astype(jnp.float32), 0)
    d_attended = d_branch
    d_context = right_transposed(d_branch, out_low).astype(narrow)
    d_query, d_key, d_value = attention(own_lengths, queries, both, d_context)
    d_query_bias = jnp.sum(d_query.astype(jnp.float32), 0)
    d_value_bias = jnp.sum(d_value.astype(jnp.float32), 0)
    d_chosen = d_pre + right_transposed(d_query, query_low)
    d_both = jnp.concatenate([d_key, d_value], 1)
    d_start = right_transposed(d_both, both_low) + rows_to_seq(
        pick, d_chosen.reshape(own, slots, width)
    ).reshape(-1, width)
    d_embedded, d_gain_zero, d_shift_zero = norm_backward(d_start, norm_zero, vec_rows[2])
    d_seg_zero = jnp.sum(jnp.where(second, 0.0, d_embedded), 0)
    d_seg_one = jnp.sum(jnp.where(second, d_embedded, 0.0), 0)
    d_embedded_low = d_embedded.astype(narrow)
    send = routes.token_rows(d_embedded_low, 0, routes.room).reshape(parts, -1, width)
    d_small = jnp.concatenate(
        [
            jnp.sum(d_embedded.reshape(own, seq_len, width), 0),
            jnp.stack(
                [
                    d_seg_zero,
                    d_seg_one,
                    d_gain_zero,
                    d_shift_zero,
                    d_query_bias,
                    d_value_bias,
                    d_out_bias,
                    d_gain_one,
                    d_shift_one,
                    d_down_bias,
                    d_gain_two,
                    d_shift_two,
                    d_turn_bias,
                    d_gain_head,
                    d_shift_head,
                ]
            ),
            d_up_bias,
            jnp.zeros((spare, width), jnp.float32),
        ],
        0,
    )
    (own_out, own_turn, own_small, own_qkv), arrived, up_blocks = sum_chips(
        [context, picked, chosen_low],
        [d_attended, d_turned, d_query],
        start_half,
        [d_key, d_value],
        d_small.T.astype(narrow),
        send,
        up_blocks,
        sizes,
        ids[9],
    )
    own_up = up_blocks.swapaxes(0, 1).reshape(up_weight.shape).astype(jnp.float32)
    d_word = routes.give(d_embedded_low, arrived.reshape(-1, width), d_word)[:rows_per]
    owned = (
        d_word,
        own_small[:, :seq_len].T,
        own_qkv,
        jnp.stack([own_out, own_turn]),
        own_up,
        own_down,
        own_small[:, seq_len:small].T,
    )
    local_squares = jnp.sum(d_bias * d_bias)
    for grad in owned:
        local_squares = local_squares + jnp.sum(grad * grad)
    spare = -(rows_per + 1) % 128
    last = jnp.concatenate([d_bias, local_squares[None], jnp.zeros((spare,), jnp.float32)])
    last = spread_row(last.reshape(8, -1), sizes, ids[10]).reshape(parts, -1)
    bias_grad = last[:, :rows_per].reshape(-1)[:vocab]
    grad_norm = jnp.sqrt(jnp.sum(last[:, rows_per]))
    factor = clip_norm / jnp.maximum(grad_norm, clip_norm)
    masters = (
        word_table,
        pos_table,
        qkv_weight,
        square_weight,
        up_weight,
        down_weight,
        vec_table,
        head_bias,
    )
    states = (
        (word_first, word_second),
        (pos_first, pos_second),
        (qkv_first, qkv_second),
        (square_first, square_second),
        (up_first, up_second),
        (down_first, down_second),
        (vec_first, vec_second),
        (bias_first, bias_second),
    )
    rates = (
        learn_rate,
        learn_rate,
        learn_rate,
        learn_rate,
        learn_rate,
        learn_rate,
        vector_rate,
        vector_rate,
    )
    grads = tuple(owned) + (bias_grad,)
    results = []
    for weight, state, grad, rate in zip(masters, states, grads, rates):
        results.extend(adam_step(weight, state[0], state[1], grad, factor, rate))
    return (
        results[0],
        results[1],
        results[2],
        results[3],
        results[4],
        results[5],
        results[6],
        results[7],
        results[8],
        results[9],
        results[10],
        results[11],
        results[12],
        results[13],
        results[14],
        results[15],
        results[16],
        results[17],
        results[18],
        results[19],
        results[20],
        results[21],
        results[22],
        results[23],
        loss_total,
        total,
        grad_norm,
    )


def solution(mesh):
    placed = (
        P(("grp", "dp"), None),
        P(("grp", "dp")),
        P(("grp", "dp"), None),
        P(("grp", "dp"), None),
        P(("pipe", "grp", "dp"), None),
        P(("pipe", "grp", "dp"), None),
        P(("pipe", "grp", "dp"), None),
        P(None, ("pipe", "grp", "dp")),
        P(None, ("pipe", "grp", "dp")),
        P(None, ("pipe", "grp", "dp")),
        P(("pipe", "grp", "dp"), None),
        P(("pipe", "grp", "dp"), None),
        P(("pipe", "grp", "dp"), None),
        P(None, ("pipe", "grp", "dp"), None),
        P(None, ("pipe", "grp", "dp"), None),
        P(None, ("pipe", "grp", "dp"), None),
        P(("pipe", "grp", "dp"), None),
        P(("pipe", "grp", "dp"), None),
        P(("pipe", "grp", "dp"), None),
        P(("pipe", "grp", "dp"), None),
        P(("pipe", "grp", "dp"), None),
        P(("pipe", "grp", "dp"), None),
        P(None, ("pipe", "grp", "dp")),
        P(None, ("pipe", "grp", "dp")),
        P(None, ("pipe", "grp", "dp")),
        P(),
        P(),
        P(),
    )
    return jax.shard_map(
        per_device,
        mesh=mesh,
        in_specs=placed,
        out_specs=(
            P(("pipe", "grp", "dp"), None),
            P(("pipe", "grp", "dp"), None),
            P(("pipe", "grp", "dp"), None),
            P(None, ("pipe", "grp", "dp")),
            P(None, ("pipe", "grp", "dp")),
            P(None, ("pipe", "grp", "dp")),
            P(("pipe", "grp", "dp"), None),
            P(("pipe", "grp", "dp"), None),
            P(("pipe", "grp", "dp"), None),
            P(None, ("pipe", "grp", "dp"), None),
            P(None, ("pipe", "grp", "dp"), None),
            P(None, ("pipe", "grp", "dp"), None),
            P(("pipe", "grp", "dp"), None),
            P(("pipe", "grp", "dp"), None),
            P(("pipe", "grp", "dp"), None),
            P(("pipe", "grp", "dp"), None),
            P(("pipe", "grp", "dp"), None),
            P(("pipe", "grp", "dp"), None),
            P(None, ("pipe", "grp", "dp")),
            P(None, ("pipe", "grp", "dp")),
            P(None, ("pipe", "grp", "dp")),
            P(),
            P(),
            P(),
            P(),
            P(),
            P(),
        ),
        check_vma=False,
    )
```

```python
import functools
import math

import jax
import jax.numpy as jnp
from jax import lax
from jax.experimental import pallas as pl
from jax.experimental.pallas import tpu as pltpu
from jax.sharding import PartitionSpec as P

H = 16
STEP = 10


beta_one = 0.9
beta_two = 0.999
learn_rate = 0.02
vector_rate = 0.2
weight_decay = 0.01
epsilon = 1e-08
clip_norm = 0.02
norm_eps = 1e-05
root_half = 0.7071067811865476
density_scale = 0.3989422804014327
AXES = ("pipe", "grp", "dp")
CHIPS = ("grp", "dp")
PLANE = ("pipe", "grp")
highest = lax.Precision.HIGHEST


def matmul(left, right):
    return jnp.dot(left, right, preferred_element_type=jnp.float32)


def left_transposed(left, right):
    return lax.dot_general(
        left, right, (((0,), (0,)), ((), ())), preferred_element_type=jnp.float32
    )


def right_transposed(left, right):
    return lax.dot_general(
        left, right, (((1,), (1,)), ((), ())), preferred_element_type=jnp.float32
    )


def norm_forward(values, gain, shift):
    center = values - jnp.mean(values, -1, keepdims=True)
    scale = lax.rsqrt(jnp.mean(center * center, -1, keepdims=True) + norm_eps)
    normal = center * scale
    return (normal * gain + shift, (normal, scale))


def norm_backward(grad, kept, gain):
    normal, scale = kept
    d_gain = jnp.sum(grad * normal, 0)
    d_shift = jnp.sum(grad, 0)
    d_norm = grad * gain
    d_input = scale * (
        d_norm
        - jnp.mean(d_norm, -1, keepdims=True)
        - normal * jnp.mean(d_norm * normal, -1, keepdims=True)
    )
    return (d_input, d_gain, d_shift)


def gelu_slope(values):
    return (
        0.5 * (1.0 + lax.erf(values * root_half))
        + values * jnp.exp(-0.5 * values * values) * density_scale
    )


def masked_counts(lengths, slots):
    return jnp.minimum(slots, (3 * lengths + 19) // 20)


def one_hot(indices, size, dtype):
    places = lax.broadcasted_iota(jnp.int32, indices.shape + (size,), indices.ndim)
    return (indices[..., None] == places).astype(dtype)


def rows_by_seq(pick, rows):
    return jnp.einsum("sjp,spw->sjw", pick, rows, precision=highest)


def rows_to_seq(pick, rows):
    return jnp.einsum("sjp,sjw->spw", pick, rows, precision=highest)


class Routes:
    def __init__(self, all_ids, all_live, rows_per):
        self.parts, tokens = all_ids.shape
        self.cells = rows_per + -rows_per % 128
        self.me = lax.axis_index(AXES)
        mean = tokens / self.parts
        self.room = max(16, int(math.ceil((mean + 2.8 * math.sqrt(mean)) / 16)) * 16)
        owners = jnp.where(all_live, all_ids // rows_per, -1)
        counts = jnp.sum(one_hot(owners, self.parts, jnp.int32), 1)
        self.more = 16
        self.rounds = (jnp.maximum(jnp.max(counts) - self.room, 0) + self.more - 1) // self.more
        mine = owners == self.me
        order = jnp.arange(tokens, dtype=jnp.int32)
        upto = (order[:, None] <= order[None, :]).astype(jnp.bfloat16)
        ranks = matmul(mine.astype(jnp.bfloat16), upto).astype(jnp.int32)
        self.out_rank = jnp.where(mine, ranks - 1, -1)
        self.out_row = all_ids - self.me * rows_per
        own_owners = lax.dynamic_index_in_dim(owners, self.me, 0, keepdims=False)
        hits = one_hot(own_owners, self.parts, jnp.bfloat16)
        ranks = jnp.sum(hits.astype(jnp.float32) * left_transposed(upto, hits), 1)
        ranks = ranks.astype(jnp.int32) - 1
        self.in_rank = ranks
        self.in_owner = own_owners

    def owner_pick(self, first, room):
        slots = first + jnp.arange(room, dtype=jnp.int32)
        at = self.out_rank[:, None, :] == slots[None, :, None]
        row = jnp.sum(jnp.where(at, self.out_row[:, None, :] + 1, 0), 2) - 1
        return one_hot(row.reshape(-1), self.cells, jnp.bfloat16)

    def token_pick(self, first, room):
        rank = self.in_rank - first
        inside = (self.in_owner >= 0) & (rank >= 0) & (rank < room)
        slot = jnp.where(inside, self.in_owner * room + rank, -1)
        return one_hot(slot, self.parts * room, jnp.bfloat16)

    def exchange(self, rows):
        shaped = rows.reshape(self.parts, -1, rows.shape[-1])
        return lax.all_to_all(shaped, AXES, 0, 0).reshape(rows.shape)

    def table_rows(self, table, first, room):
        return matmul(self.owner_pick(first, room), table).astype(jnp.bfloat16)

    def token_rows(self, rows, first, room):
        return left_transposed(self.token_pick(first, room), rows).astype(jnp.bfloat16)

    def later(self, more, start):
        def one(turn, kept):
            return kept + more(self.room + turn * self.more)

        return lax.fori_loop(0, self.rounds, one, start)

    def fetch(self, table, arrived):
        def more(first):
            rows = self.exchange(self.table_rows(table, first, self.more))
            return matmul(self.token_pick(first, self.more), rows)

        return self.later(more, matmul(self.token_pick(0, self.room), arrived))

    def give(self, rows, arrived, start):
        def more(first):
            back = self.exchange(self.token_rows(rows, first, self.more))
            return left_transposed(self.owner_pick(first, self.more), back)

        start = start + left_transposed(self.owner_pick(0, self.room), arrived)
        return self.later(more, start)


def swapped(shard):
    return lax.ppermute(shard, "pipe", [(0, 1), (1, 0)])


def both_cores(rows):
    return jnp.concatenate([rows, swapped(rows)], 0)


def half_columns(rows, index):
    half = rows.shape[1] // 2
    return lax.dynamic_slice_in_dim(rows, index * half, half, 1)


def both_halves(rows):
    pipe = lax.axis_index("pipe")
    return half_columns(rows, pipe), swapped(half_columns(rows, 1 - pipe))


def chip_sum(left, right):
    left = jnp.concatenate(both_halves(left), 0)
    return left_transposed(left, both_cores(right)).astype(jnp.bfloat16)


def chip_half(partial):
    half = partial.shape[0] // 2
    pipe = lax.axis_index("pipe")
    partial = partial.astype(jnp.bfloat16)
    keep = lax.dynamic_slice_in_dim(partial, pipe * half, half, 0)
    give = lax.dynamic_slice_in_dim(partial, (1 - pipe) * half, half, 0)
    return (keep.astype(jnp.float32) + swapped(give).astype(jnp.float32)).astype(jnp.bfloat16)


def lasting(microseconds):
    return pl.CostEstimate(
        flops=int(microseconds * 9e8), bytes_accessed=int(microseconds * 3e6), transcendentals=0
    )


def device(pipe, grp, dp):
    return {"pipe": pipe, "grp": grp, "dp": dp}


def remote(source, target, send, arrive, to):
    return pltpu.make_async_remote_copy(
        src_ref=source,
        dst_ref=target,
        send_sem=send,
        recv_sem=arrive,
        device_id=device(*to),
        device_id_type=pl.DeviceIdType.MESH,
    )


def tell(barrier, to):
    pl.semaphore_signal(
        barrier, inc=1, device_id=device(*to), device_id_type=pl.DeviceIdType.MESH
    )


def greet(others):
    barrier = pltpu.get_barrier_semaphore()
    for to in others:
        tell(barrier, to)
    pl.semaphore_wait(barrier, len(others))


class Place:
    def __init__(self, sizes):
        self.pipes, self.grps, self.dps = sizes
        self.plane_only = self.dps == 1
        self.pipe, self.grp, self.dp = [lax.axis_index(axis) for axis in AXES]
        column, row = self.grp % 2, self.grp // 2
        self.beside = 2 * row + 1 - column
        self.below = 2 * (1 - row) + column
        self.across = 3 - self.grp

    @property
    def spot(self):
        return 0 if self.plane_only else self.dp

    def plane(self):
        found = []
        for a in range(self.pipes):
            for b in range(self.grps):
                if (a, b) != (0, 0):
                    ahead = ((self.pipe + a) % self.pipes, (self.grp + b) % self.grps)
                    back = (
                        (self.pipe + self.pipes - a) % self.pipes,
                        (self.grp + self.grps - b) % self.grps,
                    )
                    found.append((ahead, back))
        return found

    def line(self, step):
        return (self.dp + step) % self.dps

    def behind(self, step):
        return (self.dp + self.dps - step) % self.dps

    def others(self):
        found = []
        for a in range(self.pipes):
            for b in range(self.grps):
                for c in range(self.dps):
                    if (a, b, c) != (0, 0, 0):
                        ahead = (
                            (self.pipe + a) % self.pipes,
                            (self.grp + b) % self.grps,
                            (self.dp + c) % self.dps,
                        )
                        back = (
                            (self.pipe + self.pipes - a) % self.pipes,
                            (self.grp + self.grps - b) % self.grps,
                            (self.dp + self.dps - c) % self.dps,
                        )
                        found.append((ahead, back))
        return found

    def index(self, pipe, grp, dp):
        return (pipe * self.grps + grp) * self.dps + dp


def swap_all(place, rows, arrived, send, arrive, own):
    me = place.index(place.pipe, place.grp, place.dp)
    copies = []
    for i, (ahead, back) in enumerate(place.others()):
        to = place.index(*ahead)
        copies.append(remote(rows.at[to], arrived.at[me], send.at[i], arrive.at[i], ahead))
        copies[-1].start()
    kept = pltpu.make_async_copy(rows.at[me], arrived.at[me], own)
    kept.start()

    def finish():
        for i, (ahead, back) in enumerate(place.others()):
            origin = place.index(*back)
            copies[i].wait_send()
            remote(rows.at[me], arrived.at[origin], send.at[i], arrive.at[i], ahead).wait_recv()
        kept.wait()

    return finish


def swap_plane(place, rows, arrived, send, arrive, own):
    me = place.pipe * place.grps + place.grp
    copies = []
    for i, (ahead, back) in enumerate(place.plane()):
        to = ahead[0] * place.grps + ahead[1]
        copies.append(
            remote(rows.at[to], arrived.at[me], send.at[i], arrive.at[i], ahead + (place.dp,))
        )
        copies[-1].start()
    kept = pltpu.make_async_copy(rows.at[me], arrived.at[me], own)
    kept.start()

    def finish():
        for i, (ahead, back) in enumerate(place.plane()):
            origin = back[0] * place.grps + back[1]
            copies[i].wait_send()
            remote(
                rows.at[me], arrived.at[origin], send.at[i], arrive.at[i], ahead + (place.dp,)
            ).wait_recv()
        kept.wait()

    return finish


def begin_kernel(sizes, row_ref, up_ref, all_ref, arrived_ref, *sems):
    send, arrive, own, plane_send, plane_arrive, plane_own = sems
    place = Place(sizes)
    others = place.others()
    greet([ahead for ahead, _ in others])
    finish = swap_plane(place, up_ref, arrived_ref, plane_send, plane_arrive, plane_own)
    me = place.index(place.pipe, place.grp, place.dp)
    copies = []
    for i, (ahead, _) in enumerate(others):
        copies.append(remote(row_ref, all_ref.at[me], send.at[i], arrive.at[i], ahead))
        copies[-1].start()
    kept = pltpu.make_async_copy(row_ref, all_ref.at[me], own)
    kept.start()
    for i, (ahead, back) in enumerate(others):
        copies[i].wait_send()
        remote(
            row_ref, all_ref.at[place.index(*back)], send.at[i], arrive.at[i], ahead
        ).wait_recv()
    kept.wait()
    finish()


def begin(row, blocks, sizes, collective):
    parts = math.prod(sizes)
    sems = pltpu.SemaphoreType.DMA((parts - 1,))
    plane_sems = pltpu.SemaphoreType.DMA((sizes[0] * sizes[1] - 1,))
    return pl.pallas_call(
        functools.partial(begin_kernel, sizes),
        out_shape=(
            jax.ShapeDtypeStruct((parts,) + row.shape, row.dtype),
            jax.ShapeDtypeStruct(blocks.shape, blocks.dtype),
        ),
        in_specs=[pl.BlockSpec(memory_space=pltpu.VMEM)] * 2,
        out_specs=[pl.BlockSpec(memory_space=pltpu.VMEM)] * 2,
        scratch_shapes=[
            sems,
            sems,
            pltpu.SemaphoreType.DMA,
            plane_sems,
            plane_sems,
            pltpu.SemaphoreType.DMA,
        ],
        compiler_params=pltpu.CompilerParams(
            collective_id=collective, has_side_effects=True, vmem_limit_bytes=8 << 20
        ),
    )(row, blocks)


def spread_kernel(sizes, row_ref, all_ref, send, arrive, own):
    place = Place(sizes)
    others = place.others()
    greet([ahead for ahead, _ in others])
    me = place.index(place.pipe, place.grp, place.dp)
    copies = []
    for i, (ahead, _) in enumerate(others):
        copies.append(remote(row_ref, all_ref.at[me], send.at[i], arrive.at[i], ahead))
        copies[-1].start()
    kept = pltpu.make_async_copy(row_ref, all_ref.at[me], own)
    kept.start()
    for i, (ahead, back) in enumerate(others):
        copies[i].wait_send()
        remote(
            row_ref, all_ref.at[place.index(*back)], send.at[i], arrive.at[i], ahead
        ).wait_recv()
    kept.wait()


def spread(row, sizes, collective):
    parts = math.prod(sizes)
    sems = pltpu.SemaphoreType.DMA((parts - 1,))
    return pl.pallas_call(
        functools.partial(spread_kernel, sizes),
        out_shape=jax.ShapeDtypeStruct((parts,) + row.shape, row.dtype),
        in_specs=[pl.BlockSpec(memory_space=pltpu.VMEM)],
        out_specs=pl.BlockSpec(memory_space=pltpu.VMEM),
        scratch_shapes=[sems, sems, pltpu.SemaphoreType.DMA],
        compiler_params=pltpu.CompilerParams(
            collective_id=collective, has_side_effects=True, vmem_limit_bytes=8 << 20
        ),
    )(row)


class Gather:
    def __init__(self, place, pieces, shards, fulls, send, arrive, own):
        self.place, self.pieces, self.shards, self.fulls = place, pieces, shards, fulls
        self.send, self.arrive, self.own = send, arrive, own
        pipe, grp, dp = place.pipe, place.grp, place.dp
        self.near = place.beside * (1 - pipe) + place.below * pipe
        self.far = place.below * (1 - pipe) + place.beside * pipe
        self.core = (1 - pipe, grp, dp)
        self.hops = place.dps - 1
        self.ends = (dp < self.hops, dp > 0)
        self.sides = ((pipe, grp, dp + 1), (pipe, grp, dp - 1))
        self.both = range(2 if self.hops else 0)
        self.waits, self.keeps = [], {}
        self.stages = [functools.partial(self.over_line, hop=hop) for hop in range(self.hops)]
        self.stages += [self.over_plane, self.pass_on, self.last]

    def partners(self):
        place = self.place
        pipe, grp, dp = place.pipe, place.grp, place.dp
        line = [(pipe, grp, place.line(k + 1)) for k in range(self.hops)]
        return line + [(pipe, self.near, dp), (pipe, self.far, dp), self.core]

    def view(self, n, *at):
        array, first, rows = self.pieces[n]
        return self.fulls[array].at[at + ((slice(None),) * (3 - len(at))) + (pl.ds(first, rows),)]

    def shard(self, n):
        array, first, rows = self.pieces[n]
        return self.shards[array].at[pl.ds(first, rows)]

    def launch(self, n, index, source, to, *at):
        copy = remote(
            source, self.view(n, *at), self.send.at[n, index], self.arrive.at[n, index], to
        )
        copy.start()
        self.waits.append(copy)

    def landed(self, n, index, *at):
        target = self.view(n, *at)
        remote(
            target, target, self.send.at[n, index], self.arrive.at[n, index], self.core
        ).wait_recv()

    def along(self, n, side, hop, finish=False):
        place, hops = self.place, self.hops
        origin = place.dp - hop if side == 0 else place.dp + hop
        here = origin >= 0 if side == 0 else origin <= hops
        index = side * hops + hop

        def copy():
            target = self.view(n, place.pipe, place.grp, origin)
            source = self.shard(n) if hop == 0 else target
            return remote(
                source, target, self.send.at[n, index], self.arrive.at[n, index], self.sides[side]
            )

        if finish:

            @pl.when(here & self.ends[side])
            def _():
                copy().wait_send()

            return
        if hop > 0:

            @pl.when(here)
            def _():
                self.landed(n, index - 1, place.pipe, place.grp, origin)

        if hop < hops:

            @pl.when(here & self.ends[side])
            def _():
                copy().start()

    def over_line(self, n, hop):
        place = self.place
        if hop == 0:
            target = self.view(n, place.pipe, place.grp, place.spot)
            self.keeps[n] = pltpu.make_async_copy(self.shard(n), target, self.own.at[n])
            self.keeps[n].start()
        for side in self.both:
            self.along(n, side, hop)

    def over_plane(self, n):
        place, first = self.place, 2 * self.hops
        pipe, grp, dp = place.pipe, place.grp, place.dp
        self.over_line(n, self.hops)
        if self.hops:
            self.keeps[n].wait()
            group, at = self.view(n, pipe, grp), (pipe, grp)
        else:
            group, at = self.shard(n), (pipe, grp, 0)
        self.launch(n, first, group, (pipe, self.near, dp), *at)
        self.launch(n, first + 1, group, (pipe, self.far, dp), *at)
        self.launch(n, first + 3, group, self.core, *at)

    def pass_on(self, n):
        pipe, first = self.place.pipe, 2 * self.hops
        self.landed(n, first, pipe, self.near)
        group = self.view(n, pipe, self.near)
        self.launch(n, first + 2, group, (pipe, self.far, self.place.dp), pipe, self.near)
        self.launch(n, first + 4, group, self.core, pipe, self.near)
        self.landed(n, first + 1, pipe, self.far)
        self.launch(n, first + 5, self.view(n, pipe, self.far), self.core, pipe, self.far)

    def last(self, n):
        pipe, first, across = self.place.pipe, 2 * self.hops, self.place.across
        self.landed(n, first + 2, pipe, across)
        self.launch(n, first + 6, self.view(n, pipe, across), self.core, pipe, across)

    def core_order(self):
        return (
            (),
            ((3, self.place.grp),),
            ((4, self.far), (5, self.near)),
            ((6, self.place.across),),
        )

    def from_core(self, n):
        for step in self.core_order():
            for index, grp in step:
                self.landed(n, 2 * self.hops + index, 1 - self.place.pipe, grp)

    def settle(self):
        for n in range(len(self.pieces)):
            for side in self.both:
                for hop in range(self.hops):
                    self.along(n, side, hop, finish=True)
        for copy in self.waits:
            copy.wait_send()
        if not self.hops:
            for keep in self.keeps.values():
                keep.wait()


LINE_TURN = 3


class LineGather(Gather):
    def __init__(self, place, shards, fulls, axes, send, arrive, own):
        super().__init__(place, [(n, 0, 0) for n in range(len(shards))], shards, fulls, send, arrive, own)
        self.axes = axes
        self.stages = [functools.partial(self.over_line, hop=hop) for hop in range(self.hops + 1)]

    def view(self, n, pipe, grp, origin):
        return self.fulls[n].at[(slice(None),) * self.axes[n] + (origin,)]

    def shard(self, n):
        return self.shards[n]

    def over_line(self, n, hop):
        super().over_line(n, hop)
        if hop == self.hops:
            self.keeps[n].wait()


def run_stages(stages, total, after=None):
    for turn in range(total + len(stages) - 1):
        for at, stage in enumerate(stages):
            if 0 <= turn - at < total:
                stage(turn - at)
        if after is not None:
            after(turn)


def gather_kernel(sizes, pieces, axes, routed, *refs):
    count, lines = max(piece[0] for piece in pieces) + 1, len(axes)
    shards, line_shards, refs = refs[:count], refs[count : count + lines], refs[count + lines :]
    if routed:
        rows_ref, refs = refs[0], refs[1:]
    fulls, line_fulls, refs = refs[:count], refs[count : count + lines], refs[count + lines :]
    if routed:
        arrived_ref, refs = refs[0], refs[1:]
    send, arrive, own, line_send, line_arrive, line_own, swap_send, swap_arrive, swap_own = refs
    place = Place(sizes)
    gather = Gather(place, pieces, shards, fulls, send, arrive, own)
    line = LineGather(place, line_shards, line_fulls, axes, line_send, line_arrive, line_own)
    greet([ahead for ahead, _ in place.others()] if routed else gather.partners())
    swaps = []

    def after(turn):
        for n in range(lines):
            if 0 <= turn - n - LINE_TURN <= gather.hops:
                line.over_line(n, turn - n - LINE_TURN)
        if turn == len(pieces) and routed:
            swaps.append(
                swap_all(place, rows_ref, arrived_ref, swap_send, swap_arrive, swap_own)
            )

    run_stages(gather.stages, len(pieces), after)
    for n in range(len(pieces)):
        gather.from_core(n)
    gather.settle()
    if lines:
        line.settle()
    for finish in swaps:
        finish()


def gather_all(shards, pieces, sizes, collective, rows=None, lines=(), axes=()):
    parts = math.prod(sizes)
    routed = rows is not None
    kinds = 2 * (sizes[2] - 1) + 7
    near = pl.BlockSpec(memory_space=pltpu.VMEM)
    out_shape = [jax.ShapeDtypeStruct(sizes + shard.shape, shard.dtype) for shard in shards]
    for line, axis in zip(lines, axes):
        shape = line.shape[:axis] + sizes[2:] + line.shape[axis:]
        out_shape.append(jax.ShapeDtypeStruct(shape, line.dtype))
    if routed:
        out_shape.append(jax.ShapeDtypeStruct(rows.shape, rows.dtype))
    operands = list(shards) + list(lines) + ([rows] if routed else [])
    sems = pltpu.SemaphoreType.DMA((len(pieces), kinds))
    line_sems = pltpu.SemaphoreType.DMA((max(len(lines), 1), kinds))
    swaps = pltpu.SemaphoreType.DMA((parts - 1 if routed else 1,))
    return pl.pallas_call(
        functools.partial(gather_kernel, sizes, tuple(pieces), tuple(axes), routed),
        out_shape=out_shape,
        in_specs=[near] * len(operands),
        out_specs=[near] + [pl.BlockSpec(memory_space=pltpu.HBM)] * (len(out_shape) - 1),
        scratch_shapes=[
            sems,
            sems,
            pltpu.SemaphoreType.DMA((len(pieces),)),
            line_sems,
            line_sems,
            pltpu.SemaphoreType.DMA((max(len(lines), 1),)),
            swaps,
            swaps,
            pltpu.SemaphoreType.DMA,
        ],
        compiler_params=pltpu.CompilerParams(
            collective_id=collective, has_side_effects=True, vmem_limit_bytes=40 << 20
        ),
        cost_estimate=lasting(110 if routed else 15),
    )(*operands)


class Sums:
    block = 16
    filled = False

    def __init__(self, place, sources, chips, others, mine, planes, lines, send, arrive, own, store):
        self.place, self.sources, self.chips, self.others = place, sources, chips, others
        self.mine, self.planes, self.lines = mine, planes, lines
        self.send, self.arrive, self.own, self.store = send, arrive, own, store
        pipe, grp, dp = place.pipe, place.grp, place.dp
        self.near = place.beside * (1 - pipe) + place.below * pipe
        self.far = place.below * (1 - pipe) + place.beside * pipe
        self.copies, self.kept = {}, {}

    def launch(self, n, index, source, target, to):
        copy = remote(source, target, self.send.at[n, index], self.arrive.at[n, index], to)
        self.copies[n, index] = copy
        copy.start()

    def keep(self, n, index, source, target):
        self.kept[n, index] = pltpu.make_async_copy(source, target, self.own.at[n, index])
        self.kept[n, index].start()

    def blocks(self, n, body):
        deep = self.mine[n].shape[2] // self.block

        def one(i, _):
            body(i // deep, pl.ds(pl.multiple_of(i % deep * self.block, self.block), self.block))
            return 0

        lax.fori_loop(0, self.place.dps * deep, one, 0)

    def to_core(self, n):
        place = self.place
        core = (1 - place.pipe, place.grp, place.dp)
        if self.filled:
            self.launch(n, 0, self.sources[n], self.others[n], core)
        elif self.chips[n] is not None:
            self.launch(n, 0, self.sources[n].at[1 - place.pipe], self.others[n], core)
            self.keep(n, 0, self.sources[n].at[place.pipe], self.chips[n])

    def to_near(self, n):
        place, chip, other = self.place, self.chips[n], self.others[n]
        part = self.sources[n]
        if chip is not None:
            if not self.filled:
                self.kept[n, 0].wait()
            self.copies[n, 0].wait_recv()
            for g in range(place.grps):

                def add(d, at, g=g):
                    left = chip[g, d, at].astype(jnp.float32)
                    chip[g, d, at] = (left + other[g, d, at].astype(jnp.float32)).astype(
                        jnp.bfloat16
                    )

                self.blocks(n, add)
            part = chip
        else:
            for j, g in enumerate((self.far, place.grp)):
                self.keep(n, j, part.at[g], self.mine[n].at[j])
        to = (place.pipe, self.near, place.dp)
        self.launch(n, 1, part.at[self.near], self.planes[n].at[1], to)
        self.launch(n, 2, part.at[place.across], self.planes[n].at[0], to)

    def to_far(self, n):
        place, mine, plane, chip = self.place, self.mine[n], self.planes[n], self.chips[n]
        if chip is None:
            self.kept[n, 0].wait()
            self.kept[n, 1].wait()
        self.copies[n, 1].wait_recv()
        self.copies[n, 2].wait_recv()
        for j, g in enumerate((self.far, place.grp)):

            def add(d, at, j=j, g=g):
                left = mine[j, d, at] if chip is None else chip[g, d, at]
                total = left.astype(jnp.float32) + plane[j, d, at].astype(jnp.float32)
                mine[j, d, at] = total.astype(jnp.bfloat16)

            self.blocks(n, add)
            if j == 0:
                self.launch(n, 3, mine.at[0], plane.at[2], (place.pipe, self.far, place.dp))

    def to_lines(self, n):
        place, mine, plane = self.place, self.mine[n], self.planes[n]
        self.copies[n, 3].wait_recv()
        hops = place.dps - 1

        def add(d, at):
            total = mine[1, d, at].astype(jnp.float32) + plane[2, d, at].astype(jnp.float32)
            if hops:
                mine[1, d, at] = total.astype(jnp.bfloat16)
            else:
                self.store(n, at, total)

        self.blocks(n, add)
        for k in range(hops):
            to = place.line(k + 1)
            self.launch(
                n, 4 + k, mine.at[1, to], self.lines[n].at[k], (place.pipe, place.grp, to)
            )

    def to_sum(self, n):
        place, mine, lines = self.place, self.mine[n], self.lines[n]
        for k in range(place.dps - 1):
            self.copies[n, 4 + k].wait_recv()

        def add(i, _):
            at = pl.ds(pl.multiple_of(i * self.block, self.block), self.block)
            total = mine[1, place.spot, at].astype(jnp.float32)
            for k in range(place.dps - 1):
                total = total + lines[k, at].astype(jnp.float32)
            self.store(n, at, total)
            return 0

        lax.fori_loop(0, mine.shape[2] // self.block, add, 0)

    def settle(self):
        for copy in self.copies.values():
            copy.wait_send()


def sum_scratch(shapes, cores, sizes):
    low = jnp.bfloat16
    _, grps, dps = sizes
    wide = [(dps,) + shape for shape in shapes]
    chips = [pltpu.VMEM((grps,) + shape, low) for shape, core in zip(wide, cores) if core]
    scratch = chips + chips
    scratch += [pltpu.VMEM((2,) + shape, low) for shape in wide]
    scratch += [pltpu.VMEM((3,) + shape, low) for shape in wide]
    scratch += [pltpu.VMEM((max(dps - 1, 1),) + shape, low) for shape in shapes]
    sems = pltpu.SemaphoreType.DMA((len(shapes), 4 + dps - 1))
    return scratch + [sems, sems, pltpu.SemaphoreType.DMA((len(shapes), 2))]


def sum_refs(refs, cores):
    total = len(cores)

    def spread_out(found):
        found = iter(found)
        return [next(found) if core else None for core in cores]

    chosen = sum(cores)
    groups = []
    for count in (chosen, chosen, total, total, total):
        groups.append(refs[:count])
        refs = refs[count:]
    chips, others, mine, planes, lines = groups
    return (spread_out(chips), spread_out(others), mine, planes, lines) + tuple(refs[:3]), refs[3:]


def reduce_kernel(sizes, pieces, *refs):
    partial, out, refs = refs[0], refs[1], refs[2:]
    place = Place(sizes)
    scratch, _ = sum_refs(refs, (True,) * len(pieces))

    def store(n, at, total):
        to = pl.multiple_of(pieces[n][0] + at.start, Sums.block)
        out[pl.ds(to, Sums.block)] = total

    sources = [partial.at[:, :, :, pl.ds(first, rows)] for first, rows in pieces]
    sums = Sums(place, sources, *scratch, store)
    line = [(place.pipe, place.grp, place.line(k + 1)) for k in range(place.dps - 1)]
    near, far = [(place.pipe, grp, place.dp) for grp in (sums.near, sums.far)]
    greet(line + [near, far, (1 - place.pipe, place.grp, place.dp)])
    stages = [sums.to_core, sums.to_near, sums.to_far, sums.to_lines]
    stages += [sums.to_sum] if place.dps > 1 else []
    run_stages(stages, len(pieces))
    sums.settle()


def reduce_all(partial, pieces, sizes, collective):
    shapes = [(rows, partial.shape[-1]) for _, rows in pieces]
    return pl.pallas_call(
        functools.partial(reduce_kernel, sizes, tuple(pieces)),
        out_shape=jax.ShapeDtypeStruct(partial.shape[-2:], jnp.float32),
        in_specs=[pl.BlockSpec(memory_space=pl.ANY)],
        out_specs=pl.BlockSpec(memory_space=pltpu.VMEM),
        scratch_shapes=sum_scratch(shapes, (True,) * len(pieces), sizes),
        cost_estimate=lasting(15),
        compiler_params=pltpu.CompilerParams(
            collective_id=collective, has_side_effects=True, vmem_limit_bytes=48 << 20
        ),
    )(partial)


def finish_kernel(sizes, *refs):
    lefts, rights, starts, talls, refs = refs[:3], refs[3:6], refs[6:8], refs[8:10], refs[10:]
    small, rows_ref, blocks_ref, refs = refs[0], refs[1], refs[2], refs[3:]
    outs, squares, arrived_ref, blocks_arrived_ref, refs = refs[:4], *refs[4:7], refs[7:]
    cores = (False, False, True, False, False, False)
    scratch, refs = sum_refs(refs, cores)
    other_lefts, other_rights, other_talls, made, refs = (
        refs[:3],
        refs[3:6],
        refs[6:8],
        refs[8:13],
        refs[13:],
    )
    swap_send, swap_arrive, swap_own, plane_send, plane_arrive, plane_own = refs[:6]
    core_send, core_arrive = refs[6:]
    place = Place(sizes)
    pipe, grp, dp = place.pipe, place.grp, place.dp
    greet([ahead for ahead, _ in place.others()])

    mine = tuple(lefts) + tuple(rights) + tuple(talls)
    theirs = tuple(other_lefts) + tuple(other_rights) + tuple(other_talls)
    exchanged = {}
    for i in (0, 3, 1, 4, 2, 5, 6, 7):
        exchanged[i] = remote(
            mine[i], theirs[i], core_send.at[i], core_arrive.at[i], (1 - pipe, grp, dp)
        )
        exchanged[i].start()

    squares[...] = jnp.zeros_like(squares)

    def store(n, at, total):
        squares[0:1, 0 : total.shape[1]] += jnp.sum(total * total, 0, keepdims=True)
        if n < 3:
            outs[n][at] = total
        else:
            outs[3][at, pl.ds((n - 3) * total.shape[1], total.shape[1])] = total

    sources = (made[0], made[1], small, made[2], made[3], made[4])
    sums = Sums(place, sources, *scratch, store)
    sums.to_core(2)
    swap = swap_all(place, rows_ref, arrived_ref, swap_send, swap_arrive, swap_own)
    plane_swap = swap_plane(
        place, blocks_ref, blocks_arrived_ref, plane_send, plane_arrive, plane_own
    )
    wide = made[0].shape[1] * made[0].shape[2]

    def form(i):
        exchanged[i].wait_recv()
        exchanged[3 + i].wait_recv()
        for g in range(place.grps):
            first = pl.multiple_of((pipe * place.grps + g) * wide, 128)
            at = pl.ds(first, wide)
            total = left_transposed(lefts[i][:, at], rights[i][...])
            total = total + left_transposed(other_lefts[i][:, at], other_rights[i][...])
            made[i][g] = total.astype(jnp.bfloat16).reshape(made[i].shape[1:])

    def form_tall(i):
        exchanged[6 + i].wait_recv()
        for g in range(place.grps):
            at = pl.ds(g * wide, wide)
            total = left_transposed(starts[0][:, at], talls[i][...])
            total = total + left_transposed(starts[1][:, at], other_talls[i][...])
            made[3 + i][g] = total.astype(jnp.bfloat16).reshape(made[3 + i].shape[1:])

    form(0)
    sums.to_near(0)
    form(1)
    sums.to_near(1)
    form(2)
    sums.to_near(3)
    sums.to_near(2)
    sums.to_far(0)
    form_tall(0)
    sums.to_near(4)
    sums.to_far(1)
    form_tall(1)
    sums.to_near(5)
    sums.to_far(3)
    sums.to_far(2)
    sums.to_lines(0)
    sums.to_lines(1)
    sums.to_lines(3)
    sums.to_far(4)
    sums.to_lines(2)
    sums.to_far(5)
    sums.to_lines(4)
    sums.to_lines(5)
    for n in (0, 1, 3, 2, 4, 5):
        sums.to_sum(n)
    sums.settle()
    for copy in exchanged.values():
        copy.wait_send()
    plane_swap()
    swap()


def finish_all(lefts, rights, starts, talls, small, rows, blocks, sizes, collective):
    low = jnp.bfloat16
    parts = math.prod(sizes)
    _, grps, dps = sizes
    width = lefts[0].shape[1]
    shape = (width // parts, rights[0].shape[1])
    shapes = [shape, shape, (small.shape[-2], small.shape[-1]), shape, shape, shape]
    made = pltpu.VMEM((grps, dps) + shape, low)
    anywhere = pl.BlockSpec(memory_space=pl.ANY)
    near = pl.BlockSpec(memory_space=pltpu.VMEM)
    swaps = pltpu.SemaphoreType.DMA((parts - 1,))
    plane_swaps = pltpu.SemaphoreType.DMA((sizes[0] * grps - 1,))
    one = pltpu.SemaphoreType.DMA
    operands = (*lefts, *rights, *starts, *talls, small, rows, blocks)
    joined = (shape[0], 3 * shape[1])
    widest = (8, max(shape[1] for shape in shapes))
    out_shape = [
        jax.ShapeDtypeStruct(shape, jnp.float32) for shape in shapes[:3] + [joined, widest]
    ]
    out_shape += [jax.ShapeDtypeStruct(extra.shape, extra.dtype) for extra in (rows, blocks)]
    return pl.pallas_call(
        functools.partial(finish_kernel, sizes),
        out_shape=out_shape,
        in_specs=[near] * 10 + [anywhere, near, near],
        out_specs=[near] * 7,
        scratch_shapes=sum_scratch(shapes, (False, False, True, False, False, False), sizes)
        + [pltpu.VMEM(item.shape, low) for item in (*lefts, *rights, *talls)]
        + [made] * 5
        + [
            swaps,
            swaps,
            one,
            plane_swaps,
            plane_swaps,
            one,
            pltpu.SemaphoreType.DMA((8,)),
            pltpu.SemaphoreType.DMA((8,)),
        ],
        compiler_params=pltpu.CompilerParams(
            collective_id=collective, has_side_effects=True, vmem_limit_bytes=56 << 20
        ),
    )(*operands)


def head_kernel(sizes, rows_per, vocab, gather_cuts, sum_cuts, *refs):
    row_ref, table, bias, info, out, word, bias_out, stats, refs = *refs[:8], refs[8:]
    full, logits, columns, laid, held, result, slopes, outgoing, refs = *refs[:8], refs[8:]
    cores = (True,) * sum_cuts
    scratch, refs = sum_refs(refs, cores)
    gather_send, gather_arrive, gather_own, swap_send, swap_arrive, swap_own = refs[:6]
    all_send, all_arrive = refs[6:]
    place = Place(sizes)
    pipes, grps, dps = sizes
    others = place.others()
    slots, width = row_ref.shape
    tall = slots // gather_cuts
    pieces = [(0, i * tall, tall) for i in range(gather_cuts)]
    gather = Gather(place, pieces, [row_ref], [full], gather_send, gather_arrive, gather_own)
    greet([ahead for ahead, _ in others])
    pipe, grp, hops = place.pipe, place.grp, dps - 1
    me = place.index(pipe, grp, place.dp)
    cells = table.shape[0]
    local = lax.broadcasted_iota(jnp.int32, (1, cells), 1)
    column = me * rows_per + local
    used = (local < rows_per) & (column < vocab)
    column = jnp.where(used, column, -1).astype(jnp.float32)
    groups = pipes * grps

    def parts(body):
        lax.fori_loop(0, pipes * grps * dps, lambda i, _: (body(i), 0)[1], 0, unroll=8)

    def spot(i):
        return i // (grps * dps), i // dps % grps, i % dps

    def fill(i):
        columns[spot(i) + (slice(None), slice(0, 8))] = info[i].T

    def form_logits(n, p, g):
        _, first, rows = pieces[n]
        at = pl.ds(first, rows)
        found = right_transposed(full[p, g, :, at].reshape(dps * rows, width), table[...])
        found = jnp.where(used, found + bias[...], -1e30)
        peak = jnp.max(found, -1, keepdims=True)
        total = jnp.sum(jnp.exp(found - peak), -1, keepdims=True)
        labels = columns[p, g, :, at, 0:1].reshape(dps * rows, 1)
        label = jnp.sum(jnp.where(column == labels, found, 0.0), -1, keepdims=True)
        logits[p, g, :, at] = found.reshape(dps, rows, cells)
        columns[p, g, :, at, 2:3] = peak.reshape(dps, rows, 1)
        columns[p, g, :, at, 3:4] = total.reshape(dps, rows, 1)
        columns[p, g, :, at, 4:5] = label.reshape(dps, rows, 1)

    def after(turn):
        if turn == 0:
            parts(fill)
        arrived = (
            ((pipe, grp),),
            ((pipe, gather.near), (pipe, gather.far)),
            ((pipe, place.across),),
            (),
        )
        for step in range(4):
            n = turn - hops - step
            if 0 <= n < gather_cuts:
                for p, g in arrived[step]:
                    form_logits(n, p, g)
                for index, g in gather.core_order()[step]:
                    gather.landed(n, 2 * hops + index, 1 - pipe, g)
                    form_logits(n, 1 - pipe, g)

    run_stages(gather.stages, gather_cuts, after)
    after(gather_cuts + hops + 2)

    def lay(i):
        laid[i] = columns[spot(i) + (slice(None), slice(0, 8))].T

    parts(lay)
    swap_all(place, laid, held, swap_send, swap_arrive, swap_own)()
    peaks = held[:, 2]
    peak = jnp.max(peaks, 0, keepdims=True)
    result[...] = jnp.zeros_like(result)
    result[0:1] = peak
    result[1:2] = jnp.sum(held[:, 3] * jnp.exp(peaks - peak), 0, keepdims=True)
    result[2:3] = jnp.sum(held[:, 4], 0, keepdims=True)
    copies = []
    for i, (ahead, _) in enumerate(others):
        copies.append(remote(result, stats.at[me], all_send.at[i], all_arrive.at[i], ahead))
        copies[-1].start()
    stats[me] = result[...]
    for i, (ahead, back) in enumerate(others):
        copies[i].wait_send()
        origin = place.index(*back)
        remote(
            result, stats.at[origin], all_send.at[i], all_arrive.at[i], ahead
        ).wait_recv()

    def back(i):
        columns[spot(i) + (slice(None), slice(8, 16))] = stats[i].T

    parts(back)

    size = slots // sum_cuts
    half = grps * dps * size

    def store(n, at, total):
        to = pl.multiple_of(n * size + at.start, Sums.block)
        out[pl.ds(to, Sums.block)] = total

    sums = Sums(place, [outgoing.at[n] for n in range(sum_cuts)], *scratch, store)
    sums.filled = True
    bias_out[...] = jnp.zeros_like(bias_out)
    word[...] = jnp.zeros_like(word)

    def form_slopes(n):
        at = pl.ds(n * size, size)

        def one(i, _):
            p, g = i // grps, i % grps
            kept = columns[p, g, :, at].reshape(dps * size, columns.shape[-1])
            found = logits[p, g, :, at].reshape(dps * size, cells)
            hits = (column == kept[:, 0:1]).astype(jnp.float32)
            slope = kept[:, 1:2] * (jnp.exp(found - kept[:, 8:9]) / kept[:, 9:10] - hits)
            bias_out[0:1] += jnp.sum(slope, 0, keepdims=True)
            slopes[n % 2, i] = slope.astype(jnp.bfloat16)
            return 0

        lax.fori_loop(0, groups, one, 0)
        for q, target in ((1 - place.pipe, outgoing.at[n]), (place.pipe, sums.chips[n])):
            left = slopes[n % 2, pl.ds(q * grps, grps)].reshape(half, cells)
            target[...] = matmul(left, table[...]).astype(jnp.bfloat16).reshape(target.shape)
        sums.to_core(n)

    def form_word(n):
        right = full[:, :, :, pl.ds(n * size, size)].reshape(pipes * half, width)
        word[...] += left_transposed(slopes[n % 2].reshape(pipes * half, cells), right)

    stages = [form_slopes, sums.to_near, sums.to_far, sums.to_lines, sums.to_sum]

    def then(turn):
        if turn < sum_cuts:
            form_word(turn)

    run_stages(stages, sum_cuts, then)
    sums.settle()
    gather.settle()


def head_all(row, table, bias, info, rows_per, vocab, sizes, collective):
    low = jnp.bfloat16
    parts = math.prod(sizes)
    pipes, grps, dps = sizes
    slots, width = row.shape
    cells = table.shape[0]
    gather_cuts, sum_cuts = 4, 8
    size = slots // sum_cuts
    near = pl.BlockSpec(memory_space=pltpu.VMEM)
    gathers = pltpu.SemaphoreType.DMA((gather_cuts, 2 * (dps - 1) + 7))
    swaps = pltpu.SemaphoreType.DMA((parts - 1,))
    return pl.pallas_call(
        functools.partial(head_kernel, sizes, rows_per, vocab, gather_cuts, sum_cuts),
        out_shape=(
            jax.ShapeDtypeStruct(row.shape, jnp.float32),
            jax.ShapeDtypeStruct(table.shape, jnp.float32),
            jax.ShapeDtypeStruct((8, cells), jnp.float32),
            jax.ShapeDtypeStruct(info.shape, jnp.float32),
        ),
        in_specs=[near] * 4,
        out_specs=[near] * 4,
        scratch_shapes=[
            pltpu.VMEM(sizes + row.shape, low),
            pltpu.VMEM(sizes + (slots, cells), jnp.float32),
            pltpu.VMEM(sizes + (slots, 16), jnp.float32),
            pltpu.VMEM(info.shape, jnp.float32),
            pltpu.VMEM(info.shape, jnp.float32),
            pltpu.VMEM(info.shape[1:], jnp.float32),
            pltpu.VMEM((2, pipes * grps, dps * size, cells), low),
            pltpu.VMEM((sum_cuts, grps, dps, size, width), low),
        ]
        + sum_scratch([(size, width)] * sum_cuts, (True,) * sum_cuts, sizes)
        + [
            gathers,
            gathers,
            pltpu.SemaphoreType.DMA((gather_cuts,)),
            swaps,
            swaps,
            pltpu.SemaphoreType.DMA,
            swaps,
            swaps,
        ],
        compiler_params=pltpu.CompilerParams(
            collective_id=collective, has_side_effects=True, vmem_limit_bytes=62 << 20
        ),
    )(row, table, bias, info)


def pair_rows(pair, first):
    pair = pair.astype(jnp.float32)
    low = jnp.bfloat16
    return jnp.concatenate(
        [jnp.where(first, pair, 0.0).astype(low), jnp.where(first, 0.0, pair).astype(low)], 0
    )


def pair_probs(rows, keys, live, scale):
    scores = jnp.where(live, right_transposed(rows, keys) * scale, -1e30)
    exp_scores = jnp.exp(scores - jnp.max(scores, -1, keepdims=True))
    return exp_scores / jnp.sum(exp_scores, -1, keepdims=True)


def attention_masks(lengths_ref, slots, seq_len, lanes):
    live = lax.broadcasted_iota(jnp.int32, (1, seq_len), 1) < lengths_ref[pl.program_id(0)]
    first = lax.broadcasted_iota(jnp.int32, (slots, lanes), 1) < lanes // 2
    return live, first


def attention_kernel(scale, lanes, lengths_ref, q_ref, k_ref, v_ref, out_ref):
    slots = q_ref.shape[0]
    live, first = attention_masks(lengths_ref, slots, k_ref.shape[0], lanes)
    for pair in range(q_ref.shape[1] // lanes):
        at = slice(pair * lanes, (pair + 1) * lanes)
        probs = pair_probs(pair_rows(q_ref[:, at], first), k_ref[:, at], live, scale)
        context = matmul(probs.astype(jnp.bfloat16), v_ref[:, at])
        out_ref[:, at] = jnp.where(first, context[:slots], context[slots:]).astype(jnp.bfloat16)


def attention_back_kernel(
    scale, lanes, lengths_ref, q_ref, k_ref, v_ref, grad_ref, dq_ref, dk_ref, dv_ref
):
    slots = q_ref.shape[0]
    low = jnp.bfloat16
    live, first = attention_masks(lengths_ref, slots, k_ref.shape[0], lanes)
    for pair in range(q_ref.shape[1] // lanes):
        at = slice(pair * lanes, (pair + 1) * lanes)
        rows, grads = pair_rows(q_ref[:, at], first), pair_rows(grad_ref[:, at], first)
        probs = pair_probs(rows, k_ref[:, at], live, scale)
        dv_ref[:, at] = left_transposed(probs.astype(low), grads).astype(low)
        d_probs = right_transposed(grads, v_ref[:, at])
        d_scores = probs * (d_probs - jnp.sum(probs * d_probs, -1, keepdims=True))
        d_scores = d_scores.astype(low)
        d_query = matmul(d_scores, k_ref[:, at]) * scale
        dq_ref[:, at] = jnp.where(first, d_query[:slots], d_query[slots:]).astype(low)
        dk_ref[:, at] = (left_transposed(d_scores, rows) * scale).astype(low)


def attention(lengths, queries, both, grads=None):
    own = lengths.shape[0]
    width = queries.shape[1]
    slots, seq_len = queries.shape[0] // own, both.shape[0] // own
    lanes = 2 * width // H
    scale = (width // H) ** (-0.5)
    cuts = 2
    part = width // cuts
    row = pl.BlockSpec((slots, part), lambda s, h: (s, h))
    keys = pl.BlockSpec((seq_len, part), lambda s, h: (s, h))
    values = pl.BlockSpec((seq_len, part), lambda s, h: (s, cuts + h))
    in_specs = [pl.BlockSpec(memory_space=pltpu.SMEM), row, keys, values]
    flat = jax.ShapeDtypeStruct(queries.shape, jnp.bfloat16)
    tall = jax.ShapeDtypeStruct((both.shape[0], width), jnp.bfloat16)
    if grads is None:
        return pl.pallas_call(
            functools.partial(attention_kernel, scale, lanes),
            grid=(own, cuts),
            out_shape=flat,
            in_specs=in_specs,
            out_specs=row,
            cost_estimate=lasting(8),
        )(lengths, queries, both, both)
    return pl.pallas_call(
        functools.partial(attention_back_kernel, scale, lanes),
        grid=(own, cuts),
        out_shape=(flat, tall, tall),
        in_specs=in_specs + [row],
        out_specs=(row, keys, keys),
        cost_estimate=lasting(11),
    )(lengths, queries, both, both, grads)


def even_pieces(array, rows, cuts):
    size = rows // cuts
    return [(array, i * size, size) for i in range(cuts)]


def start_all(row, blocks, sizes, collective):
    if collective is None:
        return lax.all_gather(row, AXES, axis=0), lax.all_to_all(blocks, PLANE, 0, 0)
    return begin(row, blocks, sizes, collective)


def gather_weights(shards, pieces, lines, axes, sizes, collective, rows):
    if collective is None:
        fulls = [lax.all_gather(shard, AXES, axis=0) for shard in shards]
        line_fulls = [
            lax.all_gather(line, "dp", axis=axis) for line, axis in zip(lines, axes)
        ]
        arrived = lax.all_to_all(rows, AXES, 0, 0)
    else:
        *fulls, arrived = gather_all(shards, pieces, sizes, collective, rows, lines, axes)
        fulls, line_fulls = fulls[: len(shards)], fulls[len(shards) :]
    return [full.reshape(-1, full.shape[-1]) for full in fulls], line_fulls, arrived


def gather_rows(shard, sizes, collective, cuts):
    if collective is None:
        axes = AXES if sizes[2] > 1 else PLANE
        return lax.all_gather(shard, axes, axis=0, tiled=True)
    (full,) = gather_all([shard], even_pieces(0, shard.shape[0], cuts), sizes, collective)
    return full.reshape(-1, full.shape[-1])


def sum_rows(partial, sizes, collective, cuts):
    if collective is None:
        axes = AXES if sizes[2] > 1 else PLANE
        total = lax.psum_scatter(partial, axes, scatter_dimension=0, tiled=True)
        return total.astype(jnp.float32)
    shaped = partial.reshape(sizes + (-1, partial.shape[1]))
    size = shaped.shape[3] // cuts
    return reduce_all(shaped, [(i * size, size) for i in range(cuts)], sizes, collective)


def sum_chips(lefts, rights, starts, talls, small, rows, blocks, sizes, collective):
    if collective is not None:
        small = small.reshape(sizes + (-1, small.shape[1]))
        *sums, squares, rows, blocks = finish_all(
            lefts, rights, starts, talls, small, rows, blocks, sizes, collective
        )
        return sums, jnp.sum(squares), rows, blocks
    made = [chip_sum(left, right) for left, right in zip(lefts, rights)]
    start = jnp.concatenate(starts, 0)
    made += [left_transposed(start, both_cores(tall)).astype(jnp.bfloat16) for tall in talls]
    partials = made[:2] + [chip_half(small)] + made[2:]
    sums = [
        lax.psum_scatter(p, CHIPS, scatter_dimension=0, tiled=True).astype(jnp.float32)
        for p in partials
    ]
    squares = sum(jnp.sum(total * total) for total in sums)
    sums = sums[:3] + [jnp.concatenate(sums[3:], 1)]
    rows = lax.all_to_all(rows, AXES, 0, 0)
    blocks = lax.all_to_all(blocks, PLANE, 0, 0)
    return sums, squares, rows, blocks


def line_shift(shard, step):
    size = lax.axis_size("dp")
    return lax.ppermute(shard, "dp", [(i, (i + step) % size) for i in range(size)])


def line_sum(partial, collective):
    partial = partial.astype(jnp.bfloat16)
    if collective is None:
        total = lax.psum_scatter(partial, "dp", scatter_dimension=0, tiled=False)
        return total.astype(jnp.float32)
    size = lax.axis_size("dp")
    me = lax.axis_index("dp")

    def entry(step):
        return lax.dynamic_index_in_dim(partial, (me + step) % size, 0, keepdims=False)

    total = entry(0).astype(jnp.float32)
    for step in range(1, size):
        total = total + line_shift(entry(step), step).astype(jnp.float32)
    return total


def spread_row(row, sizes, collective):
    if collective is None:
        return lax.all_gather(row, AXES, axis=0)
    return spread(row, sizes, collective)


def output_layer(row, table, bias, labels, weights, rows_per, vocab, sizes, collective):
    parts = math.prod(sizes)
    if collective is not None:
        bias = jnp.pad(bias, (0, table.shape[0] - rows_per))[None]
        info = jnp.stack([labels.astype(jnp.float32), weights]).reshape(2, parts, -1)
        info = jnp.pad(info.swapaxes(0, 1), ((0, 0), (0, 6), (0, 0)))
        grad, word, d_bias, stats = head_all(
            row, table, bias, info, rows_per, vocab, sizes, collective
        )
        stats = [stats[:, i].reshape(-1) for i in range(3)]
        return grad, word, d_bias[0, :rows_per], stats
    rows = gather_rows(row, sizes, None, 1)
    cells = jnp.arange(table.shape[0], dtype=jnp.int32)
    column = lax.axis_index(AXES) * rows_per + cells
    column = jnp.where((cells < rows_per) & (column < vocab), column, -1)
    bias = jnp.pad(bias, (0, table.shape[0] - rows_per))
    logits = jnp.where(column >= 0, right_transposed(rows, table) + bias, -1e30)
    own_peak = jnp.max(logits, -1)
    own_total = jnp.sum(jnp.exp(logits - own_peak[:, None]), -1)
    hits = labels[:, None] == column
    own_label = jnp.sum(jnp.where(hits, logits, 0.0), -1)
    peak = lax.pmax(own_peak, AXES)
    total, label = lax.psum((own_total * jnp.exp(own_peak - peak), own_label), AXES)
    slopes = weights[:, None] * (
        jnp.exp(logits - peak[:, None]) / total[:, None] - hits.astype(jnp.float32)
    )
    low = slopes.astype(jnp.bfloat16)
    grad = sum_rows(matmul(low, table).astype(jnp.bfloat16), sizes, None, 1)
    return grad, left_transposed(low, rows), jnp.sum(slopes, 0)[:rows_per], (peak, total, label)


def adam_step(weight, first, second, grad, factor, rate):
    clipped = grad * factor
    first = beta_one * first + (1.0 - beta_one) * clipped
    second = beta_two * second + (1.0 - beta_two) * clipped * clipped
    first_hat = first / (1.0 - beta_one**STEP)
    second_hat = second / (1.0 - beta_two**STEP)
    weight = weight - rate * (first_hat / (jnp.sqrt(second_hat) + epsilon) + weight_decay * weight)
    return (weight, first, second)


def per_device(
    token_ids,
    lengths,
    masked_at,
    labels,
    word_table,
    word_first,
    word_second,
    pos_table,
    pos_first,
    pos_second,
    qkv_weight,
    qkv_first,
    qkv_second,
    square_weight,
    square_first,
    square_second,
    up_weight,
    up_first,
    up_second,
    down_weight,
    down_first,
    down_second,
    vec_table,
    vec_first,
    vec_second,
    head_bias,
    bias_first,
    bias_second,
):
    narrow = jnp.bfloat16
    seq_len, slots = token_ids.shape[1], masked_at.shape[1]
    width = word_table.shape[1]
    vocab = head_bias.shape[0]
    rows_per = word_table.shape[0]
    parts = lax.axis_size(AXES)
    halves = lax.axis_size("pipe")
    me = lax.axis_index(AXES)
    own = token_ids.shape[0] // halves
    first_own = lax.axis_index("pipe") * own
    head_dim = width // H
    sizes = tuple(lax.axis_size(axis) for axis in AXES)
    shards = (word_table, qkv_weight, square_weight[0], up_weight, down_weight)
    direct = sizes[:2] == (2, 4) and all(shard.shape[0] % 32 == 0 for shard in shards)
    ids = tuple(range(11)) if direct else (None,) * 11
    plane_sizes = sizes[:2] + (1,)

    spare = -(seq_len + slots + 1) % 128
    packed = jnp.concatenate(
        [token_ids, labels, lengths[:, None], jnp.zeros((token_ids.shape[0], spare), jnp.int32)], 1
    )
    packed = lax.dynamic_slice_in_dim(packed, first_own, own, 0)
    planes = sizes[0] * sizes[1]
    units = up_weight.shape[1] // planes
    cut = me // sizes[2]
    blocks = up_weight.astype(narrow).reshape(up_weight.shape[0], planes, units).swapaxes(0, 1)
    packed, blocks = start_all(packed, blocks, sizes, ids[0])
    all_ids = packed[:, :, :seq_len]
    all_labels = packed[:, :, seq_len : seq_len + slots].reshape(-1)
    all_lengths = packed[:, :, seq_len + slots]
    places = jnp.arange(seq_len, dtype=jnp.int32)
    all_live = places[None, None, :] < all_lengths[:, :, None]
    all_counts = masked_counts(all_lengths, slots)
    total = jnp.sum(all_counts).astype(jnp.float32)
    slot_index = jnp.arange(slots, dtype=jnp.int32)
    all_valid = (slot_index < all_counts[:, :, None]).astype(jnp.float32).reshape(-1)
    own_lengths = lax.dynamic_slice_in_dim(lengths, first_own, own, 0)
    masked = lax.dynamic_slice_in_dim(masked_at, first_own, own, 0)

    cells = rows_per + -rows_per % 128
    word_low = jnp.pad(word_table.astype(narrow), ((0, cells - rows_per), (0, 0)))
    routes = Routes(all_ids.reshape(parts, -1), all_live.reshape(parts, -1), rows_per)
    small = pos_table.shape[0] + vec_table.shape[0]
    spare = -small % 128
    small_low = jnp.concatenate(
        [pos_table.T, vec_table.T, jnp.zeros((pos_table.shape[1], spare), jnp.float32)], 1
    ).astype(narrow)
    low = [
        small_low,
        qkv_weight.astype(narrow),
        square_weight[0].astype(narrow),
        square_weight[1].astype(narrow),
    ]
    deep = small_low.shape[0]
    pieces = [(i, 0, deep) for i in range(4)]
    send = routes.table_rows(word_low, 0, routes.room).reshape(parts, -1, width)
    (small_full, qkv_low, out_low, turn_low), (up_low, down_low), arrived = gather_weights(
        low, pieces, [blocks, down_weight.astype(narrow)], [1, 0], sizes, ids[1], send
    )
    up_low = up_low.reshape(width, units)
    down_low = down_low.reshape(units, width)
    word_rows = routes.fetch(word_low, arrived.reshape(-1, width))
    small_full = small_full.T
    pos_low = small_full[:seq_len]
    vec_rows = small_full[seq_len:small].astype(jnp.float32)
    query_low, both_low = qkv_low[:, :width], qkv_low[:, width:]

    second = (places[None, :] >= ((own_lengths + 1) // 2)[:, None]).reshape(-1, 1)
    embedded = (
        word_rows
        + jnp.tile(pos_low.astype(jnp.float32), (own, 1))
        + jnp.where(second, vec_rows[1], vec_rows[0])
    )
    start, norm_zero = norm_forward(embedded, vec_rows[2], vec_rows[3])
    start_low = start.astype(narrow)
    both_bias = jnp.concatenate([jnp.zeros_like(vec_rows[5]), vec_rows[5]])
    both = (matmul(start_low, both_low) + both_bias).astype(narrow)
    pick = one_hot(masked, seq_len, jnp.float32)
    chosen = rows_by_seq(pick, start.reshape(own, seq_len, width)).reshape(-1, width)
    chosen_low = chosen.astype(narrow)
    start_own, start_other = both_halves(start_low)
    queries = (matmul(chosen_low, query_low) + vec_rows[4]).astype(narrow)
    context = attention(own_lengths, queries, both)
    context, start_other = lax.optimization_barrier((context, start_other))
    branch = matmul(context, out_low) + vec_rows[6]
    hidden, norm_one = norm_forward(chosen + branch, vec_rows[7], vec_rows[8])
    hidden = hidden.astype(narrow)

    plane_hidden = gather_rows(hidden, plane_sizes, ids[2], 2)
    up_bias = lax.dynamic_slice_in_dim(vec_rows[15:].reshape(-1), cut * units, units, 0)
    inner = matmul(plane_hidden, up_low) + up_bias
    activ = jax.nn.gelu(inner, approximate=False).astype(narrow)
    branch = sum_rows(matmul(activ, down_low).astype(narrow), plane_sizes, ids[3], 2) + vec_rows[9]
    mixed, norm_two = norm_forward(hidden.astype(jnp.float32) + branch, vec_rows[10], vec_rows[11])
    picked = mixed.astype(narrow)
    turned = matmul(picked, turn_low) + vec_rows[12]
    normed, norm_head = norm_forward(
        jax.nn.gelu(turned, approximate=False), vec_rows[13], vec_rows[14]
    )

    bias_row = jnp.pad(head_bias, (0, parts * rows_per - vocab))
    bias_row = lax.dynamic_slice_in_dim(bias_row, me * rows_per, rows_per, 0)
    d_normed, d_word, d_bias, (peak, exp_total, label_logit) = output_layer(
        normed.astype(narrow),
        word_low,
        bias_row,
        all_labels,
        all_valid / total,
        rows_per,
        vocab,
        sizes,
        ids[4],
    )
    loss_total = jnp.sum(all_valid * (peak + jnp.log(exp_total) - label_logit))

    d_gelu, d_gain_head, d_shift_head = norm_backward(d_normed, norm_head, vec_rows[13])
    d_turned = (d_gelu * gelu_slope(turned)).astype(narrow)
    d_turn_bias = jnp.sum(d_turned.astype(jnp.float32), 0)
    d_picked = right_transposed(d_turned, turn_low)
    same = masked[:, :, None] == masked[:, None, :]
    earlier = slot_index[None, :] < slot_index[:, None]
    first_slot = jnp.logical_not(jnp.any(same & earlier, 2))
    merge = (same & first_slot[:, :, None]).astype(jnp.float32)
    d_mixed = rows_by_seq(merge, d_picked.reshape(own, slots, width)).reshape(-1, width)
    d_pre, d_gain_two, d_shift_two = norm_backward(d_mixed, norm_two, vec_rows[10])
    d_branch = d_pre.astype(narrow)
    d_down_bias = jnp.sum(d_branch.astype(jnp.float32), 0)
    plane_branch = gather_rows(d_branch, plane_sizes, ids[7], 2)
    d_down = left_transposed(activ, plane_branch).astype(narrow)
    d_inner = (right_transposed(plane_branch, down_low) * gelu_slope(inner)).astype(narrow)
    d_up_bias = jnp.sum(d_inner.astype(jnp.float32), 0)
    d_up_bias = lax.dynamic_update_slice_in_dim(
        jnp.zeros((planes * units,), jnp.float32), d_up_bias, cut * units, 0
    ).reshape(-1, width)
    d_up = left_transposed(plane_hidden, d_inner).astype(narrow)
    d_hidden = sum_rows(right_transposed(d_inner, up_low).astype(narrow), plane_sizes, ids[8], 2)
    d_hidden = (d_pre + d_hidden).astype(narrow)

    d_hidden, d_down, d_up = lax.optimization_barrier((d_hidden, d_down, d_up))
    own_down = line_sum(d_down.reshape(sizes[2], -1, width), ids[7])
    d_up = d_up.reshape(planes, sizes[2], -1, units).swapaxes(0, 1)
    up_blocks = line_sum(d_up, ids[7]).astype(narrow)
    d_pre, d_gain_one, d_shift_one = norm_backward(
        d_hidden.astype(jnp.float32), norm_one, vec_rows[7]
    )
    d_branch = d_pre.astype(narrow)
    d_out_bias = jnp.sum(d_branch.astype(jnp.float32), 0)
    d_attended = d_branch
    d_context = right_transposed(d_branch, out_low).astype(narrow)
    d_query, d_key, d_value = attention(own_lengths, queries, both, d_context)
    d_query_bias = jnp.sum(d_query.astype(jnp.float32), 0)
    d_value_bias = jnp.sum(d_value.astype(jnp.float32), 0)
    d_chosen = d_pre + right_transposed(d_query, query_low)
    d_both = jnp.concatenate([d_key, d_value], 1)
    d_start = right_transposed(d_both, both_low) + rows_to_seq(
        pick, d_chosen.reshape(own, slots, width)
    ).reshape(-1, width)
    d_embedded, d_gain_zero, d_shift_zero = norm_backward(d_start, norm_zero, vec_rows[2])
    d_seg_zero = jnp.sum(jnp.where(second, 0.0, d_embedded), 0)
    d_seg_one = jnp.sum(jnp.where(second, d_embedded, 0.0), 0)
    d_embedded_low = d_embedded.astype(narrow)
    send = routes.token_rows(d_embedded_low, 0, routes.room).reshape(parts, -1, width)
    d_small = jnp.concatenate(
        [
            jnp.sum(d_embedded.reshape(own, seq_len, width), 0),
            jnp.stack(
                [
                    d_seg_zero,
                    d_seg_one,
                    d_gain_zero,
                    d_shift_zero,
                    d_query_bias,
                    d_value_bias,
                    d_out_bias,
                    d_gain_one,
                    d_shift_one,
                    d_down_bias,
                    d_gain_two,
                    d_shift_two,
                    d_turn_bias,
                    d_gain_head,
                    d_shift_head,
                ]
            ),
            d_up_bias,
            jnp.zeros((spare, width), jnp.float32),
        ],
        0,
    )
    (own_out, own_turn, own_small, own_qkv), squares, arrived, up_blocks = sum_chips(
        [context, picked, chosen_low],
        [d_attended, d_turned, d_query],
        [start_own, start_other],
        [d_key, d_value],
        d_small.T.astype(narrow),
        send,
        up_blocks,
        sizes,
        ids[9],
    )
    own_up = up_blocks.swapaxes(0, 1).reshape(up_weight.shape).astype(jnp.float32)
    d_word = routes.give(d_embedded_low, arrived.reshape(-1, width), d_word)[:rows_per]
    owned = (
        d_word,
        own_small[:, :seq_len].T,
        own_qkv,
        jnp.stack([own_out, own_turn]),
        own_up,
        own_down,
        own_small[:, seq_len:small].T,
    )
    local_squares = squares + jnp.sum(d_bias * d_bias)
    for grad in (d_word, own_up, own_down):
        local_squares = local_squares + jnp.sum(grad * grad)
    spare = -(rows_per + 1) % 128
    last = jnp.concatenate([d_bias, local_squares[None], jnp.zeros((spare,), jnp.float32)])
    last = spread_row(last.reshape(8, -1), sizes, ids[10]).reshape(parts, -1)
    bias_grad = last[:, :rows_per].reshape(-1)[:vocab]
    grad_norm = jnp.sqrt(jnp.sum(last[:, rows_per]))
    factor = clip_norm / jnp.maximum(grad_norm, clip_norm)
    masters = (
        word_table,
        pos_table,
        qkv_weight,
        square_weight,
        up_weight,
        down_weight,
        vec_table,
        head_bias,
    )
    states = (
        (word_first, word_second),
        (pos_first, pos_second),
        (qkv_first, qkv_second),
        (square_first, square_second),
        (up_first, up_second),
        (down_first, down_second),
        (vec_first, vec_second),
        (bias_first, bias_second),
    )
    rates = (
        learn_rate,
        learn_rate,
        learn_rate,
        learn_rate,
        learn_rate,
        learn_rate,
        vector_rate,
        vector_rate,
    )
    grads = tuple(owned) + (bias_grad,)
    results = []
    for weight, state, grad, rate in zip(masters, states, grads, rates):
        results.extend(adam_step(weight, state[0], state[1], grad, factor, rate))
    return (
        results[0],
        results[1],
        results[2],
        results[3],
        results[4],
        results[5],
        results[6],
        results[7],
        results[8],
        results[9],
        results[10],
        results[11],
        results[12],
        results[13],
        results[14],
        results[15],
        results[16],
        results[17],
        results[18],
        results[19],
        results[20],
        results[21],
        results[22],
        results[23],
        loss_total,
        total,
        grad_norm,
    )


def solution(mesh):
    placed = (
        P(("grp", "dp"), None),
        P(("grp", "dp")),
        P(("grp", "dp"), None),
        P(("grp", "dp"), None),
        P(("pipe", "grp", "dp"), None),
        P(("pipe", "grp", "dp"), None),
        P(("pipe", "grp", "dp"), None),
        P(None, ("pipe", "grp", "dp")),
        P(None, ("pipe", "grp", "dp")),
        P(None, ("pipe", "grp", "dp")),
        P(("pipe", "grp", "dp"), None),
        P(("pipe", "grp", "dp"), None),
        P(("pipe", "grp", "dp"), None),
        P(None, ("pipe", "grp", "dp"), None),
        P(None, ("pipe", "grp", "dp"), None),
        P(None, ("pipe", "grp", "dp"), None),
        P(("pipe", "grp", "dp"), None),
        P(("pipe", "grp", "dp"), None),
        P(("pipe", "grp", "dp"), None),
        P(("pipe", "grp", "dp"), None),
        P(("pipe", "grp", "dp"), None),
        P(("pipe", "grp", "dp"), None),
        P(None, ("pipe", "grp", "dp")),
        P(None, ("pipe", "grp", "dp")),
        P(None, ("pipe", "grp", "dp")),
        P(),
        P(),
        P(),
    )
    return jax.shard_map(
        per_device,
        mesh=mesh,
        in_specs=placed,
        out_specs=(
            P(("pipe", "grp", "dp"), None),
            P(("pipe", "grp", "dp"), None),
            P(("pipe", "grp", "dp"), None),
            P(None, ("pipe", "grp", "dp")),
            P(None, ("pipe", "grp", "dp")),
            P(None, ("pipe", "grp", "dp")),
            P(("pipe", "grp", "dp"), None),
            P(("pipe", "grp", "dp"), None),
            P(("pipe", "grp", "dp"), None),
            P(None, ("pipe", "grp", "dp"), None),
            P(None, ("pipe", "grp", "dp"), None),
            P(None, ("pipe", "grp", "dp"), None),
            P(("pipe", "grp", "dp"), None),
            P(("pipe", "grp", "dp"), None),
            P(("pipe", "grp", "dp"), None),
            P(("pipe", "grp", "dp"), None),
            P(("pipe", "grp", "dp"), None),
            P(("pipe", "grp", "dp"), None),
            P(None, ("pipe", "grp", "dp")),
            P(None, ("pipe", "grp", "dp")),
            P(None, ("pipe", "grp", "dp")),
            P(),
            P(),
            P(),
            P(),
            P(),
            P(),
        ),
        check_vma=False,
    )
```

```python
import functools
import math

import jax
import jax.numpy as jnp
from jax import lax
from jax.experimental import pallas as pl
from jax.experimental.pallas import tpu as pltpu
from jax.sharding import PartitionSpec as P

H = 16
STEP = 10


beta_one = 0.9
beta_two = 0.999
learn_rate = 0.02
vector_rate = 0.2
weight_decay = 0.01
epsilon = 1e-08
clip_norm = 0.02
norm_eps = 1e-05
root_half = 0.7071067811865476
density_scale = 0.3989422804014327
AXES = ("pipe", "grp", "dp")
CHIPS = ("grp", "dp")
PLANE = ("pipe", "grp")
highest = lax.Precision.HIGHEST


def matmul(left, right):
    return jnp.dot(left, right, preferred_element_type=jnp.float32)


def left_transposed(left, right):
    return lax.dot_general(
        left, right, (((0,), (0,)), ((), ())), preferred_element_type=jnp.float32
    )


def right_transposed(left, right):
    return lax.dot_general(
        left, right, (((1,), (1,)), ((), ())), preferred_element_type=jnp.float32
    )


def norm_forward(values, gain, shift):
    center = values - jnp.mean(values, -1, keepdims=True)
    scale = lax.rsqrt(jnp.mean(center * center, -1, keepdims=True) + norm_eps)
    normal = center * scale
    return (normal * gain + shift, (normal, scale))


def norm_backward(grad, kept, gain):
    normal, scale = kept
    d_gain = jnp.sum(grad * normal, 0)
    d_shift = jnp.sum(grad, 0)
    d_norm = grad * gain
    d_input = scale * (
        d_norm
        - jnp.mean(d_norm, -1, keepdims=True)
        - normal * jnp.mean(d_norm * normal, -1, keepdims=True)
    )
    return (d_input, d_gain, d_shift)


def gelu_slope(values):
    return (
        0.5 * (1.0 + lax.erf(values * root_half))
        + values * jnp.exp(-0.5 * values * values) * density_scale
    )


def masked_counts(lengths, slots):
    return jnp.minimum(slots, (3 * lengths + 19) // 20)


def one_hot(indices, size, dtype):
    places = lax.broadcasted_iota(jnp.int32, indices.shape + (size,), indices.ndim)
    return (indices[..., None] == places).astype(dtype)


def rows_by_seq(pick, rows):
    return jnp.einsum("sjp,spw->sjw", pick, rows, precision=highest)


def rows_to_seq(pick, rows):
    return jnp.einsum("sjp,sjw->spw", pick, rows, precision=highest)


class Routes:
    def __init__(self, all_ids, all_live, rows_per):
        self.parts, tokens = all_ids.shape
        self.cells = rows_per + -rows_per % 128
        self.me = lax.axis_index(AXES)
        mean = tokens / self.parts
        self.room = max(16, int(math.ceil((mean + 2.8 * math.sqrt(mean)) / 16)) * 16)
        owners = jnp.where(all_live, all_ids // rows_per, -1)
        counts = jnp.sum(one_hot(owners, self.parts, jnp.int32), 1)
        self.more = 16
        self.rounds = (jnp.maximum(jnp.max(counts) - self.room, 0) + self.more - 1) // self.more
        mine = owners == self.me
        order = jnp.arange(tokens, dtype=jnp.int32)
        upto = (order[:, None] <= order[None, :]).astype(jnp.bfloat16)
        ranks = matmul(mine.astype(jnp.bfloat16), upto).astype(jnp.int32)
        self.out_rank = jnp.where(mine, ranks - 1, -1)
        self.out_row = all_ids - self.me * rows_per
        own_owners = lax.dynamic_index_in_dim(owners, self.me, 0, keepdims=False)
        hits = one_hot(own_owners, self.parts, jnp.bfloat16)
        ranks = jnp.sum(hits.astype(jnp.float32) * left_transposed(upto, hits), 1)
        ranks = ranks.astype(jnp.int32) - 1
        self.in_rank = ranks
        self.in_owner = own_owners

    def owner_pick(self, first, room):
        slots = first + jnp.arange(room, dtype=jnp.int32)
        at = self.out_rank[:, None, :] == slots[None, :, None]
        row = jnp.sum(jnp.where(at, self.out_row[:, None, :] + 1, 0), 2) - 1
        return one_hot(row.reshape(-1), self.cells, jnp.bfloat16)

    def token_pick(self, first, room):
        rank = self.in_rank - first
        inside = (self.in_owner >= 0) & (rank >= 0) & (rank < room)
        slot = jnp.where(inside, self.in_owner * room + rank, -1)
        return one_hot(slot, self.parts * room, jnp.bfloat16)

    def exchange(self, rows):
        shaped = rows.reshape(self.parts, -1, rows.shape[-1])
        return lax.all_to_all(shaped, AXES, 0, 0).reshape(rows.shape)

    def table_rows(self, table, first, room):
        return matmul(self.owner_pick(first, room), table).astype(jnp.bfloat16)

    def token_rows(self, rows, first, room):
        return left_transposed(self.token_pick(first, room), rows).astype(jnp.bfloat16)

    def later(self, more, start):
        def one(turn, kept):
            return kept + more(self.room + turn * self.more)

        return lax.fori_loop(0, self.rounds, one, start)

    def fetch(self, table, arrived):
        def more(first):
            rows = self.exchange(self.table_rows(table, first, self.more))
            return matmul(self.token_pick(first, self.more), rows)

        return self.later(more, matmul(self.token_pick(0, self.room), arrived))

    def give(self, rows, arrived, start):
        def more(first):
            back = self.exchange(self.token_rows(rows, first, self.more))
            return left_transposed(self.owner_pick(first, self.more), back)

        start = start + left_transposed(self.owner_pick(0, self.room), arrived)
        return self.later(more, start)


def swapped(shard):
    return lax.ppermute(shard, "pipe", [(0, 1), (1, 0)])


def both_cores(rows):
    return jnp.concatenate([rows, swapped(rows)], 0)


def half_columns(rows, index):
    half = rows.shape[1] // 2
    return lax.dynamic_slice_in_dim(rows, index * half, half, 1)


def both_halves(rows):
    pipe = lax.axis_index("pipe")
    return half_columns(rows, pipe), swapped(half_columns(rows, 1 - pipe))


def chip_sum(left, right):
    left = jnp.concatenate(both_halves(left), 0)
    return left_transposed(left, both_cores(right)).astype(jnp.bfloat16)


def chip_half(partial):
    half = partial.shape[0] // 2
    pipe = lax.axis_index("pipe")
    partial = partial.astype(jnp.bfloat16)
    keep = lax.dynamic_slice_in_dim(partial, pipe * half, half, 0)
    give = lax.dynamic_slice_in_dim(partial, (1 - pipe) * half, half, 0)
    return (keep.astype(jnp.float32) + swapped(give).astype(jnp.float32)).astype(jnp.bfloat16)


def lasting(microseconds):
    return pl.CostEstimate(
        flops=int(microseconds * 9e8), bytes_accessed=int(microseconds * 3e6), transcendentals=0
    )


def device(pipe, grp, dp):
    return {"pipe": pipe, "grp": grp, "dp": dp}


def remote(source, target, send, arrive, to):
    return pltpu.make_async_remote_copy(
        src_ref=source,
        dst_ref=target,
        send_sem=send,
        recv_sem=arrive,
        device_id=device(*to),
        device_id_type=pl.DeviceIdType.MESH,
    )


def tell(barrier, to):
    pl.semaphore_signal(
        barrier, inc=1, device_id=device(*to), device_id_type=pl.DeviceIdType.MESH
    )


def greet(others):
    barrier = pltpu.get_barrier_semaphore()
    for to in others:
        tell(barrier, to)
    pl.semaphore_wait(barrier, len(others))


class Place:
    def __init__(self, sizes):
        self.pipes, self.grps, self.dps = sizes
        self.plane_only = self.dps == 1
        self.pipe, self.grp, self.dp = [lax.axis_index(axis) for axis in AXES]
        column, row = self.grp % 2, self.grp // 2
        self.beside = 2 * row + 1 - column
        self.below = 2 * (1 - row) + column
        self.across = 3 - self.grp

    @property
    def spot(self):
        return 0 if self.plane_only else self.dp

    def plane(self):
        found = []
        for a in range(self.pipes):
            for b in range(self.grps):
                if (a, b) != (0, 0):
                    ahead = ((self.pipe + a) % self.pipes, (self.grp + b) % self.grps)
                    back = (
                        (self.pipe + self.pipes - a) % self.pipes,
                        (self.grp + self.grps - b) % self.grps,
                    )
                    found.append((ahead, back))
        return found

    def line(self, step):
        return (self.dp + step) % self.dps

    def behind(self, step):
        return (self.dp + self.dps - step) % self.dps

    def others(self):
        found = []
        for a in range(self.pipes):
            for b in range(self.grps):
                for c in range(self.dps):
                    if (a, b, c) != (0, 0, 0):
                        ahead = (
                            (self.pipe + a) % self.pipes,
                            (self.grp + b) % self.grps,
                            (self.dp + c) % self.dps,
                        )
                        back = (
                            (self.pipe + self.pipes - a) % self.pipes,
                            (self.grp + self.grps - b) % self.grps,
                            (self.dp + self.dps - c) % self.dps,
                        )
                        found.append((ahead, back))
        return found

    def index(self, pipe, grp, dp):
        return (pipe * self.grps + grp) * self.dps + dp


def swap_all(place, rows, arrived, send, arrive, own):
    me = place.index(place.pipe, place.grp, place.dp)
    copies = []
    for i, (ahead, back) in enumerate(place.others()):
        to = place.index(*ahead)
        copies.append(remote(rows.at[to], arrived.at[me], send.at[i], arrive.at[i], ahead))
        copies[-1].start()
    kept = pltpu.make_async_copy(rows.at[me], arrived.at[me], own)
    kept.start()

    def finish():
        for i, (ahead, back) in enumerate(place.others()):
            origin = place.index(*back)
            copies[i].wait_send()
            remote(rows.at[me], arrived.at[origin], send.at[i], arrive.at[i], ahead).wait_recv()
        kept.wait()

    return finish


def swap_plane(place, rows, arrived, send, arrive, own):
    me = place.pipe * place.grps + place.grp
    copies = []
    for i, (ahead, back) in enumerate(place.plane()):
        to = ahead[0] * place.grps + ahead[1]
        copies.append(
            remote(rows.at[to], arrived.at[me], send.at[i], arrive.at[i], ahead + (place.dp,))
        )
        copies[-1].start()
    kept = pltpu.make_async_copy(rows.at[me], arrived.at[me], own)
    kept.start()

    def finish():
        for i, (ahead, back) in enumerate(place.plane()):
            origin = back[0] * place.grps + back[1]
            copies[i].wait_send()
            remote(
                rows.at[me], arrived.at[origin], send.at[i], arrive.at[i], ahead + (place.dp,)
            ).wait_recv()
        kept.wait()

    return finish


def begin_kernel(sizes, row_ref, up_ref, all_ref, arrived_ref, *sems):
    send, arrive, own, plane_send, plane_arrive, plane_own = sems
    place = Place(sizes)
    others = place.others()
    greet([ahead for ahead, _ in others])
    finish = swap_plane(place, up_ref, arrived_ref, plane_send, plane_arrive, plane_own)
    me = place.index(place.pipe, place.grp, place.dp)
    copies = []
    for i, (ahead, _) in enumerate(others):
        copies.append(remote(row_ref, all_ref.at[me], send.at[i], arrive.at[i], ahead))
        copies[-1].start()
    kept = pltpu.make_async_copy(row_ref, all_ref.at[me], own)
    kept.start()
    for i, (ahead, back) in enumerate(others):
        copies[i].wait_send()
        remote(
            row_ref, all_ref.at[place.index(*back)], send.at[i], arrive.at[i], ahead
        ).wait_recv()
    kept.wait()
    finish()


def begin(row, blocks, sizes, collective):
    parts = math.prod(sizes)
    sems = pltpu.SemaphoreType.DMA((parts - 1,))
    plane_sems = pltpu.SemaphoreType.DMA((sizes[0] * sizes[1] - 1,))
    return pl.pallas_call(
        functools.partial(begin_kernel, sizes),
        out_shape=(
            jax.ShapeDtypeStruct((parts,) + row.shape, row.dtype),
            jax.ShapeDtypeStruct(blocks.shape, blocks.dtype),
        ),
        in_specs=[pl.BlockSpec(memory_space=pltpu.VMEM)] * 2,
        out_specs=[pl.BlockSpec(memory_space=pltpu.VMEM)] * 2,
        scratch_shapes=[
            sems,
            sems,
            pltpu.SemaphoreType.DMA,
            plane_sems,
            plane_sems,
            pltpu.SemaphoreType.DMA,
        ],
        compiler_params=pltpu.CompilerParams(
            collective_id=collective, has_side_effects=True, vmem_limit_bytes=8 << 20
        ),
    )(row, blocks)


def spread_kernel(sizes, row_ref, all_ref, send, arrive, own):
    place = Place(sizes)
    others = place.others()
    greet([ahead for ahead, _ in others])
    me = place.index(place.pipe, place.grp, place.dp)
    copies = []
    for i, (ahead, _) in enumerate(others):
        copies.append(remote(row_ref, all_ref.at[me], send.at[i], arrive.at[i], ahead))
        copies[-1].start()
    kept = pltpu.make_async_copy(row_ref, all_ref.at[me], own)
    kept.start()
    for i, (ahead, back) in enumerate(others):
        copies[i].wait_send()
        remote(
            row_ref, all_ref.at[place.index(*back)], send.at[i], arrive.at[i], ahead
        ).wait_recv()
    kept.wait()


def spread(row, sizes, collective):
    parts = math.prod(sizes)
    sems = pltpu.SemaphoreType.DMA((parts - 1,))
    return pl.pallas_call(
        functools.partial(spread_kernel, sizes),
        out_shape=jax.ShapeDtypeStruct((parts,) + row.shape, row.dtype),
        in_specs=[pl.BlockSpec(memory_space=pltpu.VMEM)],
        out_specs=pl.BlockSpec(memory_space=pltpu.VMEM),
        scratch_shapes=[sems, sems, pltpu.SemaphoreType.DMA],
        compiler_params=pltpu.CompilerParams(
            collective_id=collective, has_side_effects=True, vmem_limit_bytes=8 << 20
        ),
    )(row)


class Gather:
    def __init__(self, place, pieces, shards, fulls, send, arrive, own):
        self.place, self.pieces, self.shards, self.fulls = place, pieces, shards, fulls
        self.send, self.arrive, self.own = send, arrive, own
        pipe, grp, dp = place.pipe, place.grp, place.dp
        self.near = place.beside * (1 - pipe) + place.below * pipe
        self.far = place.below * (1 - pipe) + place.beside * pipe
        self.core = (1 - pipe, grp, dp)
        self.hops = place.dps - 1
        self.ends = (dp < self.hops, dp > 0)
        self.sides = ((pipe, grp, dp + 1), (pipe, grp, dp - 1))
        self.both = range(2 if self.hops else 0)
        self.waits, self.keeps = [], {}
        self.stages = [functools.partial(self.over_line, hop=hop) for hop in range(self.hops)]
        self.stages += [self.over_plane, self.pass_on, self.last]

    def partners(self):
        place = self.place
        pipe, grp, dp = place.pipe, place.grp, place.dp
        line = [(pipe, grp, place.line(k + 1)) for k in range(self.hops)]
        return line + [(pipe, self.near, dp), (pipe, self.far, dp), self.core]

    def view(self, n, *at):
        array, first, rows = self.pieces[n]
        return self.fulls[array].at[at + ((slice(None),) * (3 - len(at))) + (pl.ds(first, rows),)]

    def shard(self, n):
        array, first, rows = self.pieces[n]
        return self.shards[array].at[pl.ds(first, rows)]

    def launch(self, n, index, source, to, *at):
        copy = remote(
            source, self.view(n, *at), self.send.at[n, index], self.arrive.at[n, index], to
        )
        copy.start()
        self.waits.append(copy)

    def landed(self, n, index, *at):
        target = self.view(n, *at)
        remote(
            target, target, self.send.at[n, index], self.arrive.at[n, index], self.core
        ).wait_recv()

    def along(self, n, side, hop, finish=False):
        place, hops = self.place, self.hops
        origin = place.dp - hop if side == 0 else place.dp + hop
        here = origin >= 0 if side == 0 else origin <= hops
        index = side * hops + hop

        def copy():
            target = self.view(n, place.pipe, place.grp, origin)
            source = self.shard(n) if hop == 0 else target
            return remote(
                source, target, self.send.at[n, index], self.arrive.at[n, index], self.sides[side]
            )

        if finish:

            @pl.when(here & self.ends[side])
            def _():
                copy().wait_send()

            return
        if hop > 0:

            @pl.when(here)
            def _():
                self.landed(n, index - 1, place.pipe, place.grp, origin)

        if hop < hops:

            @pl.when(here & self.ends[side])
            def _():
                copy().start()

    def over_line(self, n, hop):
        place = self.place
        if hop == 0:
            target = self.view(n, place.pipe, place.grp, place.spot)
            self.keeps[n] = pltpu.make_async_copy(self.shard(n), target, self.own.at[n])
            self.keeps[n].start()
        for side in self.both:
            self.along(n, side, hop)

    def over_plane(self, n):
        place, first = self.place, 2 * self.hops
        pipe, grp, dp = place.pipe, place.grp, place.dp
        self.over_line(n, self.hops)
        if self.hops:
            self.keeps[n].wait()
            group, at = self.view(n, pipe, grp), (pipe, grp)
        else:
            group, at = self.shard(n), (pipe, grp, 0)
        self.launch(n, first, group, (pipe, self.near, dp), *at)
        self.launch(n, first + 1, group, (pipe, self.far, dp), *at)
        self.launch(n, first + 3, group, self.core, *at)

    def pass_on(self, n):
        pipe, first = self.place.pipe, 2 * self.hops
        self.landed(n, first, pipe, self.near)
        group = self.view(n, pipe, self.near)
        self.launch(n, first + 2, group, (pipe, self.far, self.place.dp), pipe, self.near)
        self.launch(n, first + 4, group, self.core, pipe, self.near)
        self.landed(n, first + 1, pipe, self.far)
        self.launch(n, first + 5, self.view(n, pipe, self.far), self.core, pipe, self.far)

    def last(self, n):
        pipe, first, across = self.place.pipe, 2 * self.hops, self.place.across
        self.landed(n, first + 2, pipe, across)
        self.launch(n, first + 6, self.view(n, pipe, across), self.core, pipe, across)

    def core_order(self):
        return (
            (),
            ((3, self.place.grp),),
            ((4, self.far), (5, self.near)),
            ((6, self.place.across),),
        )

    def from_core(self, n):
        for step in self.core_order():
            for index, grp in step:
                self.landed(n, 2 * self.hops + index, 1 - self.place.pipe, grp)

    def settle(self):
        for n in range(len(self.pieces)):
            for side in self.both:
                for hop in range(self.hops):
                    self.along(n, side, hop, finish=True)
        for copy in self.waits:
            copy.wait_send()
        if not self.hops:
            for keep in self.keeps.values():
                keep.wait()


LINE_TURN = 3


class LineGather(Gather):
    def __init__(self, place, shards, fulls, axes, send, arrive, own):
        super().__init__(place, [(n, 0, 0) for n in range(len(shards))], shards, fulls, send, arrive, own)
        self.axes = axes
        self.stages = [functools.partial(self.over_line, hop=hop) for hop in range(self.hops + 1)]

    def view(self, n, pipe, grp, origin):
        return self.fulls[n].at[(slice(None),) * self.axes[n] + (origin,)]

    def shard(self, n):
        return self.shards[n]

    def over_line(self, n, hop):
        super().over_line(n, hop)
        if hop == self.hops:
            self.keeps[n].wait()


def run_stages(stages, total, after=None):
    for turn in range(total + len(stages) - 1):
        for at, stage in enumerate(stages):
            if 0 <= turn - at < total:
                stage(turn - at)
        if after is not None:
            after(turn)


def gather_kernel(sizes, pieces, axes, routed, *refs):
    count, lines = max(piece[0] for piece in pieces) + 1, len(axes)
    shards, line_shards, refs = refs[:count], refs[count : count + lines], refs[count + lines :]
    if routed:
        rows_ref, refs = refs[0], refs[1:]
    fulls, line_fulls, refs = refs[:count], refs[count : count + lines], refs[count + lines :]
    if routed:
        arrived_ref, refs = refs[0], refs[1:]
    send, arrive, own, line_send, line_arrive, line_own, swap_send, swap_arrive, swap_own = refs
    place = Place(sizes)
    gather = Gather(place, pieces, shards, fulls, send, arrive, own)
    line = LineGather(place, line_shards, line_fulls, axes, line_send, line_arrive, line_own)
    greet([ahead for ahead, _ in place.others()] if routed else gather.partners())
    swaps = []

    def after(turn):
        for n in range(lines):
            if 0 <= turn - n - LINE_TURN <= gather.hops:
                line.over_line(n, turn - n - LINE_TURN)
        if turn == len(pieces) and routed:
            swaps.append(
                swap_all(place, rows_ref, arrived_ref, swap_send, swap_arrive, swap_own)
            )

    run_stages(gather.stages, len(pieces), after)
    for n in range(len(pieces)):
        gather.from_core(n)
    gather.settle()
    if lines:
        line.settle()
    for finish in swaps:
        finish()


def gather_all(shards, pieces, sizes, collective, rows=None, lines=(), axes=()):
    parts = math.prod(sizes)
    routed = rows is not None
    kinds = 2 * (sizes[2] - 1) + 7
    near = pl.BlockSpec(memory_space=pltpu.VMEM)
    out_shape = [jax.ShapeDtypeStruct(sizes + shard.shape, shard.dtype) for shard in shards]
    for line, axis in zip(lines, axes):
        shape = line.shape[:axis] + sizes[2:] + line.shape[axis:]
        out_shape.append(jax.ShapeDtypeStruct(shape, line.dtype))
    if routed:
        out_shape.append(jax.ShapeDtypeStruct(rows.shape, rows.dtype))
    operands = list(shards) + list(lines) + ([rows] if routed else [])
    sems = pltpu.SemaphoreType.DMA((len(pieces), kinds))
    line_sems = pltpu.SemaphoreType.DMA((max(len(lines), 1), kinds))
    swaps = pltpu.SemaphoreType.DMA((parts - 1 if routed else 1,))
    return pl.pallas_call(
        functools.partial(gather_kernel, sizes, tuple(pieces), tuple(axes), routed),
        out_shape=out_shape,
        in_specs=[near] * len(operands),
        out_specs=[near] + [pl.BlockSpec(memory_space=pltpu.HBM)] * (len(out_shape) - 1),
        scratch_shapes=[
            sems,
            sems,
            pltpu.SemaphoreType.DMA((len(pieces),)),
            line_sems,
            line_sems,
            pltpu.SemaphoreType.DMA((max(len(lines), 1),)),
            swaps,
            swaps,
            pltpu.SemaphoreType.DMA,
        ],
        compiler_params=pltpu.CompilerParams(
            collective_id=collective,
            has_side_effects=True,
            vmem_limit_bytes=(60 if routed else 16) << 20,
        ),
        cost_estimate=lasting(110 if routed else 15),
    )(*operands)


class Sums:
    block = 16
    filled = False

    def __init__(self, place, sources, chips, others, mine, planes, lines, send, arrive, own, store):
        self.place, self.sources, self.chips, self.others = place, sources, chips, others
        self.mine, self.planes, self.lines = mine, planes, lines
        self.send, self.arrive, self.own, self.store = send, arrive, own, store
        pipe, grp, dp = place.pipe, place.grp, place.dp
        self.near = place.beside * (1 - pipe) + place.below * pipe
        self.far = place.below * (1 - pipe) + place.beside * pipe
        self.copies, self.kept = {}, {}

    def launch(self, n, index, source, target, to):
        copy = remote(source, target, self.send.at[n, index], self.arrive.at[n, index], to)
        self.copies[n, index] = copy
        copy.start()

    def keep(self, n, index, source, target):
        self.kept[n, index] = pltpu.make_async_copy(source, target, self.own.at[n, index])
        self.kept[n, index].start()

    def blocks(self, n, body):
        deep = self.mine[n].shape[2] // self.block

        def one(i, _):
            body(i // deep, pl.ds(pl.multiple_of(i % deep * self.block, self.block), self.block))
            return 0

        lax.fori_loop(0, self.place.dps * deep, one, 0)

    def to_core(self, n):
        place = self.place
        core = (1 - place.pipe, place.grp, place.dp)
        if self.filled:
            self.launch(n, 0, self.sources[n], self.others[n], core)
        elif self.chips[n] is not None:
            self.launch(n, 0, self.sources[n].at[1 - place.pipe], self.others[n], core)
            self.keep(n, 0, self.sources[n].at[place.pipe], self.chips[n])

    def to_near(self, n):
        place, chip, other = self.place, self.chips[n], self.others[n]
        part = self.sources[n]
        if chip is not None:
            if not self.filled:
                self.kept[n, 0].wait()
            self.copies[n, 0].wait_recv()
            for g in range(place.grps):

                def add(d, at, g=g):
                    left = chip[g, d, at].astype(jnp.float32)
                    chip[g, d, at] = (left + other[g, d, at].astype(jnp.float32)).astype(
                        jnp.bfloat16
                    )

                self.blocks(n, add)
            part = chip
        else:
            for j, g in enumerate((self.far, place.grp)):
                self.keep(n, j, part.at[g], self.mine[n].at[j])
        to = (place.pipe, self.near, place.dp)
        self.launch(n, 1, part.at[self.near], self.planes[n].at[1], to)
        self.launch(n, 2, part.at[place.across], self.planes[n].at[0], to)

    def to_far(self, n):
        place, mine, plane, chip = self.place, self.mine[n], self.planes[n], self.chips[n]
        if chip is None:
            self.kept[n, 0].wait()
            self.kept[n, 1].wait()
        self.copies[n, 1].wait_recv()
        self.copies[n, 2].wait_recv()
        for j, g in enumerate((self.far, place.grp)):

            def add(d, at, j=j, g=g):
                left = mine[j, d, at] if chip is None else chip[g, d, at]
                total = left.astype(jnp.float32) + plane[j, d, at].astype(jnp.float32)
                mine[j, d, at] = total.astype(jnp.bfloat16)

            self.blocks(n, add)
            if j == 0:
                self.launch(n, 3, mine.at[0], plane.at[2], (place.pipe, self.far, place.dp))

    def to_lines(self, n):
        place, mine, plane = self.place, self.mine[n], self.planes[n]
        self.copies[n, 3].wait_recv()
        hops = place.dps - 1

        def add(d, at):
            total = mine[1, d, at].astype(jnp.float32) + plane[2, d, at].astype(jnp.float32)
            if hops:
                mine[1, d, at] = total.astype(jnp.bfloat16)
            else:
                self.store(n, at, total)

        self.blocks(n, add)
        for k in range(hops):
            to = place.line(k + 1)
            self.launch(
                n, 4 + k, mine.at[1, to], self.lines[n].at[k], (place.pipe, place.grp, to)
            )

    def to_sum(self, n):
        place, mine, lines = self.place, self.mine[n], self.lines[n]
        for k in range(place.dps - 1):
            self.copies[n, 4 + k].wait_recv()

        def add(i, _):
            at = pl.ds(pl.multiple_of(i * self.block, self.block), self.block)
            total = mine[1, place.spot, at].astype(jnp.float32)
            for k in range(place.dps - 1):
                total = total + lines[k, at].astype(jnp.float32)
            self.store(n, at, total)
            return 0

        lax.fori_loop(0, mine.shape[2] // self.block, add, 0)

    def settle(self):
        for copy in self.copies.values():
            copy.wait_send()


def sum_scratch(shapes, cores, sizes):
    low = jnp.bfloat16
    _, grps, dps = sizes
    wide = [(dps,) + shape for shape in shapes]
    chips = [pltpu.VMEM((grps,) + shape, low) for shape, core in zip(wide, cores) if core]
    scratch = chips + chips
    scratch += [pltpu.VMEM((2,) + shape, low) for shape in wide]
    scratch += [pltpu.VMEM((3,) + shape, low) for shape in wide]
    scratch += [pltpu.VMEM((max(dps - 1, 1),) + shape, low) for shape in shapes]
    sems = pltpu.SemaphoreType.DMA((len(shapes), 4 + dps - 1))
    return scratch + [sems, sems, pltpu.SemaphoreType.DMA((len(shapes), 2))]


def sum_refs(refs, cores):
    total = len(cores)

    def spread_out(found):
        found = iter(found)
        return [next(found) if core else None for core in cores]

    chosen = sum(cores)
    groups = []
    for count in (chosen, chosen, total, total, total):
        groups.append(refs[:count])
        refs = refs[count:]
    chips, others, mine, planes, lines = groups
    return (spread_out(chips), spread_out(others), mine, planes, lines) + tuple(refs[:3]), refs[3:]


def reduce_kernel(sizes, pieces, *refs):
    partial, out, refs = refs[0], refs[1], refs[2:]
    place = Place(sizes)
    scratch, _ = sum_refs(refs, (True,) * len(pieces))

    def store(n, at, total):
        to = pl.multiple_of(pieces[n][0] + at.start, Sums.block)
        out[pl.ds(to, Sums.block)] = total

    sources = [partial.at[:, :, :, pl.ds(first, rows)] for first, rows in pieces]
    sums = Sums(place, sources, *scratch, store)
    line = [(place.pipe, place.grp, place.line(k + 1)) for k in range(place.dps - 1)]
    near, far = [(place.pipe, grp, place.dp) for grp in (sums.near, sums.far)]
    greet(line + [near, far, (1 - place.pipe, place.grp, place.dp)])
    stages = [sums.to_core, sums.to_near, sums.to_far, sums.to_lines]
    stages += [sums.to_sum] if place.dps > 1 else []
    run_stages(stages, len(pieces))
    sums.settle()


def reduce_all(partial, pieces, sizes, collective):
    shapes = [(rows, partial.shape[-1]) for _, rows in pieces]
    return pl.pallas_call(
        functools.partial(reduce_kernel, sizes, tuple(pieces)),
        out_shape=jax.ShapeDtypeStruct(partial.shape[-2:], jnp.float32),
        in_specs=[pl.BlockSpec(memory_space=pl.ANY)],
        out_specs=pl.BlockSpec(memory_space=pltpu.VMEM),
        scratch_shapes=sum_scratch(shapes, (True,) * len(pieces), sizes),
        cost_estimate=lasting(15),
        compiler_params=pltpu.CompilerParams(
            collective_id=collective, has_side_effects=True, vmem_limit_bytes=48 << 20
        ),
    )(partial)


def finish_kernel(sizes, *refs):
    lefts, rights, starts, talls, refs = refs[:3], refs[3:6], refs[6:8], refs[8:10], refs[10:]
    small, rows_ref, blocks_ref, refs = refs[0], refs[1], refs[2], refs[3:]
    outs, squares, arrived_ref, blocks_arrived_ref, refs = refs[:4], *refs[4:7], refs[7:]
    cores = (False, False, True, False, False, False)
    scratch, refs = sum_refs(refs, cores)
    other_lefts, other_rights, other_talls, made, refs = (
        refs[:3],
        refs[3:6],
        refs[6:8],
        refs[8:13],
        refs[13:],
    )
    swap_send, swap_arrive, swap_own, plane_send, plane_arrive, plane_own = refs[:6]
    core_send, core_arrive = refs[6:]
    place = Place(sizes)
    pipe, grp, dp = place.pipe, place.grp, place.dp
    greet([ahead for ahead, _ in place.others()])

    mine = tuple(lefts) + tuple(rights) + tuple(talls)
    theirs = tuple(other_lefts) + tuple(other_rights) + tuple(other_talls)
    exchanged = {}
    for i in (0, 3, 1, 4, 2, 5, 6, 7):
        exchanged[i] = remote(
            mine[i], theirs[i], core_send.at[i], core_arrive.at[i], (1 - pipe, grp, dp)
        )
        exchanged[i].start()

    squares[...] = jnp.zeros_like(squares)

    def store(n, at, total):
        squares[0:1, 0 : total.shape[1]] += jnp.sum(total * total, 0, keepdims=True)
        if n < 3:
            outs[n][at] = total
        else:
            outs[3][at, pl.ds((n - 3) * total.shape[1], total.shape[1])] = total

    sources = (made[0], made[1], small, made[2], made[3], made[4])
    sums = Sums(place, sources, *scratch, store)
    sums.to_core(2)
    swap = swap_all(place, rows_ref, arrived_ref, swap_send, swap_arrive, swap_own)
    plane_swap = swap_plane(
        place, blocks_ref, blocks_arrived_ref, plane_send, plane_arrive, plane_own
    )
    wide = made[0].shape[1] * made[0].shape[2]

    def form(i):
        exchanged[i].wait_recv()
        exchanged[3 + i].wait_recv()
        for g in range(place.grps):
            first = pl.multiple_of((pipe * place.grps + g) * wide, 128)
            at = pl.ds(first, wide)
            total = left_transposed(lefts[i][:, at], rights[i][...])
            total = total + left_transposed(other_lefts[i][:, at], other_rights[i][...])
            made[i][g] = total.astype(jnp.bfloat16).reshape(made[i].shape[1:])

    def form_tall(i):
        exchanged[6 + i].wait_recv()
        for g in range(place.grps):
            at = pl.ds(g * wide, wide)
            total = left_transposed(starts[0][:, at], talls[i][...])
            total = total + left_transposed(starts[1][:, at], other_talls[i][...])
            made[3 + i][g] = total.astype(jnp.bfloat16).reshape(made[3 + i].shape[1:])

    form(0)
    sums.to_near(0)
    form(1)
    sums.to_near(1)
    form(2)
    sums.to_near(3)
    sums.to_near(2)
    sums.to_far(0)
    form_tall(0)
    sums.to_near(4)
    sums.to_far(1)
    form_tall(1)
    sums.to_near(5)
    sums.to_far(3)
    sums.to_far(2)
    sums.to_lines(0)
    sums.to_lines(1)
    sums.to_lines(3)
    sums.to_far(4)
    sums.to_lines(2)
    sums.to_far(5)
    sums.to_lines(4)
    sums.to_lines(5)
    for n in (0, 1, 3, 2, 4, 5):
        sums.to_sum(n)
    sums.settle()
    for copy in exchanged.values():
        copy.wait_send()
    plane_swap()
    swap()


def finish_all(lefts, rights, starts, talls, small, rows, blocks, sizes, collective):
    low = jnp.bfloat16
    parts = math.prod(sizes)
    _, grps, dps = sizes
    width = lefts[0].shape[1]
    shape = (width // parts, rights[0].shape[1])
    shapes = [shape, shape, (small.shape[-2], small.shape[-1]), shape, shape, shape]
    made = pltpu.VMEM((grps, dps) + shape, low)
    anywhere = pl.BlockSpec(memory_space=pl.ANY)
    near = pl.BlockSpec(memory_space=pltpu.VMEM)
    swaps = pltpu.SemaphoreType.DMA((parts - 1,))
    plane_swaps = pltpu.SemaphoreType.DMA((sizes[0] * grps - 1,))
    one = pltpu.SemaphoreType.DMA
    operands = (*lefts, *rights, *starts, *talls, small, rows, blocks)
    joined = (shape[0], 3 * shape[1])
    widest = (8, max(shape[1] for shape in shapes))
    out_shape = [
        jax.ShapeDtypeStruct(shape, jnp.float32) for shape in shapes[:3] + [joined, widest]
    ]
    out_shape += [jax.ShapeDtypeStruct(extra.shape, extra.dtype) for extra in (rows, blocks)]
    return pl.pallas_call(
        functools.partial(finish_kernel, sizes),
        out_shape=out_shape,
        in_specs=[near] * 10 + [anywhere, near, near],
        out_specs=[near] * 7,
        scratch_shapes=sum_scratch(shapes, (False, False, True, False, False, False), sizes)
        + [pltpu.VMEM(item.shape, low) for item in (*lefts, *rights, *talls)]
        + [made] * 5
        + [
            swaps,
            swaps,
            one,
            plane_swaps,
            plane_swaps,
            one,
            pltpu.SemaphoreType.DMA((8,)),
            pltpu.SemaphoreType.DMA((8,)),
        ],
        compiler_params=pltpu.CompilerParams(
            collective_id=collective, has_side_effects=True, vmem_limit_bytes=56 << 20
        ),
    )(*operands)


def head_kernel(sizes, rows_per, vocab, gather_cuts, sum_cuts, *refs):
    row_ref, table, bias, info, out, word, bias_out, stats, refs = *refs[:8], refs[8:]
    full, logits, columns, laid, held, result, slopes, outgoing, refs = *refs[:8], refs[8:]
    cores = (True,) * sum_cuts
    scratch, refs = sum_refs(refs, cores)
    gather_send, gather_arrive, gather_own, swap_send, swap_arrive, swap_own = refs[:6]
    all_send, all_arrive = refs[6:]
    place = Place(sizes)
    pipes, grps, dps = sizes
    others = place.others()
    slots, width = row_ref.shape
    tall = slots // gather_cuts
    pieces = [(0, i * tall, tall) for i in range(gather_cuts)]
    gather = Gather(place, pieces, [row_ref], [full], gather_send, gather_arrive, gather_own)
    greet([ahead for ahead, _ in others])
    pipe, grp, hops = place.pipe, place.grp, dps - 1
    me = place.index(pipe, grp, place.dp)
    cells = table.shape[0]
    local = lax.broadcasted_iota(jnp.int32, (1, cells), 1)
    column = me * rows_per + local
    used = (local < rows_per) & (column < vocab)
    column = jnp.where(used, column, -1).astype(jnp.float32)
    groups = pipes * grps

    def parts(body):
        lax.fori_loop(0, pipes * grps * dps, lambda i, _: (body(i), 0)[1], 0, unroll=8)

    def spot(i):
        return i // (grps * dps), i // dps % grps, i % dps

    def fill(i):
        columns[spot(i) + (slice(None), slice(0, 8))] = info[i].T

    def form_logits(n, p, g):
        _, first, rows = pieces[n]
        at = pl.ds(first, rows)
        found = right_transposed(full[p, g, :, at].reshape(dps * rows, width), table[...])
        found = jnp.where(used, found + bias[...], -1e30)
        peak = jnp.max(found, -1, keepdims=True)
        total = jnp.sum(jnp.exp(found - peak), -1, keepdims=True)
        labels = columns[p, g, :, at, 0:1].reshape(dps * rows, 1)
        label = jnp.sum(jnp.where(column == labels, found, 0.0), -1, keepdims=True)
        logits[p, g, :, at] = found.reshape(dps, rows, cells)
        columns[p, g, :, at, 2:3] = peak.reshape(dps, rows, 1)
        columns[p, g, :, at, 3:4] = total.reshape(dps, rows, 1)
        columns[p, g, :, at, 4:5] = label.reshape(dps, rows, 1)

    def after(turn):
        if turn == 0:
            parts(fill)
        arrived = (
            ((pipe, grp),),
            ((pipe, gather.near), (pipe, gather.far)),
            ((pipe, place.across),),
            (),
        )
        for step in range(4):
            n = turn - hops - step
            if 0 <= n < gather_cuts:
                for p, g in arrived[step]:
                    form_logits(n, p, g)
                for index, g in gather.core_order()[step]:
                    gather.landed(n, 2 * hops + index, 1 - pipe, g)
                    form_logits(n, 1 - pipe, g)

    run_stages(gather.stages, gather_cuts, after)
    after(gather_cuts + hops + 2)

    def lay(i):
        laid[i] = columns[spot(i) + (slice(None), slice(0, 8))].T

    parts(lay)
    swap_all(place, laid, held, swap_send, swap_arrive, swap_own)()
    peaks = held[:, 2]
    peak = jnp.max(peaks, 0, keepdims=True)
    result[...] = jnp.zeros_like(result)
    result[0:1] = peak
    result[1:2] = jnp.sum(held[:, 3] * jnp.exp(peaks - peak), 0, keepdims=True)
    result[2:3] = jnp.sum(held[:, 4], 0, keepdims=True)
    copies = []
    for i, (ahead, _) in enumerate(others):
        copies.append(remote(result, stats.at[me], all_send.at[i], all_arrive.at[i], ahead))
        copies[-1].start()
    stats[me] = result[...]
    for i, (ahead, back) in enumerate(others):
        copies[i].wait_send()
        origin = place.index(*back)
        remote(
            result, stats.at[origin], all_send.at[i], all_arrive.at[i], ahead
        ).wait_recv()

    def back(i):
        columns[spot(i) + (slice(None), slice(8, 16))] = stats[i].T

    parts(back)

    size = slots // sum_cuts
    half = grps * dps * size

    def store(n, at, total):
        to = pl.multiple_of(n * size + at.start, Sums.block)
        out[pl.ds(to, Sums.block)] = total

    sums = Sums(place, [outgoing.at[n] for n in range(sum_cuts)], *scratch, store)
    sums.filled = True
    bias_out[...] = jnp.zeros_like(bias_out)
    word[...] = jnp.zeros_like(word)

    def form_slopes(n):
        at = pl.ds(n * size, size)

        def one(i, _):
            p, g = i // grps, i % grps
            kept = columns[p, g, :, at].reshape(dps * size, columns.shape[-1])
            found = logits[p, g, :, at].reshape(dps * size, cells)
            hits = (column == kept[:, 0:1]).astype(jnp.float32)
            slope = kept[:, 1:2] * (jnp.exp(found - kept[:, 8:9]) / kept[:, 9:10] - hits)
            bias_out[0:1] += jnp.sum(slope, 0, keepdims=True)
            slopes[n % 2, i] = slope.astype(jnp.bfloat16)
            return 0

        lax.fori_loop(0, groups, one, 0)
        for q, target in ((1 - place.pipe, outgoing.at[n]), (place.pipe, sums.chips[n])):
            left = slopes[n % 2, pl.ds(q * grps, grps)].reshape(half, cells)
            target[...] = matmul(left, table[...]).astype(jnp.bfloat16).reshape(target.shape)
        sums.to_core(n)

    def form_word(n):
        right = full[:, :, :, pl.ds(n * size, size)].reshape(pipes * half, width)
        word[...] += left_transposed(slopes[n % 2].reshape(pipes * half, cells), right)

    stages = [form_slopes, sums.to_near, sums.to_far, sums.to_lines, sums.to_sum]

    def then(turn):
        if turn < sum_cuts:
            form_word(turn)

    run_stages(stages, sum_cuts, then)
    sums.settle()
    gather.settle()


def head_all(row, table, bias, info, rows_per, vocab, sizes, collective):
    low = jnp.bfloat16
    parts = math.prod(sizes)
    pipes, grps, dps = sizes
    slots, width = row.shape
    cells = table.shape[0]
    gather_cuts, sum_cuts = 4, 8
    size = slots // sum_cuts
    near = pl.BlockSpec(memory_space=pltpu.VMEM)
    gathers = pltpu.SemaphoreType.DMA((gather_cuts, 2 * (dps - 1) + 7))
    swaps = pltpu.SemaphoreType.DMA((parts - 1,))
    return pl.pallas_call(
        functools.partial(head_kernel, sizes, rows_per, vocab, gather_cuts, sum_cuts),
        out_shape=(
            jax.ShapeDtypeStruct(row.shape, jnp.float32),
            jax.ShapeDtypeStruct(table.shape, jnp.float32),
            jax.ShapeDtypeStruct((8, cells), jnp.float32),
            jax.ShapeDtypeStruct(info.shape, jnp.float32),
        ),
        in_specs=[near] * 4,
        out_specs=[near] * 4,
        scratch_shapes=[
            pltpu.VMEM(sizes + row.shape, low),
            pltpu.VMEM(sizes + (slots, cells), jnp.float32),
            pltpu.VMEM(sizes + (slots, 16), jnp.float32),
            pltpu.VMEM(info.shape, jnp.float32),
            pltpu.VMEM(info.shape, jnp.float32),
            pltpu.VMEM(info.shape[1:], jnp.float32),
            pltpu.VMEM((2, pipes * grps, dps * size, cells), low),
            pltpu.VMEM((sum_cuts, grps, dps, size, width), low),
        ]
        + sum_scratch([(size, width)] * sum_cuts, (True,) * sum_cuts, sizes)
        + [
            gathers,
            gathers,
            pltpu.SemaphoreType.DMA((gather_cuts,)),
            swaps,
            swaps,
            pltpu.SemaphoreType.DMA,
            swaps,
            swaps,
        ],
        compiler_params=pltpu.CompilerParams(
            collective_id=collective, has_side_effects=True, vmem_limit_bytes=62 << 20
        ),
    )(row, table, bias, info)


def pair_rows(pair, first):
    pair = pair.astype(jnp.float32)
    low = jnp.bfloat16
    return jnp.concatenate(
        [jnp.where(first, pair, 0.0).astype(low), jnp.where(first, 0.0, pair).astype(low)], 0
    )


def pair_probs(rows, keys, live, scale):
    scores = jnp.where(live, right_transposed(rows, keys) * scale, -1e30)
    exp_scores = jnp.exp(scores - jnp.max(scores, -1, keepdims=True))
    return exp_scores / jnp.sum(exp_scores, -1, keepdims=True)


def attention_masks(lengths_ref, slots, seq_len, lanes):
    live = lax.broadcasted_iota(jnp.int32, (1, seq_len), 1) < lengths_ref[pl.program_id(0)]
    first = lax.broadcasted_iota(jnp.int32, (slots, lanes), 1) < lanes // 2
    return live, first


def attention_kernel(scale, lanes, lengths_ref, q_ref, k_ref, v_ref, out_ref):
    slots = q_ref.shape[0]
    live, first = attention_masks(lengths_ref, slots, k_ref.shape[0], lanes)
    for pair in range(q_ref.shape[1] // lanes):
        at = slice(pair * lanes, (pair + 1) * lanes)
        probs = pair_probs(pair_rows(q_ref[:, at], first), k_ref[:, at], live, scale)
        context = matmul(probs.astype(jnp.bfloat16), v_ref[:, at])
        out_ref[:, at] = jnp.where(first, context[:slots], context[slots:]).astype(jnp.bfloat16)


def attention_back_kernel(
    scale, lanes, lengths_ref, q_ref, k_ref, v_ref, grad_ref, dq_ref, dk_ref, dv_ref
):
    slots = q_ref.shape[0]
    low = jnp.bfloat16
    live, first = attention_masks(lengths_ref, slots, k_ref.shape[0], lanes)
    for pair in range(q_ref.shape[1] // lanes):
        at = slice(pair * lanes, (pair + 1) * lanes)
        rows, grads = pair_rows(q_ref[:, at], first), pair_rows(grad_ref[:, at], first)
        probs = pair_probs(rows, k_ref[:, at], live, scale)
        dv_ref[:, at] = left_transposed(probs.astype(low), grads).astype(low)
        d_probs = right_transposed(grads, v_ref[:, at])
        d_scores = probs * (d_probs - jnp.sum(probs * d_probs, -1, keepdims=True))
        d_scores = d_scores.astype(low)
        d_query = matmul(d_scores, k_ref[:, at]) * scale
        dq_ref[:, at] = jnp.where(first, d_query[:slots], d_query[slots:]).astype(low)
        dk_ref[:, at] = (left_transposed(d_scores, rows) * scale).astype(low)


def attention(lengths, queries, both, grads=None):
    own = lengths.shape[0]
    width = queries.shape[1]
    slots, seq_len = queries.shape[0] // own, both.shape[0] // own
    lanes = 2 * width // H
    scale = (width // H) ** (-0.5)
    cuts = 2
    part = width // cuts
    row = pl.BlockSpec((slots, part), lambda s, h: (s, h))
    keys = pl.BlockSpec((seq_len, part), lambda s, h: (s, h))
    values = pl.BlockSpec((seq_len, part), lambda s, h: (s, cuts + h))
    in_specs = [pl.BlockSpec(memory_space=pltpu.SMEM), row, keys, values]
    flat = jax.ShapeDtypeStruct(queries.shape, jnp.bfloat16)
    tall = jax.ShapeDtypeStruct((both.shape[0], width), jnp.bfloat16)
    if grads is None:
        return pl.pallas_call(
            functools.partial(attention_kernel, scale, lanes),
            grid=(own, cuts),
            out_shape=flat,
            in_specs=in_specs,
            out_specs=row,
            cost_estimate=lasting(8),
        )(lengths, queries, both, both)
    return pl.pallas_call(
        functools.partial(attention_back_kernel, scale, lanes),
        grid=(own, cuts),
        out_shape=(flat, tall, tall),
        in_specs=in_specs + [row],
        out_specs=(row, keys, keys),
        cost_estimate=lasting(11),
    )(lengths, queries, both, both, grads)


def even_pieces(array, rows, cuts):
    size = rows // cuts
    return [(array, i * size, size) for i in range(cuts)]


def start_all(row, blocks, sizes, collective):
    if collective is None:
        return lax.all_gather(row, AXES, axis=0), lax.all_to_all(blocks, PLANE, 0, 0)
    return begin(row, blocks, sizes, collective)


def gather_weights(shards, pieces, lines, axes, sizes, collective, rows):
    if collective is None:
        fulls = [lax.all_gather(shard, AXES, axis=0) for shard in shards]
        line_fulls = [
            lax.all_gather(line, "dp", axis=axis) for line, axis in zip(lines, axes)
        ]
        arrived = lax.all_to_all(rows, AXES, 0, 0)
    else:
        *fulls, arrived = gather_all(shards, pieces, sizes, collective, rows, lines, axes)
        fulls, line_fulls = fulls[: len(shards)], fulls[len(shards) :]
    return [full.reshape(-1, full.shape[-1]) for full in fulls], line_fulls, arrived


def gather_rows(shard, sizes, collective, cuts):
    if collective is None:
        axes = AXES if sizes[2] > 1 else PLANE
        return lax.all_gather(shard, axes, axis=0, tiled=True)
    (full,) = gather_all([shard], even_pieces(0, shard.shape[0], cuts), sizes, collective)
    return full.reshape(-1, full.shape[-1])


def sum_rows(partial, sizes, collective, cuts):
    if collective is None:
        axes = AXES if sizes[2] > 1 else PLANE
        total = lax.psum_scatter(partial, axes, scatter_dimension=0, tiled=True)
        return total.astype(jnp.float32)
    shaped = partial.reshape(sizes + (-1, partial.shape[1]))
    size = shaped.shape[3] // cuts
    return reduce_all(shaped, [(i * size, size) for i in range(cuts)], sizes, collective)


def sum_chips(lefts, rights, starts, talls, small, rows, blocks, sizes, collective):
    if collective is not None:
        small = small.reshape(sizes + (-1, small.shape[1]))
        *sums, squares, rows, blocks = finish_all(
            lefts, rights, starts, talls, small, rows, blocks, sizes, collective
        )
        return sums, jnp.sum(squares), rows, blocks
    made = [chip_sum(left, right) for left, right in zip(lefts, rights)]
    start = jnp.concatenate(starts, 0)
    made += [left_transposed(start, both_cores(tall)).astype(jnp.bfloat16) for tall in talls]
    partials = made[:2] + [chip_half(small)] + made[2:]
    sums = [
        lax.psum_scatter(p, CHIPS, scatter_dimension=0, tiled=True).astype(jnp.float32)
        for p in partials
    ]
    squares = sum(jnp.sum(total * total) for total in sums)
    sums = sums[:3] + [jnp.concatenate(sums[3:], 1)]
    rows = lax.all_to_all(rows, AXES, 0, 0)
    blocks = lax.all_to_all(blocks, PLANE, 0, 0)
    return sums, squares, rows, blocks


def line_shift(shard, step):
    size = lax.axis_size("dp")
    return lax.ppermute(shard, "dp", [(i, (i + step) % size) for i in range(size)])


def line_sum(partial, collective):
    partial = partial.astype(jnp.bfloat16)
    if collective is None:
        total = lax.psum_scatter(partial, "dp", scatter_dimension=0, tiled=False)
        return total.astype(jnp.float32)
    size = lax.axis_size("dp")
    me = lax.axis_index("dp")

    def entry(step):
        return lax.dynamic_index_in_dim(partial, (me + step) % size, 0, keepdims=False)

    total = entry(0).astype(jnp.float32)
    for step in range(1, size):
        total = total + line_shift(entry(step), step).astype(jnp.float32)
    return total


def spread_row(row, sizes, collective):
    if collective is None:
        return lax.all_gather(row, AXES, axis=0)
    return spread(row, sizes, collective)


def output_layer(row, table, bias, labels, weights, rows_per, vocab, sizes, collective):
    parts = math.prod(sizes)
    if collective is not None:
        bias = jnp.pad(bias, (0, table.shape[0] - rows_per))[None]
        info = jnp.stack([labels.astype(jnp.float32), weights]).reshape(2, parts, -1)
        info = jnp.pad(info.swapaxes(0, 1), ((0, 0), (0, 6), (0, 0)))
        grad, word, d_bias, stats = head_all(
            row, table, bias, info, rows_per, vocab, sizes, collective
        )
        stats = [stats[:, i].reshape(-1) for i in range(3)]
        return grad, word, d_bias[0, :rows_per], stats
    rows = gather_rows(row, sizes, None, 1)
    cells = jnp.arange(table.shape[0], dtype=jnp.int32)
    column = lax.axis_index(AXES) * rows_per + cells
    column = jnp.where((cells < rows_per) & (column < vocab), column, -1)
    bias = jnp.pad(bias, (0, table.shape[0] - rows_per))
    logits = jnp.where(column >= 0, right_transposed(rows, table) + bias, -1e30)
    own_peak = jnp.max(logits, -1)
    own_total = jnp.sum(jnp.exp(logits - own_peak[:, None]), -1)
    hits = labels[:, None] == column
    own_label = jnp.sum(jnp.where(hits, logits, 0.0), -1)
    peak = lax.pmax(own_peak, AXES)
    total, label = lax.psum((own_total * jnp.exp(own_peak - peak), own_label), AXES)
    slopes = weights[:, None] * (
        jnp.exp(logits - peak[:, None]) / total[:, None] - hits.astype(jnp.float32)
    )
    low = slopes.astype(jnp.bfloat16)
    grad = sum_rows(matmul(low, table).astype(jnp.bfloat16), sizes, None, 1)
    return grad, left_transposed(low, rows), jnp.sum(slopes, 0)[:rows_per], (peak, total, label)


def adam_step(weight, first, second, grad, factor, rate):
    clipped = grad * factor
    first = beta_one * first + (1.0 - beta_one) * clipped
    second = beta_two * second + (1.0 - beta_two) * clipped * clipped
    first_hat = first / (1.0 - beta_one**STEP)
    second_hat = second / (1.0 - beta_two**STEP)
    weight = weight - rate * (first_hat / (jnp.sqrt(second_hat) + epsilon) + weight_decay * weight)
    return (weight, first, second)


def per_device(
    token_ids,
    lengths,
    masked_at,
    labels,
    word_table,
    word_first,
    word_second,
    pos_table,
    pos_first,
    pos_second,
    qkv_weight,
    qkv_first,
    qkv_second,
    square_weight,
    square_first,
    square_second,
    up_weight,
    up_first,
    up_second,
    down_weight,
    down_first,
    down_second,
    vec_table,
    vec_first,
    vec_second,
    head_bias,
    bias_first,
    bias_second,
):
    narrow = jnp.bfloat16
    seq_len, slots = token_ids.shape[1], masked_at.shape[1]
    width = word_table.shape[1]
    vocab = head_bias.shape[0]
    rows_per = word_table.shape[0]
    parts = lax.axis_size(AXES)
    halves = lax.axis_size("pipe")
    me = lax.axis_index(AXES)
    own = token_ids.shape[0] // halves
    first_own = lax.axis_index("pipe") * own
    head_dim = width // H
    sizes = tuple(lax.axis_size(axis) for axis in AXES)
    shards = (word_table, qkv_weight, square_weight[0], up_weight, down_weight)
    direct = sizes[:2] == (2, 4) and all(shard.shape[0] % 32 == 0 for shard in shards)
    ids = tuple(range(11)) if direct else (None,) * 11
    plane_sizes = sizes[:2] + (1,)

    spare = -(seq_len + slots + 1) % 128
    packed = jnp.concatenate(
        [token_ids, labels, lengths[:, None], jnp.zeros((token_ids.shape[0], spare), jnp.int32)], 1
    )
    packed = lax.dynamic_slice_in_dim(packed, first_own, own, 0)
    planes = sizes[0] * sizes[1]
    units = up_weight.shape[1] // planes
    cut = me // sizes[2]
    blocks = up_weight.astype(narrow).reshape(up_weight.shape[0], planes, units).swapaxes(0, 1)
    packed, blocks = start_all(packed, blocks, sizes, ids[0])
    all_ids = packed[:, :, :seq_len]
    all_labels = packed[:, :, seq_len : seq_len + slots].reshape(-1)
    all_lengths = packed[:, :, seq_len + slots]
    places = jnp.arange(seq_len, dtype=jnp.int32)
    all_live = places[None, None, :] < all_lengths[:, :, None]
    all_counts = masked_counts(all_lengths, slots)
    total = jnp.sum(all_counts).astype(jnp.float32)
    slot_index = jnp.arange(slots, dtype=jnp.int32)
    all_valid = (slot_index < all_counts[:, :, None]).astype(jnp.float32).reshape(-1)
    own_lengths = lax.dynamic_slice_in_dim(lengths, first_own, own, 0)
    masked = lax.dynamic_slice_in_dim(masked_at, first_own, own, 0)

    cells = rows_per + -rows_per % 128
    word_low = jnp.pad(word_table.astype(narrow), ((0, cells - rows_per), (0, 0)))
    routes = Routes(all_ids.reshape(parts, -1), all_live.reshape(parts, -1), rows_per)
    small = pos_table.shape[0] + vec_table.shape[0]
    spare = -small % 128
    small_low = jnp.concatenate(
        [pos_table.T, vec_table.T, jnp.zeros((pos_table.shape[1], spare), jnp.float32)], 1
    ).astype(narrow)
    low = [
        small_low,
        qkv_weight.astype(narrow),
        square_weight[0].astype(narrow),
        square_weight[1].astype(narrow),
    ]
    deep = small_low.shape[0]
    pieces = [(i, 0, deep) for i in range(4)]
    send = routes.table_rows(word_low, 0, routes.room).reshape(parts, -1, width)
    (small_full, qkv_low, out_low, turn_low), (up_low, down_low), arrived = gather_weights(
        low, pieces, [blocks, down_weight.astype(narrow)], [1, 0], sizes, ids[1], send
    )
    up_low = up_low.reshape(width, units)
    down_low = down_low.reshape(units, width)
    word_rows = routes.fetch(word_low, arrived.reshape(-1, width))
    small_full = small_full.T
    pos_low = small_full[:seq_len]
    vec_rows = small_full[seq_len:small].astype(jnp.float32)
    query_low, both_low = qkv_low[:, :width], qkv_low[:, width:]

    second = (places[None, :] >= ((own_lengths + 1) // 2)[:, None]).reshape(-1, 1)
    embedded = (
        word_rows
        + jnp.tile(pos_low.astype(jnp.float32), (own, 1))
        + jnp.where(second, vec_rows[1], vec_rows[0])
    )
    start, norm_zero = norm_forward(embedded, vec_rows[2], vec_rows[3])
    start_low = start.astype(narrow)
    both_bias = jnp.concatenate([jnp.zeros_like(vec_rows[5]), vec_rows[5]])
    both = (matmul(start_low, both_low) + both_bias).astype(narrow)
    pick = one_hot(masked, seq_len, jnp.float32)
    chosen = rows_by_seq(pick, start.reshape(own, seq_len, width)).reshape(-1, width)
    chosen_low = chosen.astype(narrow)
    start_own, start_other = both_halves(start_low)
    queries = (matmul(chosen_low, query_low) + vec_rows[4]).astype(narrow)
    context = attention(own_lengths, queries, both)
    context, start_other = lax.optimization_barrier((context, start_other))
    branch = matmul(context, out_low) + vec_rows[6]
    hidden, norm_one = norm_forward(chosen + branch, vec_rows[7], vec_rows[8])
    hidden = hidden.astype(narrow)

    plane_hidden = gather_rows(hidden, plane_sizes, ids[2], 2)
    up_bias = lax.dynamic_slice_in_dim(vec_rows[15:].reshape(-1), cut * units, units, 0)
    inner = matmul(plane_hidden, up_low) + up_bias
    activ = jax.nn.gelu(inner, approximate=False).astype(narrow)
    branch = sum_rows(matmul(activ, down_low).astype(narrow), plane_sizes, ids[3], 2) + vec_rows[9]
    mixed, norm_two = norm_forward(hidden.astype(jnp.float32) + branch, vec_rows[10], vec_rows[11])
    picked = mixed.astype(narrow)
    turned = matmul(picked, turn_low) + vec_rows[12]
    normed, norm_head = norm_forward(
        jax.nn.gelu(turned, approximate=False), vec_rows[13], vec_rows[14]
    )

    bias_row = jnp.pad(head_bias, (0, parts * rows_per - vocab))
    bias_row = lax.dynamic_slice_in_dim(bias_row, me * rows_per, rows_per, 0)
    d_normed, d_word, d_bias, (peak, exp_total, label_logit) = output_layer(
        normed.astype(narrow),
        word_low,
        bias_row,
        all_labels,
        all_valid / total,
        rows_per,
        vocab,
        sizes,
        ids[4],
    )
    loss_total = jnp.sum(all_valid * (peak + jnp.log(exp_total) - label_logit))

    d_gelu, d_gain_head, d_shift_head = norm_backward(d_normed, norm_head, vec_rows[13])
    d_turned = (d_gelu * gelu_slope(turned)).astype(narrow)
    d_turn_bias = jnp.sum(d_turned.astype(jnp.float32), 0)
    d_picked = right_transposed(d_turned, turn_low)
    same = masked[:, :, None] == masked[:, None, :]
    earlier = slot_index[None, :] < slot_index[:, None]
    first_slot = jnp.logical_not(jnp.any(same & earlier, 2))
    merge = (same & first_slot[:, :, None]).astype(jnp.float32)
    d_mixed = rows_by_seq(merge, d_picked.reshape(own, slots, width)).reshape(-1, width)
    d_pre, d_gain_two, d_shift_two = norm_backward(d_mixed, norm_two, vec_rows[10])
    d_branch = d_pre.astype(narrow)
    d_down_bias = jnp.sum(d_branch.astype(jnp.float32), 0)
    plane_branch = gather_rows(d_branch, plane_sizes, ids[7], 2)
    d_down = left_transposed(activ, plane_branch).astype(narrow)
    d_inner = (right_transposed(plane_branch, down_low) * gelu_slope(inner)).astype(narrow)
    d_up_bias = jnp.sum(d_inner.astype(jnp.float32), 0)
    d_up_bias = lax.dynamic_update_slice_in_dim(
        jnp.zeros((planes * units,), jnp.float32), d_up_bias, cut * units, 0
    ).reshape(-1, width)
    d_up = left_transposed(plane_hidden, d_inner).astype(narrow)
    d_hidden = sum_rows(right_transposed(d_inner, up_low).astype(narrow), plane_sizes, ids[8], 2)
    d_hidden = (d_pre + d_hidden).astype(narrow)

    d_hidden, d_down, d_up = lax.optimization_barrier((d_hidden, d_down, d_up))
    own_down = line_sum(d_down.reshape(sizes[2], -1, width), ids[7])
    d_up = d_up.reshape(planes, sizes[2], -1, units).swapaxes(0, 1)
    up_blocks = line_sum(d_up, ids[7]).astype(narrow)
    d_pre, d_gain_one, d_shift_one = norm_backward(
        d_hidden.astype(jnp.float32), norm_one, vec_rows[7]
    )
    d_branch = d_pre.astype(narrow)
    d_out_bias = jnp.sum(d_branch.astype(jnp.float32), 0)
    d_attended = d_branch
    d_context = right_transposed(d_branch, out_low).astype(narrow)
    d_query, d_key, d_value = attention(own_lengths, queries, both, d_context)
    d_query_bias = jnp.sum(d_query.astype(jnp.float32), 0)
    d_value_bias = jnp.sum(d_value.astype(jnp.float32), 0)
    d_chosen = d_pre + right_transposed(d_query, query_low)
    d_both = jnp.concatenate([d_key, d_value], 1)
    d_start = right_transposed(d_both, both_low) + rows_to_seq(
        pick, d_chosen.reshape(own, slots, width)
    ).reshape(-1, width)
    d_embedded, d_gain_zero, d_shift_zero = norm_backward(d_start, norm_zero, vec_rows[2])
    d_seg_zero = jnp.sum(jnp.where(second, 0.0, d_embedded), 0)
    d_seg_one = jnp.sum(jnp.where(second, d_embedded, 0.0), 0)
    d_embedded_low = d_embedded.astype(narrow)
    send = routes.token_rows(d_embedded_low, 0, routes.room).reshape(parts, -1, width)
    d_small = jnp.concatenate(
        [
            jnp.sum(d_embedded.reshape(own, seq_len, width), 0),
            jnp.stack(
                [
                    d_seg_zero,
                    d_seg_one,
                    d_gain_zero,
                    d_shift_zero,
                    d_query_bias,
                    d_value_bias,
                    d_out_bias,
                    d_gain_one,
                    d_shift_one,
                    d_down_bias,
                    d_gain_two,
                    d_shift_two,
                    d_turn_bias,
                    d_gain_head,
                    d_shift_head,
                ]
            ),
            d_up_bias,
            jnp.zeros((spare, width), jnp.float32),
        ],
        0,
    )
    (own_out, own_turn, own_small, own_qkv), squares, arrived, up_blocks = sum_chips(
        [context, picked, chosen_low],
        [d_attended, d_turned, d_query],
        [start_own, start_other],
        [d_key, d_value],
        d_small.T.astype(narrow),
        send,
        up_blocks,
        sizes,
        ids[9],
    )
    own_up = up_blocks.swapaxes(0, 1).reshape(up_weight.shape).astype(jnp.float32)
    d_word = routes.give(d_embedded_low, arrived.reshape(-1, width), d_word)[:rows_per]
    owned = (
        d_word,
        own_small[:, :seq_len].T,
        own_qkv,
        jnp.stack([own_out, own_turn]),
        own_up,
        own_down,
        own_small[:, seq_len:small].T,
    )
    local_squares = squares + jnp.sum(d_bias * d_bias)
    for grad in (d_word, own_up, own_down):
        local_squares = local_squares + jnp.sum(grad * grad)
    spare = -(rows_per + 1) % 128
    last = jnp.concatenate([d_bias, local_squares[None], jnp.zeros((spare,), jnp.float32)])
    last = spread_row(last.reshape(8, -1), sizes, ids[10]).reshape(parts, -1)
    bias_grad = last[:, :rows_per].reshape(-1)[:vocab]
    grad_norm = jnp.sqrt(jnp.sum(last[:, rows_per]))
    factor = clip_norm / jnp.maximum(grad_norm, clip_norm)
    masters = (
        word_table,
        pos_table,
        qkv_weight,
        square_weight,
        up_weight,
        down_weight,
        vec_table,
        head_bias,
    )
    states = (
        (word_first, word_second),
        (pos_first, pos_second),
        (qkv_first, qkv_second),
        (square_first, square_second),
        (up_first, up_second),
        (down_first, down_second),
        (vec_first, vec_second),
        (bias_first, bias_second),
    )
    rates = (
        learn_rate,
        learn_rate,
        learn_rate,
        learn_rate,
        learn_rate,
        learn_rate,
        vector_rate,
        vector_rate,
    )
    grads = tuple(owned) + (bias_grad,)
    results = []
    for weight, state, grad, rate in zip(masters, states, grads, rates):
        results.extend(adam_step(weight, state[0], state[1], grad, factor, rate))
    return (
        results[0],
        results[1],
        results[2],
        results[3],
        results[4],
        results[5],
        results[6],
        results[7],
        results[8],
        results[9],
        results[10],
        results[11],
        results[12],
        results[13],
        results[14],
        results[15],
        results[16],
        results[17],
        results[18],
        results[19],
        results[20],
        results[21],
        results[22],
        results[23],
        loss_total,
        total,
        grad_norm,
    )


def solution(mesh):
    placed = (
        P(("grp", "dp"), None),
        P(("grp", "dp")),
        P(("grp", "dp"), None),
        P(("grp", "dp"), None),
        P(("pipe", "grp", "dp"), None),
        P(("pipe", "grp", "dp"), None),
        P(("pipe", "grp", "dp"), None),
        P(None, ("pipe", "grp", "dp")),
        P(None, ("pipe", "grp", "dp")),
        P(None, ("pipe", "grp", "dp")),
        P(("pipe", "grp", "dp"), None),
        P(("pipe", "grp", "dp"), None),
        P(("pipe", "grp", "dp"), None),
        P(None, ("pipe", "grp", "dp"), None),
        P(None, ("pipe", "grp", "dp"), None),
        P(None, ("pipe", "grp", "dp"), None),
        P(("pipe", "grp", "dp"), None),
        P(("pipe", "grp", "dp"), None),
        P(("pipe", "grp", "dp"), None),
        P(("pipe", "grp", "dp"), None),
        P(("pipe", "grp", "dp"), None),
        P(("pipe", "grp", "dp"), None),
        P(None, ("pipe", "grp", "dp")),
        P(None, ("pipe", "grp", "dp")),
        P(None, ("pipe", "grp", "dp")),
        P(),
        P(),
        P(),
    )
    return jax.shard_map(
        per_device,
        mesh=mesh,
        in_specs=placed,
        out_specs=(
            P(("pipe", "grp", "dp"), None),
            P(("pipe", "grp", "dp"), None),
            P(("pipe", "grp", "dp"), None),
            P(None, ("pipe", "grp", "dp")),
            P(None, ("pipe", "grp", "dp")),
            P(None, ("pipe", "grp", "dp")),
            P(("pipe", "grp", "dp"), None),
            P(("pipe", "grp", "dp"), None),
            P(("pipe", "grp", "dp"), None),
            P(None, ("pipe", "grp", "dp"), None),
            P(None, ("pipe", "grp", "dp"), None),
            P(None, ("pipe", "grp", "dp"), None),
            P(("pipe", "grp", "dp"), None),
            P(("pipe", "grp", "dp"), None),
            P(("pipe", "grp", "dp"), None),
            P(("pipe", "grp", "dp"), None),
            P(("pipe", "grp", "dp"), None),
            P(("pipe", "grp", "dp"), None),
            P(None, ("pipe", "grp", "dp")),
            P(None, ("pipe", "grp", "dp")),
            P(None, ("pipe", "grp", "dp")),
            P(),
            P(),
            P(),
            P(),
            P(),
            P(),
        ),
        check_vma=False,
    )
```
